32 devices in a mesh: fsdp: 2 (over x), ctx: 16 (over z, y, core).
Axes of the slice: x: 2, y: 2, z: 4, core: 2. Of those that a mesh axis runs over, the one named last changes fastest.
Arguments:
- tokens: bfloat16 [8192, 1024], P(('fsdp', 'ctx')), may hold values from -6 to 6
- block_pairs: int32 [16], replicated, may hold values from 0 to 15, each once
- norm_gain: bfloat16 [1024], P('fsdp'), may hold values from 0.5 to 1.5
- norm_bias: bfloat16 [1024], P('fsdp'), may hold values from -4 to 4
- qkv_weight: bfloat16 [1024, 3072], P(None, 'fsdp'), may hold values from -0.1875 to 0.1875
- out_weight: bfloat16 [1024, 1024], P('fsdp'), may hold values from -3 to 3
- up_weight: bfloat16 [1024, 4096], P(None, 'fsdp'), may hold values from -0.1875 to 0.1875
- up_bias: bfloat16 [4096], P('fsdp'), may hold values from -6 to 6
- down_weight: bfloat16 [4096, 1024], P('fsdp'), may hold values from -0.09375 to 0.09375
- down_bias: bfloat16 [1024], P('fsdp'), may hold values from -4 to 4
- cotangent: bfloat16 [8192, 1024], P(('fsdp', 'ctx')), may hold values from -6 to 6
Outputs:
- mixed: bfloat16 [8192, 1024], P(('fsdp', 'ctx'))
- tokens_grad: bfloat16 [8192, 1024], P(('fsdp', 'ctx'))
- norm_gain_grad: float32 [1024], P('fsdp')
- norm_bias_grad: float32 [1024], P('fsdp')
- qkv_weight_grad: float32 [1024, 3072], P(None, 'fsdp')
- out_weight_grad: float32 [1024, 1024], P('fsdp')
- up_weight_grad: float32 [1024, 4096], P(None, 'fsdp')
- up_bias_grad: float32 [4096], P('fsdp')
- down_weight_grad: float32 [4096, 1024], P('fsdp')
- down_bias_grad: float32 [1024], P('fsdp')
The draws below stay inside these ranges and needn't reach their ends.
Inputs may be any that keep to these rules, and one draw needn't show every extreme that they name: a permutation: each ctx device holds block block_pairs[c] and its mirror 2 * (number of ctx devices) - 1 - block_pairs[c] of every sequence.
All inputs are finite; a program needn't handle non-finite values.
Results may differ from the reference program's by a relative error of at most 0.012.
Values may be sent and summed in bfloat16 or wider, within the bound.
A program may use at most 576 MiB of HBM per device.

```python
import math
import jax
import jax.numpy as jnp
from jax import lax

D = 1024
FF = 4096
HEAD_DIM = 64
ROT_DIM = 32
HEADS = 16
SEQ_DEV_TOK = 128
SEQS = 2
LENGTH = 2048
TOKENS = 8192
N_FSDP = 2
N_CTX = 16


def block_scale(key, extent, shards, low, top_value):
    gain = 1.0
    for position, shards_of in shards:
        heights = jax.random.uniform(jax.random.fold_in(jax.random.fold_in(key, 6), position), (shards_of,), jnp.float32, low / len(shards), top_value / len(shards))
        gain = gain * jnp.repeat(jnp.exp(heights), extent[position] // shards_of).reshape((-1,) + (1,) * (len(extent) - 1 - position))
    return gain


def normal_values(rng, extent, scale, bound, cuts=(), kind=jnp.bfloat16):
    values = jax.random.normal(rng, extent, jnp.float32) * scale
    if len(cuts) > 0:
        values = block_scale(rng, extent, cuts, -0.22, 0.18) * values
    return jnp.clip(values, min=-bound, max=bound).astype(kind)


def setup_inputs(seed: int = 0) -> dict:
    seeds = jax.random.split(jax.random.key(seed), 12)
    return {
        "tokens": normal_values(seeds[0], (TOKENS, D), 1.0, 6.0, ((0, 32),)),
        "block_pairs": jax.random.permutation(seeds[1], N_CTX).astype(jnp.int32),
        "norm_gain": jnp.clip(1.0 + 0.1 * jax.random.normal(seeds[2], (D,), jnp.float32), 0.5, 1.5).astype(jnp.bfloat16),
        "norm_bias": normal_values(seeds[3], (D,), 0.3, 4.0, ((0, 2),)),
        "qkv_weight": normal_values(seeds[4], (D, 3 * D), D ** -0.5, 0.1875, ((1, 2),)),
        "out_weight": normal_values(seeds[5], (D, D), (max(D * 8 // LENGTH, 1)) ** -0.5, 3.0, ((0, 2),)),
        "up_weight": normal_values(seeds[6], (D, FF), D ** -0.5, 0.1875, ((1, 2),)),
        "up_bias": normal_values(seeds[7], (FF,), 0.5, 6.0, ((0, 2),)),
        "down_weight": normal_values(seeds[8], (FF, D), FF ** -0.5, 0.09375, ((0, 2),)),
        "down_bias": normal_values(seeds[9], (D,), 0.3, 4.0, ((0, 2),)),
        "cotangent": normal_values(seeds[10], (TOKENS, D), 1.0, 6.0, ((0, 32),)),
    }


@jax.custom_vjp
def low(v):
    return lax.optimization_barrier(v.astype(jnp.bfloat16)).astype(jnp.float32)

@jax.custom_vjp
def low_back(v):
    return v

def low_keep(v):
    return (low(v), None)

def low_pass(kept, grad):
    return (grad,)

def back_keep(v):
    return (v, None)

def back_low(kept, grad):
    return (low(grad),)
low.defvjp(low_keep, low_pass)
low_back.defvjp(back_keep, back_low)
EPS = 1e-05
HIGHEST = lax.Precision.HIGHEST
masked_score = -1e+30

def layer_norm(values, gain_values, shift_values):
    center = values - lax.optimization_barrier(jnp.mean(values, axis=-1, keepdims=True))
    spread = lax.optimization_barrier(jnp.mean(center * center, axis=-1, keepdims=True))
    return center * lax.rsqrt(spread + EPS) * gain_values + shift_values

def rotary(values, cosine, sine):
    turned = values[..., :ROT_DIM]
    remain = values[..., ROT_DIM:]
    even_part = turned[..., 0::2]
    odd_part = turned[..., 1::2]
    new_even = even_part * cosine - odd_part * sine
    new_odd = odd_part * cosine + even_part * sine
    paired = jnp.stack((new_even, new_odd), axis=-1).reshape(turned.shape)
    return jnp.concatenate((paired, remain), axis=-1)

def angles(places):
    steps_up = jnp.arange(0, ROT_DIM, 2).astype(jnp.float32)
    speeds = 10000.0 ** (-steps_up / ROT_DIM)
    phase = places.astype(jnp.float32)[:, None] * speeds[None, :]
    return (jnp.cos(phase), jnp.sin(phase))

def token_places(block_pairs):
    half_rows = SEQ_DEV_TOK // 2
    within = jnp.arange(SEQ_DEV_TOK).astype(jnp.int32)
    chosen = block_pairs.astype(jnp.int32)[:, None]
    block_index = jnp.where(within[None, :] < half_rows, chosen, 2 * N_CTX - 1 - chosen)
    return (block_index * half_rows + within[None, :] % half_rows).reshape(-1)

def sequence_forward(seq_tokens, places, cosine, sine, params):
    gain_values, shift_values, w_qkv, w_out, w_up, b_up, w_down, b_down = params
    length_rows = seq_tokens.shape[0]
    normed = low(layer_norm(seq_tokens, gain_values, shift_values))
    mixed_qkv = low_back(jnp.dot(normed, w_qkv, precision=HIGHEST))
    parts = mixed_qkv.reshape(length_rows, 3, HEADS, HEAD_DIM)
    queries = low(rotary(parts[:, 0], cosine[:, None, :], sine[:, None, :]))
    key_rows = low(rotary(parts[:, 1], cosine[:, None, :], sine[:, None, :]))
    value_rows = low(parts[:, 2])
    block_rows = math.gcd(length_rows, 512)

    def attend_block(item):
        query_block, query_places = item
        scores = low_back(jnp.einsum('qhe,khe->hqk', query_block, key_rows, precision=HIGHEST) * HEAD_DIM ** (-0.5))
        allowed = places[None, None, :] <= query_places[None, :, None]
        scores = jnp.where(allowed, scores, masked_score)
        highest = lax.optimization_barrier(jnp.max(scores, axis=-1, keepdims=True))
        weights = jnp.exp(scores - highest)
        chances = weights / lax.optimization_barrier(jnp.sum(weights, axis=-1, keepdims=True))
        return jnp.einsum('hqk,khe->qhe', low(chances), value_rows, precision=HIGHEST)
    blocks_out = lax.map(jax.checkpoint(attend_block), (queries.reshape(length_rows // block_rows, block_rows, HEADS, HEAD_DIM), places.reshape(length_rows // block_rows, block_rows)))
    attended = low(low_back(blocks_out.reshape(length_rows, HEADS * HEAD_DIM)))
    attention = jnp.dot(attended, w_out, precision=HIGHEST)
    up_pre = low_back(jnp.dot(normed, w_up, precision=HIGHEST) + b_up)
    hidden = low(jax.nn.gelu(up_pre, approximate=True))
    return seq_tokens + attention + jnp.dot(hidden, w_down, precision=HIGHEST) + b_down

def reference(tokens, block_pairs, norm_gain, norm_bias, qkv_weight, out_weight, up_weight, up_bias, down_weight, down_bias, cotangent):
    seq_total = N_FSDP * SEQS
    length_rows = SEQ_DEV_TOK * N_CTX

    def arrange(array):
        shaped = array.astype(jnp.float32).reshape(N_FSDP, N_CTX, SEQ_DEV_TOK, SEQS, D)
        return shaped.transpose(0, 3, 1, 2, 4).reshape(seq_total, length_rows, D)

    def restore(array):
        shaped = array.reshape(N_FSDP, SEQS, N_CTX, SEQ_DEV_TOK, D)
        return shaped.transpose(0, 2, 3, 1, 4).reshape(N_FSDP * N_CTX * SEQ_DEV_TOK * SEQS, D)
    places = token_places(block_pairs)
    cosine, sine = angles(places)
    params = tuple((entry.astype(jnp.float32) for entry in (norm_gain, norm_bias, qkv_weight, out_weight, up_weight, up_bias, down_weight, down_bias)))

    def forward(sequences, weights):

        def step(carry, seq_tokens):
            return (carry, sequence_forward(seq_tokens, places, cosine, sine, weights))
        _, results = lax.scan(step, jnp.zeros((), jnp.float32), sequences)
        return results
    results, pullback = jax.vjp(forward, arrange(tokens), params)
    input_grads, param_grads = pullback(arrange(cotangent))
    gain_grad, shift_grad, qkv_grad, out_grad, up_grad, upb_grad, down_grad, downb_grad = param_grads
    return (restore(results).astype(jnp.bfloat16), restore(input_grads).astype(jnp.bfloat16), gain_grad, shift_grad, qkv_grad, out_grad, up_grad, upb_grad, down_grad, downb_grad)
```

```python
import functools
import math

import jax
import jax.numpy as jnp
from jax import lax
from jax.experimental import pallas as pl
from jax.experimental.pallas import tpu as pltpu
from jax.sharding import PartitionSpec as P

D = 1024
HEAD_DIM = 64
ROT_DIM = 32
HEADS = 16
SEQ_DEV_TOK = 128
SEQS = 2


EPS = 1e-05
HIGHEST = lax.Precision.HIGHEST
masked_score = -1e30


def layer_norm(values, gain_values, shift_values):
    center = values - jnp.mean(values, axis=-1, keepdims=True)
    spread = jnp.mean(center * center, axis=-1, keepdims=True)
    return center * lax.rsqrt(spread + EPS) * gain_values + shift_values


def rotary_tables(places, window):
    lanes = jnp.arange(window, dtype=jnp.int32)
    within_head = lanes % HEAD_DIM
    turning = within_head < ROT_DIM
    steps_up = (within_head // 2 * 2).astype(jnp.float32)
    speeds = 10000.0 ** (-steps_up / ROT_DIM)
    phase = places.astype(jnp.float32)[:, None] * speeds[None, :]
    cos_full = jnp.where(turning[None, :], jnp.cos(phase), 1.0)
    sin_full = jnp.where(turning[None, :], jnp.sin(phase), 0.0)
    row_lane = lanes[:, None]
    col_lane = lanes[None, :]
    same_head = row_lane // HEAD_DIM == col_lane // HEAD_DIM
    col_within = col_lane % HEAD_DIM
    col_turns = same_head & (col_within < ROT_DIM)
    even_col = col_within % 2 == 0
    minus_part = jnp.where(col_turns & even_col & (row_lane == col_lane + 1), -1.0, 0.0)
    plus_part = jnp.where(
        col_turns & jnp.logical_not(even_col) & (row_lane == col_lane - 1), 1.0, 0.0
    )
    swap_table = (minus_part + plus_part).astype(jnp.float32)
    return (cos_full, sin_full, swap_table)


def smooth_gate(values):
    return jax.nn.gelu(values, approximate=True)


def positions(first_row, row_count, pair_table, devices, seq_rows):
    indices = first_row + jnp.arange(row_count, dtype=jnp.int32)
    owners = indices // seq_rows
    within = indices % seq_rows
    half_rows = seq_rows // 2
    matches = owners[:, None] == jnp.arange(devices, dtype=jnp.int32)[None, :]
    chosen = jnp.sum(jnp.where(matches, pair_table[None, :], 0), axis=1)
    block_index = jnp.where(within < half_rows, chosen, 2 * devices - 1 - chosen)
    return block_index * half_rows + within % half_rows


def in_groups(row_count, seq_rows):
    group_rows = math.gcd(row_count // seq_rows, 8) * seq_rows
    return (group_rows, row_count // group_rows)


def split_groups(array, group_rows, turns):
    return array.reshape((turns, group_rows) + array.shape[1:])


def grad_scores(
    query_rows,
    out_grads,
    log_sums,
    row_dots,
    query_places,
    key_rows,
    value_rows,
    key_places,
    factor,
):
    scores = (
        jnp.einsum("qshe,kshe->shqk", query_rows, key_rows, preferred_element_type=jnp.float32)
        * factor
    )
    allowed = key_places[None, :] <= query_places[:, None]
    chances = jnp.exp(jnp.where(allowed, scores - log_sums[..., None], masked_score))
    prob_grads = jnp.einsum(
        "qshe,kshe->shqk", out_grads, value_rows, preferred_element_type=jnp.float32
    )
    return (chances, (chances * (prob_grads - row_dots[..., None])).astype(jnp.bfloat16))


def per_device(
    tokens,
    block_pairs,
    norm_gain,
    norm_bias,
    qkv_weight,
    out_weight,
    up_weight,
    up_bias,
    down_weight,
    down_bias,
    cotangent,
):
    devices = lax.axis_size("ctx")
    own_index = lax.axis_index("ctx")
    seq_rows = SEQ_DEV_TOK
    seq_count = SEQS
    heads = HEADS
    head_size = HEAD_DIM
    width = D
    factor = HEAD_DIM ** (-0.5)
    all_rows = seq_rows * seq_count
    window = math.gcd(width, 128)
    gathered = (
        lax.all_gather(norm_gain, "fsdp", axis=0, tiled=True),
        lax.all_gather(norm_bias, "fsdp", axis=0, tiled=True),
        lax.all_gather(qkv_weight, "fsdp", axis=1, tiled=True),
        lax.all_gather(out_weight, "fsdp", axis=0, tiled=True),
        lax.all_gather(up_weight, "fsdp", axis=1, tiled=True),
        lax.all_gather(up_bias, "fsdp", axis=0, tiled=True),
        lax.all_gather(down_weight, "fsdp", axis=0, tiled=True),
        lax.all_gather(down_bias, "fsdp", axis=0, tiled=True),
    )
    gain_low, shift_low, w_qkv, w_out, w_up, b_up, w_down, b_down = gathered
    inputs = tokens.astype(jnp.float32)
    gain_values = gain_low.astype(jnp.float32)
    shift_values = shift_low.astype(jnp.float32)
    normed_low = layer_norm(inputs, gain_values, shift_values).astype(jnp.bfloat16)
    mixed_qkv = jnp.dot(normed_low, w_qkv, preferred_element_type=jnp.float32).reshape(
        seq_rows, seq_count, 3 * width
    )
    own_places = positions(own_index * seq_rows, seq_rows, block_pairs, devices, seq_rows)
    cos_full, sin_full, swap_table = rotary_tables(own_places, window)

    def turn_both(values):
        shaped = values.reshape(seq_rows, seq_count, 2 * width // window, window)
        swapped = jnp.einsum("rsgw,wv->rsgv", shaped, swap_table, precision=HIGHEST)
        turned_rows = shaped * cos_full[:, None, None, :] + swapped * sin_full[:, None, None, :]
        return turned_rows.reshape(seq_rows, seq_count, 2 * width)

    query_key = mixed_qkv[:, :, : 2 * width]
    turned = turn_both(query_key)
    queries = (
        turned[:, :, :width].astype(jnp.bfloat16).reshape(seq_rows, seq_count, heads, head_size)
    )
    key_rows = (
        turned[:, :, width:].astype(jnp.bfloat16).reshape(seq_rows, seq_count, heads, head_size)
    )
    value_rows = (
        mixed_qkv[:, :, 2 * width :]
        .astype(jnp.bfloat16)
        .reshape(seq_rows, seq_count, heads, head_size)
    )
    start_state = (
        jnp.full((seq_count, heads, seq_rows), masked_score, jnp.float32),
        jnp.zeros((seq_count, heads, seq_rows), jnp.float32),
        jnp.zeros((seq_count, heads, seq_rows, head_size), jnp.float32),
    )
    piece_keys = lax.all_gather(key_rows, "ctx", axis=0, tiled=True)
    piece_values = lax.all_gather(value_rows, "ctx", axis=0, tiled=True)
    group_rows, turns = in_groups(piece_keys.shape[0], seq_rows)

    def attend_step(inner, item):
        block_keys, block_values, turn = item
        key_places = positions(turn * group_rows, group_rows, block_pairs, devices, seq_rows)
        scores = (
            jnp.einsum("qshe,kshe->shqk", queries, block_keys, preferred_element_type=jnp.float32)
            * factor
        )
        allowed = key_places[None, :] <= own_places[:, None]
        running, totals, accum = inner
        fresh = jnp.maximum(running, jnp.max(jnp.where(allowed, scores, masked_score), axis=-1))
        weights = jnp.exp(jnp.where(allowed, scores - fresh[..., None], masked_score))
        fading = jnp.exp(running - fresh)
        totals = totals * fading + jnp.sum(weights, axis=-1)
        accum = accum * fading[..., None] + jnp.einsum(
            "shqk,kshe->shqe",
            weights.astype(jnp.bfloat16),
            block_values,
            preferred_element_type=jnp.float32,
        )
        return ((fresh, totals, accum), None)

    inner, _ = lax.scan(
        attend_step,
        start_state,
        (
            split_groups(piece_keys, group_rows, turns),
            split_groups(piece_values, group_rows, turns),
            jnp.arange(turns, dtype=jnp.int32),
        ),
    )
    running, totals, accum = inner
    log_sums = running + jnp.log(totals)
    attended = jnp.transpose(accum / totals[..., None], (2, 0, 1, 3))
    attn_low = attended.reshape(all_rows, width).astype(jnp.bfloat16)
    attention = jnp.dot(attn_low, w_out, preferred_element_type=jnp.float32)
    up_pre = jnp.dot(normed_low, w_up, preferred_element_type=jnp.float32) + b_up.astype(
        jnp.float32
    )
    hidden_low = smooth_gate(up_pre).astype(jnp.bfloat16)
    result = (
        inputs
        + attention
        + jnp.dot(hidden_low, w_down, preferred_element_type=jnp.float32)
        + b_down.astype(jnp.float32)
    )
    mixed = result.astype(jnp.bfloat16)
    again = (
        lax.all_gather(norm_gain, "fsdp", axis=0, tiled=True),
        lax.all_gather(norm_bias, "fsdp", axis=0, tiled=True),
        lax.all_gather(qkv_weight, "fsdp", axis=1, tiled=True),
        lax.all_gather(out_weight, "fsdp", axis=0, tiled=True),
        lax.all_gather(up_weight, "fsdp", axis=1, tiled=True),
        lax.all_gather(up_bias, "fsdp", axis=0, tiled=True),
        lax.all_gather(down_weight, "fsdp", axis=0, tiled=True),
        lax.all_gather(down_bias, "fsdp", axis=0, tiled=True),
    )
    gain_low, shift_low, w_qkv, w_out, w_up, b_up, w_down, b_down = again
    out_grad = cotangent.astype(jnp.float32)
    attn_grads = (
        jnp.einsum("td,ed->te", cotangent, w_out, preferred_element_type=jnp.float32)
        .astype(jnp.bfloat16)
        .reshape(seq_rows, seq_count, heads, head_size)
    )
    dots_rows = jnp.sum(attn_grads.astype(jnp.float32) * attended, axis=-1)
    row_dots = jnp.transpose(dots_rows, (1, 2, 0))
    empty_rows = jnp.zeros((seq_rows, seq_count, heads, head_size), jnp.float32)
    whole_keys, whole_values = (
        lax.all_gather(key_rows, "ctx", axis=0, tiled=True),
        lax.all_gather(value_rows, "ctx", axis=0, tiled=True),
    )
    piece_keys = whole_keys
    piece_values = whole_values
    query_group_rows, turns = in_groups(piece_keys.shape[0], seq_rows)

    def query_step(inner, item):
        block_keys, block_values, turn = item
        key_places = positions(
            0 + turn * query_group_rows, query_group_rows, block_pairs, devices, seq_rows
        )
        chances, score_grads = grad_scores(
            queries,
            attn_grads,
            log_sums,
            row_dots,
            own_places,
            block_keys,
            block_values,
            key_places,
            factor,
        )
        return (
            inner
            + jnp.einsum(
                "shqk,kshe->qshe", score_grads, block_keys, preferred_element_type=jnp.float32
            )
            * factor,
            None,
        )

    inner, _ = lax.scan(
        query_step,
        empty_rows,
        (
            split_groups(piece_keys, query_group_rows, turns),
            split_groups(piece_values, query_group_rows, turns),
            jnp.arange(turns, dtype=jnp.int32),
        ),
    )
    query_grad = inner
    piece_keys = whole_keys
    piece_values = whole_values
    key_group_rows, turns = in_groups(seq_rows * lax.axis_size("ctx"), seq_rows)

    def key_step(inner, item):
        block_keys, block_values, turn = item
        key_places = positions(
            turn * key_group_rows, key_group_rows, block_pairs, devices, seq_rows
        )
        chances, score_grads = grad_scores(
            queries,
            attn_grads,
            log_sums,
            row_dots,
            own_places,
            block_keys,
            block_values,
            key_places,
            factor,
        )
        key_part = (
            jnp.einsum("shqk,qshe->kshe", score_grads, queries, preferred_element_type=jnp.float32)
            * factor
        )
        value_part = jnp.einsum(
            "shqk,qshe->kshe",
            chances.astype(jnp.bfloat16),
            attn_grads,
            preferred_element_type=jnp.float32,
        )
        stacked = jnp.stack(
            (
                key_part.reshape(key_group_rows, seq_count, width),
                value_part.reshape(key_group_rows, seq_count, width),
            ),
            axis=2,
        )
        return (inner, stacked)

    _, blocks_out = lax.scan(
        key_step,
        jnp.zeros((), jnp.float32),
        (
            split_groups(piece_keys, key_group_rows, turns),
            split_groups(piece_values, key_group_rows, turns),
            jnp.arange(turns, dtype=jnp.int32),
        ),
    )
    summed_terms = lax.psum_scatter(
        blocks_out.reshape(seq_rows * lax.axis_size("ctx"), seq_count, 2, width),
        "ctx",
        scatter_dimension=0,
        tiled=True,
    )
    key_grad = summed_terms[:, :, 0].reshape(seq_rows, seq_count, heads, head_size)
    value_grad = summed_terms[:, :, 1].reshape(seq_rows, seq_count, heads, head_size)
    _, turn_back = jax.vjp(turn_both, query_key)
    both_grads = jnp.concatenate(
        (
            query_grad.reshape(seq_rows, seq_count, width),
            key_grad.reshape(seq_rows, seq_count, width),
        ),
        axis=2,
    )
    (pre_grads,) = turn_back(both_grads)
    qkv_grad = (
        jnp.concatenate((pre_grads, value_grad.reshape(seq_rows, seq_count, width)), axis=2)
        .reshape(all_rows, 3 * width)
        .astype(jnp.bfloat16)
    )
    hidden_grad = jnp.einsum("td,fd->tf", cotangent, w_down, preferred_element_type=jnp.float32)
    _, gate_back = jax.vjp(smooth_gate, up_pre)
    (up_grad,) = gate_back(hidden_grad)
    up_low = up_grad.astype(jnp.bfloat16)
    normed_grad = jnp.einsum(
        "tc,dc->td", qkv_grad, w_qkv, preferred_element_type=jnp.float32
    ) + jnp.einsum("tf,df->td", up_low, w_up, preferred_element_type=jnp.float32)
    _, norm_back = jax.vjp(
        layer_norm, inputs, gain_low.astype(jnp.float32), shift_low.astype(jnp.float32)
    )
    input_part, gain_grad, shift_grad = norm_back(normed_grad)
    tokens_grad = (out_grad + input_part).astype(jnp.bfloat16)
    qkv_wgrad = jnp.einsum("td,tc->dc", normed_low, qkv_grad, preferred_element_type=jnp.float32)
    out_wgrad = jnp.einsum("td,te->de", attn_low, cotangent, preferred_element_type=jnp.float32)
    up_wgrad = jnp.einsum("td,tf->df", normed_low, up_low, preferred_element_type=jnp.float32)
    up_bgrad = jnp.sum(up_low.astype(jnp.float32), axis=0)
    down_wgrad = jnp.einsum("tf,td->fd", hidden_low, cotangent, preferred_element_type=jnp.float32)
    down_bgrad = jnp.sum(out_grad, axis=0)
    shares = (
        lax.psum_scatter(
            gain_grad.astype(jnp.bfloat16), "fsdp", scatter_dimension=0, tiled=True
        ).astype(jnp.float32),
        lax.psum_scatter(
            shift_grad.astype(jnp.bfloat16), "fsdp", scatter_dimension=0, tiled=True
        ).astype(jnp.float32),
        lax.psum_scatter(
            qkv_wgrad.astype(jnp.bfloat16), "fsdp", scatter_dimension=1, tiled=True
        ).astype(jnp.float32),
        lax.psum_scatter(
            out_wgrad.astype(jnp.bfloat16), "fsdp", scatter_dimension=0, tiled=True
        ).astype(jnp.float32),
        lax.psum_scatter(
            up_wgrad.astype(jnp.bfloat16), "fsdp", scatter_dimension=1, tiled=True
        ).astype(jnp.float32),
        lax.psum_scatter(
            up_bgrad.astype(jnp.bfloat16), "fsdp", scatter_dimension=0, tiled=True
        ).astype(jnp.float32),
        lax.psum_scatter(
            down_wgrad.astype(jnp.bfloat16), "fsdp", scatter_dimension=0, tiled=True
        ).astype(jnp.float32),
        lax.psum_scatter(
            down_bgrad.astype(jnp.bfloat16), "fsdp", scatter_dimension=0, tiled=True
        ).astype(jnp.float32),
    )
    share_gain, share_shift, share_qkv, share_out, share_up, share_upb, share_down, share_downb = (
        shares
    )
    totals_out = lax.psum(
        (
            share_gain,
            share_shift,
            share_qkv,
            share_out,
            share_up,
            share_upb,
            share_down,
            share_downb,
        ),
        "ctx",
    )
    sum_gain, sum_shift, sum_qkv, sum_out, sum_up, sum_upb, sum_down, sum_downb = totals_out
    return (
        mixed,
        tokens_grad,
        sum_gain,
        sum_shift,
        sum_qkv,
        sum_out,
        sum_up,
        sum_upb,
        sum_down,
        sum_downb,
    )


F32 = jnp.float32
BF16 = jnp.bfloat16
FF = 4096
FSDP = 2
CHIPS = 8
ROWS = SEQ_DEV_TOK * SEQS
ALL = 4 * ROWS
LENGTH = CHIPS * 2 * SEQ_DEV_TOK
HALF = SEQ_DEV_TOK // 2
QB = 256
NCH = 12
MASKS = (1, 2, 4)
SCALE = HEAD_DIM**-0.5


def fits(mesh):
    return mesh.shape["fsdp"] == FSDP and mesh.shape["ctx"] == 2 * CHIPS


def dot(left, right):
    return lax.dot_general(left, right, (((1,), (0,)), ((), ())), preferred_element_type=F32)


def dot_nt(left, right):
    return lax.dot_general(left, right, (((1,), (1,)), ((), ())), preferred_element_type=F32)


def dot_tn(left, right):
    return lax.dot_general(left, right, (((0,), (0,)), ((), ())), preferred_element_type=F32)


def turn(values, cosine, sine):
    lane = lax.broadcasted_iota(jnp.int32, values.shape, 1)
    width = values.shape[1]
    other = jnp.where(
        lane % 2 == 0, pltpu.roll(values, width - 1, 1), pltpu.roll(values, 1, 1)
    )
    return values * cosine + other * sine


def gate(values):
    inner = 0.7978845608028654 * (values + 0.044715 * values * values * values)
    th = jnp.tanh(inner)
    half = 0.5 * (1.0 + th)
    slope = half + (0.5 * values) * (1.0 - th * th) * (
        0.7978845608028654 * (1.0 + 3 * 0.044715 * values * values)
    )
    return values * half, slope


def fused_kernel(
    places_ref,
    halves_ref,
    blocks_ref,
    vec_ref,
    upb_ref,
    cos_ref,
    sin_ref,
    scos_ref,
    ssin_ref,
    tok_ref,
    cot_ref,
    wqkv_h,
    wout_h,
    wup_h,
    wdn_h,
    mixed_ref,
    tgrad_ref,
    small_ref,
    odn,
    oup,
    oqkv,
    oout,
    vall,
    xs,
    nrm,
    gal,
    wq,
    wout,
    wup,
    wdn,
    hid,
    upg,
    sbuf,
    rbuf,
    aq,
    ag,
    ak,
    av,
    akt,
    avt,
    agt,
    sco,
    dka,
    dva,
    osrt,
    rb2,
    aall,
    dqkv,
    mats,
    rs0,
    rs1,
    rs2,
    xsw,
    own_acc,
    red_s,
    red_x,
    red_r,
    red_xr,
    sm,
    smg,
    sma,
    lsem,
    gsend,
    grecv,
    asend,
    arecv,
    osend,
    orecv,
    rssend,
    rsrecv,
    agsend,
    agrecv,
    clocal,
    csend,
    crecv,
    dsend,
    drecv,
    smsend,
    smrecv,
):
    f = lax.axis_index("fsdp")
    c = lax.axis_index("ctx")
    k = c % 2
    p = c // 2
    zz = p // 2
    yy = p % 2
    xpart = (1 - f, c)
    sibling = (f, 2 * p + 1 - k)
    diagonal = (1 - f, 2 * p + 1 - k)
    own = 2 * f + k
    sibb = 2 * f + 1 - k
    xb = 2 * (1 - f) + k
    dg = 2 * (1 - f) + 1 - k
    MESH = pl.DeviceIdType.MESH

    def member(q):
        return (f, 2 * q + k)

    def remote(src, dst, ssem, rsem, device):
        return pltpu.make_async_remote_copy(
            src_ref=src,
            dst_ref=dst,
            send_sem=ssem,
            recv_sem=rsem,
            device_id=device,
            device_id_type=MESH,
        )

    def rows(b):
        return pl.ds(pl.multiple_of(b * ROWS, ROWS), ROWS)

    def lanes(i, n):
        return pl.ds(pl.multiple_of(i * n, n), n)

    loads = [
        pltpu.make_async_copy(wqkv_h.at[:, lanes(k, 256)], wq.at[f], lsem.at[0]),
        pltpu.make_async_copy(
            wqkv_h.at[:, pl.ds(pl.multiple_of(1024 + 256 * k, 256), 256)], wq.at[1 + f], lsem.at[1]
        ),
        pltpu.make_async_copy(wup_h.at[:, lanes(k, 1024)], wup, lsem.at[2]),
        pltpu.make_async_copy(wdn_h.at[lanes(k, 1024), :], wdn, lsem.at[3]),
        pltpu.make_async_copy(wout_h.at[lanes(k, 256), :], wout, lsem.at[4]),
    ]
    for load in loads:
        load.start()

    barrier = pltpu.get_barrier_semaphore()
    for device in [xpart, sibling, diagonal] + [member(p ^ i) for i in range(1, CHIPS)]:
        pl.semaphore_signal(barrier, inc=1, device_id=device, device_id_type=MESH)
    pl.semaphore_wait(barrier, 3 + CHIPS - 1)

    vec_copy = remote(vec_ref, vall.at[f], gsend.at[0], grecv.at[0], xpart)
    vec_copy.start()
    swap_copy = remote(
        wqkv_h.at[:, pl.ds(pl.multiple_of(512 + 256 * k, 256), 256)],
        wq.at[2 * f],
        gsend.at[1],
        grecv.at[1],
        xpart,
    )
    swap_copy.start()
    vall[f] = vec_ref[...]
    vec_copy.wait()
    gain = jnp.concatenate([vall[0, 0:1, :], vall[1, 0:1, :]], axis=1).astype(F32)
    shift = jnp.concatenate([vall[0, 1:2, :], vall[1, 1:2, :]], axis=1).astype(F32)
    down_b = jnp.concatenate([vall[0, 2:3, :], vall[1, 2:3, :]], axis=1).astype(F32)

    step = 64

    def norm_rows(i, carry):
        here = pl.ds(pl.multiple_of(i * step, step), step)
        there = pl.ds(pl.multiple_of(own * ROWS + i * step, step), step)
        row = lax.broadcasted_iota(jnp.int32, (step, ROWS), 0) + i * step
        col = lax.broadcasted_iota(jnp.int32, (step, ROWS), 1)
        pick = (col == 2 * (row % SEQ_DEV_TOK) + row // SEQ_DEV_TOK).astype(F32).astype(BF16)
        values = dot(pick, tok_ref[...])
        gal[there, :] = dot(pick, cot_ref[...]).astype(BF16)
        xs[here, :] = values.astype(BF16)
        center = values - jnp.mean(values, axis=1, keepdims=True)
        spread = jnp.mean(center * center, axis=1, keepdims=True)
        nrm[there, :] = (center * lax.rsqrt(spread + EPS) * gain + shift).astype(BF16)
        return carry

    lax.fori_loop(0, ROWS // step, norm_rows, 0)

    def spread_copy(buf, b, n, device):
        return remote(buf.at[rows(b)], buf.at[rows(b)], gsend.at[n], grecv.at[n], device)

    n_sib = spread_copy(nrm, own, 2, sibling)
    n_x = spread_copy(nrm, own, 3, xpart)
    g_sib = spread_copy(gal, own, 4, sibling)
    g_x = spread_copy(gal, own, 5, xpart)
    for copy in (n_sib, n_x, g_sib, g_x):
        copy.start()
    for load in loads:
        load.wait()

    def feed_block(b):
        def part(i, carry):
            cols = lanes(i, 256)
            up = dot(nrm[rows(b), :], wup[:, cols]) + upb_ref[0:1, cols].astype(F32)
            value, slope = gate(up)
            hid[rows(b), cols] = value.astype(BF16)
            back = dot_nt(gal[rows(b), :], wdn[cols, :])
            upg[rows(b), cols] = (back * slope).astype(BF16)
            return carry

        lax.fori_loop(0, 4, part, 0)

    def put_heads(first, second, fq, kq, t):
        for h in range(4):
            sbuf[2 * h + fq, t, kq] = jnp.concatenate(
                [first[:, 64 * h : 64 * h + 64], second[:, 64 * h : 64 * h + 64]], axis=1
            ).reshape(4, HALF, 128)

    def turned(values, kq):
        parts = []
        for s in range(SEQS):
            line = []
            for half in range(2):
                piece = values[128 * s : 128 * s + 128, 128 * half : 128 * half + 128]
                line.append(turn(piece, cos_ref[kq], sin_ref[kq]))
            parts.append(jnp.concatenate(line, axis=1))
        return jnp.concatenate(parts, axis=0).astype(BF16)

    def qk_block(b, fq, kq):
        normed = nrm[rows(b), :]
        query = dot(normed, wq[0])
        key = dot(normed, wq[1])
        put_heads(turned(query, kq) * BF16(SCALE), turned(key, kq), fq, kq, 0)

    def vg_block(b, fq, kq):
        value = dot(nrm[rows(b), :], wq[2]).astype(BF16)
        grads = dot_nt(gal[rows(b), :], wout[...]).astype(BF16)
        put_heads(value, grads, fq, kq, 1)

    def in_copy(q, t, kq):
        return remote(
            sbuf.at[q, t, kq],
            rbuf.at[2 * p + kq, t],
            asend.at[q, t, kq],
            arecv.at[p, t, kq],
            member(q),
        )

    def send_block(fq, kq, t):
        for i in range(4):
            q = 2 * (zz ^ i) + fq
            if i == 0:

                @pl.when(fq == yy)
                def _():
                    pltpu.make_async_copy(
                        sbuf.at[q, t, kq], rbuf.at[2 * p + kq, t], arecv.at[p, t, kq]
                    ).start()

                @pl.when(fq != yy)
                def _():
                    in_copy(q, t, kq).start()
            else:
                in_copy(q, t, kq).start()

    def sent_block(fq, kq, t):
        for i in range(4):
            q = 2 * (zz ^ i) + fq
            if i == 0:

                @pl.when(fq != yy)
                def _():
                    in_copy(q, t, kq).wait_send()
            else:
                in_copy(q, t, kq).wait_send()

    feed_block(own)
    n_sib.wait_recv()
    g_sib.wait_recv()
    feed_block(sibb)
    swap_copy.wait_recv()
    for b, kq in ((own, k), (sibb, 1 - k)):
        qk_block(b, f, kq)
        send_block(f, kq, 0)
        vg_block(b, f, kq)
        send_block(f, kq, 1)
    n_x.wait_recv()
    n_dg = spread_copy(nrm, xb, 6, sibling)
    n_dg.start()
    qk_block(xb, 1 - f, k)
    send_block(1 - f, k, 0)
    n_dg.wait_recv()
    qk_block(dg, 1 - f, 1 - k)
    send_block(1 - f, 1 - k, 0)
    g_x.wait_recv()
    g_dg = spread_copy(gal, xb, 7, sibling)
    g_dg.start()
    vg_block(xb, 1 - f, k)
    send_block(1 - f, k, 1)
    g_dg.wait_recv()
    vg_block(dg, 1 - f, 1 - k)
    send_block(1 - f, 1 - k, 1)
    feed_block(xb)
    feed_block(dg)

    def down_part(i, carry):
        full = dot_tn(hid[:, lanes(i, 256)], gal[...]).astype(BF16)
        for cc in range(4):
            mats[cc, lanes(i, 256), :] = full[:, 256 * cc : 256 * cc + 256]
        return carry

    lax.fori_loop(0, 4, down_part, 0)

    def up_part(i, carry):
        full = dot_tn(nrm[:, lanes(i, 256)], upg[...]).astype(BF16)
        for cc in range(4):
            mats[4 + cc, lanes(i, 256), :] = full[:, 256 * cc : 256 * cc + 256]
        return carry

    lax.fori_loop(0, 4, up_part, 0)

    sm[...] = jnp.zeros_like(sm)
    sm[0:1, :] = jnp.sum(upg[...].astype(F32), axis=0, keepdims=True)
    sm[2:3, :] = jnp.sum(gal[...].astype(F32), axis=0, keepdims=True)

    def bit(mask):
        return (p // mask) % 2

    def base(ph):
        at = 0
        for j in range(ph):
            at = at + bit(MASKS[j]) * (512 >> j)
        return at

    rsb = (rs0, rs1, rs2)

    def chunk_rows(ph, side, n):
        return pl.ds(pl.multiple_of(base(ph) + side * n, n), n)

    def rs_copy(ch, ph):
        n = 512 >> ph
        side = bit(MASKS[ph])
        return remote(
            mats.at[ch, chunk_rows(ph, 1 - side, n)],
            rsb[ph].at[ch],
            rssend.at[ch, ph],
            rsrecv.at[ch, ph],
            member(p ^ MASKS[ph]),
        )

    def rs_add(ch, ph):
        n = 512 >> ph
        at = base(ph) + bit(MASKS[ph]) * n
        rs_copy(ch, ph).wait_recv()

        def add(i, carry):
            here = pl.ds(pl.multiple_of(at + i * 128, 128), 128)
            there = pl.ds(pl.multiple_of(i * 128, 128), 128)
            mats[ch, here, :] = (
                mats[ch, here, :].astype(F32) + rsb[ph][ch, there, :].astype(F32)
            ).astype(BF16)
            return carry

        lax.fori_loop(0, n // 128, add, 0)

    def out_slice(ch, kk, at, n):
        there = pl.ds(pl.multiple_of(at, n), n)
        if ch < 4:
            return odn.at[pl.ds(pl.multiple_of(kk * 1024 + at, n), n), 256 * ch : 256 * ch + 256]
        if ch < 8:
            cols = pl.ds(pl.multiple_of(kk * 1024 + (ch - 4) * 256, 256), 256)
            return oup.at[there, cols]
        if ch < 11:
            start = (0, 1024, 512)[ch - 8]
            return oqkv.at[there, pl.ds(pl.multiple_of(start + kk * 256, 256), 256)]
        return oout.at[there, pl.ds(pl.multiple_of(kk * 256, 256), 256)]

    def shard(ch):
        if ch == 10:
            return xsw
        return mats.at[ch, pl.ds(pl.multiple_of(base(3), 128), 128)]

    def swap_shard():
        return remote(
            mats.at[10, pl.ds(pl.multiple_of(base(3), 128), 128)],
            xsw,
            gsend.at[8],
            grecv.at[8],
            xpart,
        )

    def local_copy(ch):
        return pltpu.make_async_copy(shard(ch), out_slice(ch, k, base(3), 128), clocal.at[ch])

    def ag_copy(ch, ph):
        n = 512 >> ph
        at = base(ph) + bit(MASKS[ph]) * n
        src = shard(ch) if ph == 2 else out_slice(ch, k, at, n)
        return remote(
            src,
            out_slice(ch, k, at, n),
            agsend.at[ch, ph],
            agrecv.at[ch, ph],
            member(p ^ MASKS[ph]),
        )

    def core_copy(ch):
        return remote(
            out_slice(ch, k, 0, 1024),
            out_slice(ch, k, 0, 1024),
            csend.at[ch],
            crecv.at[ch],
            sibling,
        )

    def advance(ch, stage):
        if stage == 0:
            rs_copy(ch, 0).start()
        elif stage <= 2:
            rs_add(ch, stage - 1)
            rs_copy(ch, stage).start()
        elif stage == 3:
            rs_add(ch, 2)
            if ch == 10:
                swap_shard().start()
                swap_shard().wait_recv()
            local_copy(ch).start()
            ag_copy(ch, 2).start()
        elif stage == 4:
            ag_copy(ch, 2).wait_recv()
            local_copy(ch).wait()
            ag_copy(ch, 1).start()
        elif stage == 5:
            ag_copy(ch, 1).wait_recv()
            ag_copy(ch, 0).start()
        elif stage == 6:
            ag_copy(ch, 0).wait_recv()
            core_copy(ch).start()
        elif stage == 7:
            core_copy(ch).wait_recv()

    def settle(ch):
        for ph in range(3):
            rs_copy(ch, ph).wait_send()
            ag_copy(ch, ph).wait_send()
        core_copy(ch).wait_send()
        if ch == 10:
            swap_shard().wait_send()

    for ch in range(8):
        advance(ch, 0)

    for fq, kq in ((f, k), (f, 1 - k), (1 - f, k), (1 - f, 1 - k)):
        for t in range(2):
            sent_block(fq, kq, t)
    for q in range(CHIPS):
        for t in range(2):
            for kq in range(2):
                pltpu.make_async_copy(
                    rbuf.at[2 * q + kq, t], rbuf.at[2 * q + kq, t], arecv.at[q, t, kq]
                ).wait()

    def load_half(place, t, u):
        return rbuf[places_ref[place], t, 2 * u + halves_ref[place]]

    def sort_rows(i, carry):
        for u in range(SEQS):
            here = pl.ds(pl.multiple_of(i * 128, 128), 128)
            qk = jnp.concatenate([load_half(2 * i, 0, u), load_half(2 * i + 1, 0, u)], axis=0)
            vg = jnp.concatenate([load_half(2 * i, 1, u), load_half(2 * i + 1, 1, u)], axis=0)
            aq[u, here, :] = qk[:, :64]
            ak[u, here, :] = qk[:, 64:]
            av[u, here, :] = vg[:, :64]
            ag[u, here, :] = vg[:, 64:]
            akt[u, :, here] = qk.T[64:, :]
            vgt = vg.T
            avt[u, :, here] = vgt[:64, :]
            agt[u, :, here] = vgt[64:, :]
        return carry

    lax.fori_loop(0, LENGTH // 128, sort_rows, 0)

    def spot(i):
        return pl.ds(pl.multiple_of(i * QB, QB), QB)

    def query_block(u, qb):
        query = aq[u, spot(qb), :]
        grads = ag[u, spot(qb), :]

        def fold(values):
            return values.reshape(QB // 8, 8, QB)

        def scores(kb, top):
            tile = dot_nt(ak[u, spot(kb), :], query)
            sco[spot(kb), :] = tile
            return jnp.maximum(top, jnp.max(fold(tile), axis=0))

        top = lax.fori_loop(0, qb, scores, jnp.full((8, QB), masked_score, F32))
        tile = dot_nt(ak[u, spot(qb), :], query)
        row = lax.broadcasted_iota(jnp.int32, (QB, QB), 0)
        col = lax.broadcasted_iota(jnp.int32, (QB, QB), 1)
        tile = jnp.where(row <= col, tile, masked_score)
        sco[spot(qb), :] = tile
        top = jnp.maximum(top, jnp.max(fold(tile), axis=0))
        top = jnp.max(top, axis=0, keepdims=True)

        def weigh(kb, carry):
            total, mix = carry
            weights = jnp.exp(sco[spot(kb), :] - top)
            sco[spot(kb), :] = weights
            total = total + jnp.sum(fold(weights), axis=0)
            mix = mix + dot(avt[u, :, spot(kb)], weights.astype(BF16))
            return total, mix

        total, mix = lax.fori_loop(
            0, qb + 1, weigh, (jnp.zeros((8, QB), F32), jnp.zeros((HEAD_DIM, QB), F32))
        )
        inverse = 1.0 / jnp.sum(total, axis=0, keepdims=True)
        mix = mix * inverse
        dots = jnp.sum(agt[u, :, spot(qb)].astype(F32) * mix, axis=0, keepdims=True)

        def backward(kb, back):
            chances = sco[spot(kb), :] * inverse
            slopes = dot_nt(av[u, spot(kb), :], grads)
            score_grads = (chances * (slopes - dots)).astype(BF16)
            dva[spot(kb), :] += dot(chances.astype(BF16), grads)
            dka[spot(kb), :] += dot(score_grads, query)
            return back + dot(akt[u, :, spot(kb)], score_grads)

        back = lax.fori_loop(0, qb + 1, backward, jnp.zeros((HEAD_DIM, QB), F32))
        both = jnp.concatenate([mix, back * SCALE], axis=0).T
        both = turn(both, scos_ref[spot(qb), :], ssin_ref[spot(qb), :]).astype(BF16)
        osrt[0, pl.ds(qb * (QB // HALF), QB // HALF)] = both.reshape(QB // HALF, HALF, 128)

    def unit(u):
        dka[...] = jnp.zeros_like(dka)
        dva[...] = jnp.zeros_like(dva)

        def one(qb, carry):
            query_block(u, qb)
            return carry

        lax.fori_loop(0, LENGTH // QB, one, 0)

        def pack(i, carry):
            both = jnp.concatenate([dva[spot(i), :], dka[spot(i), :]], axis=1)
            both = turn(both, scos_ref[spot(i), :], ssin_ref[spot(i), :]).astype(BF16)
            osrt[1, pl.ds(i * (QB // HALF), QB // HALF)] = both.reshape(QB // HALF, HALF, 128)
            return carry

        lax.fori_loop(0, LENGTH // QB, pack, 0)

        def unsort(i, carry):
            for t in range(2):
                for half in range(2):
                    sbuf[i // 2, u, t, 2 * (i % 2) + half] = osrt[t, blocks_ref[2 * i + half]]
            return carry

        lax.fori_loop(0, 2 * CHIPS, unsort, 0)
        for i in range(CHIPS):
            q = p ^ i
            if i == 0:
                pltpu.make_async_copy(sbuf.at[p, u], rb2.at[p, u], orecv.at[p, u]).start()
            else:
                out_copy(q, u).start()

    def out_copy(q, u):
        return remote(
            sbuf.at[q, u], rb2.at[p, u], osend.at[q, u], orecv.at[p, u], member(q)
        )

    unit(0)
    for ch in range(4):
        advance(ch, 1)
    unit(1)
    for ch in range(4, 8):
        advance(ch, 1)
    for ch in range(4):
        advance(ch, 2)

    for q in range(CHIPS):
        for u in range(SEQS):
            pltpu.make_async_copy(rb2.at[q, u], rb2.at[q, u], orecv.at[q, u]).wait()

    for fq in range(2):
        for kq in range(2):
            for u in range(SEQS):
                at = (2 * fq + kq) * ROWS + u * 128
                here = slice(at, at + 128)
                two = slice(2 * kq, 2 * kq + 2)
                for pair in range(2):
                    cols = slice(128 * pair, 128 * pair + 128)
                    x0 = rb2[4 * pair + fq, u, 0, two].reshape(128, 128)
                    x1 = rb2[4 * pair + 2 + fq, u, 0, two].reshape(128, 128)
                    y0 = rb2[4 * pair + fq, u, 1, two].reshape(128, 128)
                    y1 = rb2[4 * pair + 2 + fq, u, 1, two].reshape(128, 128)
                    aall[here, cols] = jnp.concatenate([x0[:, :64], x1[:, :64]], axis=1)
                    dqkv[0, here, cols] = jnp.concatenate([x0[:, 64:], x1[:, 64:]], axis=1)
                    dqkv[2, here, cols] = jnp.concatenate([y0[:, :64], y1[:, :64]], axis=1)
                    dqkv[1, here, cols] = jnp.concatenate([y0[:, 64:], y1[:, 64:]], axis=1)

    def att_part(i, carry):
        here = lanes(i, 256)
        left = nrm[:, here]
        for slot in range(3):
            at = 8 + (slot - f + 3) % 3
            mats[at, here, :] = dot_tn(left, dqkv[slot]).astype(BF16)
        mats[11, here, :] = dot_tn(gal[:, here], aall[...]).astype(BF16)
        return carry

    lax.fori_loop(0, 4, att_part, 0)
    for ch in range(8, 12):
        advance(ch, 0)

    def normed_part(b, cols):
        here = rows(b)
        total = dot_nt(upg[here, :], wup[cols, :])
        for slot in range(3):
            total = total + dot_nt(dqkv[slot, here, :], wq[slot, cols, :])
        return total

    def mixed_part(b, cols):
        here = rows(b)
        return dot(hid[here, :], wdn[:, cols]) + dot(aall[here, :], wout[:, cols])

    def reduce_copies(n):
        return (
            remote(red_s.at[n, 0], red_r.at[n, 0], dsend.at[n, 0], drecv.at[n, 0], sibling),
            remote(red_s.at[n, 1], red_r.at[n, 1], dsend.at[n, 1], drecv.at[n, 1], sibling),
            remote(red_x.at[n], red_xr.at[n], dsend.at[n, 2], drecv.at[n, 2], xpart),
        )

    parts = (normed_part, mixed_part)

    def reduce_first(n):
        copies = reduce_copies(n)
        for slot, b in ((1, dg), (0, sibb)):

            def fill(i, carry):
                red_s[n, slot, :, lanes(i, 256)] = parts[n](b, lanes(i, 256)).astype(BF16)
                return carry

            lax.fori_loop(0, 4, fill, 0)
            copies[slot].start()

    def reduce_second(n):
        copies = reduce_copies(n)
        copies[1].wait_recv()

        def fill(i, carry):
            cols = lanes(i, 256)
            red_x[n, :, cols] = (
                parts[n](xb, cols) + red_r[n, 1, :, cols].astype(F32)
            ).astype(BF16)
            return carry

        lax.fori_loop(0, 4, fill, 0)
        copies[2].start()

    def reduce_third(n):
        copies = reduce_copies(n)

        def fill(i, carry):
            cols = lanes(i, 256)
            own_acc[n, :, cols] = parts[n](own, cols)
            return carry

        lax.fori_loop(0, 4, fill, 0)
        copies[0].wait_recv()
        copies[2].wait_recv()

        def finish(i, carry):
            cols = lanes(i, 256)
            own_acc[n, :, cols] = (
                own_acc[n, :, cols]
                + red_r[n, 0, :, cols].astype(F32)
                + red_xr[n, :, cols].astype(F32)
            )
            return carry

        lax.fori_loop(0, 4, finish, 0)

    def out_pick():
        row = lax.broadcasted_iota(jnp.int32, (ROWS, ROWS), 0)
        col = lax.broadcasted_iota(jnp.int32, (ROWS, ROWS), 1)
        return (row == 2 * (col % SEQ_DEV_TOK) + col // SEQ_DEV_TOK).astype(F32).astype(BF16)

    reduce_first(0)
    reduce_second(0)
    reduce_first(1)
    reduce_second(1)
    for ch in range(4, 8):
        advance(ch, 2)
    for ch in range(4):
        advance(ch, 3)
    reduce_third(0)

    def back_rows(i, carry):
        dgain, dshift = carry
        here = pl.ds(pl.multiple_of(i * step, step), step)
        there = pl.ds(pl.multiple_of(own * ROWS + i * step, step), step)
        values = xs[here, :].astype(F32)
        center = values - jnp.mean(values, axis=1, keepdims=True)
        spread = lax.rsqrt(jnp.mean(center * center, axis=1, keepdims=True) + EPS)
        hat = center * spread
        grads = own_acc[0, here, :]
        dgain = dgain + jnp.sum(grads * hat, axis=0, keepdims=True)
        dshift = dshift + jnp.sum(grads, axis=0, keepdims=True)
        inner = grads * gain
        inner = spread * (
            inner
            - jnp.mean(inner, axis=1, keepdims=True)
            - hat * jnp.mean(inner * hat, axis=1, keepdims=True)
        )
        xs2 = gal[there, :].astype(F32) + inner
        red_s[0, 0, here, :] = xs2.astype(BF16)
        return dgain, dshift

    reduce_copies(0)[0].wait_send()
    dgain, dshift = lax.fori_loop(
        0, ROWS // step, back_rows, (jnp.zeros((1, D), F32), jnp.zeros((1, D), F32))
    )
    tgrad_ref[...] = dot(out_pick(), red_s[0, 0]).astype(BF16)
    sm[3:4, :] = dgain
    sm[4:5, :] = dshift

    small_copies = [
        remote(sm, smg.at[own], smsend.at[0], smrecv.at[own], sibling),
        remote(sm, smg.at[own], smsend.at[1], smrecv.at[own], xpart),
        remote(sm, smg.at[own], smsend.at[2], smrecv.at[own], diagonal),
    ]
    for copy in small_copies:
        copy.start()

    reduce_third(1)
    reduce_copies(1)[0].wait_send()

    def mixed_rows(i, carry):
        here = pl.ds(pl.multiple_of(i * step, step), step)
        red_s[1, 0, here, :] = (xs[here, :].astype(F32) + own_acc[1, here, :] + down_b).astype(
            BF16
        )
        return carry

    lax.fori_loop(0, ROWS // step, mixed_rows, 0)
    mixed_ref[...] = dot(out_pick(), red_s[1, 0]).astype(BF16)

    smg[own] = sm[...]
    for b in (sibb, xb, dg):
        remote(sm, smg.at[b], smsend.at[0], smrecv.at[b], sibling).wait_recv()
    for copy in small_copies:
        copy.wait_send()
    first_b = 2 * f
    sma[p, 0:1, :] = smg[first_b, 0:1, :]
    sma[p, 1:2, :] = smg[first_b + 1, 0:1, :]
    sma[p, 2:3, :] = sm[2:3, :]
    sma[p, 3:8, :] = smg[0, 3:8, :] + smg[1, 3:8, :] + smg[2, 3:8, :] + smg[3, 3:8, :]
    sm_copies = [
        remote(sma.at[p], sma.at[p], smsend.at[2 + i], smrecv.at[3 + i], member(p ^ i))
        for i in range(1, CHIPS)
    ]
    for copy in sm_copies:
        copy.start()

    for ch in range(8, 12):
        advance(ch, 1)
    for stage in range(4, 8):
        for ch in range(8):
            if stage - 1 > 2 or ch >= 4:
                pass
            if stage == 4 and ch >= 4:
                advance(ch, 3)
            advance(ch, stage)
        if stage - 2 <= 5:
            for ch in range(8, 12):
                advance(ch, stage - 2)
    for stage in (6, 7):
        for ch in range(8, 12):
            advance(ch, stage)

    total = jnp.zeros((8, D), F32)
    for copy in sm_copies:
        copy.wait()
    for q in range(CHIPS):
        total = total + sma[q]
    small_ref[...] = total

    for copy in (vec_copy,):
        pass
    swap_copy.wait_send()
    for copy in (n_sib, n_x, g_sib, g_x, n_dg, g_dg):
        copy.wait_send()
    for u in range(SEQS):
        for i in range(1, CHIPS):
            out_copy(p ^ i, u).wait_send()
    for n in range(2):
        copies = reduce_copies(n)
        copies[1].wait_send()
        copies[2].wait_send()
    for ch in range(NCH):
        settle(ch)


def head_tables(places):
    lane = jnp.arange(HEAD_DIM, dtype=jnp.int32)
    speeds = 10000.0 ** (-(lane // 2 * 2).astype(F32) / ROT_DIM)
    phase = places.astype(F32)[:, None] * speeds[None, :]
    turning = (lane < ROT_DIM)[None, :]
    sign = jnp.where(lane % 2 == 0, -1.0, 1.0)[None, :]
    return jnp.where(turning, jnp.cos(phase), 1.0), jnp.where(turning, jnp.sin(phase) * sign, 0.0)


def fused_device(
    tokens,
    block_pairs,
    norm_gain,
    norm_bias,
    qkv_weight,
    out_weight,
    up_weight,
    up_bias,
    down_weight,
    down_bias,
    cotangent,
):
    f = lax.axis_index("fsdp")
    c = lax.axis_index("ctx")
    order = jnp.stack((block_pairs, 4 * CHIPS - 1 - block_pairs), axis=1).reshape(4 * CHIPS)
    hits = order[None, :] == jnp.arange(4 * CHIPS, dtype=jnp.int32)[:, None]
    places = jnp.sum(
        jnp.where(hits, jnp.arange(4 * CHIPS, dtype=jnp.int32)[None, :], 0), axis=1
    ).astype(jnp.int32)
    holders = places // 2
    halves = places % 2
    first = lax.dynamic_slice(block_pairs, (c // 2 * 2,), (2,))
    row = jnp.arange(SEQ_DEV_TOK, dtype=jnp.int32)
    blocks = jnp.where(row[None, :] < HALF, first[:, None], 4 * CHIPS - 1 - first[:, None])
    own_places = (blocks * HALF + row[None, :] % HALF).reshape(-1)
    cosine, sine = head_tables(own_places)
    cos_tab = jnp.tile(cosine, (1, 2)).reshape(2, SEQ_DEV_TOK, 128)
    sin_tab = jnp.tile(sine, (1, 2)).reshape(2, SEQ_DEV_TOK, 128)
    all_cos, all_sin = head_tables(jnp.arange(LENGTH, dtype=jnp.int32))
    scos = jnp.concatenate((jnp.ones_like(all_cos), all_cos), axis=1)
    ssin = jnp.concatenate((jnp.zeros_like(all_sin), -all_sin), axis=1)
    vec = jnp.concatenate(
        (
            norm_gain[None],
            norm_bias[None],
            down_bias[None],
            jnp.zeros((13, norm_gain.shape[0]), BF16),
        ),
        axis=0,
    )
    upb = lax.dynamic_slice(up_bias, (c % 2 * 1024,), (1024,))[None]

    vm = pl.BlockSpec(memory_space=pltpu.VMEM)
    sme = pl.BlockSpec(memory_space=pltpu.SMEM)
    hbm = pl.BlockSpec(memory_space=pl.ANY)
    dma = pltpu.SemaphoreType.DMA
    scratch = [
        pltpu.VMEM((2, 16, 512), BF16),
        pltpu.VMEM((ROWS, D), BF16),
        pltpu.VMEM((ALL, D), BF16),
        pltpu.VMEM((ALL, D), BF16),
        pltpu.VMEM((3, D, 256), BF16),
        pltpu.VMEM((256, D), BF16),
        pltpu.VMEM((D, 1024), BF16),
        pltpu.VMEM((1024, D), BF16),
        pltpu.VMEM((ALL, 1024), BF16),
        pltpu.VMEM((ALL, 1024), BF16),
        pltpu.VMEM((CHIPS, 2, 2, 4, HALF, 128), BF16),
        pltpu.VMEM((2 * CHIPS, 2, 4, HALF, 128), BF16),
        pltpu.VMEM((SEQS, LENGTH, HEAD_DIM), BF16),
        pltpu.VMEM((SEQS, LENGTH, HEAD_DIM), BF16),
        pltpu.VMEM((SEQS, LENGTH, HEAD_DIM), BF16),
        pltpu.VMEM((SEQS, LENGTH, HEAD_DIM), BF16),
        pltpu.VMEM((SEQS, HEAD_DIM, LENGTH), BF16),
        pltpu.VMEM((SEQS, HEAD_DIM, LENGTH), BF16),
        pltpu.VMEM((SEQS, HEAD_DIM, LENGTH), BF16),
        pltpu.VMEM((LENGTH, QB), F32),
        pltpu.VMEM((LENGTH, HEAD_DIM), F32),
        pltpu.VMEM((LENGTH, HEAD_DIM), F32),
        pltpu.VMEM((2, 4 * CHIPS, HALF, 128), BF16),
        pltpu.VMEM((CHIPS, SEQS, 2, 4, HALF, 128), BF16),
        pltpu.VMEM((ALL, 256), BF16),
        pltpu.VMEM((3, ALL, 256), BF16),
        pltpu.VMEM((NCH, 1024, 256), BF16),
        pltpu.VMEM((NCH, 512, 256), BF16),
        pltpu.VMEM((NCH, 256, 256), BF16),
        pltpu.VMEM((NCH, 128, 256), BF16),
        pltpu.VMEM((128, 256), BF16),
        pltpu.VMEM((2, ROWS, D), F32),
        pltpu.VMEM((2, 2, ROWS, D), BF16),
        pltpu.VMEM((2, ROWS, D), BF16),
        pltpu.VMEM((2, 2, ROWS, D), BF16),
        pltpu.VMEM((2, ROWS, D), BF16),
        pltpu.VMEM((8, D), F32),
        pltpu.VMEM((4, 8, D), F32),
        pltpu.VMEM((CHIPS, 8, D), F32),
        dma((5,)),
        dma((9,)),
        dma((9,)),
        dma((CHIPS, 2, 2)),
        dma((CHIPS, 2, 2)),
        dma((CHIPS, SEQS)),
        dma((CHIPS, SEQS)),
        dma((NCH, 3)),
        dma((NCH, 3)),
        dma((NCH, 3)),
        dma((NCH, 3)),
        dma((NCH,)),
        dma((NCH,)),
        dma((NCH,)),
        dma((2, 3)),
        dma((2, 3)),
        dma((10,)),
        dma((11,)),
    ]
    mixed, tokens_grad, small, dn, up, qkv, out_t = pl.pallas_call(
        fused_kernel,
        out_shape=(
            jax.ShapeDtypeStruct((ROWS, D), BF16),
            jax.ShapeDtypeStruct((ROWS, D), BF16),
            jax.ShapeDtypeStruct((8, D), F32),
            jax.ShapeDtypeStruct((FF // FSDP, D), BF16),
            jax.ShapeDtypeStruct((D, FF // FSDP), BF16),
            jax.ShapeDtypeStruct((D, 3 * D // FSDP), BF16),
            jax.ShapeDtypeStruct((D, D // FSDP), BF16),
        ),
        in_specs=[sme, sme, sme] + [vm] * 8 + [hbm] * 4,
        out_specs=(vm, vm, vm, hbm, hbm, hbm, hbm),
        scratch_shapes=scratch,
        compiler_params=pltpu.CompilerParams(
            collective_id=0, has_side_effects=True, vmem_limit_bytes=63 * 2**20
        ),
    )(
        holders,
        halves,
        order,
        vec,
        upb,
        cos_tab,
        sin_tab,
        scos,
        ssin,
        tokens,
        cotangent,
        qkv_weight,
        out_weight,
        up_weight,
        down_weight,
    )
    half = D // FSDP
    return (
        mixed,
        tokens_grad,
        lax.dynamic_slice(small[3], (f * half,), (half,)),
        lax.dynamic_slice(small[4], (f * half,), (half,)),
        qkv.astype(F32),
        out_t.astype(F32).T,
        up.astype(F32),
        small[0:2].reshape(-1),
        dn.astype(F32),
        lax.dynamic_slice(small[2], (f * half,), (half,)),
    )


def solution(mesh):
    in_specs = (
        P(("fsdp", "ctx"), None),
        P(),
        P("fsdp"),
        P("fsdp"),
        P(None, "fsdp"),
        P("fsdp", None),
        P(None, "fsdp"),
        P("fsdp"),
        P("fsdp", None),
        P("fsdp"),
        P(("fsdp", "ctx"), None),
    )
    out_specs = (
        P(("fsdp", "ctx"), None),
        P(("fsdp", "ctx"), None),
        P("fsdp"),
        P("fsdp"),
        P(None, "fsdp"),
        P("fsdp", None),
        P(None, "fsdp"),
        P("fsdp"),
        P("fsdp", None),
        P("fsdp"),
    )
    plan = fused_device if fits(mesh) else per_device
    return jax.shard_map(
        plan, mesh=mesh, in_specs=in_specs, out_specs=out_specs, check_vma=False
    )
```

```python
import functools
import math

import jax
import jax.numpy as jnp
import numpy as np
from jax import lax
from jax.experimental import pallas as pl
from jax.experimental.pallas import tpu as pltpu
from jax.sharding import PartitionSpec as P

D = 1024
HEAD_DIM = 64
ROT_DIM = 32
HEADS = 16
SEQ_DEV_TOK = 128
SEQS = 2


EPS = 1e-05
HIGHEST = lax.Precision.HIGHEST
masked_score = -1e30


def layer_norm(values, gain_values, shift_values):
    center = values - jnp.mean(values, axis=-1, keepdims=True)
    spread = jnp.mean(center * center, axis=-1, keepdims=True)
    return center * lax.rsqrt(spread + EPS) * gain_values + shift_values


def rotary_tables(places, window):
    lanes = jnp.arange(window, dtype=jnp.int32)
    within_head = lanes % HEAD_DIM
    turning = within_head < ROT_DIM
    steps_up = (within_head // 2 * 2).astype(jnp.float32)
    speeds = 10000.0 ** (-steps_up / ROT_DIM)
    phase = places.astype(jnp.float32)[:, None] * speeds[None, :]
    cos_full = jnp.where(turning[None, :], jnp.cos(phase), 1.0)
    sin_full = jnp.where(turning[None, :], jnp.sin(phase), 0.0)
    row_lane = lanes[:, None]
    col_lane = lanes[None, :]
    same_head = row_lane // HEAD_DIM == col_lane // HEAD_DIM
    col_within = col_lane % HEAD_DIM
    col_turns = same_head & (col_within < ROT_DIM)
    even_col = col_within % 2 == 0
    minus_part = jnp.where(col_turns & even_col & (row_lane == col_lane + 1), -1.0, 0.0)
    plus_part = jnp.where(
        col_turns & jnp.logical_not(even_col) & (row_lane == col_lane - 1), 1.0, 0.0
    )
    swap_table = (minus_part + plus_part).astype(jnp.float32)
    return (cos_full, sin_full, swap_table)


def smooth_gate(values):
    return jax.nn.gelu(values, approximate=True)


def positions(first_row, row_count, pair_table, devices, seq_rows):
    indices = first_row + jnp.arange(row_count, dtype=jnp.int32)
    owners = indices // seq_rows
    within = indices % seq_rows
    half_rows = seq_rows // 2
    matches = owners[:, None] == jnp.arange(devices, dtype=jnp.int32)[None, :]
    chosen = jnp.sum(jnp.where(matches, pair_table[None, :], 0), axis=1)
    block_index = jnp.where(within < half_rows, chosen, 2 * devices - 1 - chosen)
    return block_index * half_rows + within % half_rows


def in_groups(row_count, seq_rows):
    group_rows = math.gcd(row_count // seq_rows, 8) * seq_rows
    return (group_rows, row_count // group_rows)


def split_groups(array, group_rows, turns):
    return array.reshape((turns, group_rows) + array.shape[1:])


def grad_scores(
    query_rows,
    out_grads,
    log_sums,
    row_dots,
    query_places,
    key_rows,
    value_rows,
    key_places,
    factor,
):
    scores = (
        jnp.einsum("qshe,kshe->shqk", query_rows, key_rows, preferred_element_type=jnp.float32)
        * factor
    )
    allowed = key_places[None, :] <= query_places[:, None]
    chances = jnp.exp(jnp.where(allowed, scores - log_sums[..., None], masked_score))
    prob_grads = jnp.einsum(
        "qshe,kshe->shqk", out_grads, value_rows, preferred_element_type=jnp.float32
    )
    return (chances, (chances * (prob_grads - row_dots[..., None])).astype(jnp.bfloat16))


def per_device(
    tokens,
    block_pairs,
    norm_gain,
    norm_bias,
    qkv_weight,
    out_weight,
    up_weight,
    up_bias,
    down_weight,
    down_bias,
    cotangent,
):
    devices = lax.axis_size("ctx")
    own_index = lax.axis_index("ctx")
    seq_rows = SEQ_DEV_TOK
    seq_count = SEQS
    heads = HEADS
    head_size = HEAD_DIM
    width = D
    factor = HEAD_DIM ** (-0.5)
    all_rows = seq_rows * seq_count
    window = math.gcd(width, 128)
    gathered = (
        lax.all_gather(norm_gain, "fsdp", axis=0, tiled=True),
        lax.all_gather(norm_bias, "fsdp", axis=0, tiled=True),
        lax.all_gather(qkv_weight, "fsdp", axis=1, tiled=True),
        lax.all_gather(out_weight, "fsdp", axis=0, tiled=True),
        lax.all_gather(up_weight, "fsdp", axis=1, tiled=True),
        lax.all_gather(up_bias, "fsdp", axis=0, tiled=True),
        lax.all_gather(down_weight, "fsdp", axis=0, tiled=True),
        lax.all_gather(down_bias, "fsdp", axis=0, tiled=True),
    )
    gain_low, shift_low, w_qkv, w_out, w_up, b_up, w_down, b_down = gathered
    inputs = tokens.astype(jnp.float32)
    gain_values = gain_low.astype(jnp.float32)
    shift_values = shift_low.astype(jnp.float32)
    normed_low = layer_norm(inputs, gain_values, shift_values).astype(jnp.bfloat16)
    mixed_qkv = jnp.dot(normed_low, w_qkv, preferred_element_type=jnp.float32).reshape(
        seq_rows, seq_count, 3 * width
    )
    own_places = positions(own_index * seq_rows, seq_rows, block_pairs, devices, seq_rows)
    cos_full, sin_full, swap_table = rotary_tables(own_places, window)

    def turn_both(values):
        shaped = values.reshape(seq_rows, seq_count, 2 * width // window, window)
        swapped = jnp.einsum("rsgw,wv->rsgv", shaped, swap_table, precision=HIGHEST)
        turned_rows = shaped * cos_full[:, None, None, :] + swapped * sin_full[:, None, None, :]
        return turned_rows.reshape(seq_rows, seq_count, 2 * width)

    query_key = mixed_qkv[:, :, : 2 * width]
    turned = turn_both(query_key)
    queries = (
        turned[:, :, :width].astype(jnp.bfloat16).reshape(seq_rows, seq_count, heads, head_size)
    )
    key_rows = (
        turned[:, :, width:].astype(jnp.bfloat16).reshape(seq_rows, seq_count, heads, head_size)
    )
    value_rows = (
        mixed_qkv[:, :, 2 * width :]
        .astype(jnp.bfloat16)
        .reshape(seq_rows, seq_count, heads, head_size)
    )
    start_state = (
        jnp.full((seq_count, heads, seq_rows), masked_score, jnp.float32),
        jnp.zeros((seq_count, heads, seq_rows), jnp.float32),
        jnp.zeros((seq_count, heads, seq_rows, head_size), jnp.float32),
    )
    piece_keys = lax.all_gather(key_rows, "ctx", axis=0, tiled=True)
    piece_values = lax.all_gather(value_rows, "ctx", axis=0, tiled=True)
    group_rows, turns = in_groups(piece_keys.shape[0], seq_rows)

    def attend_step(inner, item):
        block_keys, block_values, turn = item
        key_places = positions(turn * group_rows, group_rows, block_pairs, devices, seq_rows)
        scores = (
            jnp.einsum("qshe,kshe->shqk", queries, block_keys, preferred_element_type=jnp.float32)
            * factor
        )
        allowed = key_places[None, :] <= own_places[:, None]
        running, totals, accum = inner
        fresh = jnp.maximum(running, jnp.max(jnp.where(allowed, scores, masked_score), axis=-1))
        weights = jnp.exp(jnp.where(allowed, scores - fresh[..., None], masked_score))
        fading = jnp.exp(running - fresh)
        totals = totals * fading + jnp.sum(weights, axis=-1)
        accum = accum * fading[..., None] + jnp.einsum(
            "shqk,kshe->shqe",
            weights.astype(jnp.bfloat16),
            block_values,
            preferred_element_type=jnp.float32,
        )
        return ((fresh, totals, accum), None)

    inner, _ = lax.scan(
        attend_step,
        start_state,
        (
            split_groups(piece_keys, group_rows, turns),
            split_groups(piece_values, group_rows, turns),
            jnp.arange(turns, dtype=jnp.int32),
        ),
    )
    running, totals, accum = inner
    log_sums = running + jnp.log(totals)
    attended = jnp.transpose(accum / totals[..., None], (2, 0, 1, 3))
    attn_low = attended.reshape(all_rows, width).astype(jnp.bfloat16)
    attention = jnp.dot(attn_low, w_out, preferred_element_type=jnp.float32)
    up_pre = jnp.dot(normed_low, w_up, preferred_element_type=jnp.float32) + b_up.astype(
        jnp.float32
    )
    hidden_low = smooth_gate(up_pre).astype(jnp.bfloat16)
    result = (
        inputs
        + attention
        + jnp.dot(hidden_low, w_down, preferred_element_type=jnp.float32)
        + b_down.astype(jnp.float32)
    )
    mixed = result.astype(jnp.bfloat16)
    again = (
        lax.all_gather(norm_gain, "fsdp", axis=0, tiled=True),
        lax.all_gather(norm_bias, "fsdp", axis=0, tiled=True),
        lax.all_gather(qkv_weight, "fsdp", axis=1, tiled=True),
        lax.all_gather(out_weight, "fsdp", axis=0, tiled=True),
        lax.all_gather(up_weight, "fsdp", axis=1, tiled=True),
        lax.all_gather(up_bias, "fsdp", axis=0, tiled=True),
        lax.all_gather(down_weight, "fsdp", axis=0, tiled=True),
        lax.all_gather(down_bias, "fsdp", axis=0, tiled=True),
    )
    gain_low, shift_low, w_qkv, w_out, w_up, b_up, w_down, b_down = again
    out_grad = cotangent.astype(jnp.float32)
    attn_grads = (
        jnp.einsum("td,ed->te", cotangent, w_out, preferred_element_type=jnp.float32)
        .astype(jnp.bfloat16)
        .reshape(seq_rows, seq_count, heads, head_size)
    )
    dots_rows = jnp.sum(attn_grads.astype(jnp.float32) * attended, axis=-1)
    row_dots = jnp.transpose(dots_rows, (1, 2, 0))
    empty_rows = jnp.zeros((seq_rows, seq_count, heads, head_size), jnp.float32)
    whole_keys, whole_values = (
        lax.all_gather(key_rows, "ctx", axis=0, tiled=True),
        lax.all_gather(value_rows, "ctx", axis=0, tiled=True),
    )
    piece_keys = whole_keys
    piece_values = whole_values
    query_group_rows, turns = in_groups(piece_keys.shape[0], seq_rows)

    def query_step(inner, item):
        block_keys, block_values, turn = item
        key_places = positions(
            0 + turn * query_group_rows, query_group_rows, block_pairs, devices, seq_rows
        )
        chances, score_grads = grad_scores(
            queries,
            attn_grads,
            log_sums,
            row_dots,
            own_places,
            block_keys,
            block_values,
            key_places,
            factor,
        )
        return (
            inner
            + jnp.einsum(
                "shqk,kshe->qshe", score_grads, block_keys, preferred_element_type=jnp.float32
            )
            * factor,
            None,
        )

    inner, _ = lax.scan(
        query_step,
        empty_rows,
        (
            split_groups(piece_keys, query_group_rows, turns),
            split_groups(piece_values, query_group_rows, turns),
            jnp.arange(turns, dtype=jnp.int32),
        ),
    )
    query_grad = inner
    piece_keys = whole_keys
    piece_values = whole_values
    key_group_rows, turns = in_groups(seq_rows * lax.axis_size("ctx"), seq_rows)

    def key_step(inner, item):
        block_keys, block_values, turn = item
        key_places = positions(
            turn * key_group_rows, key_group_rows, block_pairs, devices, seq_rows
        )
        chances, score_grads = grad_scores(
            queries,
            attn_grads,
            log_sums,
            row_dots,
            own_places,
            block_keys,
            block_values,
            key_places,
            factor,
        )
        key_part = (
            jnp.einsum("shqk,qshe->kshe", score_grads, queries, preferred_element_type=jnp.float32)
            * factor
        )
        value_part = jnp.einsum(
            "shqk,qshe->kshe",
            chances.astype(jnp.bfloat16),
            attn_grads,
            preferred_element_type=jnp.float32,
        )
        stacked = jnp.stack(
            (
                key_part.reshape(key_group_rows, seq_count, width),
                value_part.reshape(key_group_rows, seq_count, width),
            ),
            axis=2,
        )
        return (inner, stacked)

    _, blocks_out = lax.scan(
        key_step,
        jnp.zeros((), jnp.float32),
        (
            split_groups(piece_keys, key_group_rows, turns),
            split_groups(piece_values, key_group_rows, turns),
            jnp.arange(turns, dtype=jnp.int32),
        ),
    )
    summed_terms = lax.psum_scatter(
        blocks_out.reshape(seq_rows * lax.axis_size("ctx"), seq_count, 2, width),
        "ctx",
        scatter_dimension=0,
        tiled=True,
    )
    key_grad = summed_terms[:, :, 0].reshape(seq_rows, seq_count, heads, head_size)
    value_grad = summed_terms[:, :, 1].reshape(seq_rows, seq_count, heads, head_size)
    _, turn_back = jax.vjp(turn_both, query_key)
    both_grads = jnp.concatenate(
        (
            query_grad.reshape(seq_rows, seq_count, width),
            key_grad.reshape(seq_rows, seq_count, width),
        ),
        axis=2,
    )
    (pre_grads,) = turn_back(both_grads)
    qkv_grad = (
        jnp.concatenate((pre_grads, value_grad.reshape(seq_rows, seq_count, width)), axis=2)
        .reshape(all_rows, 3 * width)
        .astype(jnp.bfloat16)
    )
    hidden_grad = jnp.einsum("td,fd->tf", cotangent, w_down, preferred_element_type=jnp.float32)
    _, gate_back = jax.vjp(smooth_gate, up_pre)
    (up_grad,) = gate_back(hidden_grad)
    up_low = up_grad.astype(jnp.bfloat16)
    normed_grad = jnp.einsum(
        "tc,dc->td", qkv_grad, w_qkv, preferred_element_type=jnp.float32
    ) + jnp.einsum("tf,df->td", up_low, w_up, preferred_element_type=jnp.float32)
    _, norm_back = jax.vjp(
        layer_norm, inputs, gain_low.astype(jnp.float32), shift_low.astype(jnp.float32)
    )
    input_part, gain_grad, shift_grad = norm_back(normed_grad)
    tokens_grad = (out_grad + input_part).astype(jnp.bfloat16)
    qkv_wgrad = jnp.einsum("td,tc->dc", normed_low, qkv_grad, preferred_element_type=jnp.float32)
    out_wgrad = jnp.einsum("td,te->de", attn_low, cotangent, preferred_element_type=jnp.float32)
    up_wgrad = jnp.einsum("td,tf->df", normed_low, up_low, preferred_element_type=jnp.float32)
    up_bgrad = jnp.sum(up_low.astype(jnp.float32), axis=0)
    down_wgrad = jnp.einsum("tf,td->fd", hidden_low, cotangent, preferred_element_type=jnp.float32)
    down_bgrad = jnp.sum(out_grad, axis=0)
    shares = (
        lax.psum_scatter(
            gain_grad.astype(jnp.bfloat16), "fsdp", scatter_dimension=0, tiled=True
        ).astype(jnp.float32),
        lax.psum_scatter(
            shift_grad.astype(jnp.bfloat16), "fsdp", scatter_dimension=0, tiled=True
        ).astype(jnp.float32),
        lax.psum_scatter(
            qkv_wgrad.astype(jnp.bfloat16), "fsdp", scatter_dimension=1, tiled=True
        ).astype(jnp.float32),
        lax.psum_scatter(
            out_wgrad.astype(jnp.bfloat16), "fsdp", scatter_dimension=0, tiled=True
        ).astype(jnp.float32),
        lax.psum_scatter(
            up_wgrad.astype(jnp.bfloat16), "fsdp", scatter_dimension=1, tiled=True
        ).astype(jnp.float32),
        lax.psum_scatter(
            up_bgrad.astype(jnp.bfloat16), "fsdp", scatter_dimension=0, tiled=True
        ).astype(jnp.float32),
        lax.psum_scatter(
            down_wgrad.astype(jnp.bfloat16), "fsdp", scatter_dimension=0, tiled=True
        ).astype(jnp.float32),
        lax.psum_scatter(
            down_bgrad.astype(jnp.bfloat16), "fsdp", scatter_dimension=0, tiled=True
        ).astype(jnp.float32),
    )
    share_gain, share_shift, share_qkv, share_out, share_up, share_upb, share_down, share_downb = (
        shares
    )
    totals_out = lax.psum(
        (
            share_gain,
            share_shift,
            share_qkv,
            share_out,
            share_up,
            share_upb,
            share_down,
            share_downb,
        ),
        "ctx",
    )
    sum_gain, sum_shift, sum_qkv, sum_out, sum_up, sum_upb, sum_down, sum_downb = totals_out
    return (
        mixed,
        tokens_grad,
        sum_gain,
        sum_shift,
        sum_qkv,
        sum_out,
        sum_up,
        sum_upb,
        sum_down,
        sum_downb,
    )


F32 = jnp.float32
BF16 = jnp.bfloat16
FF = 4096
FSDP = 2
CHIPS = 8
ROWS = SEQ_DEV_TOK * SEQS
ALL = 4 * ROWS
LENGTH = CHIPS * 2 * SEQ_DEV_TOK
HALF = SEQ_DEV_TOK // 2
QB = 512
NCH = 12
MASKS = (1, 2, 4)
SCATTER = {10: (1, 0, 2), 11: (1, 0, 2)}
GATHER = {10: (2, 0, 1), 11: (2, 0, 1)}
SCALE = HEAD_DIM**-0.5


def fits(mesh):
    return mesh.shape["fsdp"] == FSDP and mesh.shape["ctx"] == 2 * CHIPS


def dot(left, right):
    return lax.dot_general(left, right, (((1,), (0,)), ((), ())), preferred_element_type=F32)


def dot_nt(left, right):
    return lax.dot_general(left, right, (((1,), (1,)), ((), ())), preferred_element_type=F32)


def dot_tn(left, right):
    return lax.dot_general(left, right, (((0,), (0,)), ((), ())), preferred_element_type=F32)


def turn(values, cosine, sine):
    lane = lax.broadcasted_iota(jnp.int32, values.shape, 1)
    width = values.shape[1]
    other = jnp.where(
        lane % 2 == 0, pltpu.roll(values, width - 1, 1), pltpu.roll(values, 1, 1)
    )
    return values * cosine + other * sine


def gate(values):
    inner = 0.7978845608028654 * (values + 0.044715 * values * values * values)
    th = jnp.tanh(inner)
    half = 0.5 * (1.0 + th)
    slope = half + (0.5 * values) * (1.0 - th * th) * (
        0.7978845608028654 * (1.0 + 3 * 0.044715 * values * values)
    )
    return values * half, slope


def fused_kernel(
    spots_ref,
    vec_ref,
    turns_h,
    tok_ref,
    cot_ref,
    wqkv_h,
    wout_h,
    wup_h,
    wdn_h,
    mixed_ref,
    tgrad_ref,
    small_ref,
    odn,
    oup,
    oqkv,
    oout,
    turns,
    vecf,
    vall,
    xs,
    nrm,
    gal,
    wq,
    wout,
    wup,
    wdn,
    hid,
    upg,
    sbuf,
    rbuf,
    aq,
    ag,
    ak,
    av,
    akt,
    avt,
    agt,
    sco,
    dka,
    dva,
    osrt,
    rb2,
    aall,
    dqkv,
    mats,
    rs0,
    rs1,
    rs2,
    xsw,
    own_acc,
    red_s,
    red_x,
    red_r,
    red_xr,
    sm,
    smg,
    sma,
    lsem,
    gsend,
    grecv,
    asend,
    arecv,
    osend,
    orecv,
    rssend,
    rsrecv,
    agsend,
    agrecv,
    clocal,
    csend,
    crecv,
    dsend,
    drecv,
    smsend,
    smrecv,
):
    f = lax.axis_index("fsdp")
    c = lax.axis_index("ctx")
    k = c % 2
    p = c // 2
    zz = p // 2
    yy = p % 2
    xpart = (1 - f, c)
    sibling = (f, 2 * p + 1 - k)
    diagonal = (1 - f, 2 * p + 1 - k)
    own = 2 * f + k
    sibb = 2 * f + 1 - k
    xb = 2 * (1 - f) + k
    dg = 2 * (1 - f) + 1 - k
    MESH = pl.DeviceIdType.MESH

    def member(q):
        return (f, 2 * q + k)

    def remote(src, dst, ssem, rsem, device):
        return pltpu.make_async_remote_copy(
            src_ref=src,
            dst_ref=dst,
            send_sem=ssem,
            recv_sem=rsem,
            device_id=device,
            device_id_type=MESH,
        )

    def rows(b):
        return pl.ds(pl.multiple_of(b * ROWS, ROWS), ROWS)

    def lanes(i, n):
        return pl.ds(pl.multiple_of(i * n, n), n)

    loads = [
        pltpu.make_async_copy(wqkv_h.at[:, lanes(k, 256)], wq.at[f], lsem.at[0]),
        pltpu.make_async_copy(
            wqkv_h.at[:, pl.ds(pl.multiple_of(1024 + 256 * k, 256), 256)], wq.at[1 + f], lsem.at[1]
        ),
        pltpu.make_async_copy(wup_h.at[:, lanes(k, 1024)], wup, lsem.at[2]),
        pltpu.make_async_copy(wdn_h.at[lanes(k, 1024), :], wdn, lsem.at[3]),
        pltpu.make_async_copy(wout_h.at[lanes(k, 256), :], wout, lsem.at[4]),
        pltpu.make_async_copy(turns_h, turns, lsem.at[5]),
    ]
    for load in loads:
        load.start()
    barrier = pltpu.get_barrier_semaphore()
    for device in [xpart, sibling, diagonal] + [member(p ^ i) for i in range(1, CHIPS)]:
        pl.semaphore_signal(barrier, inc=1, device_id=device, device_id_type=MESH)
    pl.semaphore_wait(barrier, 3 + CHIPS - 1)

    vec_copy = remote(vec_ref, vall.at[f], gsend.at[0], grecv.at[0], xpart)
    vec_copy.start()
    swap_copy = remote(
        wqkv_h.at[:, pl.ds(pl.multiple_of(512 + 256 * k, 256), 256)],
        wq.at[2 * f],
        gsend.at[1],
        grecv.at[1],
        xpart,
    )
    swap_copy.start()
    vall[f] = vec_ref[...]
    vecf[...] = vec_ref[...].astype(F32)
    vec_copy.wait()
    gain = jnp.concatenate([vall[0, 0:1, :], vall[1, 0:1, :]], axis=1).astype(F32)
    shift = jnp.concatenate([vall[0, 1:2, :], vall[1, 1:2, :]], axis=1).astype(F32)
    down_b = jnp.concatenate([vall[0, 2:3, :], vall[1, 2:3, :]], axis=1).astype(F32)

    step = 64

    def norm_rows(i, carry):
        here = pl.ds(pl.multiple_of(i * step, step), step)
        there = pl.ds(pl.multiple_of(own * ROWS + i * step, step), step)
        row = lax.broadcasted_iota(jnp.int32, (step, ROWS), 0) + i * step
        col = lax.broadcasted_iota(jnp.int32, (step, ROWS), 1)
        pick = (col == 2 * (row % SEQ_DEV_TOK) + row // SEQ_DEV_TOK).astype(F32).astype(BF16)
        values = dot(pick, tok_ref[...])
        gal[there, :] = dot(pick, cot_ref[...]).astype(BF16)
        xs[here, :] = values.astype(BF16)
        center = values - jnp.mean(values, axis=1, keepdims=True)
        spread = jnp.mean(center * center, axis=1, keepdims=True)
        nrm[there, :] = (center * lax.rsqrt(spread + EPS) * gain + shift).astype(BF16)
        return carry

    lax.fori_loop(0, ROWS // step, norm_rows, 0)

    def spread_copy(buf, b, n, device):
        return remote(buf.at[rows(b)], buf.at[rows(b)], gsend.at[n], grecv.at[n], device)

    n_sib = spread_copy(nrm, own, 2, sibling)
    n_x = spread_copy(nrm, own, 3, xpart)
    g_sib = spread_copy(gal, own, 4, sibling)
    g_x = spread_copy(gal, own, 5, xpart)
    for copy in (n_sib, n_x, g_sib, g_x):
        copy.start()
    for load in loads:
        load.wait()

    def up_part_of(b, i):
        at = k * 1024 + i * 256
        bias = vecf[pl.ds(3 + at // 512, 1), pl.ds(pl.multiple_of(at % 512, 256), 256)]
        return gate(dot(nrm[rows(b), :], wup[:, lanes(i, 256)]) + bias)

    def feed_block(b):
        def part(i, carry):
            cols = lanes(i, 256)
            value, slope = up_part_of(b, i)
            hid[rows(b), cols] = value.astype(BF16)
            back = dot_nt(gal[rows(b), :], wdn[cols, :])
            upg[rows(b), cols] = (back * slope).astype(BF16)
            return carry

        lax.fori_loop(0, 4, part, 0)

    def feed_up(b, n):
        def part(i, carry):
            cols = lanes(i, 256)
            value, slope = up_part_of(b, i)
            hid[rows(b), cols] = value.astype(BF16)
            own_acc[n, :, cols] = slope
            return carry

        lax.fori_loop(0, 4, part, 0)

    def feed_back(b, n):
        def part(i, carry):
            cols = lanes(i, 256)
            back = dot_nt(gal[rows(b), :], wdn[cols, :])
            upg[rows(b), cols] = (back * own_acc[n, :, cols]).astype(BF16)
            return carry

        lax.fori_loop(0, 4, part, 0)

    def put_heads(first, second, fq, kq, t):
        for h in range(4):
            sbuf[2 * h + fq, t, kq] = jnp.concatenate(
                [first[:, 64 * h : 64 * h + 64], second[:, 64 * h : 64 * h + 64]], axis=1
            ).reshape(4, HALF, 128)

    def turned(values, kq):
        table = jnp.concatenate(
            [turns[spots_ref[64 + 2 * (2 * p + kq) + half]] for half in range(2)], axis=0
        )
        cosine = jnp.concatenate([table[:, :64], table[:, :64]], axis=1)
        sine = jnp.concatenate([table[:, 64:], table[:, 64:]], axis=1)
        parts = []
        for s in range(SEQS):
            line = []
            for half in range(2):
                piece = values[128 * s : 128 * s + 128, 128 * half : 128 * half + 128]
                line.append(turn(piece, cosine, sine))
            parts.append(jnp.concatenate(line, axis=1))
        return jnp.concatenate(parts, axis=0).astype(BF16)

    def kg_block(b, fq, kq):
        key = dot(nrm[rows(b), :], wq[1])
        grads = dot_nt(gal[rows(b), :], wout[...]).astype(BF16)
        put_heads(turned(key, kq), grads, fq, kq, 0)

    def qv_block(b, fq, kq):
        query = dot(nrm[rows(b), :], wq[0])
        value = dot(nrm[rows(b), :], wq[2]).astype(BF16)
        put_heads(turned(query, kq) * BF16(SCALE), value, fq, kq, 1)

    def in_copy(q, t, kq):
        return remote(
            sbuf.at[q, t, kq],
            rbuf.at[2 * p + kq, t],
            asend.at[q, t, kq],
            arecv.at[p, t, kq],
            member(q),
        )

    def send_block(fq, kq, t):
        for i in range(4):
            q = 2 * (zz ^ i) + fq
            if i == 0:

                @pl.when(fq == yy)
                def _():
                    pltpu.make_async_copy(
                        sbuf.at[q, t, kq], rbuf.at[2 * p + kq, t], arecv.at[p, t, kq]
                    ).start()

                @pl.when(fq != yy)
                def _():
                    in_copy(q, t, kq).start()
            else:
                in_copy(q, t, kq).start()

    def sent_block(fq, kq, t):
        for i in range(4):
            q = 2 * (zz ^ i) + fq
            if i == 0:

                @pl.when(fq != yy)
                def _():
                    in_copy(q, t, kq).wait_send()
            else:
                in_copy(q, t, kq).wait_send()

    kg_block(own, f, k)
    send_block(f, k, 0)
    n_sib.wait_recv()
    g_sib.wait_recv()
    kg_block(sibb, f, 1 - k)
    send_block(f, 1 - k, 0)
    feed_block(own)
    feed_block(sibb)
    swap_copy.wait_recv()
    for b, kq in ((own, k), (sibb, 1 - k)):
        qv_block(b, f, kq)
        send_block(f, kq, 1)
    n_x.wait_recv()
    n_dg = spread_copy(nrm, xb, 6, sibling)
    n_dg.start()
    qv_block(xb, 1 - f, k)
    send_block(1 - f, k, 1)
    n_dg.wait_recv()
    qv_block(dg, 1 - f, 1 - k)
    send_block(1 - f, 1 - k, 1)
    feed_up(xb, 0)
    feed_up(dg, 1)
    g_x.wait_recv()
    g_dg = spread_copy(gal, xb, 7, sibling)
    g_dg.start()
    kg_block(xb, 1 - f, k)
    send_block(1 - f, k, 0)
    g_dg.wait_recv()
    kg_block(dg, 1 - f, 1 - k)
    send_block(1 - f, 1 - k, 0)
    feed_back(xb, 0)
    feed_back(dg, 1)

    def store_rows(ch, i, values):
        mats[ch, i // 2, i % 2] = values.reshape(2, 128, 256)

    def down_part(i, carry):
        full = dot_tn(hid[:, lanes(i, 256)], gal[...]).astype(BF16)
        for cc in range(4):
            store_rows(cc, i, full[:, 256 * cc : 256 * cc + 256])
        return carry

    def up_part(i, carry):
        full = dot_tn(nrm[:, lanes(i, 256)], upg[...]).astype(BF16)
        for cc in range(4):
            store_rows(4 + cc, i, full[:, 256 * cc : 256 * cc + 256])
        return carry

    sm[...] = jnp.zeros_like(sm)
    sm[0:1, :] = jnp.sum(upg[...].astype(F32), axis=0, keepdims=True)
    sm[2:3, :] = jnp.sum(gal[...].astype(F32), axis=0, keepdims=True)

    bits = [(p // mask) % 2 for mask in MASKS]
    every = slice(None)

    def block_index(free, other=None):
        return tuple(
            every if dim in free else (1 - bits[dim] if dim == other else bits[dim])
            for dim in range(3)
        )

    def scatter_order(ch):
        return SCATTER.get(ch, (0, 1, 2))

    def gather_order(ch):
        return GATHER.get(ch, (2, 1, 0))

    rsb = (rs0, rs1, rs2)

    def rs_copy(ch, ph):
        order = scatter_order(ch)
        return remote(
            mats.at[(ch,) + block_index(order[ph + 1 :], order[ph])],
            rsb[ph].at[ch],
            rssend.at[ch, ph],
            rsrecv.at[ch, ph],
            member(p ^ MASKS[order[ph]]),
        )

    def rs_add(ch, ph):
        free = sorted(scatter_order(ch)[ph + 1 :])
        rs_copy(ch, ph).wait_recv()
        for n in range(2 ** len(free)):
            spot = {dim: (n >> i) % 2 for i, dim in enumerate(free)}
            here = (ch,) + tuple(spot.get(dim, bits[dim]) for dim in range(3))
            there = (ch,) + tuple(spot[dim] for dim in free)
            mats[here] = (mats[here].astype(F32) + rsb[ph][there].astype(F32)).astype(BF16)

    def out_slice(ch, kk, index):
        if ch < 4:
            return odn.at[(kk,) + index + (every, slice(256 * ch, 256 * ch + 256))]
        if ch < 8:
            start, out = kk * 1024 + (ch - 4) * 256, oup
        elif ch < 11:
            start, out = (0, 1024, 512)[ch - 8] + kk * 256, oqkv
        else:
            start, out = kk * 256, oout
        return out.at[index + (every, pl.ds(pl.multiple_of(start, 256), 256))]

    def shard(ch):
        if ch == 10:
            return xsw
        return mats.at[(ch,) + block_index(())]

    def swap_shard():
        return remote(
            mats.at[(10,) + block_index(())], xsw, gsend.at[8], grecv.at[8], xpart
        )

    def local_copy(ch):
        return pltpu.make_async_copy(
            shard(ch), out_slice(ch, k, block_index(())), clocal.at[ch]
        )

    def ag_copy(ch, step):
        order = gather_order(ch)
        there = out_slice(ch, k, block_index(order[:step]))
        return remote(
            shard(ch) if step == 0 else there,
            there,
            agsend.at[ch, step],
            agrecv.at[ch, step],
            member(p ^ MASKS[order[step]]),
        )

    def core_copy(ch):
        return remote(
            out_slice(ch, k, (every,) * 3),
            out_slice(ch, k, (every,) * 3),
            csend.at[ch],
            crecv.at[ch],
            sibling,
        )

    def advance(ch, stage):
        if stage == 0:
            rs_copy(ch, 0).start()
        elif stage <= 2:
            rs_add(ch, stage - 1)
            rs_copy(ch, stage).start()
        elif stage == 3:
            rs_add(ch, 2)
            if ch == 10:
                swap_shard().start()
                swap_shard().wait_recv()
            local_copy(ch).start()
            ag_copy(ch, 0).start()
        elif stage == 4:
            ag_copy(ch, 0).wait_recv()
            local_copy(ch).wait()
            ag_copy(ch, 1).start()
        elif stage == 5:
            ag_copy(ch, 1).wait_recv()
            ag_copy(ch, 2).start()
        elif stage == 6:
            ag_copy(ch, 2).wait_recv()
            core_copy(ch).start()
        elif stage == 7:
            core_copy(ch).wait_recv()

    def settle(ch):
        for ph in range(3):
            rs_copy(ch, ph).wait_send()
            ag_copy(ch, ph).wait_send()
        core_copy(ch).wait_send()
        if ch == 10:
            swap_shard().wait_send()

    lax.fori_loop(0, 4, down_part, 0)
    for ch in range(4):
        advance(ch, 0)
    lax.fori_loop(0, 4, up_part, 0)
    for ch in range(4, 8):
        advance(ch, 0)

    for fq, kq in ((f, k), (f, 1 - k), (1 - f, k), (1 - f, 1 - k)):
        for t in range(2):
            sent_block(fq, kq, t)
    for q in range(CHIPS):
        for t in range(2):
            for kq in range(2):
                pltpu.make_async_copy(
                    rbuf.at[2 * q + kq, t], rbuf.at[2 * q + kq, t], arecv.at[q, t, kq]
                ).wait()

    def load_half(place, t, u):
        return rbuf[spots_ref[place], t, 2 * u + spots_ref[32 + place]]

    def sort_unit(u):
        def sort_rows(i, carry):
            here = pl.ds(pl.multiple_of(i * 128, 128), 128)
            kg = jnp.concatenate([load_half(2 * i, 0, u), load_half(2 * i + 1, 0, u)], axis=0)
            qv = jnp.concatenate([load_half(2 * i, 1, u), load_half(2 * i + 1, 1, u)], axis=0)
            ak[here, :] = kg[:, :64]
            ag[here, :] = kg[:, 64:]
            aq[here, :] = qv[:, :64]
            av[here, :] = qv[:, 64:]
            kgt = kg.T
            akt[:, here] = kgt[:64, :]
            agt[:, here] = kgt[64:, :]
            avt[:, here] = qv.T[64:, :]
            return carry

        lax.fori_loop(0, LENGTH // 128, sort_rows, 0)

    def fold(values):
        return values.reshape(values.shape[0] // 8, 8, values.shape[1])

    def query_block(qb):
        mine = slice(qb * QB, qb * QB + QB)
        tiles = [slice(i * QB, i * QB + QB) for i in range(qb + 1)]
        query = aq[mine, :]
        grads = ag[mine, :]
        top = jnp.full((8, QB), masked_score, F32)
        for i, tile in enumerate(tiles):
            score = dot_nt(ak[tile, :], query)
            if i == qb:
                row = lax.broadcasted_iota(jnp.int32, (QB, QB), 0)
                col = lax.broadcasted_iota(jnp.int32, (QB, QB), 1)
                score = jnp.where(row <= col, score, masked_score)
            sco[tile, :] = score
            top = jnp.maximum(top, jnp.max(fold(score), axis=0))
        top = jnp.max(top, axis=0, keepdims=True)
        total = jnp.zeros((8, QB), F32)
        mix = jnp.zeros((HEAD_DIM, QB), F32)
        for tile in tiles:
            weights = jnp.exp(sco[tile, :] - top)
            sco[tile, :] = weights
            total = total + jnp.sum(fold(weights), axis=0)
            mix = mix + dot(avt[:, tile], weights.astype(BF16))
        inverse = 1.0 / jnp.sum(total, axis=0, keepdims=True)
        mix = mix * inverse
        dots = jnp.sum(agt[:, mine].astype(F32) * mix, axis=0, keepdims=True)
        back = jnp.zeros((HEAD_DIM, QB), F32)
        for i, tile in enumerate(tiles):
            chances = sco[tile, :] * inverse
            slopes = dot_nt(av[tile, :], grads)
            score_grads = (chances * (slopes - dots)).astype(BF16)
            value_part = dot(chances.astype(BF16), grads)
            key_part = dot(score_grads, query)
            if i == qb:
                dva[tile, :] = value_part
                dka[tile, :] = key_part
            else:
                dva[tile, :] += value_part
                dka[tile, :] += key_part
            back = back + dot(akt[:, tile], score_grads)
        place(0, qb, jnp.concatenate([mix, back * SCALE], axis=0).T)

    def place(t, qb, both):
        n = QB // HALF
        table = turns[qb * n : qb * n + n].reshape(QB, 128)
        cosine = jnp.concatenate([jnp.ones((QB, 64), F32), table[:, :64]], axis=1)
        sine = jnp.concatenate([jnp.zeros((QB, 64), F32), -table[:, 64:]], axis=1)
        osrt[t, qb * n : qb * n + n] = turn(both, cosine, sine).astype(BF16).reshape(n, HALF, 128)

    def finish_unit(u):
        for qb in range(LENGTH // QB):
            mine = slice(qb * QB, qb * QB + QB)
            place(1, qb, jnp.concatenate([dva[mine, :], dka[mine, :]], axis=1))

        def unsort(i, carry):
            for t in range(2):
                for half in range(2):
                    sbuf[i // 2, u, t, 2 * (i % 2) + half] = osrt[t, spots_ref[64 + 2 * i + half]]
            return carry

        lax.fori_loop(0, 2 * CHIPS, unsort, 0)
        for i in range(CHIPS):
            q = p ^ i
            if i == 0:
                pltpu.make_async_copy(sbuf.at[p, u], rb2.at[p, u], orecv.at[p, u]).start()
            else:
                out_copy(q, u).start()

    def out_copy(q, u):
        return remote(
            sbuf.at[q, u], rb2.at[p, u], osend.at[q, u], orecv.at[p, u], member(q)
        )

    ticks = {
        (0, 1): [(0, 1)],
        (0, 2): [(1, 1), (0, 2)],
        (0, 3): [(2, 1), (1, 2)],
        (1, 1): [(3, 1)],
        (1, 2): [(4, 1)],
        (1, 3): [(5, 1)],
    }

    def run(*steps):
        for ch, stage in steps:
            advance(ch, stage)

    for u in range(SEQS):
        sort_unit(u)
        for qb in range(LENGTH // QB):
            query_block(qb)
            if qb == LENGTH // QB - 1:
                finish_unit(u)
            for ch, stage in ticks.get((u, qb), []):
                advance(ch, stage)
    run((2, 2), (3, 2), (6, 1), (4, 2), (7, 1), (5, 2))

    for q in range(CHIPS):
        for u in range(SEQS):
            pltpu.make_async_copy(rb2.at[q, u], rb2.at[q, u], orecv.at[q, u]).wait()

    for fq in range(2):
        for kq in range(2):
            for u in range(SEQS):
                at = (2 * fq + kq) * ROWS + u * 128
                here = slice(at, at + 128)
                two = slice(2 * kq, 2 * kq + 2)
                for pair in range(2):
                    cols = slice(128 * pair, 128 * pair + 128)
                    x0 = rb2[4 * pair + fq, u, 0, two].reshape(128, 128)
                    x1 = rb2[4 * pair + 2 + fq, u, 0, two].reshape(128, 128)
                    y0 = rb2[4 * pair + fq, u, 1, two].reshape(128, 128)
                    y1 = rb2[4 * pair + 2 + fq, u, 1, two].reshape(128, 128)
                    aall[here, cols] = jnp.concatenate([x0[:, :64], x1[:, :64]], axis=1)
                    dqkv[0, here, cols] = jnp.concatenate([x0[:, 64:], x1[:, 64:]], axis=1)
                    dqkv[2, here, cols] = jnp.concatenate([y0[:, :64], y1[:, :64]], axis=1)
                    dqkv[1, here, cols] = jnp.concatenate([y0[:, 64:], y1[:, 64:]], axis=1)

    def att_part(i, carry):
        here = lanes(i, 256)
        left = nrm[:, here]
        for slot in range(3):
            at = 8 + (slot - f + 3) % 3
            store_rows(at, i, dot_tn(left, dqkv[slot]).astype(BF16))
        store_rows(11, i, dot_tn(gal[:, here], aall[...]).astype(BF16))
        return carry

    lax.fori_loop(0, 4, att_part, 0)
    run((8, 0), (10, 0), (9, 0), (11, 0))

    def normed_part(b, cols):
        here = rows(b)
        total = dot_nt(upg[here, :], wup[cols, :])
        for slot in range(3):
            total = total + dot_nt(dqkv[slot, here, :], wq[slot, cols, :])
        return total

    def mixed_part(b, cols):
        here = rows(b)
        return dot(hid[here, :], wdn[:, cols]) + dot(aall[here, :], wout[:, cols])

    def reduce_copies(n):
        return (
            remote(red_s.at[n, 0], red_r.at[n, 0], dsend.at[n, 0], drecv.at[n, 0], sibling),
            remote(red_s.at[n, 1], red_r.at[n, 1], dsend.at[n, 1], drecv.at[n, 1], sibling),
            remote(red_x.at[n], red_xr.at[n], dsend.at[n, 2], drecv.at[n, 2], xpart),
        )

    parts = (normed_part, mixed_part)

    def reduce_first(n):
        copies = reduce_copies(n)
        for slot, b in ((1, dg), (0, sibb)):

            def fill(i, carry):
                red_s[n, slot, :, lanes(i, 256)] = parts[n](b, lanes(i, 256)).astype(BF16)
                return carry

            lax.fori_loop(0, 4, fill, 0)
            copies[slot].start()

    def reduce_second(n):
        copies = reduce_copies(n)
        copies[1].wait_recv()

        def fill(i, carry):
            cols = lanes(i, 256)
            red_x[n, :, cols] = (
                parts[n](xb, cols) + red_r[n, 1, :, cols].astype(F32)
            ).astype(BF16)
            return carry

        lax.fori_loop(0, 4, fill, 0)
        copies[2].start()

    def reduce_third(n):
        copies = reduce_copies(n)

        def fill(i, carry):
            cols = lanes(i, 256)
            own_acc[n, :, cols] = parts[n](own, cols)
            return carry

        lax.fori_loop(0, 4, fill, 0)
        copies[0].wait_recv()
        copies[2].wait_recv()

        def finish(i, carry):
            cols = lanes(i, 256)
            own_acc[n, :, cols] = (
                own_acc[n, :, cols]
                + red_r[n, 0, :, cols].astype(F32)
                + red_xr[n, :, cols].astype(F32)
            )
            return carry

        lax.fori_loop(0, 4, finish, 0)

    def out_pick():
        row = lax.broadcasted_iota(jnp.int32, (ROWS, ROWS), 0)
        col = lax.broadcasted_iota(jnp.int32, (ROWS, ROWS), 1)
        return (row == 2 * (col % SEQ_DEV_TOK) + col // SEQ_DEV_TOK).astype(F32).astype(BF16)

    reduce_first(0)
    run((6, 2), (0, 3), (1, 3), (7, 2), (2, 3), (3, 3), (4, 3), (5, 3))
    reduce_second(0)
    run((6, 3), (7, 3), (0, 4), (1, 4), (2, 4), (10, 1), (8, 1))
    reduce_first(1)
    run((3, 4), (4, 4), (0, 5), (1, 5))
    reduce_second(1)
    run((11, 1), (9, 1), (10, 2), (8, 2), (5, 4), (6, 4), (7, 4), (2, 5), (3, 5))
    reduce_third(0)

    def back_rows(i, carry):
        dgain, dshift = carry
        here = pl.ds(pl.multiple_of(i * step, step), step)
        there = pl.ds(pl.multiple_of(own * ROWS + i * step, step), step)
        values = xs[here, :].astype(F32)
        center = values - jnp.mean(values, axis=1, keepdims=True)
        spread = lax.rsqrt(jnp.mean(center * center, axis=1, keepdims=True) + EPS)
        hat = center * spread
        grads = own_acc[0, here, :]
        dgain = dgain + jnp.sum(grads * hat, axis=0, keepdims=True)
        dshift = dshift + jnp.sum(grads, axis=0, keepdims=True)
        inner = grads * gain
        inner = spread * (
            inner
            - jnp.mean(inner, axis=1, keepdims=True)
            - hat * jnp.mean(inner * hat, axis=1, keepdims=True)
        )
        xs2 = gal[there, :].astype(F32) + inner
        red_s[0, 0, here, :] = xs2.astype(BF16)
        return dgain, dshift

    reduce_copies(0)[0].wait_send()
    dgain, dshift = lax.fori_loop(
        0, ROWS // step, back_rows, (jnp.zeros((1, D), F32), jnp.zeros((1, D), F32))
    )
    tgrad_ref[...] = dot(out_pick(), red_s[0, 0]).astype(BF16)
    sm[3:4, :] = dgain
    sm[4:5, :] = dshift

    small_copies = [
        remote(sm, smg.at[own], smsend.at[0], smrecv.at[own], sibling),
        remote(sm, smg.at[own], smsend.at[1], smrecv.at[own], xpart),
        remote(sm, smg.at[own], smsend.at[2], smrecv.at[own], diagonal),
    ]
    for copy in small_copies:
        copy.start()

    run((11, 2), (9, 2), (10, 3), (8, 3), (4, 5), (5, 5), (0, 6), (1, 6))
    reduce_third(1)
    reduce_copies(1)[0].wait_send()

    def mixed_rows(i, carry):
        here = pl.ds(pl.multiple_of(i * step, step), step)
        red_s[1, 0, here, :] = (xs[here, :].astype(F32) + own_acc[1, here, :] + down_b).astype(
            BF16
        )
        return carry

    lax.fori_loop(0, ROWS // step, mixed_rows, 0)
    mixed_ref[...] = dot(out_pick(), red_s[1, 0]).astype(BF16)

    smg[own] = sm[...]
    for b in (sibb, xb, dg):
        remote(sm, smg.at[b], smsend.at[0], smrecv.at[b], sibling).wait_recv()
    for copy in small_copies:
        copy.wait_send()
    first_b = 2 * f
    sma[p, 0:1, :] = smg[first_b, 0:1, :]
    sma[p, 1:2, :] = smg[first_b + 1, 0:1, :]
    sma[p, 2:3, :] = sm[2:3, :]
    sma[p, 3:8, :] = smg[0, 3:8, :] + smg[1, 3:8, :] + smg[2, 3:8, :] + smg[3, 3:8, :]
    sm_copies = [
        remote(sma.at[p], sma.at[p], smsend.at[2 + i], smrecv.at[3 + i], member(p ^ i))
        for i in range(1, CHIPS)
    ]
    for copy in sm_copies:
        copy.start()

    run((11, 3), (9, 3), (10, 4), (8, 4), (6, 5), (7, 5), (2, 6), (3, 6))
    run((11, 4), (9, 4), (10, 5), (8, 5), (4, 6), (5, 6), (11, 5), (9, 5), (6, 6), (7, 6))
    run((10, 6), (8, 6), (11, 6), (9, 6))
    run(*((ch, 7) for ch in range(NCH)))
    total = jnp.zeros((8, D), F32)
    for copy in sm_copies:
        copy.wait()
    for q in range(CHIPS):
        total = total + sma[q]
    small_ref[...] = total

    for copy in (vec_copy,):
        pass
    swap_copy.wait_send()
    for copy in (n_sib, n_x, g_sib, g_x, n_dg, g_dg):
        copy.wait_send()
    for u in range(SEQS):
        for i in range(1, CHIPS):
            out_copy(p ^ i, u).wait_send()
    for n in range(2):
        copies = reduce_copies(n)
        copies[1].wait_send()
        copies[2].wait_send()
    for ch in range(NCH):
        settle(ch)


def widen_kernel(
    dn_h,
    up_h,
    qkv_h,
    out_h,
    small,
    mixed_in,
    tgrad_in,
    dn_o,
    up_o,
    qkv_o,
    out_o,
    mixed_o,
    tgrad_o,
    gain_o,
    shift_o,
    upb_o,
    downb_o,
    dn_b,
    up_b,
    qkv_b,
    out_b,
    dn_f,
    up_f,
    qkv_f,
    out_f,
    isem,
    osem,
):
    f = lax.axis_index("fsdp")
    sources = (up_h, dn_h, qkv_h, out_h)
    brief = (up_b, dn_b, qkv_b, out_b)
    wide = (up_f, dn_f, qkv_f, out_f)
    results = (up_o, dn_o, qkv_o, out_o)
    heights = (128, 256, 128, 128)

    def fetch(n, i):
        if n == 1:
            src = dn_h.at[pl.ds(2 * i, 2)]
        else:
            src = sources[n].at[i]
        return pltpu.make_async_copy(src, brief[n].at[i], isem.at[n, i])

    def put(n, i):
        if n == 3:
            return pltpu.make_async_copy(out_f, out_o, osem.at[3, 0])
        rows = pl.ds(i * heights[n], heights[n])
        return pltpu.make_async_copy(wide[n].at[rows], results[n].at[rows], osem.at[n, i])

    for n in range(4):
        for i in range(8):
            fetch(n, i).start()
    half = D // FSDP
    low_half = f == 0
    pick = jnp.where(low_half, small[:, :half], small[:, half:])
    gain_o[...] = pick[3]
    shift_o[...] = pick[4]
    downb_o[...] = pick[2]
    upb_o[:1024] = small[0]
    upb_o[1024:] = small[1]
    mixed_o[...] = mixed_in[...]
    tgrad_o[...] = tgrad_in[...]
    for n in range(4):
        for i in range(8):
            fetch(n, i).wait()
            values = brief[n][i].astype(F32)
            if n == 3:
                out_f[:, i * 128 : i * 128 + 128] = values.T
            else:
                wide[n][i * heights[n] : (i + 1) * heights[n], :] = values.reshape(
                    heights[n], -1
                )
                put(n, i).start()
    put(3, 0).start()
    for n in range(3):
        for i in range(8):
            put(n, i).wait()
    put(3, 0).wait()


def widen(dn, up, qkv, out_t, small, mixed, tokens_grad):
    vm = pl.BlockSpec(memory_space=pltpu.VMEM)
    hbm = pl.BlockSpec(memory_space=pl.ANY)
    half = D // FSDP
    feeds = FF // FSDP
    heads = 3 * D // FSDP
    return pl.pallas_call(
        widen_kernel,
        out_shape=(
            jax.ShapeDtypeStruct((feeds, D), F32),
            jax.ShapeDtypeStruct((D, feeds), F32),
            jax.ShapeDtypeStruct((D, heads), F32),
            jax.ShapeDtypeStruct((half, D), F32),
            jax.ShapeDtypeStruct((ROWS, D), BF16),
            jax.ShapeDtypeStruct((ROWS, D), BF16),
            jax.ShapeDtypeStruct((half,), F32),
            jax.ShapeDtypeStruct((half,), F32),
            jax.ShapeDtypeStruct((feeds,), F32),
            jax.ShapeDtypeStruct((half,), F32),
        ),
        in_specs=[hbm] * 4 + [vm] * 3,
        out_specs=(hbm,) * 4 + (vm,) * 6,
        scratch_shapes=[
            pltpu.VMEM((8, 2, 128, D), BF16),
            pltpu.VMEM((8, 128, feeds), BF16),
            pltpu.VMEM((8, 128, heads), BF16),
            pltpu.VMEM((8, 128, half), BF16),
            pltpu.VMEM((feeds, D), F32),
            pltpu.VMEM((D, feeds), F32),
            pltpu.VMEM((D, heads), F32),
            pltpu.VMEM((half, D), F32),
            pltpu.SemaphoreType.DMA((4, 8)),
            pltpu.SemaphoreType.DMA((4, 8)),
        ],
        compiler_params=pltpu.CompilerParams(vmem_limit_bytes=56 * 2**20),
    )(
        dn.reshape(16, 128, D),
        up.reshape(8, 128, feeds),
        qkv.reshape(8, 128, heads),
        out_t.reshape(8, 128, half),
        small,
        mixed,
        tokens_grad,
    )


def turn_table():
    lane = np.arange(HEAD_DIM)
    speeds = (10000.0 ** (-(lane // 2 * 2) / ROT_DIM)).astype(np.float32)
    phase = np.arange(LENGTH, dtype=np.float32)[:, None] * speeds[None, :]
    turning = (lane < ROT_DIM)[None, :]
    sign = np.where(lane % 2 == 0, -1.0, 1.0)[None, :]
    cosine = np.where(turning, np.cos(phase), 1.0)
    sine = np.where(turning, np.sin(phase) * sign, 0.0)
    table = np.concatenate((cosine, sine), axis=1).astype(np.float32)
    return table.reshape(4 * CHIPS, HALF, 2 * HEAD_DIM)


def fused_device(
    tokens,
    block_pairs,
    norm_gain,
    norm_bias,
    qkv_weight,
    out_weight,
    up_weight,
    up_bias,
    down_weight,
    down_bias,
    cotangent,
):
    order = jnp.stack((block_pairs, 4 * CHIPS - 1 - block_pairs), axis=1).reshape(4 * CHIPS)
    numbers = jnp.arange(4 * CHIPS, dtype=jnp.int32)
    hits = order[None, :] == numbers[:, None]
    spots = jnp.concatenate(
        (
            jnp.sum(jnp.where(hits, numbers[None, :] // 2, 0), axis=1),
            jnp.sum(jnp.where(hits, numbers[None, :] % 2, 0), axis=1),
            order,
        )
    ).astype(jnp.int32)
    vec = jnp.concatenate(
        (
            norm_gain,
            norm_bias,
            down_bias,
            up_bias,
            jnp.zeros((9 * norm_gain.shape[0],), BF16),
        )
    ).reshape(16, norm_gain.shape[0])

    vm = pl.BlockSpec(memory_space=pltpu.VMEM)
    sme = pl.BlockSpec(memory_space=pltpu.SMEM)
    hbm = pl.BlockSpec(memory_space=pl.ANY)
    dma = pltpu.SemaphoreType.DMA
    scratch = [
        pltpu.VMEM((4 * CHIPS, HALF, 128), F32),
        pltpu.VMEM((16, 512), F32),
        pltpu.VMEM((2, 16, 512), BF16),
        pltpu.VMEM((ROWS, D), BF16),
        pltpu.VMEM((ALL, D), BF16),
        pltpu.VMEM((ALL, D), BF16),
        pltpu.VMEM((3, D, 256), BF16),
        pltpu.VMEM((256, D), BF16),
        pltpu.VMEM((D, 1024), BF16),
        pltpu.VMEM((1024, D), BF16),
        pltpu.VMEM((ALL, 1024), BF16),
        pltpu.VMEM((ALL, 1024), BF16),
        pltpu.VMEM((CHIPS, 2, 2, 4, HALF, 128), BF16),
        pltpu.VMEM((2 * CHIPS, 2, 4, HALF, 128), BF16),
        pltpu.VMEM((LENGTH, HEAD_DIM), BF16),
        pltpu.VMEM((LENGTH, HEAD_DIM), BF16),
        pltpu.VMEM((LENGTH, HEAD_DIM), BF16),
        pltpu.VMEM((LENGTH, HEAD_DIM), BF16),
        pltpu.VMEM((HEAD_DIM, LENGTH), BF16),
        pltpu.VMEM((HEAD_DIM, LENGTH), BF16),
        pltpu.VMEM((HEAD_DIM, LENGTH), BF16),
        pltpu.VMEM((LENGTH, QB), F32),
        pltpu.VMEM((LENGTH, HEAD_DIM), F32),
        pltpu.VMEM((LENGTH, HEAD_DIM), F32),
        pltpu.VMEM((2, 4 * CHIPS, HALF, 128), BF16),
        pltpu.VMEM((CHIPS, SEQS, 2, 4, HALF, 128), BF16),
        pltpu.VMEM((ALL, 256), BF16),
        pltpu.VMEM((3, ALL, 256), BF16),
        pltpu.VMEM((NCH, 2, 2, 2, 128, 256), BF16),
        pltpu.VMEM((NCH, 2, 2, 128, 256), BF16),
        pltpu.VMEM((NCH, 2, 128, 256), BF16),
        pltpu.VMEM((NCH, 128, 256), BF16),
        pltpu.VMEM((128, 256), BF16),
        pltpu.VMEM((2, ROWS, D), F32),
        pltpu.VMEM((2, 2, ROWS, D), BF16),
        pltpu.VMEM((2, ROWS, D), BF16),
        pltpu.VMEM((2, 2, ROWS, D), BF16),
        pltpu.VMEM((2, ROWS, D), BF16),
        pltpu.VMEM((8, D), F32),
        pltpu.VMEM((4, 8, D), F32),
        pltpu.VMEM((CHIPS, 8, D), F32),
        dma((6,)),
        dma((9,)),
        dma((9,)),
        dma((CHIPS, 2, 2)),
        dma((CHIPS, 2, 2)),
        dma((CHIPS, SEQS)),
        dma((CHIPS, SEQS)),
        dma((NCH, 3)),
        dma((NCH, 3)),
        dma((NCH, 3)),
        dma((NCH, 3)),
        dma((NCH,)),
        dma((NCH,)),
        dma((NCH,)),
        dma((2, 3)),
        dma((2, 3)),
        dma((10,)),
        dma((11,)),
    ]
    mixed, tokens_grad, small, dn, up, qkv, out_t = pl.pallas_call(
        fused_kernel,
        out_shape=(
            jax.ShapeDtypeStruct((ROWS, D), BF16),
            jax.ShapeDtypeStruct((ROWS, D), BF16),
            jax.ShapeDtypeStruct((8, D), F32),
            jax.ShapeDtypeStruct((2, 2, 2, 2, 128, D), BF16),
            jax.ShapeDtypeStruct((2, 2, 2, 128, FF // FSDP), BF16),
            jax.ShapeDtypeStruct((2, 2, 2, 128, 3 * D // FSDP), BF16),
            jax.ShapeDtypeStruct((2, 2, 2, 128, D // FSDP), BF16),
        ),
        in_specs=[sme, vm, hbm, vm, vm] + [hbm] * 4,
        out_specs=(vm, vm, vm, hbm, hbm, hbm, hbm),
        scratch_shapes=scratch,
        compiler_params=pltpu.CompilerParams(
            collective_id=0, has_side_effects=True, vmem_limit_bytes=63 * 2**20
        ),
    )(
        spots,
        vec,
        jnp.asarray(turn_table()),
        tokens,
        cotangent,
        qkv_weight,
        out_weight,
        up_weight,
        down_weight,
    )
    dn, up, qkv, out, mixed, tokens_grad, gain, shift, upb, downb = widen(
        dn, up, qkv, out_t, small, mixed, tokens_grad
    )
    return mixed, tokens_grad, gain, shift, qkv, out, up, upb, dn, downb


def solution(mesh):
    in_specs = (
        P(("fsdp", "ctx"), None),
        P(),
        P("fsdp"),
        P("fsdp"),
        P(None, "fsdp"),
        P("fsdp", None),
        P(None, "fsdp"),
        P("fsdp"),
        P("fsdp", None),
        P("fsdp"),
        P(("fsdp", "ctx"), None),
    )
    out_specs = (
        P(("fsdp", "ctx"), None),
        P(("fsdp", "ctx"), None),
        P("fsdp"),
        P("fsdp"),
        P(None, "fsdp"),
        P("fsdp", None),
        P(None, "fsdp"),
        P("fsdp"),
        P("fsdp", None),
        P("fsdp"),
    )
    plan = fused_device if fits(mesh) else per_device
    return jax.shard_map(
        plan, mesh=mesh, in_specs=in_specs, out_specs=out_specs, check_vma=False
    )
```

```python
import functools
import math

import jax
import jax.numpy as jnp
import numpy as np
from jax import lax
from jax.experimental import pallas as pl
from jax.experimental.pallas import tpu as pltpu
from jax.sharding import PartitionSpec as P

D = 1024
HEAD_DIM = 64
ROT_DIM = 32
HEADS = 16
SEQ_DEV_TOK = 128
SEQS = 2


EPS = 1e-05
HIGHEST = lax.Precision.HIGHEST
masked_score = -1e30


def layer_norm(values, gain_values, shift_values):
    center = values - jnp.mean(values, axis=-1, keepdims=True)
    spread = jnp.mean(center * center, axis=-1, keepdims=True)
    return center * lax.rsqrt(spread + EPS) * gain_values + shift_values


def rotary_tables(places, window):
    lanes = jnp.arange(window, dtype=jnp.int32)
    within_head = lanes % HEAD_DIM
    turning = within_head < ROT_DIM
    steps_up = (within_head // 2 * 2).astype(jnp.float32)
    speeds = 10000.0 ** (-steps_up / ROT_DIM)
    phase = places.astype(jnp.float32)[:, None] * speeds[None, :]
    cos_full = jnp.where(turning[None, :], jnp.cos(phase), 1.0)
    sin_full = jnp.where(turning[None, :], jnp.sin(phase), 0.0)
    row_lane = lanes[:, None]
    col_lane = lanes[None, :]
    same_head = row_lane // HEAD_DIM == col_lane // HEAD_DIM
    col_within = col_lane % HEAD_DIM
    col_turns = same_head & (col_within < ROT_DIM)
    even_col = col_within % 2 == 0
    minus_part = jnp.where(col_turns & even_col & (row_lane == col_lane + 1), -1.0, 0.0)
    plus_part = jnp.where(
        col_turns & jnp.logical_not(even_col) & (row_lane == col_lane - 1), 1.0, 0.0
    )
    swap_table = (minus_part + plus_part).astype(jnp.float32)
    return (cos_full, sin_full, swap_table)


def smooth_gate(values):
    return jax.nn.gelu(values, approximate=True)


def positions(first_row, row_count, pair_table, devices, seq_rows):
    indices = first_row + jnp.arange(row_count, dtype=jnp.int32)
    owners = indices // seq_rows
    within = indices % seq_rows
    half_rows = seq_rows // 2
    matches = owners[:, None] == jnp.arange(devices, dtype=jnp.int32)[None, :]
    chosen = jnp.sum(jnp.where(matches, pair_table[None, :], 0), axis=1)
    block_index = jnp.where(within < half_rows, chosen, 2 * devices - 1 - chosen)
    return block_index * half_rows + within % half_rows


def in_groups(row_count, seq_rows):
    group_rows = math.gcd(row_count // seq_rows, 8) * seq_rows
    return (group_rows, row_count // group_rows)


def split_groups(array, group_rows, turns):
    return array.reshape((turns, group_rows) + array.shape[1:])


def grad_scores(
    query_rows,
    out_grads,
    log_sums,
    row_dots,
    query_places,
    key_rows,
    value_rows,
    key_places,
    factor,
):
    scores = (
        jnp.einsum("qshe,kshe->shqk", query_rows, key_rows, preferred_element_type=jnp.float32)
        * factor
    )
    allowed = key_places[None, :] <= query_places[:, None]
    chances = jnp.exp(jnp.where(allowed, scores - log_sums[..., None], masked_score))
    prob_grads = jnp.einsum(
        "qshe,kshe->shqk", out_grads, value_rows, preferred_element_type=jnp.float32
    )
    return (chances, (chances * (prob_grads - row_dots[..., None])).astype(jnp.bfloat16))


def per_device(
    tokens,
    block_pairs,
    norm_gain,
    norm_bias,
    qkv_weight,
    out_weight,
    up_weight,
    up_bias,
    down_weight,
    down_bias,
    cotangent,
):
    devices = lax.axis_size("ctx")
    own_index = lax.axis_index("ctx")
    seq_rows = SEQ_DEV_TOK
    seq_count = SEQS
    heads = HEADS
    head_size = HEAD_DIM
    width = D
    factor = HEAD_DIM ** (-0.5)
    all_rows = seq_rows * seq_count
    window = math.gcd(width, 128)
    gathered = (
        lax.all_gather(norm_gain, "fsdp", axis=0, tiled=True),
        lax.all_gather(norm_bias, "fsdp", axis=0, tiled=True),
        lax.all_gather(qkv_weight, "fsdp", axis=1, tiled=True),
        lax.all_gather(out_weight, "fsdp", axis=0, tiled=True),
        lax.all_gather(up_weight, "fsdp", axis=1, tiled=True),
        lax.all_gather(up_bias, "fsdp", axis=0, tiled=True),
        lax.all_gather(down_weight, "fsdp", axis=0, tiled=True),
        lax.all_gather(down_bias, "fsdp", axis=0, tiled=True),
    )
    gain_low, shift_low, w_qkv, w_out, w_up, b_up, w_down, b_down = gathered
    inputs = tokens.astype(jnp.float32)
    gain_values = gain_low.astype(jnp.float32)
    shift_values = shift_low.astype(jnp.float32)
    normed_low = layer_norm(inputs, gain_values, shift_values).astype(jnp.bfloat16)
    mixed_qkv = jnp.dot(normed_low, w_qkv, preferred_element_type=jnp.float32).reshape(
        seq_rows, seq_count, 3 * width
    )
    own_places = positions(own_index * seq_rows, seq_rows, block_pairs, devices, seq_rows)
    cos_full, sin_full, swap_table = rotary_tables(own_places, window)

    def turn_both(values):
        shaped = values.reshape(seq_rows, seq_count, 2 * width // window, window)
        swapped = jnp.einsum("rsgw,wv->rsgv", shaped, swap_table, precision=HIGHEST)
        turned_rows = shaped * cos_full[:, None, None, :] + swapped * sin_full[:, None, None, :]
        return turned_rows.reshape(seq_rows, seq_count, 2 * width)

    query_key = mixed_qkv[:, :, : 2 * width]
    turned = turn_both(query_key)
    queries = (
        turned[:, :, :width].astype(jnp.bfloat16).reshape(seq_rows, seq_count, heads, head_size)
    )
    key_rows = (
        turned[:, :, width:].astype(jnp.bfloat16).reshape(seq_rows, seq_count, heads, head_size)
    )
    value_rows = (
        mixed_qkv[:, :, 2 * width :]
        .astype(jnp.bfloat16)
        .reshape(seq_rows, seq_count, heads, head_size)
    )
    start_state = (
        jnp.full((seq_count, heads, seq_rows), masked_score, jnp.float32),
        jnp.zeros((seq_count, heads, seq_rows), jnp.float32),
        jnp.zeros((seq_count, heads, seq_rows, head_size), jnp.float32),
    )
    piece_keys = lax.all_gather(key_rows, "ctx", axis=0, tiled=True)
    piece_values = lax.all_gather(value_rows, "ctx", axis=0, tiled=True)
    group_rows, turns = in_groups(piece_keys.shape[0], seq_rows)

    def attend_step(inner, item):
        block_keys, block_values, turn = item
        key_places = positions(turn * group_rows, group_rows, block_pairs, devices, seq_rows)
        scores = (
            jnp.einsum("qshe,kshe->shqk", queries, block_keys, preferred_element_type=jnp.float32)
            * factor
        )
        allowed = key_places[None, :] <= own_places[:, None]
        running, totals, accum = inner
        fresh = jnp.maximum(running, jnp.max(jnp.where(allowed, scores, masked_score), axis=-1))
        weights = jnp.exp(jnp.where(allowed, scores - fresh[..., None], masked_score))
        fading = jnp.exp(running - fresh)
        totals = totals * fading + jnp.sum(weights, axis=-1)
        accum = accum * fading[..., None] + jnp.einsum(
            "shqk,kshe->shqe",
            weights.astype(jnp.bfloat16),
            block_values,
            preferred_element_type=jnp.float32,
        )
        return ((fresh, totals, accum), None)

    inner, _ = lax.scan(
        attend_step,
        start_state,
        (
            split_groups(piece_keys, group_rows, turns),
            split_groups(piece_values, group_rows, turns),
            jnp.arange(turns, dtype=jnp.int32),
        ),
    )
    running, totals, accum = inner
    log_sums = running + jnp.log(totals)
    attended = jnp.transpose(accum / totals[..., None], (2, 0, 1, 3))
    attn_low = attended.reshape(all_rows, width).astype(jnp.bfloat16)
    attention = jnp.dot(attn_low, w_out, preferred_element_type=jnp.float32)
    up_pre = jnp.dot(normed_low, w_up, preferred_element_type=jnp.float32) + b_up.astype(
        jnp.float32
    )
    hidden_low = smooth_gate(up_pre).astype(jnp.bfloat16)
    result = (
        inputs
        + attention
        + jnp.dot(hidden_low, w_down, preferred_element_type=jnp.float32)
        + b_down.astype(jnp.float32)
    )
    mixed = result.astype(jnp.bfloat16)
    again = (
        lax.all_gather(norm_gain, "fsdp", axis=0, tiled=True),
        lax.all_gather(norm_bias, "fsdp", axis=0, tiled=True),
        lax.all_gather(qkv_weight, "fsdp", axis=1, tiled=True),
        lax.all_gather(out_weight, "fsdp", axis=0, tiled=True),
        lax.all_gather(up_weight, "fsdp", axis=1, tiled=True),
        lax.all_gather(up_bias, "fsdp", axis=0, tiled=True),
        lax.all_gather(down_weight, "fsdp", axis=0, tiled=True),
        lax.all_gather(down_bias, "fsdp", axis=0, tiled=True),
    )
    gain_low, shift_low, w_qkv, w_out, w_up, b_up, w_down, b_down = again
    out_grad = cotangent.astype(jnp.float32)
    attn_grads = (
        jnp.einsum("td,ed->te", cotangent, w_out, preferred_element_type=jnp.float32)
        .astype(jnp.bfloat16)
        .reshape(seq_rows, seq_count, heads, head_size)
    )
    dots_rows = jnp.sum(attn_grads.astype(jnp.float32) * attended, axis=-1)
    row_dots = jnp.transpose(dots_rows, (1, 2, 0))
    empty_rows = jnp.zeros((seq_rows, seq_count, heads, head_size), jnp.float32)
    whole_keys, whole_values = (
        lax.all_gather(key_rows, "ctx", axis=0, tiled=True),
        lax.all_gather(value_rows, "ctx", axis=0, tiled=True),
    )
    piece_keys = whole_keys
    piece_values = whole_values
    query_group_rows, turns = in_groups(piece_keys.shape[0], seq_rows)

    def query_step(inner, item):
        block_keys, block_values, turn = item
        key_places = positions(
            0 + turn * query_group_rows, query_group_rows, block_pairs, devices, seq_rows
        )
        chances, score_grads = grad_scores(
            queries,
            attn_grads,
            log_sums,
            row_dots,
            own_places,
            block_keys,
            block_values,
            key_places,
            factor,
        )
        return (
            inner
            + jnp.einsum(
                "shqk,kshe->qshe", score_grads, block_keys, preferred_element_type=jnp.float32
            )
            * factor,
            None,
        )

    inner, _ = lax.scan(
        query_step,
        empty_rows,
        (
            split_groups(piece_keys, query_group_rows, turns),
            split_groups(piece_values, query_group_rows, turns),
            jnp.arange(turns, dtype=jnp.int32),
        ),
    )
    query_grad = inner
    piece_keys = whole_keys
    piece_values = whole_values
    key_group_rows, turns = in_groups(seq_rows * lax.axis_size("ctx"), seq_rows)

    def key_step(inner, item):
        block_keys, block_values, turn = item
        key_places = positions(
            turn * key_group_rows, key_group_rows, block_pairs, devices, seq_rows
        )
        chances, score_grads = grad_scores(
            queries,
            attn_grads,
            log_sums,
            row_dots,
            own_places,
            block_keys,
            block_values,
            key_places,
            factor,
        )
        key_part = (
            jnp.einsum("shqk,qshe->kshe", score_grads, queries, preferred_element_type=jnp.float32)
            * factor
        )
        value_part = jnp.einsum(
            "shqk,qshe->kshe",
            chances.astype(jnp.bfloat16),
            attn_grads,
            preferred_element_type=jnp.float32,
        )
        stacked = jnp.stack(
            (
                key_part.reshape(key_group_rows, seq_count, width),
                value_part.reshape(key_group_rows, seq_count, width),
            ),
            axis=2,
        )
        return (inner, stacked)

    _, blocks_out = lax.scan(
        key_step,
        jnp.zeros((), jnp.float32),
        (
            split_groups(piece_keys, key_group_rows, turns),
            split_groups(piece_values, key_group_rows, turns),
            jnp.arange(turns, dtype=jnp.int32),
        ),
    )
    summed_terms = lax.psum_scatter(
        blocks_out.reshape(seq_rows * lax.axis_size("ctx"), seq_count, 2, width),
        "ctx",
        scatter_dimension=0,
        tiled=True,
    )
    key_grad = summed_terms[:, :, 0].reshape(seq_rows, seq_count, heads, head_size)
    value_grad = summed_terms[:, :, 1].reshape(seq_rows, seq_count, heads, head_size)
    _, turn_back = jax.vjp(turn_both, query_key)
    both_grads = jnp.concatenate(
        (
            query_grad.reshape(seq_rows, seq_count, width),
            key_grad.reshape(seq_rows, seq_count, width),
        ),
        axis=2,
    )
    (pre_grads,) = turn_back(both_grads)
    qkv_grad = (
        jnp.concatenate((pre_grads, value_grad.reshape(seq_rows, seq_count, width)), axis=2)
        .reshape(all_rows, 3 * width)
        .astype(jnp.bfloat16)
    )
    hidden_grad = jnp.einsum("td,fd->tf", cotangent, w_down, preferred_element_type=jnp.float32)
    _, gate_back = jax.vjp(smooth_gate, up_pre)
    (up_grad,) = gate_back(hidden_grad)
    up_low = up_grad.astype(jnp.bfloat16)
    normed_grad = jnp.einsum(
        "tc,dc->td", qkv_grad, w_qkv, preferred_element_type=jnp.float32
    ) + jnp.einsum("tf,df->td", up_low, w_up, preferred_element_type=jnp.float32)
    _, norm_back = jax.vjp(
        layer_norm, inputs, gain_low.astype(jnp.float32), shift_low.astype(jnp.float32)
    )
    input_part, gain_grad, shift_grad = norm_back(normed_grad)
    tokens_grad = (out_grad + input_part).astype(jnp.bfloat16)
    qkv_wgrad = jnp.einsum("td,tc->dc", normed_low, qkv_grad, preferred_element_type=jnp.float32)
    out_wgrad = jnp.einsum("td,te->de", attn_low, cotangent, preferred_element_type=jnp.float32)
    up_wgrad = jnp.einsum("td,tf->df", normed_low, up_low, preferred_element_type=jnp.float32)
    up_bgrad = jnp.sum(up_low.astype(jnp.float32), axis=0)
    down_wgrad = jnp.einsum("tf,td->fd", hidden_low, cotangent, preferred_element_type=jnp.float32)
    down_bgrad = jnp.sum(out_grad, axis=0)
    shares = (
        lax.psum_scatter(
            gain_grad.astype(jnp.bfloat16), "fsdp", scatter_dimension=0, tiled=True
        ).astype(jnp.float32),
        lax.psum_scatter(
            shift_grad.astype(jnp.bfloat16), "fsdp", scatter_dimension=0, tiled=True
        ).astype(jnp.float32),
        lax.psum_scatter(
            qkv_wgrad.astype(jnp.bfloat16), "fsdp", scatter_dimension=1, tiled=True
        ).astype(jnp.float32),
        lax.psum_scatter(
            out_wgrad.astype(jnp.bfloat16), "fsdp", scatter_dimension=0, tiled=True
        ).astype(jnp.float32),
        lax.psum_scatter(
            up_wgrad.astype(jnp.bfloat16), "fsdp", scatter_dimension=1, tiled=True
        ).astype(jnp.float32),
        lax.psum_scatter(
            up_bgrad.astype(jnp.bfloat16), "fsdp", scatter_dimension=0, tiled=True
        ).astype(jnp.float32),
        lax.psum_scatter(
            down_wgrad.astype(jnp.bfloat16), "fsdp", scatter_dimension=0, tiled=True
        ).astype(jnp.float32),
        lax.psum_scatter(
            down_bgrad.astype(jnp.bfloat16), "fsdp", scatter_dimension=0, tiled=True
        ).astype(jnp.float32),
    )
    share_gain, share_shift, share_qkv, share_out, share_up, share_upb, share_down, share_downb = (
        shares
    )
    totals_out = lax.psum(
        (
            share_gain,
            share_shift,
            share_qkv,
            share_out,
            share_up,
            share_upb,
            share_down,
            share_downb,
        ),
        "ctx",
    )
    sum_gain, sum_shift, sum_qkv, sum_out, sum_up, sum_upb, sum_down, sum_downb = totals_out
    return (
        mixed,
        tokens_grad,
        sum_gain,
        sum_shift,
        sum_qkv,
        sum_out,
        sum_up,
        sum_upb,
        sum_down,
        sum_downb,
    )


F32 = jnp.float32
BF16 = jnp.bfloat16
FF = 4096
FSDP = 2
CHIPS = 8
ROWS = SEQ_DEV_TOK * SEQS
ALL = 4 * ROWS
LENGTH = CHIPS * 2 * SEQ_DEV_TOK
HALF = SEQ_DEV_TOK // 2
QB = 512
NCH = 12
MASKS = (1, 2, 4)
SCATTER = {0: (2, 1, 0), 3: (1, 0, 2), 7: (1, 0, 2)}
GATHER = {2: (1, 2, 0), 3: (2, 0, 1), 4: (1, 2, 0), 5: (1, 2, 0), 6: (2, 0, 1), 7: (1, 2, 0), 8: (1, 2, 0), 9: (0, 2, 1), 10: (2, 0, 1)}
SCALE = HEAD_DIM**-0.5


def fits(mesh):
    return mesh.shape["fsdp"] == FSDP and mesh.shape["ctx"] == 2 * CHIPS


def dot(left, right):
    return lax.dot_general(left, right, (((1,), (0,)), ((), ())), preferred_element_type=F32)


def dot_nt(left, right):
    return lax.dot_general(left, right, (((1,), (1,)), ((), ())), preferred_element_type=F32)


def dot_tn(left, right):
    return lax.dot_general(left, right, (((0,), (0,)), ((), ())), preferred_element_type=F32)


def turn(values, cosine, sine):
    lane = lax.broadcasted_iota(jnp.int32, values.shape, 1)
    width = values.shape[1]
    other = jnp.where(
        lane % 2 == 0, pltpu.roll(values, width - 1, 1), pltpu.roll(values, 1, 1)
    )
    return values * cosine + other * sine


def gate(values):
    inner = 0.7978845608028654 * (values + 0.044715 * values * values * values)
    th = jnp.tanh(inner)
    half = 0.5 * (1.0 + th)
    slope = half + (0.5 * values) * (1.0 - th * th) * (
        0.7978845608028654 * (1.0 + 3 * 0.044715 * values * values)
    )
    return values * half, slope


def fused_kernel(
    pairs_ref,
    gain_ref,
    shift_ref,
    downb_ref,
    upb_ref,
    turns_h,
    tok_ref,
    cot_ref,
    wqkv_h,
    wout_h,
    wup_h,
    wdn_h,
    mixed_ref,
    tgrad_ref,
    small_ref,
    odn,
    oup,
    oqkv,
    oout,
    spots_ref,
    turns,
    vall,
    xs,
    nrm,
    gal,
    wq,
    wout,
    wup,
    wdn,
    hid,
    upg,
    sbuf,
    rbuf,
    aq,
    ag,
    ak,
    av,
    akt,
    avt,
    agt,
    sco,
    dka,
    dva,
    osrt,
    rb2,
    aall,
    dqkv,
    mats,
    rs0,
    rs1,
    rs2,
    xsw,
    own_acc,
    red_s,
    red_x,
    red_r,
    red_xr,
    sm,
    smg,
    sma,
    lsem,
    gsend,
    grecv,
    asend,
    arecv,
    osend,
    orecv,
    rssend,
    rsrecv,
    agsend,
    agrecv,
    clocal,
    csend,
    crecv,
    dsend,
    drecv,
    smsend,
    smrecv,
):
    f = lax.axis_index("fsdp")
    c = lax.axis_index("ctx")
    k = c % 2
    p = c // 2
    zz = p // 2
    yy = p % 2
    xpart = (1 - f, c)
    sibling = (f, 2 * p + 1 - k)
    diagonal = (1 - f, 2 * p + 1 - k)
    own = 2 * f + k
    sibb = 2 * f + 1 - k
    xb = 2 * (1 - f) + k
    dg = 2 * (1 - f) + 1 - k
    MESH = pl.DeviceIdType.MESH

    def member(q):
        return (f, 2 * q + k)

    def remote(src, dst, ssem, rsem, device):
        return pltpu.make_async_remote_copy(
            src_ref=src,
            dst_ref=dst,
            send_sem=ssem,
            recv_sem=rsem,
            device_id=device,
            device_id_type=MESH,
        )

    def rows(b):
        return pl.ds(pl.multiple_of(b * ROWS, ROWS), ROWS)

    def lanes(i, n):
        return pl.ds(pl.multiple_of(i * n, n), n)

    loads = [
        pltpu.make_async_copy(wqkv_h.at[:, lanes(k, 256)], wq.at[f], lsem.at[0]),
        pltpu.make_async_copy(
            wqkv_h.at[:, pl.ds(pl.multiple_of(1024 + 256 * k, 256), 256)], wq.at[1 + f], lsem.at[1]
        ),
        pltpu.make_async_copy(wup_h.at[:, lanes(k, 1024)], wup, lsem.at[2]),
        pltpu.make_async_copy(wdn_h.at[lanes(k, 1024), :], wdn, lsem.at[3]),
        pltpu.make_async_copy(wout_h.at[lanes(k, 256), :], wout, lsem.at[4]),
        pltpu.make_async_copy(turns_h, turns, lsem.at[5]),
    ]
    for load in loads:
        load.start()
    barrier = pltpu.get_barrier_semaphore()
    for device in [xpart, sibling, diagonal] + [member(p ^ i) for i in range(1, CHIPS)]:
        pl.semaphore_signal(barrier, inc=1, device_id=device, device_id_type=MESH)
    pl.semaphore_wait(barrier, 3 + CHIPS - 1)

    def row_of(ref, at):
        return ref[pl.ds(at, 512)].astype(F32).reshape(1, 512)

    vall[f] = jnp.concatenate(
        [row_of(gain_ref, 0), row_of(shift_ref, 0), row_of(downb_ref, 0)]
        + [row_of(upb_ref, 512 * i) for i in range(4)]
        + [jnp.zeros((1, 512), F32)],
        axis=0,
    )
    vec_copy = remote(vall.at[f], vall.at[f], gsend.at[0], grecv.at[0], xpart)
    vec_copy.start()
    swap_copy = remote(
        wqkv_h.at[:, pl.ds(pl.multiple_of(512 + 256 * k, 256), 256)],
        wq.at[2 * f],
        gsend.at[1],
        grecv.at[1],
        xpart,
    )
    swap_copy.start()

    def table_row(b, carry):
        holder = jnp.int32(0)
        half = jnp.int32(0)
        for i in range(2 * CHIPS):
            first = (pairs_ref[i] == b).astype(jnp.int32)
            last = (4 * CHIPS - 1 - pairs_ref[i] == b).astype(jnp.int32)
            holder = holder + i * (first + last)
            half = half + last
        spots_ref[b] = jnp.minimum(holder, 2 * CHIPS - 1)
        spots_ref[4 * CHIPS + b] = jnp.minimum(half, 1)
        return carry

    lax.fori_loop(0, 4 * CHIPS, table_row, 0)

    def table_pair(i, carry):
        spots_ref[64 + 2 * i] = pairs_ref[i]
        spots_ref[64 + 2 * i + 1] = 4 * CHIPS - 1 - pairs_ref[i]
        return carry

    lax.fori_loop(0, 2 * CHIPS, table_pair, 0)
    vec_copy.wait()
    gain = jnp.concatenate([vall[0, 0:1, :], vall[1, 0:1, :]], axis=1).astype(F32)
    shift = jnp.concatenate([vall[0, 1:2, :], vall[1, 1:2, :]], axis=1).astype(F32)
    down_b = jnp.concatenate([vall[0, 2:3, :], vall[1, 2:3, :]], axis=1).astype(F32)

    step = 64

    def norm_rows(i, carry):
        here = pl.ds(pl.multiple_of(i * step, step), step)
        there = pl.ds(pl.multiple_of(own * ROWS + i * step, step), step)
        row = lax.broadcasted_iota(jnp.int32, (step, ROWS), 0) + i * step
        col = lax.broadcasted_iota(jnp.int32, (step, ROWS), 1)
        pick = (col == 2 * (row % SEQ_DEV_TOK) + row // SEQ_DEV_TOK).astype(F32).astype(BF16)
        values = dot(pick, tok_ref[...])
        gal[there, :] = dot(pick, cot_ref[...]).astype(BF16)
        xs[here, :] = values.astype(BF16)
        center = values - jnp.mean(values, axis=1, keepdims=True)
        spread = jnp.mean(center * center, axis=1, keepdims=True)
        nrm[there, :] = (center * lax.rsqrt(spread + EPS) * gain + shift).astype(BF16)
        return carry

    lax.fori_loop(0, ROWS // step, norm_rows, 0)

    def spread_copy(buf, b, n, device):
        return remote(buf.at[rows(b)], buf.at[rows(b)], gsend.at[n], grecv.at[n], device)

    n_sib = spread_copy(nrm, own, 2, sibling)
    n_x = spread_copy(nrm, own, 3, xpart)
    g_sib = spread_copy(gal, own, 4, sibling)
    g_x = spread_copy(gal, own, 5, xpart)
    for copy in (n_sib, n_x, g_sib, g_x):
        copy.start()
    for load in loads:
        load.wait()

    def up_part_of(b, i):
        at = k * 1024 + i * 256
        bias = vall[f, pl.ds(3 + at // 512, 1), pl.ds(pl.multiple_of(at % 512, 256), 256)]
        return gate(dot(nrm[rows(b), :], wup[:, lanes(i, 256)]) + bias)

    def feed_block(b):
        def part(i, carry):
            cols = lanes(i, 256)
            value, slope = up_part_of(b, i)
            hid[rows(b), cols] = value.astype(BF16)
            back = dot_nt(gal[rows(b), :], wdn[cols, :])
            upg[rows(b), cols] = (back * slope).astype(BF16)
            return carry

        lax.fori_loop(0, 4, part, 0)

    def feed_up(b, n):
        def part(i, carry):
            cols = lanes(i, 256)
            value, slope = up_part_of(b, i)
            hid[rows(b), cols] = value.astype(BF16)
            own_acc[n, :, cols] = slope
            return carry

        lax.fori_loop(0, 4, part, 0)

    def feed_back(b, n):
        def part(i, carry):
            cols = lanes(i, 256)
            back = dot_nt(gal[rows(b), :], wdn[cols, :])
            upg[rows(b), cols] = (back * own_acc[n, :, cols]).astype(BF16)
            return carry

        lax.fori_loop(0, 4, part, 0)

    def put_heads(first, second, fq, kq, t):
        for h in range(4):
            sbuf[2 * h + fq, t, kq] = jnp.concatenate(
                [first[:, 64 * h : 64 * h + 64], second[:, 64 * h : 64 * h + 64]], axis=1
            ).reshape(4, HALF, 128)

    def turned(values, kq):
        table = jnp.concatenate(
            [turns[spots_ref[64 + 2 * (2 * p + kq) + half]] for half in range(2)], axis=0
        )
        cosine = jnp.concatenate([table[:, :64], table[:, :64]], axis=1)
        sine = jnp.concatenate([table[:, 64:], table[:, 64:]], axis=1)
        parts = []
        for s in range(SEQS):
            line = []
            for half in range(2):
                piece = values[128 * s : 128 * s + 128, 128 * half : 128 * half + 128]
                line.append(turn(piece, cosine, sine))
            parts.append(jnp.concatenate(line, axis=1))
        return jnp.concatenate(parts, axis=0).astype(BF16)

    def kg_block(b, fq, kq):
        key = dot(nrm[rows(b), :], wq[1])
        grads = dot_nt(gal[rows(b), :], wout[...]).astype(BF16)
        put_heads(turned(key, kq), grads, fq, kq, 0)

    def qv_block(b, fq, kq):
        query = dot(nrm[rows(b), :], wq[0])
        value = dot(nrm[rows(b), :], wq[2]).astype(BF16)
        put_heads(turned(query, kq) * BF16(SCALE), value, fq, kq, 1)

    def in_copy(q, t, kq):
        return remote(
            sbuf.at[q, t, kq],
            rbuf.at[2 * p + kq, t],
            asend.at[q, t, kq],
            arecv.at[p, t, kq],
            member(q),
        )

    def send_block(fq, kq, t):
        for i in range(4):
            q = 2 * (zz ^ i) + fq
            if i == 0:

                @pl.when(fq == yy)
                def _():
                    pltpu.make_async_copy(
                        sbuf.at[q, t, kq], rbuf.at[2 * p + kq, t], arecv.at[p, t, kq]
                    ).start()

                @pl.when(fq != yy)
                def _():
                    in_copy(q, t, kq).start()
            else:
                in_copy(q, t, kq).start()

    def sent_block(fq, kq, t):
        for i in range(4):
            q = 2 * (zz ^ i) + fq
            if i == 0:

                @pl.when(fq != yy)
                def _():
                    in_copy(q, t, kq).wait_send()
            else:
                in_copy(q, t, kq).wait_send()

    kg_block(own, f, k)
    send_block(f, k, 0)
    n_sib.wait_recv()
    g_sib.wait_recv()
    kg_block(sibb, f, 1 - k)
    send_block(f, 1 - k, 0)
    feed_block(own)
    feed_block(sibb)
    swap_copy.wait_recv()
    for b, kq in ((own, k), (sibb, 1 - k)):
        qv_block(b, f, kq)
        send_block(f, kq, 1)
    n_x.wait_recv()
    n_dg = spread_copy(nrm, xb, 6, sibling)
    n_dg.start()
    qv_block(xb, 1 - f, k)
    send_block(1 - f, k, 1)
    n_dg.wait_recv()
    qv_block(dg, 1 - f, 1 - k)
    send_block(1 - f, 1 - k, 1)
    feed_up(xb, 0)
    feed_up(dg, 1)
    g_x.wait_recv()
    g_dg = spread_copy(gal, xb, 7, sibling)
    g_dg.start()
    kg_block(xb, 1 - f, k)
    send_block(1 - f, k, 0)
    g_dg.wait_recv()
    kg_block(dg, 1 - f, 1 - k)
    send_block(1 - f, 1 - k, 0)
    feed_back(xb, 0)
    feed_back(dg, 1)

    def store_rows(ch, i, values):
        mats[ch, i // 2, i % 2] = values.reshape(2, 128, 256)

    def down_part(i, carry):
        full = dot_tn(hid[:, lanes(i, 256)], gal[...]).astype(BF16)
        for cc in range(4):
            store_rows(cc, i, full[:, 256 * cc : 256 * cc + 256])
        return carry

    def up_part(i, carry):
        full = dot_tn(nrm[:, lanes(i, 256)], upg[...]).astype(BF16)
        for cc in range(4):
            store_rows(4 + cc, i, full[:, 256 * cc : 256 * cc + 256])
        return carry

    bits = [(p // mask) % 2 for mask in MASKS]
    every = slice(None)

    def block_index(free, other=None):
        return tuple(
            every if dim in free else (1 - bits[dim] if dim == other else bits[dim])
            for dim in range(3)
        )

    def scatter_order(ch):
        return SCATTER.get(ch, (0, 1, 2))

    def gather_order(ch):
        return GATHER.get(ch, (2, 1, 0))

    rsb = (rs0, rs1, rs2)

    def rs_copy(ch, ph):
        order = scatter_order(ch)
        return remote(
            mats.at[(ch,) + block_index(order[ph + 1 :], order[ph])],
            rsb[ph].at[ch],
            rssend.at[ch, ph],
            rsrecv.at[ch, ph],
            member(p ^ MASKS[order[ph]]),
        )

    def rs_add(ch, ph):
        free = sorted(scatter_order(ch)[ph + 1 :])
        rs_copy(ch, ph).wait_recv()
        for n in range(2 ** len(free)):
            spot = {dim: (n >> i) % 2 for i, dim in enumerate(free)}
            here = (ch,) + tuple(spot.get(dim, bits[dim]) for dim in range(3))
            there = (ch,) + tuple(spot[dim] for dim in free)
            mats[here] = (mats[here].astype(F32) + rsb[ph][there].astype(F32)).astype(BF16)

    def out_slice(ch, kk, index):
        if ch < 4:
            return odn.at[(kk,) + index + (every, slice(256 * ch, 256 * ch + 256))]
        if ch < 8:
            start, out = kk * 1024 + (ch - 4) * 256, oup
        elif ch < 11:
            start, out = (0, 1024, 512)[ch - 8] + kk * 256, oqkv
        else:
            start, out = kk * 256, oout
        return out.at[index + (every, pl.ds(pl.multiple_of(start, 256), 256))]

    def shard(ch):
        if ch == 10:
            return xsw
        return mats.at[(ch,) + block_index(())]

    def swap_shard():
        return remote(
            mats.at[(10,) + block_index(())], xsw, gsend.at[8], grecv.at[8], xpart
        )

    def local_copy(ch):
        return pltpu.make_async_copy(
            shard(ch), out_slice(ch, k, block_index(())), clocal.at[ch]
        )

    def ag_copy(ch, step):
        order = gather_order(ch)
        there = out_slice(ch, k, block_index(order[:step]))
        return remote(
            shard(ch) if step == 0 else there,
            there,
            agsend.at[ch, step],
            agrecv.at[ch, step],
            member(p ^ MASKS[order[step]]),
        )

    def core_copy(ch):
        return remote(
            out_slice(ch, k, (every,) * 3),
            out_slice(ch, k, (every,) * 3),
            csend.at[ch],
            crecv.at[ch],
            sibling,
        )

    def advance(ch, stage):
        if stage == 0:
            rs_copy(ch, 0).start()
        elif stage <= 2:
            rs_add(ch, stage - 1)
            rs_copy(ch, stage).start()
        elif stage == 3:
            rs_add(ch, 2)
            if ch == 10:
                swap_shard().start()
                swap_shard().wait_recv()
            local_copy(ch).start()
            ag_copy(ch, 0).start()
        elif stage == 4:
            ag_copy(ch, 0).wait_recv()
            local_copy(ch).wait()
            ag_copy(ch, 1).start()
        elif stage == 5:
            ag_copy(ch, 1).wait_recv()
            ag_copy(ch, 2).start()
        elif stage == 6:
            ag_copy(ch, 2).wait_recv()
            core_copy(ch).start()
        elif stage == 7:
            core_copy(ch).wait_recv()

    def settle(ch):
        for ph in range(3):
            rs_copy(ch, ph).wait_send()
            ag_copy(ch, ph).wait_send()
        core_copy(ch).wait_send()
        if ch == 10:
            swap_shard().wait_send()

    def load_half(place, t, u):
        return rbuf[spots_ref[place], t, 2 * u + spots_ref[32 + place]]

    def sort_unit(u):
        def sort_rows(i, carry):
            here = pl.ds(pl.multiple_of(i * 128, 128), 128)
            kg = jnp.concatenate([load_half(2 * i, 0, u), load_half(2 * i + 1, 0, u)], axis=0)
            qv = jnp.concatenate([load_half(2 * i, 1, u), load_half(2 * i + 1, 1, u)], axis=0)
            ak[here, :] = kg[:, :64]
            ag[here, :] = kg[:, 64:]
            aq[here, :] = qv[:, :64]
            av[here, :] = qv[:, 64:]
            kgt = kg.T
            akt[:, here] = kgt[:64, :]
            agt[:, here] = kgt[64:, :]
            avt[:, here] = qv.T[64:, :]
            return carry

        lax.fori_loop(0, LENGTH // 128, sort_rows, 0)

    def fold(values):
        return values.reshape(values.shape[0] // 8, 8, values.shape[1])

    def query_block(qb):
        mine = slice(qb * QB, qb * QB + QB)
        tiles = [slice(i * QB, i * QB + QB) for i in range(qb + 1)]
        query = aq[mine, :]
        grads = ag[mine, :]
        top = jnp.full((8, QB), masked_score, F32)
        for i, tile in enumerate(tiles):
            score = dot_nt(ak[tile, :], query)
            if i == qb:
                row = lax.broadcasted_iota(jnp.int32, (QB, QB), 0)
                col = lax.broadcasted_iota(jnp.int32, (QB, QB), 1)
                score = jnp.where(row <= col, score, masked_score)
            sco[tile, :] = score
            top = jnp.maximum(top, jnp.max(fold(score), axis=0))
        top = jnp.max(top, axis=0, keepdims=True)
        total = jnp.zeros((8, QB), F32)
        mix = jnp.zeros((HEAD_DIM, QB), F32)
        for tile in tiles:
            weights = jnp.exp(sco[tile, :] - top)
            sco[tile, :] = weights
            total = total + jnp.sum(fold(weights), axis=0)
            mix = mix + dot(avt[:, tile], weights.astype(BF16))
        inverse = 1.0 / jnp.sum(total, axis=0, keepdims=True)
        mix = mix * inverse
        dots = jnp.sum(agt[:, mine].astype(F32) * mix, axis=0, keepdims=True)
        back = jnp.zeros((HEAD_DIM, QB), F32)
        for i, tile in enumerate(tiles):
            chances = sco[tile, :] * inverse
            slopes = dot_nt(av[tile, :], grads)
            score_grads = (chances * (slopes - dots)).astype(BF16)
            value_part = dot(chances.astype(BF16), grads)
            key_part = dot(score_grads, query)
            if qb == LENGTH // QB - 1:
                dva[tile, :] = value_part
                dka[tile, :] = key_part
            else:
                dva[tile, :] += value_part
                dka[tile, :] += key_part
            back = back + dot(akt[:, tile], score_grads)
        place(0, qb, jnp.concatenate([mix, back * SCALE], axis=0).T)

    def place(t, qb, both):
        n = QB // HALF
        table = turns[qb * n : qb * n + n].reshape(QB, 128)
        cosine = jnp.concatenate([jnp.ones((QB, 64), F32), table[:, :64]], axis=1)
        sine = jnp.concatenate([jnp.zeros((QB, 64), F32), -table[:, 64:]], axis=1)
        osrt[t, qb * n : qb * n + n] = turn(both, cosine, sine).astype(BF16).reshape(n, HALF, 128)

    def finish_half(u, half):
        for qb in (2 * half, 2 * half + 1):
            mine = slice(qb * QB, qb * QB + QB)
            place(1, qb, jnp.concatenate([dva[mine, :], dka[mine, :]], axis=1))

        def unsort(i, carry):
            for t in range(2):
                sbuf[i // 2, u, t, 2 * half + i % 2] = osrt[t, spots_ref[64 + 2 * i + half]]
            return carry

        lax.fori_loop(0, 2 * CHIPS, unsort, 0)

    def send_half(u, half):
        pltpu.make_async_copy(
            out_part(sbuf, p, u, half), out_part(rb2, p, u, half), orecv.at[p, u, half]
        ).start()
        for i in (4, 6, 2, 5, 7, 3, 1):
            out_copy(p ^ i, u, half).start()

    def out_part(buf, q, u, half):
        return buf.at[q, u, :, pl.ds(2 * half, 2)]

    def out_copy(q, u, half):
        return remote(
            out_part(sbuf, q, u, half),
            out_part(rb2, p, u, half),
            osend.at[q, u, half],
            orecv.at[p, u, half],
            member(q),
        )

    def run(*steps):
        for ch, stage in steps:
            advance(ch, stage)

    def out_rows(q, u, t, kq):
        return jnp.concatenate([rb2[q, u, t, kq], rb2[q, u, t, 2 + kq]], axis=0)

    def att_part(i, carry):
        here = lanes(i, 256)
        left = nrm[:, here]
        for slot in range(3):
            at = 8 + (slot - f + 3) % 3
            store_rows(at, i, dot_tn(left, dqkv[slot]).astype(BF16))
        store_rows(11, i, dot_tn(gal[:, here], aall[...]).astype(BF16))
        return carry

    def normed_part(b, cols):
        here = rows(b)
        total = dot_nt(upg[here, :], wup[cols, :])
        for slot in range(3):
            total = total + dot_nt(dqkv[slot, here, :], wq[slot, cols, :])
        return total

    def mixed_part(b, cols):
        here = rows(b)
        return dot(hid[here, :], wdn[:, cols]) + dot(aall[here, :], wout[:, cols])

    def reduce_copies(n):
        return (
            remote(red_s.at[n, 0], red_r.at[n, 0], dsend.at[n, 0], drecv.at[n, 0], sibling),
            remote(red_s.at[n, 1], red_r.at[n, 1], dsend.at[n, 1], drecv.at[n, 1], sibling),
            remote(red_x.at[n], red_xr.at[n], dsend.at[n, 2], drecv.at[n, 2], xpart),
        )

    parts = (normed_part, mixed_part)

    def reduce_first(n):
        copies = reduce_copies(n)
        for slot, b in ((1, dg), (0, sibb)):

            def fill(i, carry):
                red_s[n, slot, :, lanes(i, 256)] = parts[n](b, lanes(i, 256)).astype(BF16)
                return carry

            lax.fori_loop(0, 4, fill, 0)
            copies[slot].start()

    def reduce_second(n):
        copies = reduce_copies(n)
        copies[1].wait_recv()

        def fill(i, carry):
            cols = lanes(i, 256)
            red_x[n, :, cols] = (
                parts[n](xb, cols) + red_r[n, 1, :, cols].astype(F32)
            ).astype(BF16)
            return carry

        lax.fori_loop(0, 4, fill, 0)
        copies[2].start()

    def reduce_third(n):
        copies = reduce_copies(n)

        def fill(i, carry):
            cols = lanes(i, 256)
            own_acc[n, :, cols] = parts[n](own, cols)
            return carry

        lax.fori_loop(0, 4, fill, 0)
        copies[0].wait_recv()
        copies[2].wait_recv()

        def finish(i, carry):
            cols = lanes(i, 256)
            own_acc[n, :, cols] = (
                own_acc[n, :, cols]
                + red_r[n, 0, :, cols].astype(F32)
                + red_xr[n, :, cols].astype(F32)
            )
            return carry

        lax.fori_loop(0, 4, finish, 0)

    def out_pick():
        row = lax.broadcasted_iota(jnp.int32, (ROWS, ROWS), 0)
        col = lax.broadcasted_iota(jnp.int32, (ROWS, ROWS), 1)
        return (row == 2 * (col % SEQ_DEV_TOK) + col // SEQ_DEV_TOK).astype(F32).astype(BF16)

    def back_rows(i, carry):
        dgain, dshift = carry
        here = pl.ds(pl.multiple_of(i * step, step), step)
        there = pl.ds(pl.multiple_of(own * ROWS + i * step, step), step)
        values = xs[here, :].astype(F32)
        center = values - jnp.mean(values, axis=1, keepdims=True)
        spread = lax.rsqrt(jnp.mean(center * center, axis=1, keepdims=True) + EPS)
        hat = center * spread
        grads = own_acc[0, here, :]
        dgain = dgain + jnp.sum(grads * hat, axis=0, keepdims=True)
        dshift = dshift + jnp.sum(grads, axis=0, keepdims=True)
        inner = grads * gain
        inner = spread * (
            inner
            - jnp.mean(inner, axis=1, keepdims=True)
            - hat * jnp.mean(inner * hat, axis=1, keepdims=True)
        )
        xs2 = gal[there, :].astype(F32) + inner
        red_s[0, 0, here, :] = xs2.astype(BF16)
        return dgain, dshift

    def mixed_rows(i, carry):
        here = pl.ds(pl.multiple_of(i * step, step), step)
        red_s[1, 0, here, :] = (xs[here, :].astype(F32) + own_acc[1, here, :] + down_b).astype(
            BF16
        )
        return carry

    lax.fori_loop(0, 4, down_part, 0)
    run((1, 0), (3, 0))
    lax.fori_loop(0, 4, up_part, 0)
    sm[...] = jnp.zeros_like(sm)
    sm[0:1, :] = jnp.sum(upg[...].astype(F32), axis=0, keepdims=True)
    sm[2:3, :] = jnp.sum(gal[...].astype(F32), axis=0, keepdims=True)
    run((0, 0), (2, 0))
    for fq, kq in ((f, k), (f, 1 - k), (1 - f, k), (1 - f, 1 - k)):
        for t in range(2):
            sent_block(fq, kq, t)
    for q in range(CHIPS):
        for t in range(2):
            for kq in range(2):
                pltpu.make_async_copy(
                    rbuf.at[2 * q + kq, t], rbuf.at[2 * q + kq, t], arecv.at[q, t, kq]
                ).wait()

    sort_unit(0)
    query_block(3)
    query_block(2)
    finish_half(0, 1)
    run((1, 1))
    send_half(0, 1)
    run((6, 0))
    query_block(1)
    query_block(0)
    finish_half(0, 0)
    send_half(0, 0)
    run((5, 0))
    sort_unit(1)
    query_block(3)
    query_block(2)
    finish_half(1, 1)
    send_half(1, 1)
    query_block(1)
    query_block(0)
    finish_half(1, 0)
    run((4, 0), (7, 0))
    send_half(1, 0)
    run((7, 1), (4, 1), (5, 1), (1, 2), (2, 1))
    for q in range(CHIPS):
        for u in range(SEQS):
            for half in range(2):
                arrived = out_part(rb2, q, u, half)
                pltpu.make_async_copy(arrived, arrived, orecv.at[q, u, half]).wait()

    for fq in range(2):
        for kq in range(2):
            for u in range(SEQS):
                at = (2 * fq + kq) * ROWS + u * 128
                here = slice(at, at + 128)
                for pair in range(2):
                    cols = slice(128 * pair, 128 * pair + 128)
                    x0 = out_rows(4 * pair + fq, u, 0, kq)
                    x1 = out_rows(4 * pair + 2 + fq, u, 0, kq)
                    y0 = out_rows(4 * pair + fq, u, 1, kq)
                    y1 = out_rows(4 * pair + 2 + fq, u, 1, kq)
                    aall[here, cols] = jnp.concatenate([x0[:, :64], x1[:, :64]], axis=1)
                    dqkv[0, here, cols] = jnp.concatenate([x0[:, 64:], x1[:, 64:]], axis=1)
                    dqkv[2, here, cols] = jnp.concatenate([y0[:, :64], y1[:, :64]], axis=1)
                    dqkv[1, here, cols] = jnp.concatenate([y0[:, 64:], y1[:, 64:]], axis=1)

    run((3, 1), (4, 2))
    lax.fori_loop(0, 4, att_part, 0)
    run((5, 2), (0, 1), (3, 2), (2, 2), (4, 3), (6, 1), (8, 0))
    reduce_first(0)
    reduce_first(1)
    run((3, 3), (7, 2), (0, 2), (8, 1))
    reduce_second(0)
    run((10, 0), (7, 3), (9, 0), (3, 4), (0, 3), (5, 3))
    reduce_second(1)
    run((1, 3), (6, 2), (11, 0), (0, 4), (4, 4), (7, 4), (0, 5), (10, 1))
    run((8, 2), (9, 1), (1, 4), (5, 4), (10, 2), (6, 3), (0, 6), (4, 5))
    run((9, 2), (2, 3), (4, 6), (8, 3), (11, 1), (1, 5), (6, 4), (2, 4))
    run((5, 5), (7, 5), (10, 3), (9, 3), (6, 5), (8, 4), (5, 6), (11, 2))
    run((3, 5), (2, 5), (5, 7), (11, 3), (10, 4), (9, 4))
    reduce_third(0)
    reduce_copies(0)[0].wait_send()
    dgain, dshift = lax.fori_loop(
        0, ROWS // step, back_rows, (jnp.zeros((1, D), F32), jnp.zeros((1, D), F32))
    )
    tgrad_ref[...] = dot(out_pick(), red_s[0, 0]).astype(BF16)
    sm[3:4, :] = dgain
    sm[4:5, :] = dshift

    small_copies = [
        remote(sm, smg.at[own], smsend.at[0], smrecv.at[own], sibling),
        remote(sm, smg.at[own], smsend.at[1], smrecv.at[own], xpart),
        remote(sm, smg.at[own], smsend.at[2], smrecv.at[own], diagonal),
    ]
    for copy in small_copies:
        copy.start()

    run((1, 6))
    reduce_third(1)
    reduce_copies(1)[0].wait_send()
    lax.fori_loop(0, ROWS // step, mixed_rows, 0)
    mixed_ref[...] = dot(out_pick(), red_s[1, 0]).astype(BF16)

    smg[own] = sm[...]
    for b in (sibb, xb, dg):
        remote(sm, smg.at[b], smsend.at[0], smrecv.at[b], sibling).wait_recv()
    for copy in small_copies:
        copy.wait_send()
    first_b = 2 * f
    sma[p, 0:1, :] = smg[first_b, 0:1, :]
    sma[p, 1:2, :] = smg[first_b + 1, 0:1, :]
    sma[p, 2:3, :] = sm[2:3, :]
    sma[p, 3:8, :] = smg[0, 3:8, :] + smg[1, 3:8, :] + smg[2, 3:8, :] + smg[3, 3:8, :]
    sm_copies = [
        remote(sma.at[p], sma.at[p], smsend.at[2 + i], smrecv.at[3 + i], member(p ^ i))
        for i in range(1, CHIPS)
    ]
    for copy in sm_copies:
        copy.start()

    run((11, 4), (2, 6), (6, 6), (7, 6), (10, 5), (8, 5), (6, 7), (9, 5))
    run((2, 7), (11, 5), (3, 6), (8, 6), (8, 7), (10, 6), (4, 7), (11, 6))
    run((10, 7), (9, 6), (3, 7), (11, 7), (1, 7), (0, 7), (9, 7), (7, 7))
    total = jnp.zeros((8, D), F32)
    for copy in sm_copies:
        copy.wait()
    for q in range(CHIPS):
        total = total + sma[q]
    small_ref[...] = total

    for copy in (vec_copy,):
        pass
    swap_copy.wait_send()
    for copy in (n_sib, n_x, g_sib, g_x, n_dg, g_dg):
        copy.wait_send()
    for u in range(SEQS):
        for i in range(1, CHIPS):
            for half in range(2):
                out_copy(p ^ i, u, half).wait_send()
    for n in range(2):
        copies = reduce_copies(n)
        copies[1].wait_send()
        copies[2].wait_send()
    for ch in range(NCH):
        settle(ch)


def widen_kernel(
    dn_h,
    up_h,
    qkv_h,
    out_h,
    small,
    mixed_in,
    tgrad_in,
    dn_o,
    up_o,
    qkv_o,
    out_o,
    mixed_o,
    tgrad_o,
    gain_o,
    shift_o,
    upb_o,
    downb_o,
    dn_b,
    up_b,
    qkv_b,
    out_b,
    dn_f,
    up_f,
    qkv_f,
    out_f,
    isem,
    osem,
):
    f = lax.axis_index("fsdp")
    sources = (up_h, dn_h, qkv_h, out_h)
    brief = (up_b, dn_b, qkv_b, out_b)
    wide = (up_f, dn_f, qkv_f, out_f)
    results = (up_o, dn_o, qkv_o, out_o)
    heights = (128, 256, 128, 128)

    def fetch(n, i):
        if n == 1:
            src = dn_h.at[pl.ds(2 * i, 2)]
        else:
            src = sources[n].at[i]
        return pltpu.make_async_copy(src, brief[n].at[i], isem.at[n, i])

    def put(n, i):
        if n == 3:
            return pltpu.make_async_copy(out_f, out_o, osem.at[3, 0])
        rows = pl.ds(i * heights[n], heights[n])
        return pltpu.make_async_copy(wide[n].at[rows], results[n].at[rows], osem.at[n, i])

    for n in range(4):
        for i in range(8):
            fetch(n, i).start()
    half = D // FSDP
    low_half = f == 0
    pick = jnp.where(low_half, small[:, :half], small[:, half:])
    gain_o[...] = pick[3]
    shift_o[...] = pick[4]
    downb_o[...] = pick[2]
    upb_o[:1024] = small[0]
    upb_o[1024:] = small[1]
    mixed_o[...] = mixed_in[...]
    tgrad_o[...] = tgrad_in[...]
    for n in range(4):
        for i in range(8):
            fetch(n, i).wait()
            values = brief[n][i].astype(F32)
            if n == 3:
                out_f[:, i * 128 : i * 128 + 128] = values.T
            else:
                wide[n][i * heights[n] : (i + 1) * heights[n], :] = values.reshape(
                    heights[n], -1
                )
                put(n, i).start()
    put(3, 0).start()
    for n in range(3):
        for i in range(8):
            put(n, i).wait()
    put(3, 0).wait()


def widen(dn, up, qkv, out_t, small, mixed, tokens_grad):
    vm = pl.BlockSpec(memory_space=pltpu.VMEM)
    hbm = pl.BlockSpec(memory_space=pl.ANY)
    half = D // FSDP
    feeds = FF // FSDP
    heads = 3 * D // FSDP
    return pl.pallas_call(
        widen_kernel,
        out_shape=(
            jax.ShapeDtypeStruct((feeds, D), F32),
            jax.ShapeDtypeStruct((D, feeds), F32),
            jax.ShapeDtypeStruct((D, heads), F32),
            jax.ShapeDtypeStruct((half, D), F32),
            jax.ShapeDtypeStruct((ROWS, D), BF16),
            jax.ShapeDtypeStruct((ROWS, D), BF16),
            jax.ShapeDtypeStruct((half,), F32),
            jax.ShapeDtypeStruct((half,), F32),
            jax.ShapeDtypeStruct((feeds,), F32),
            jax.ShapeDtypeStruct((half,), F32),
        ),
        in_specs=[hbm] * 4 + [vm] * 3,
        out_specs=(hbm,) * 4 + (vm,) * 6,
        scratch_shapes=[
            pltpu.VMEM((8, 2, 128, D), BF16),
            pltpu.VMEM((8, 128, feeds), BF16),
            pltpu.VMEM((8, 128, heads), BF16),
            pltpu.VMEM((8, 128, half), BF16),
            pltpu.VMEM((feeds, D), F32),
            pltpu.VMEM((D, feeds), F32),
            pltpu.VMEM((D, heads), F32),
            pltpu.VMEM((half, D), F32),
            pltpu.SemaphoreType.DMA((4, 8)),
            pltpu.SemaphoreType.DMA((4, 8)),
        ],
        compiler_params=pltpu.CompilerParams(vmem_limit_bytes=56 * 2**20),
    )(
        dn.reshape(16, 128, D),
        up.reshape(8, 128, feeds),
        qkv.reshape(8, 128, heads),
        out_t.reshape(8, 128, half),
        small,
        mixed,
        tokens_grad,
    )


def turn_table():
    lane = np.arange(HEAD_DIM)
    speeds = (10000.0 ** (-(lane // 2 * 2) / ROT_DIM)).astype(np.float32)
    phase = np.arange(LENGTH, dtype=np.float32)[:, None] * speeds[None, :]
    turning = (lane < ROT_DIM)[None, :]
    sign = np.where(lane % 2 == 0, -1.0, 1.0)[None, :]
    cosine = np.where(turning, np.cos(phase), 1.0)
    sine = np.where(turning, np.sin(phase) * sign, 0.0)
    table = np.concatenate((cosine, sine), axis=1).astype(np.float32)
    return table.reshape(4 * CHIPS, HALF, 2 * HEAD_DIM)


def fused_device(
    tokens,
    block_pairs,
    norm_gain,
    norm_bias,
    qkv_weight,
    out_weight,
    up_weight,
    up_bias,
    down_weight,
    down_bias,
    cotangent,
):
    vm = pl.BlockSpec(memory_space=pltpu.VMEM)
    sme = pl.BlockSpec(memory_space=pltpu.SMEM)
    hbm = pl.BlockSpec(memory_space=pl.ANY)
    dma = pltpu.SemaphoreType.DMA
    scratch = [
        pltpu.SMEM((96,), jnp.int32),
        pltpu.VMEM((4 * CHIPS, HALF, 128), F32),
        pltpu.VMEM((2, 8, 512), F32),
        pltpu.VMEM((ROWS, D), BF16),
        pltpu.VMEM((ALL, D), BF16),
        pltpu.VMEM((ALL, D), BF16),
        pltpu.VMEM((3, D, 256), BF16),
        pltpu.VMEM((256, D), BF16),
        pltpu.VMEM((D, 1024), BF16),
        pltpu.VMEM((1024, D), BF16),
        pltpu.VMEM((ALL, 1024), BF16),
        pltpu.VMEM((ALL, 1024), BF16),
        pltpu.VMEM((CHIPS, 2, 2, 4, HALF, 128), BF16),
        pltpu.VMEM((2 * CHIPS, 2, 4, HALF, 128), BF16),
        pltpu.VMEM((LENGTH, HEAD_DIM), BF16),
        pltpu.VMEM((LENGTH, HEAD_DIM), BF16),
        pltpu.VMEM((LENGTH, HEAD_DIM), BF16),
        pltpu.VMEM((LENGTH, HEAD_DIM), BF16),
        pltpu.VMEM((HEAD_DIM, LENGTH), BF16),
        pltpu.VMEM((HEAD_DIM, LENGTH), BF16),
        pltpu.VMEM((HEAD_DIM, LENGTH), BF16),
        pltpu.VMEM((LENGTH, QB), F32),
        pltpu.VMEM((LENGTH, HEAD_DIM), F32),
        pltpu.VMEM((LENGTH, HEAD_DIM), F32),
        pltpu.VMEM((2, 4 * CHIPS, HALF, 128), BF16),
        pltpu.VMEM((CHIPS, SEQS, 2, 4, HALF, 128), BF16),
        pltpu.VMEM((ALL, 256), BF16),
        pltpu.VMEM((3, ALL, 256), BF16),
        pltpu.VMEM((NCH, 2, 2, 2, 128, 256), BF16),
        pltpu.VMEM((NCH, 2, 2, 128, 256), BF16),
        pltpu.VMEM((NCH, 2, 128, 256), BF16),
        pltpu.VMEM((NCH, 128, 256), BF16),
        pltpu.VMEM((128, 256), BF16),
        pltpu.VMEM((2, ROWS, D), F32),
        pltpu.VMEM((2, 2, ROWS, D), BF16),
        pltpu.VMEM((2, ROWS, D), BF16),
        pltpu.VMEM((2, 2, ROWS, D), BF16),
        pltpu.VMEM((2, ROWS, D), BF16),
        pltpu.VMEM((8, D), F32),
        pltpu.VMEM((4, 8, D), F32),
        pltpu.VMEM((CHIPS, 8, D), F32),
        dma((6,)),
        dma((9,)),
        dma((9,)),
        dma((CHIPS, 2, 2)),
        dma((CHIPS, 2, 2)),
        dma((CHIPS, SEQS, 2)),
        dma((CHIPS, SEQS, 2)),
        dma((NCH, 3)),
        dma((NCH, 3)),
        dma((NCH, 3)),
        dma((NCH, 3)),
        dma((NCH,)),
        dma((NCH,)),
        dma((NCH,)),
        dma((2, 3)),
        dma((2, 3)),
        dma((10,)),
        dma((11,)),
    ]
    mixed, tokens_grad, small, dn, up, qkv, out_t = pl.pallas_call(
        fused_kernel,
        out_shape=(
            jax.ShapeDtypeStruct((ROWS, D), BF16),
            jax.ShapeDtypeStruct((ROWS, D), BF16),
            jax.ShapeDtypeStruct((8, D), F32),
            jax.ShapeDtypeStruct((2, 2, 2, 2, 128, D), BF16),
            jax.ShapeDtypeStruct((2, 2, 2, 128, FF // FSDP), BF16),
            jax.ShapeDtypeStruct((2, 2, 2, 128, 3 * D // FSDP), BF16),
            jax.ShapeDtypeStruct((2, 2, 2, 128, D // FSDP), BF16),
        ),
        in_specs=[sme] + [vm] * 4 + [hbm, vm, vm] + [hbm] * 4,
        out_specs=(vm, vm, vm, hbm, hbm, hbm, hbm),
        scratch_shapes=scratch,
        compiler_params=pltpu.CompilerParams(
            collective_id=0, has_side_effects=True, vmem_limit_bytes=63 * 2**20
        ),
    )(
        block_pairs,
        norm_gain,
        norm_bias,
        down_bias,
        up_bias,
        jnp.asarray(turn_table()),
        tokens,
        cotangent,
        qkv_weight,
        out_weight,
        up_weight,
        down_weight,
    )
    dn, up, qkv, out, mixed, tokens_grad, gain, shift, upb, downb = widen(
        dn, up, qkv, out_t, small, mixed, tokens_grad
    )
    return mixed, tokens_grad, gain, shift, qkv, out, up, upb, dn, downb


def solution(mesh):
    in_specs = (
        P(("fsdp", "ctx"), None),
        P(),
        P("fsdp"),
        P("fsdp"),
        P(None, "fsdp"),
        P("fsdp", None),
        P(None, "fsdp"),
        P("fsdp"),
        P("fsdp", None),
        P("fsdp"),
        P(("fsdp", "ctx"), None),
    )
    out_specs = (
        P(("fsdp", "ctx"), None),
        P(("fsdp", "ctx"), None),
        P("fsdp"),
        P("fsdp"),
        P(None, "fsdp"),
        P("fsdp", None),
        P(None, "fsdp"),
        P("fsdp"),
        P("fsdp", None),
        P("fsdp"),
    )
    plan = fused_device if fits(mesh) else per_device
    return jax.shard_map(
        plan, mesh=mesh, in_specs=in_specs, out_specs=out_specs, check_vma=False
    )
```

```python
import functools
import math

import jax
import jax.numpy as jnp
import numpy as np
from jax import lax
from jax.experimental import pallas as pl
from jax.experimental.pallas import tpu as pltpu
from jax.sharding import PartitionSpec as P

D = 1024
HEAD_DIM = 64
ROT_DIM = 32
HEADS = 16
SEQ_DEV_TOK = 128
SEQS = 2


EPS = 1e-05
HIGHEST = lax.Precision.HIGHEST
masked_score = -1e30


def layer_norm(values, gain_values, shift_values):
    center = values - jnp.mean(values, axis=-1, keepdims=True)
    spread = jnp.mean(center * center, axis=-1, keepdims=True)
    return center * lax.rsqrt(spread + EPS) * gain_values + shift_values


def rotary_tables(places, window):
    lanes = jnp.arange(window, dtype=jnp.int32)
    within_head = lanes % HEAD_DIM
    turning = within_head < ROT_DIM
    steps_up = (within_head // 2 * 2).astype(jnp.float32)
    speeds = 10000.0 ** (-steps_up / ROT_DIM)
    phase = places.astype(jnp.float32)[:, None] * speeds[None, :]
    cos_full = jnp.where(turning[None, :], jnp.cos(phase), 1.0)
    sin_full = jnp.where(turning[None, :], jnp.sin(phase), 0.0)
    row_lane = lanes[:, None]
    col_lane = lanes[None, :]
    same_head = row_lane // HEAD_DIM == col_lane // HEAD_DIM
    col_within = col_lane % HEAD_DIM
    col_turns = same_head & (col_within < ROT_DIM)
    even_col = col_within % 2 == 0
    minus_part = jnp.where(col_turns & even_col & (row_lane == col_lane + 1), -1.0, 0.0)
    plus_part = jnp.where(
        col_turns & jnp.logical_not(even_col) & (row_lane == col_lane - 1), 1.0, 0.0
    )
    swap_table = (minus_part + plus_part).astype(jnp.float32)
    return (cos_full, sin_full, swap_table)


def smooth_gate(values):
    return jax.nn.gelu(values, approximate=True)


def positions(first_row, row_count, pair_table, devices, seq_rows):
    indices = first_row + jnp.arange(row_count, dtype=jnp.int32)
    owners = indices // seq_rows
    within = indices % seq_rows
    half_rows = seq_rows // 2
    matches = owners[:, None] == jnp.arange(devices, dtype=jnp.int32)[None, :]
    chosen = jnp.sum(jnp.where(matches, pair_table[None, :], 0), axis=1)
    block_index = jnp.where(within < half_rows, chosen, 2 * devices - 1 - chosen)
    return block_index * half_rows + within % half_rows


def in_groups(row_count, seq_rows):
    group_rows = math.gcd(row_count // seq_rows, 8) * seq_rows
    return (group_rows, row_count // group_rows)


def split_groups(array, group_rows, turns):
    return array.reshape((turns, group_rows) + array.shape[1:])


def grad_scores(
    query_rows,
    out_grads,
    log_sums,
    row_dots,
    query_places,
    key_rows,
    value_rows,
    key_places,
    factor,
):
    scores = (
        jnp.einsum("qshe,kshe->shqk", query_rows, key_rows, preferred_element_type=jnp.float32)
        * factor
    )
    allowed = key_places[None, :] <= query_places[:, None]
    chances = jnp.exp(jnp.where(allowed, scores - log_sums[..., None], masked_score))
    prob_grads = jnp.einsum(
        "qshe,kshe->shqk", out_grads, value_rows, preferred_element_type=jnp.float32
    )
    return (chances, (chances * (prob_grads - row_dots[..., None])).astype(jnp.bfloat16))


def per_device(
    tokens,
    block_pairs,
    norm_gain,
    norm_bias,
    qkv_weight,
    out_weight,
    up_weight,
    up_bias,
    down_weight,
    down_bias,
    cotangent,
):
    devices = lax.axis_size("ctx")
    own_index = lax.axis_index("ctx")
    seq_rows = SEQ_DEV_TOK
    seq_count = SEQS
    heads = HEADS
    head_size = HEAD_DIM
    width = D
    factor = HEAD_DIM ** (-0.5)
    all_rows = seq_rows * seq_count
    window = math.gcd(width, 128)
    gathered = (
        lax.all_gather(norm_gain, "fsdp", axis=0, tiled=True),
        lax.all_gather(norm_bias, "fsdp", axis=0, tiled=True),
        lax.all_gather(qkv_weight, "fsdp", axis=1, tiled=True),
        lax.all_gather(out_weight, "fsdp", axis=0, tiled=True),
        lax.all_gather(up_weight, "fsdp", axis=1, tiled=True),
        lax.all_gather(up_bias, "fsdp", axis=0, tiled=True),
        lax.all_gather(down_weight, "fsdp", axis=0, tiled=True),
        lax.all_gather(down_bias, "fsdp", axis=0, tiled=True),
    )
    gain_low, shift_low, w_qkv, w_out, w_up, b_up, w_down, b_down = gathered
    inputs = tokens.astype(jnp.float32)
    gain_values = gain_low.astype(jnp.float32)
    shift_values = shift_low.astype(jnp.float32)
    normed_low = layer_norm(inputs, gain_values, shift_values).astype(jnp.bfloat16)
    mixed_qkv = jnp.dot(normed_low, w_qkv, preferred_element_type=jnp.float32).reshape(
        seq_rows, seq_count, 3 * width
    )
    own_places = positions(own_index * seq_rows, seq_rows, block_pairs, devices, seq_rows)
    cos_full, sin_full, swap_table = rotary_tables(own_places, window)

    def turn_both(values):
        shaped = values.reshape(seq_rows, seq_count, 2 * width // window, window)
        swapped = jnp.einsum("rsgw,wv->rsgv", shaped, swap_table, precision=HIGHEST)
        turned_rows = shaped * cos_full[:, None, None, :] + swapped * sin_full[:, None, None, :]
        return turned_rows.reshape(seq_rows, seq_count, 2 * width)

    query_key = mixed_qkv[:, :, : 2 * width]
    turned = turn_both(query_key)
    queries = (
        turned[:, :, :width].astype(jnp.bfloat16).reshape(seq_rows, seq_count, heads, head_size)
    )
    key_rows = (
        turned[:, :, width:].astype(jnp.bfloat16).reshape(seq_rows, seq_count, heads, head_size)
    )
    value_rows = (
        mixed_qkv[:, :, 2 * width :]
        .astype(jnp.bfloat16)
        .reshape(seq_rows, seq_count, heads, head_size)
    )
    start_state = (
        jnp.full((seq_count, heads, seq_rows), masked_score, jnp.float32),
        jnp.zeros((seq_count, heads, seq_rows), jnp.float32),
        jnp.zeros((seq_count, heads, seq_rows, head_size), jnp.float32),
    )
    piece_keys = lax.all_gather(key_rows, "ctx", axis=0, tiled=True)
    piece_values = lax.all_gather(value_rows, "ctx", axis=0, tiled=True)
    group_rows, turns = in_groups(piece_keys.shape[0], seq_rows)

    def attend_step(inner, item):
        block_keys, block_values, turn = item
        key_places = positions(turn * group_rows, group_rows, block_pairs, devices, seq_rows)
        scores = (
            jnp.einsum("qshe,kshe->shqk", queries, block_keys, preferred_element_type=jnp.float32)
            * factor
        )
        allowed = key_places[None, :] <= own_places[:, None]
        running, totals, accum = inner
        fresh = jnp.maximum(running, jnp.max(jnp.where(allowed, scores, masked_score), axis=-1))
        weights = jnp.exp(jnp.where(allowed, scores - fresh[..., None], masked_score))
        fading = jnp.exp(running - fresh)
        totals = totals * fading + jnp.sum(weights, axis=-1)
        accum = accum * fading[..., None] + jnp.einsum(
            "shqk,kshe->shqe",
            weights.astype(jnp.bfloat16),
            block_values,
            preferred_element_type=jnp.float32,
        )
        return ((fresh, totals, accum), None)

    inner, _ = lax.scan(
        attend_step,
        start_state,
        (
            split_groups(piece_keys, group_rows, turns),
            split_groups(piece_values, group_rows, turns),
            jnp.arange(turns, dtype=jnp.int32),
        ),
    )
    running, totals, accum = inner
    log_sums = running + jnp.log(totals)
    attended = jnp.transpose(accum / totals[..., None], (2, 0, 1, 3))
    attn_low = attended.reshape(all_rows, width).astype(jnp.bfloat16)
    attention = jnp.dot(attn_low, w_out, preferred_element_type=jnp.float32)
    up_pre = jnp.dot(normed_low, w_up, preferred_element_type=jnp.float32) + b_up.astype(
        jnp.float32
    )
    hidden_low = smooth_gate(up_pre).astype(jnp.bfloat16)
    result = (
        inputs
        + attention
        + jnp.dot(hidden_low, w_down, preferred_element_type=jnp.float32)
        + b_down.astype(jnp.float32)
    )
    mixed = result.astype(jnp.bfloat16)
    again = (
        lax.all_gather(norm_gain, "fsdp", axis=0, tiled=True),
        lax.all_gather(norm_bias, "fsdp", axis=0, tiled=True),
        lax.all_gather(qkv_weight, "fsdp", axis=1, tiled=True),
        lax.all_gather(out_weight, "fsdp", axis=0, tiled=True),
        lax.all_gather(up_weight, "fsdp", axis=1, tiled=True),
        lax.all_gather(up_bias, "fsdp", axis=0, tiled=True),
        lax.all_gather(down_weight, "fsdp", axis=0, tiled=True),
        lax.all_gather(down_bias, "fsdp", axis=0, tiled=True),
    )
    gain_low, shift_low, w_qkv, w_out, w_up, b_up, w_down, b_down = again
    out_grad = cotangent.astype(jnp.float32)
    attn_grads = (
        jnp.einsum("td,ed->te", cotangent, w_out, preferred_element_type=jnp.float32)
        .astype(jnp.bfloat16)
        .reshape(seq_rows, seq_count, heads, head_size)
    )
    dots_rows = jnp.sum(attn_grads.astype(jnp.float32) * attended, axis=-1)
    row_dots = jnp.transpose(dots_rows, (1, 2, 0))
    empty_rows = jnp.zeros((seq_rows, seq_count, heads, head_size), jnp.float32)
    whole_keys, whole_values = (
        lax.all_gather(key_rows, "ctx", axis=0, tiled=True),
        lax.all_gather(value_rows, "ctx", axis=0, tiled=True),
    )
    piece_keys = whole_keys
    piece_values = whole_values
    query_group_rows, turns = in_groups(piece_keys.shape[0], seq_rows)

    def query_step(inner, item):
        block_keys, block_values, turn = item
        key_places = positions(
            0 + turn * query_group_rows, query_group_rows, block_pairs, devices, seq_rows
        )
        chances, score_grads = grad_scores(
            queries,
            attn_grads,
            log_sums,
            row_dots,
            own_places,
            block_keys,
            block_values,
            key_places,
            factor,
        )
        return (
            inner
            + jnp.einsum(
                "shqk,kshe->qshe", score_grads, block_keys, preferred_element_type=jnp.float32
            )
            * factor,
            None,
        )

    inner, _ = lax.scan(
        query_step,
        empty_rows,
        (
            split_groups(piece_keys, query_group_rows, turns),
            split_groups(piece_values, query_group_rows, turns),
            jnp.arange(turns, dtype=jnp.int32),
        ),
    )
    query_grad = inner
    piece_keys = whole_keys
    piece_values = whole_values
    key_group_rows, turns = in_groups(seq_rows * lax.axis_size("ctx"), seq_rows)

    def key_step(inner, item):
        block_keys, block_values, turn = item
        key_places = positions(
            turn * key_group_rows, key_group_rows, block_pairs, devices, seq_rows
        )
        chances, score_grads = grad_scores(
            queries,
            attn_grads,
            log_sums,
            row_dots,
            own_places,
            block_keys,
            block_values,
            key_places,
            factor,
        )
        key_part = (
            jnp.einsum("shqk,qshe->kshe", score_grads, queries, preferred_element_type=jnp.float32)
            * factor
        )
        value_part = jnp.einsum(
            "shqk,qshe->kshe",
            chances.astype(jnp.bfloat16),
            attn_grads,
            preferred_element_type=jnp.float32,
        )
        stacked = jnp.stack(
            (
                key_part.reshape(key_group_rows, seq_count, width),
                value_part.reshape(key_group_rows, seq_count, width),
            ),
            axis=2,
        )
        return (inner, stacked)

    _, blocks_out = lax.scan(
        key_step,
        jnp.zeros((), jnp.float32),
        (
            split_groups(piece_keys, key_group_rows, turns),
            split_groups(piece_values, key_group_rows, turns),
            jnp.arange(turns, dtype=jnp.int32),
        ),
    )
    summed_terms = lax.psum_scatter(
        blocks_out.reshape(seq_rows * lax.axis_size("ctx"), seq_count, 2, width),
        "ctx",
        scatter_dimension=0,
        tiled=True,
    )
    key_grad = summed_terms[:, :, 0].reshape(seq_rows, seq_count, heads, head_size)
    value_grad = summed_terms[:, :, 1].reshape(seq_rows, seq_count, heads, head_size)
    _, turn_back = jax.vjp(turn_both, query_key)
    both_grads = jnp.concatenate(
        (
            query_grad.reshape(seq_rows, seq_count, width),
            key_grad.reshape(seq_rows, seq_count, width),
        ),
        axis=2,
    )
    (pre_grads,) = turn_back(both_grads)
    qkv_grad = (
        jnp.concatenate((pre_grads, value_grad.reshape(seq_rows, seq_count, width)), axis=2)
        .reshape(all_rows, 3 * width)
        .astype(jnp.bfloat16)
    )
    hidden_grad = jnp.einsum("td,fd->tf", cotangent, w_down, preferred_element_type=jnp.float32)
    _, gate_back = jax.vjp(smooth_gate, up_pre)
    (up_grad,) = gate_back(hidden_grad)
    up_low = up_grad.astype(jnp.bfloat16)
    normed_grad = jnp.einsum(
        "tc,dc->td", qkv_grad, w_qkv, preferred_element_type=jnp.float32
    ) + jnp.einsum("tf,df->td", up_low, w_up, preferred_element_type=jnp.float32)
    _, norm_back = jax.vjp(
        layer_norm, inputs, gain_low.astype(jnp.float32), shift_low.astype(jnp.float32)
    )
    input_part, gain_grad, shift_grad = norm_back(normed_grad)
    tokens_grad = (out_grad + input_part).astype(jnp.bfloat16)
    qkv_wgrad = jnp.einsum("td,tc->dc", normed_low, qkv_grad, preferred_element_type=jnp.float32)
    out_wgrad = jnp.einsum("td,te->de", attn_low, cotangent, preferred_element_type=jnp.float32)
    up_wgrad = jnp.einsum("td,tf->df", normed_low, up_low, preferred_element_type=jnp.float32)
    up_bgrad = jnp.sum(up_low.astype(jnp.float32), axis=0)
    down_wgrad = jnp.einsum("tf,td->fd", hidden_low, cotangent, preferred_element_type=jnp.float32)
    down_bgrad = jnp.sum(out_grad, axis=0)
    shares = (
        lax.psum_scatter(
            gain_grad.astype(jnp.bfloat16), "fsdp", scatter_dimension=0, tiled=True
        ).astype(jnp.float32),
        lax.psum_scatter(
            shift_grad.astype(jnp.bfloat16), "fsdp", scatter_dimension=0, tiled=True
        ).astype(jnp.float32),
        lax.psum_scatter(
            qkv_wgrad.astype(jnp.bfloat16), "fsdp", scatter_dimension=1, tiled=True
        ).astype(jnp.float32),
        lax.psum_scatter(
            out_wgrad.astype(jnp.bfloat16), "fsdp", scatter_dimension=0, tiled=True
        ).astype(jnp.float32),
        lax.psum_scatter(
            up_wgrad.astype(jnp.bfloat16), "fsdp", scatter_dimension=1, tiled=True
        ).astype(jnp.float32),
        lax.psum_scatter(
            up_bgrad.astype(jnp.bfloat16), "fsdp", scatter_dimension=0, tiled=True
        ).astype(jnp.float32),
        lax.psum_scatter(
            down_wgrad.astype(jnp.bfloat16), "fsdp", scatter_dimension=0, tiled=True
        ).astype(jnp.float32),
        lax.psum_scatter(
            down_bgrad.astype(jnp.bfloat16), "fsdp", scatter_dimension=0, tiled=True
        ).astype(jnp.float32),
    )
    share_gain, share_shift, share_qkv, share_out, share_up, share_upb, share_down, share_downb = (
        shares
    )
    totals_out = lax.psum(
        (
            share_gain,
            share_shift,
            share_qkv,
            share_out,
            share_up,
            share_upb,
            share_down,
            share_downb,
        ),
        "ctx",
    )
    sum_gain, sum_shift, sum_qkv, sum_out, sum_up, sum_upb, sum_down, sum_downb = totals_out
    return (
        mixed,
        tokens_grad,
        sum_gain,
        sum_shift,
        sum_qkv,
        sum_out,
        sum_up,
        sum_upb,
        sum_down,
        sum_downb,
    )


F32 = jnp.float32
BF16 = jnp.bfloat16
FF = 4096
FSDP = 2
CHIPS = 8
ROWS = SEQ_DEV_TOK * SEQS
ALL = 4 * ROWS
LENGTH = CHIPS * 2 * SEQ_DEV_TOK
HALF = SEQ_DEV_TOK // 2
QB = 512
NCH = 12
MASKS = (1, 2, 4)
SCATTER = {2: (1, 0, 2), 4: (1, 0, 2), 7: (2, 0, 1)}
GATHER = {2: (2, 0, 1), 4: (2, 0, 1), 6: (1, 2, 0), 9: (1, 0, 2), 10: (1, 2, 0), 11: (1, 2, 0)}
SCALE = HEAD_DIM**-0.5


def fits(mesh):
    return mesh.shape["fsdp"] == FSDP and mesh.shape["ctx"] == 2 * CHIPS


def dot(left, right):
    return lax.dot_general(left, right, (((1,), (0,)), ((), ())), preferred_element_type=F32)


def dot_nt(left, right):
    return lax.dot_general(left, right, (((1,), (1,)), ((), ())), preferred_element_type=F32)


def dot_tn(left, right):
    return lax.dot_general(left, right, (((0,), (0,)), ((), ())), preferred_element_type=F32)


def turn(values, cosine, sine):
    lane = lax.broadcasted_iota(jnp.int32, values.shape, 1)
    width = values.shape[1]
    other = jnp.where(
        lane % 2 == 0, pltpu.roll(values, width - 1, 1), pltpu.roll(values, 1, 1)
    )
    return values * cosine + other * sine


def gate(values):
    inner = 0.7978845608028654 * (values + 0.044715 * values * values * values)
    th = jnp.tanh(inner)
    half = 0.5 * (1.0 + th)
    slope = half + (0.5 * values) * (1.0 - th * th) * (
        0.7978845608028654 * (1.0 + 3 * 0.044715 * values * values)
    )
    return values * half, slope


def fused_kernel(
    pairs_ref,
    gain_ref,
    shift_ref,
    downb_ref,
    upb_ref,
    turns_h,
    tok_ref,
    cot_ref,
    wqkv_h,
    wout_h,
    wup_h,
    wdn_h,
    mixed_ref,
    tgrad_ref,
    small_ref,
    odn,
    oup,
    oqkv,
    oout,
    spots_ref,
    turns,
    vall,
    xs,
    nrm,
    gal,
    wq,
    wout,
    wup,
    wdn,
    hid,
    upg,
    sbuf,
    rbuf,
    aq,
    ag,
    ak,
    av,
    akt,
    avt,
    agt,
    sco,
    dka,
    dva,
    osrt,
    rb2,
    aall,
    dqkv,
    mats,
    rs0,
    rs1,
    rs2,
    xsw,
    own_acc,
    red_s,
    red_x,
    red_r,
    red_xr,
    sm,
    smg,
    sma,
    lsem,
    gsend,
    grecv,
    asend,
    arecv,
    osend,
    orecv,
    rssend,
    rsrecv,
    agsend,
    agrecv,
    clocal,
    csend,
    crecv,
    dsend,
    drecv,
    smsend,
    smrecv,
):
    f = lax.axis_index("fsdp")
    c = lax.axis_index("ctx")
    k = c % 2
    p = c // 2
    zz = p // 2
    yy = p % 2
    xpart = (1 - f, c)
    sibling = (f, 2 * p + 1 - k)
    diagonal = (1 - f, 2 * p + 1 - k)
    own = 2 * f + k
    sibb = 2 * f + 1 - k
    xb = 2 * (1 - f) + k
    dg = 2 * (1 - f) + 1 - k
    MESH = pl.DeviceIdType.MESH

    def member(q):
        return (f, 2 * q + k)

    def remote(src, dst, ssem, rsem, device):
        return pltpu.make_async_remote_copy(
            src_ref=src,
            dst_ref=dst,
            send_sem=ssem,
            recv_sem=rsem,
            device_id=device,
            device_id_type=MESH,
        )

    def rows(b):
        return pl.ds(pl.multiple_of(b * ROWS, ROWS), ROWS)

    def lanes(i, n):
        return pl.ds(pl.multiple_of(i * n, n), n)

    loads = [
        pltpu.make_async_copy(wqkv_h.at[:, lanes(k, 256)], wq.at[f], lsem.at[0]),
        pltpu.make_async_copy(
            wqkv_h.at[:, pl.ds(pl.multiple_of(1024 + 256 * k, 256), 256)], wq.at[1 + f], lsem.at[1]
        ),
        pltpu.make_async_copy(wup_h.at[:, lanes(k, 1024)], wup, lsem.at[2]),
        pltpu.make_async_copy(wdn_h.at[lanes(k, 1024), :], wdn, lsem.at[3]),
        pltpu.make_async_copy(wout_h.at[lanes(k, 256), :], wout, lsem.at[4]),
        pltpu.make_async_copy(turns_h, turns, lsem.at[5]),
    ]
    for load in loads:
        load.start()
    barrier = pltpu.get_barrier_semaphore()
    for device in [xpart, sibling, diagonal] + [member(p ^ i) for i in range(1, CHIPS)]:
        pl.semaphore_signal(barrier, inc=1, device_id=device, device_id_type=MESH)
    pl.semaphore_wait(barrier, 3 + CHIPS - 1)

    def row_of(ref, at):
        return ref[pl.ds(at, 512)].astype(F32).reshape(1, 512)

    vall[f] = jnp.concatenate(
        [row_of(gain_ref, 0), row_of(shift_ref, 0), row_of(downb_ref, 0)]
        + [row_of(upb_ref, 512 * i) for i in range(4)]
        + [jnp.zeros((1, 512), F32)],
        axis=0,
    )
    vec_copy = remote(vall.at[f], vall.at[f], gsend.at[0], grecv.at[0], xpart)
    vec_copy.start()
    swap_copy = remote(
        wqkv_h.at[:, pl.ds(pl.multiple_of(512 + 256 * k, 256), 256)],
        wq.at[2 * f],
        gsend.at[1],
        grecv.at[1],
        xpart,
    )
    swap_copy.start()

    def table_row(b, carry):
        holder = jnp.int32(0)
        half = jnp.int32(0)
        for i in range(2 * CHIPS):
            first = (pairs_ref[i] == b).astype(jnp.int32)
            last = (4 * CHIPS - 1 - pairs_ref[i] == b).astype(jnp.int32)
            holder = holder + i * (first + last)
            half = half + last
        spots_ref[b] = jnp.minimum(holder, 2 * CHIPS - 1)
        spots_ref[4 * CHIPS + b] = jnp.minimum(half, 1)
        return carry

    lax.fori_loop(0, 4 * CHIPS, table_row, 0)

    def table_pair(i, carry):
        spots_ref[64 + 2 * i] = pairs_ref[i]
        spots_ref[64 + 2 * i + 1] = 4 * CHIPS - 1 - pairs_ref[i]
        return carry

    lax.fori_loop(0, 2 * CHIPS, table_pair, 0)
    vec_copy.wait()
    gain = jnp.concatenate([vall[0, 0:1, :], vall[1, 0:1, :]], axis=1).astype(F32)
    shift = jnp.concatenate([vall[0, 1:2, :], vall[1, 1:2, :]], axis=1).astype(F32)
    down_b = jnp.concatenate([vall[0, 2:3, :], vall[1, 2:3, :]], axis=1).astype(F32)

    step = 64

    def norm_rows(i, carry):
        here = pl.ds(pl.multiple_of(i * step, step), step)
        there = pl.ds(pl.multiple_of(own * ROWS + i * step, step), step)
        row = lax.broadcasted_iota(jnp.int32, (step, ROWS), 0) + i * step
        col = lax.broadcasted_iota(jnp.int32, (step, ROWS), 1)
        pick = (col == 2 * (row % SEQ_DEV_TOK) + row // SEQ_DEV_TOK).astype(F32).astype(BF16)
        values = dot(pick, tok_ref[...])
        gal[there, :] = dot(pick, cot_ref[...]).astype(BF16)
        xs[here, :] = values.astype(BF16)
        center = values - jnp.mean(values, axis=1, keepdims=True)
        spread = jnp.mean(center * center, axis=1, keepdims=True)
        nrm[there, :] = (center * lax.rsqrt(spread + EPS) * gain + shift).astype(BF16)
        return carry

    lax.fori_loop(0, ROWS // step, norm_rows, 0)

    def spread_copy(buf, b, n, device):
        return remote(buf.at[rows(b)], buf.at[rows(b)], gsend.at[n], grecv.at[n], device)

    n_sib = spread_copy(nrm, own, 2, sibling)
    n_x = spread_copy(nrm, own, 3, xpart)
    g_sib = spread_copy(gal, own, 4, sibling)
    g_x = spread_copy(gal, own, 5, xpart)
    n_dg = spread_copy(nrm, xb, 6, sibling)
    g_dg = spread_copy(gal, xb, 7, sibling)

    def up_part_of(b, i):
        at = k * 1024 + i * 256
        bias = vall[f, pl.ds(3 + at // 512, 1), pl.ds(pl.multiple_of(at % 512, 256), 256)]
        return gate(dot(nrm[rows(b), :], wup[:, lanes(i, 256)]) + bias)

    def feed_block(b):
        def part(i, carry):
            cols = lanes(i, 256)
            value, slope = up_part_of(b, i)
            hid[rows(b), cols] = value.astype(BF16)
            back = dot_nt(gal[rows(b), :], wdn[cols, :])
            upg[rows(b), cols] = (back * slope).astype(BF16)
            return carry

        lax.fori_loop(0, 4, part, 0)

    def feed_up(b, n):
        def part(i, carry):
            cols = lanes(i, 256)
            value, slope = up_part_of(b, i)
            hid[rows(b), cols] = value.astype(BF16)
            own_acc[n, :, cols] = slope
            return carry

        lax.fori_loop(0, 4, part, 0)

    def feed_back(b, n):
        def part(i, carry):
            cols = lanes(i, 256)
            back = dot_nt(gal[rows(b), :], wdn[cols, :])
            upg[rows(b), cols] = (back * own_acc[n, :, cols]).astype(BF16)
            return carry

        lax.fori_loop(0, 4, part, 0)

    def put_heads(first, second, fq, kq, t):
        for h in range(4):
            sbuf[2 * h + fq, t, kq] = jnp.concatenate(
                [first[:, 64 * h : 64 * h + 64], second[:, 64 * h : 64 * h + 64]], axis=1
            ).reshape(4, HALF, 128)

    def turned(values, kq):
        table = jnp.concatenate(
            [turns[spots_ref[64 + 2 * (2 * p + kq) + half]] for half in range(2)], axis=0
        )
        cosine = jnp.concatenate([table[:, :64], table[:, :64]], axis=1)
        sine = jnp.concatenate([table[:, 64:], table[:, 64:]], axis=1)
        parts = []
        for s in range(SEQS):
            line = []
            for half in range(2):
                piece = values[128 * s : 128 * s + 128, 128 * half : 128 * half + 128]
                line.append(turn(piece, cosine, sine))
            parts.append(jnp.concatenate(line, axis=1))
        return jnp.concatenate(parts, axis=0).astype(BF16)

    def kg_block(b, fq, kq):
        key = dot(nrm[rows(b), :], wq[1])
        grads = dot_nt(gal[rows(b), :], wout[...]).astype(BF16)
        put_heads(turned(key, kq), grads, fq, kq, 0)

    def qv_block(b, fq, kq):
        query = dot(nrm[rows(b), :], wq[0])
        value = dot(nrm[rows(b), :], wq[2]).astype(BF16)
        put_heads(turned(query, kq) * BF16(SCALE), value, fq, kq, 1)

    def in_copy(q, t, kq):
        return remote(
            sbuf.at[q, t, kq],
            rbuf.at[2 * p + kq, t],
            asend.at[q, t, kq],
            arecv.at[p, t, kq],
            member(q),
        )

    def send_block(fq, kq, t):
        for i in range(4):
            q = 2 * (zz ^ i) + fq
            if i == 0:

                @pl.when(fq == yy)
                def _():
                    pltpu.make_async_copy(
                        sbuf.at[q, t, kq], rbuf.at[2 * p + kq, t], arecv.at[p, t, kq]
                    ).start()

                @pl.when(fq != yy)
                def _():
                    in_copy(q, t, kq).start()
            else:
                in_copy(q, t, kq).start()

    def sent_block(fq, kq, t):
        for i in range(4):
            q = 2 * (zz ^ i) + fq
            if i == 0:

                @pl.when(fq != yy)
                def _():
                    in_copy(q, t, kq).wait_send()
            else:
                in_copy(q, t, kq).wait_send()

    def store_rows(ch, i, values):
        mats[ch, i // 2, i % 2] = values.reshape(2, 128, 256)

    def down_part(i, carry):
        full = dot_tn(hid[:, lanes(i, 256)], gal[...]).astype(BF16)
        for cc in range(4):
            store_rows(cc, i, full[:, 256 * cc : 256 * cc + 256])
        return carry

    def up_part(i, carry):
        full = dot_tn(nrm[:, lanes(i, 256)], upg[...]).astype(BF16)
        for cc in range(4):
            store_rows(4 + cc, i, full[:, 256 * cc : 256 * cc + 256])
        return carry

    bits = [(p // mask) % 2 for mask in MASKS]
    every = slice(None)

    def block_index(free, other=None):
        return tuple(
            every if dim in free else (1 - bits[dim] if dim == other else bits[dim])
            for dim in range(3)
        )

    def scatter_order(ch):
        return SCATTER.get(ch, (0, 1, 2))

    def gather_order(ch):
        return GATHER.get(ch, (2, 1, 0))

    rsb = (rs0, rs1, rs2)

    def rs_copy(ch, ph):
        order = scatter_order(ch)
        return remote(
            mats.at[(ch,) + block_index(order[ph + 1 :], order[ph])],
            rsb[ph].at[ch],
            rssend.at[ch, ph],
            rsrecv.at[ch, ph],
            member(p ^ MASKS[order[ph]]),
        )

    def rs_add(ch, ph):
        free = sorted(scatter_order(ch)[ph + 1 :])
        rs_copy(ch, ph).wait_recv()
        for n in range(2 ** len(free)):
            spot = {dim: (n >> i) % 2 for i, dim in enumerate(free)}
            here = (ch,) + tuple(spot.get(dim, bits[dim]) for dim in range(3))
            there = (ch,) + tuple(spot[dim] for dim in free)
            mats[here] = (mats[here].astype(F32) + rsb[ph][there].astype(F32)).astype(BF16)

    def out_slice(ch, kk, index):
        if ch < 4:
            return odn.at[(kk,) + index + (every, slice(256 * ch, 256 * ch + 256))]
        if ch < 8:
            start, out = kk * 1024 + (ch - 4) * 256, oup
        elif ch < 11:
            start, out = (0, 1024, 512)[ch - 8] + kk * 256, oqkv
        else:
            start, out = kk * 256, oout
        return out.at[index + (every, pl.ds(pl.multiple_of(start, 256), 256))]

    def shard(ch):
        if ch == 10:
            return xsw
        return mats.at[(ch,) + block_index(())]

    def swap_shard():
        return remote(
            mats.at[(10,) + block_index(())], xsw, gsend.at[8], grecv.at[8], xpart
        )

    def local_copy(ch):
        return pltpu.make_async_copy(
            shard(ch), out_slice(ch, k, block_index(())), clocal.at[ch]
        )

    def ag_copy(ch, step):
        order = gather_order(ch)
        there = out_slice(ch, k, block_index(order[:step]))
        return remote(
            shard(ch) if step == 0 else there,
            there,
            agsend.at[ch, step],
            agrecv.at[ch, step],
            member(p ^ MASKS[order[step]]),
        )

    def core_copy(ch):
        return remote(
            out_slice(ch, k, (every,) * 3),
            out_slice(ch, k, (every,) * 3),
            csend.at[ch],
            crecv.at[ch],
            sibling,
        )

    def advance(ch, stage):
        if stage == 0:
            rs_copy(ch, 0).start()
        elif stage <= 2:
            rs_add(ch, stage - 1)
            rs_copy(ch, stage).start()
        elif stage == 3:
            rs_add(ch, 2)
            if ch == 10:
                swap_shard().start()
                swap_shard().wait_recv()
            local_copy(ch).start()
            ag_copy(ch, 0).start()
        elif stage == 4:
            ag_copy(ch, 0).wait_recv()
            local_copy(ch).wait()
            ag_copy(ch, 1).start()
        elif stage == 5:
            ag_copy(ch, 1).wait_recv()
            ag_copy(ch, 2).start()
        elif stage == 6:
            ag_copy(ch, 2).wait_recv()
            core_copy(ch).start()
        elif stage == 7:
            core_copy(ch).wait_recv()

    def settle(ch):
        for ph in range(3):
            rs_copy(ch, ph).wait_send()
            ag_copy(ch, ph).wait_send()
        core_copy(ch).wait_send()
        if ch == 10:
            swap_shard().wait_send()

    def load_half(place, t, u):
        return rbuf[spots_ref[place], t, 2 * u + spots_ref[32 + place]]

    def sort_unit(u):
        def sort_rows(i, carry):
            here = pl.ds(pl.multiple_of(i * 128, 128), 128)
            kg = jnp.concatenate([load_half(2 * i, 0, u), load_half(2 * i + 1, 0, u)], axis=0)
            qv = jnp.concatenate([load_half(2 * i, 1, u), load_half(2 * i + 1, 1, u)], axis=0)
            ak[here, :] = kg[:, :64]
            ag[here, :] = kg[:, 64:]
            aq[here, :] = qv[:, :64]
            av[here, :] = qv[:, 64:]
            kgt = kg.T
            akt[:, here] = kgt[:64, :]
            agt[:, here] = kgt[64:, :]
            avt[:, here] = qv.T[64:, :]
            return carry

        lax.fori_loop(0, LENGTH // 128, sort_rows, 0)

    def fold(values):
        return values.reshape(values.shape[0] // 8, 8, values.shape[1])

    def query_block(qb):
        mine = slice(qb * QB, qb * QB + QB)
        tiles = [slice(i * QB, i * QB + QB) for i in range(qb + 1)]
        query = aq[mine, :]
        grads = ag[mine, :]
        top = jnp.full((8, QB), masked_score, F32)
        for i, tile in enumerate(tiles):
            score = dot_nt(ak[tile, :], query)
            if i == qb:
                row = lax.broadcasted_iota(jnp.int32, (QB, QB), 0)
                col = lax.broadcasted_iota(jnp.int32, (QB, QB), 1)
                score = jnp.where(row <= col, score, masked_score)
            sco[tile, :] = score
            top = jnp.maximum(top, jnp.max(fold(score), axis=0))
        top = jnp.max(top, axis=0, keepdims=True)
        total = jnp.zeros((8, QB), F32)
        mix = jnp.zeros((HEAD_DIM, QB), F32)
        for tile in tiles:
            weights = jnp.exp(sco[tile, :] - top)
            sco[tile, :] = weights
            total = total + jnp.sum(fold(weights), axis=0)
            mix = mix + dot(avt[:, tile], weights.astype(BF16))
        inverse = 1.0 / jnp.sum(total, axis=0, keepdims=True)
        mix = mix * inverse
        dots = jnp.sum(agt[:, mine].astype(F32) * mix, axis=0, keepdims=True)
        back = jnp.zeros((HEAD_DIM, QB), F32)
        for i, tile in enumerate(tiles):
            chances = sco[tile, :] * inverse
            slopes = dot_nt(av[tile, :], grads)
            score_grads = (chances * (slopes - dots)).astype(BF16)
            value_part = dot(chances.astype(BF16), grads)
            key_part = dot(score_grads, query)
            if qb == LENGTH // QB - 1:
                dva[tile, :] = value_part
                dka[tile, :] = key_part
            else:
                dva[tile, :] += value_part
                dka[tile, :] += key_part
            back = back + dot(akt[:, tile], score_grads)
        place(0, qb, jnp.concatenate([mix, back * SCALE], axis=0).T)

    def place(t, qb, both):
        n = QB // HALF
        table = turns[qb * n : qb * n + n].reshape(QB, 128)
        cosine = jnp.concatenate([jnp.ones((QB, 64), F32), table[:, :64]], axis=1)
        sine = jnp.concatenate([jnp.zeros((QB, 64), F32), -table[:, 64:]], axis=1)
        osrt[t, qb * n : qb * n + n] = turn(both, cosine, sine).astype(BF16).reshape(n, HALF, 128)

    def finish_half(u, half):
        for qb in (2 * half, 2 * half + 1):
            mine = slice(qb * QB, qb * QB + QB)
            place(1, qb, jnp.concatenate([dva[mine, :], dka[mine, :]], axis=1))

        def unsort(i, carry):
            for t in range(2):
                sbuf[i // 2, u, t, 2 * half + i % 2] = osrt[t, spots_ref[64 + 2 * i + half]]
            return carry

        lax.fori_loop(0, 2 * CHIPS, unsort, 0)

    def send_half(u, half):
        pltpu.make_async_copy(
            out_part(sbuf, p, u, half), out_part(rb2, p, u, half), orecv.at[p, u, half]
        ).start()
        for i in (4, 6, 2, 5, 7, 3, 1):
            out_copy(p ^ i, u, half).start()

    def out_part(buf, q, u, half):
        return buf.at[q, u, :, pl.ds(2 * half, 2)]

    def out_copy(q, u, half):
        return remote(
            out_part(sbuf, q, u, half),
            out_part(rb2, p, u, half),
            osend.at[q, u, half],
            orecv.at[p, u, half],
            member(q),
        )

    def run(*steps):
        for ch, stage in steps:
            advance(ch, stage)

    def out_rows(q, u, t, kq):
        return jnp.concatenate([rb2[q, u, t, kq], rb2[q, u, t, 2 + kq]], axis=0)

    def att_part(i, carry):
        here = lanes(i, 256)
        left = nrm[:, here]
        for slot in range(3):
            at = 8 + (slot - f + 3) % 3
            store_rows(at, i, dot_tn(left, dqkv[slot]).astype(BF16))
        store_rows(11, i, dot_tn(gal[:, here], aall[...]).astype(BF16))
        return carry

    def normed_part(b, cols):
        here = rows(b)
        total = dot_nt(upg[here, :], wup[cols, :])
        for slot in range(3):
            total = total + dot_nt(dqkv[slot, here, :], wq[slot, cols, :])
        return total

    def mixed_part(b, cols):
        here = rows(b)
        return dot(hid[here, :], wdn[:, cols]) + dot(aall[here, :], wout[:, cols])

    def reduce_copies(n):
        return (
            remote(red_s.at[n, 0], red_r.at[n, 0], dsend.at[n, 0], drecv.at[n, 0], sibling),
            remote(red_s.at[n, 1], red_r.at[n, 1], dsend.at[n, 1], drecv.at[n, 1], sibling),
            remote(red_x.at[n], red_xr.at[n], dsend.at[n, 2], drecv.at[n, 2], xpart),
        )

    parts = (normed_part, mixed_part)

    def reduce_first(n):
        copies = reduce_copies(n)
        for slot, b in ((1, dg), (0, sibb)):

            def fill(i, carry):
                red_s[n, slot, :, lanes(i, 256)] = parts[n](b, lanes(i, 256)).astype(BF16)
                return carry

            lax.fori_loop(0, 4, fill, 0)
            copies[slot].start()

    def reduce_second(n):
        copies = reduce_copies(n)
        copies[1].wait_recv()

        def fill(i, carry):
            cols = lanes(i, 256)
            red_x[n, :, cols] = (
                parts[n](xb, cols) + red_r[n, 1, :, cols].astype(F32)
            ).astype(BF16)
            return carry

        lax.fori_loop(0, 4, fill, 0)
        copies[2].start()

    def reduce_third(n):
        copies = reduce_copies(n)

        def fill(i, carry):
            cols = lanes(i, 256)
            own_acc[n, :, cols] = parts[n](own, cols)
            return carry

        lax.fori_loop(0, 4, fill, 0)
        copies[0].wait_recv()
        copies[2].wait_recv()

        def finish(i, carry):
            cols = lanes(i, 256)
            own_acc[n, :, cols] = (
                own_acc[n, :, cols]
                + red_r[n, 0, :, cols].astype(F32)
                + red_xr[n, :, cols].astype(F32)
            )
            return carry

        lax.fori_loop(0, 4, finish, 0)

    def out_pick():
        row = lax.broadcasted_iota(jnp.int32, (ROWS, ROWS), 0)
        col = lax.broadcasted_iota(jnp.int32, (ROWS, ROWS), 1)
        return (row == 2 * (col % SEQ_DEV_TOK) + col // SEQ_DEV_TOK).astype(F32).astype(BF16)

    def back_rows(i, carry):
        dgain, dshift = carry
        here = pl.ds(pl.multiple_of(i * step, step), step)
        there = pl.ds(pl.multiple_of(own * ROWS + i * step, step), step)
        values = xs[here, :].astype(F32)
        center = values - jnp.mean(values, axis=1, keepdims=True)
        spread = lax.rsqrt(jnp.mean(center * center, axis=1, keepdims=True) + EPS)
        hat = center * spread
        grads = own_acc[0, here, :]
        dgain = dgain + jnp.sum(grads * hat, axis=0, keepdims=True)
        dshift = dshift + jnp.sum(grads, axis=0, keepdims=True)
        inner = grads * gain
        inner = spread * (
            inner
            - jnp.mean(inner, axis=1, keepdims=True)
            - hat * jnp.mean(inner * hat, axis=1, keepdims=True)
        )
        xs2 = gal[there, :].astype(F32) + inner
        red_s[0, 0, here, :] = xs2.astype(BF16)
        return dgain, dshift

    def mixed_rows(i, carry):
        here = pl.ds(pl.multiple_of(i * step, step), step)
        red_s[1, 0, here, :] = (xs[here, :].astype(F32) + own_acc[1, here, :] + down_b).astype(
            BF16
        )
        return carry

    for copy in (n_sib, n_x):
        copy.start()
    for copy in (g_sib, g_x):
        copy.start()
    for load in loads:
        load.wait()
    kg_block(own, f, k)
    send_block(f, k, 0)
    n_sib.wait_recv()
    g_sib.wait_recv()
    kg_block(sibb, f, 1 - k)
    send_block(f, 1 - k, 0)
    feed_block(own)
    swap_copy.wait_recv()
    qv_block(own, f, k)
    send_block(f, k, 1)
    qv_block(sibb, f, 1 - k)
    send_block(f, 1 - k, 1)
    n_x.wait_recv()
    n_dg.start()
    qv_block(xb, 1 - f, k)
    send_block(1 - f, k, 1)
    n_dg.wait_recv()
    feed_up(dg, 1)
    feed_up(xb, 0)
    qv_block(dg, 1 - f, 1 - k)
    send_block(1 - f, 1 - k, 1)
    g_x.wait_recv()
    g_dg.start()
    kg_block(xb, 1 - f, k)
    send_block(1 - f, k, 0)
    feed_block(sibb)
    g_dg.wait_recv()
    kg_block(dg, 1 - f, 1 - k)
    send_block(1 - f, 1 - k, 0)
    feed_back(dg, 1)
    lax.fori_loop(0, 4, down_part, 0)
    run((2, 0), (1, 0))
    feed_back(xb, 0)
    lax.fori_loop(0, 4, up_part, 0)
    sm[...] = jnp.zeros_like(sm)
    sm[0:1, :] = jnp.sum(upg[...].astype(F32), axis=0, keepdims=True)
    sm[2:3, :] = jnp.sum(gal[...].astype(F32), axis=0, keepdims=True)
    run((7, 0))
    for fq, kq in ((f, k), (f, 1 - k), (1 - f, k), (1 - f, 1 - k)):
        for t in range(2):
            sent_block(fq, kq, t)
    for q in range(CHIPS):
        for t in range(2):
            for kq in range(2):
                pltpu.make_async_copy(
                    rbuf.at[2 * q + kq, t], rbuf.at[2 * q + kq, t], arecv.at[q, t, kq]
                ).wait()

    run((6, 0), (5, 0), (0, 0))
    sort_unit(0)
    run((4, 0))
    query_block(3)
    query_block(2)
    finish_half(0, 1)
    send_half(0, 1)
    query_block(1)
    query_block(0)
    finish_half(0, 0)
    run((7, 1), (3, 0), (5, 1))
    send_half(0, 0)
    sort_unit(1)
    query_block(3)
    query_block(2)
    finish_half(1, 1)
    send_half(1, 1)
    run((2, 1), (6, 1))
    query_block(1)
    query_block(0)
    finish_half(1, 0)
    run((0, 1))
    send_half(1, 0)
    run((6, 2), (0, 2), (3, 1), (2, 2), (7, 2))
    for q in range(CHIPS):
        for u in range(SEQS):
            for half in range(2):
                arrived = out_part(rb2, q, u, half)
                pltpu.make_async_copy(arrived, arrived, orecv.at[q, u, half]).wait()

    for fq in range(2):
        for kq in range(2):
            for u in range(SEQS):
                at = (2 * fq + kq) * ROWS + u * 128
                here = slice(at, at + 128)
                for pair in range(2):
                    cols = slice(128 * pair, 128 * pair + 128)
                    x0 = out_rows(4 * pair + fq, u, 0, kq)
                    x1 = out_rows(4 * pair + 2 + fq, u, 0, kq)
                    y0 = out_rows(4 * pair + fq, u, 1, kq)
                    y1 = out_rows(4 * pair + 2 + fq, u, 1, kq)
                    aall[here, cols] = jnp.concatenate([x0[:, :64], x1[:, :64]], axis=1)
                    dqkv[0, here, cols] = jnp.concatenate([x0[:, 64:], x1[:, 64:]], axis=1)
                    dqkv[2, here, cols] = jnp.concatenate([y0[:, :64], y1[:, :64]], axis=1)
                    dqkv[1, here, cols] = jnp.concatenate([y0[:, 64:], y1[:, 64:]], axis=1)

    run((1, 1))
    lax.fori_loop(0, 4, att_part, 0)
    run((5, 2), (8, 0), (6, 3), (7, 3), (0, 3), (4, 1), (8, 1), (9, 0))
    reduce_first(0)
    run((1, 2), (0, 4), (10, 0))
    reduce_first(1)
    run((3, 2), (5, 3), (11, 0), (9, 1), (7, 4), (6, 4), (8, 2), (1, 3))
    run((2, 3))
    reduce_second(1)
    run((10, 1), (3, 3), (0, 5))
    reduce_second(0)
    run((9, 2), (11, 1), (6, 5), (1, 4), (7, 5), (2, 4), (11, 2), (3, 4))
    run((9, 3), (10, 2), (1, 5), (6, 6), (11, 3), (5, 4), (4, 2))
    reduce_third(0)
    reduce_copies(0)[0].wait_send()
    dgain, dshift = lax.fori_loop(
        0, ROWS // step, back_rows, (jnp.zeros((1, D), F32), jnp.zeros((1, D), F32))
    )
    tgrad_ref[...] = dot(out_pick(), red_s[0, 0]).astype(BF16)
    sm[3:4, :] = dgain
    sm[4:5, :] = dshift

    small_copies = [
        remote(sm, smg.at[own], smsend.at[0], smrecv.at[own], sibling),
        remote(sm, smg.at[own], smsend.at[1], smrecv.at[own], xpart),
        remote(sm, smg.at[own], smsend.at[2], smrecv.at[own], diagonal),
    ]
    for copy in small_copies:
        copy.start()

    run((3, 5), (8, 3), (10, 3), (9, 4), (4, 3), (8, 4), (5, 5), (11, 4))
    run((10, 4), (4, 4), (1, 6), (8, 5), (6, 7), (7, 6), (2, 5), (9, 5))
    run((11, 5), (3, 6), (0, 6), (5, 6), (10, 5), (7, 7), (4, 5))
    reduce_third(1)
    reduce_copies(1)[0].wait_send()
    lax.fori_loop(0, ROWS // step, mixed_rows, 0)
    mixed_ref[...] = dot(out_pick(), red_s[1, 0]).astype(BF16)

    run((1, 7), (2, 6), (8, 6), (11, 6))
    smg[own] = sm[...]
    for b in (sibb, xb, dg):
        remote(sm, smg.at[b], smsend.at[0], smrecv.at[b], sibling).wait_recv()
    for copy in small_copies:
        copy.wait_send()
    first_b = 2 * f
    sma[p, 0:1, :] = smg[first_b, 0:1, :]
    sma[p, 1:2, :] = smg[first_b + 1, 0:1, :]
    sma[p, 2:3, :] = sm[2:3, :]
    sma[p, 3:8, :] = smg[0, 3:8, :] + smg[1, 3:8, :] + smg[2, 3:8, :] + smg[3, 3:8, :]
    sm_copies = [
        remote(sma.at[p], sma.at[p], smsend.at[2 + i], smrecv.at[3 + i], member(p ^ i))
        for i in range(1, CHIPS)
    ]
    for copy in sm_copies:
        copy.start()

    run((11, 7), (3, 7), (5, 7), (4, 6), (9, 6), (8, 7), (10, 6), (2, 7))
    run((10, 7), (0, 7), (9, 7), (4, 7))
    total = jnp.zeros((8, D), F32)
    for copy in sm_copies:
        copy.wait()
    for q in range(CHIPS):
        total = total + sma[q]
    small_ref[...] = total

    for copy in (vec_copy,):
        pass
    swap_copy.wait_send()
    for copy in (n_sib, n_x, g_sib, g_x, n_dg, g_dg):
        copy.wait_send()
    for u in range(SEQS):
        for i in range(1, CHIPS):
            for half in range(2):
                out_copy(p ^ i, u, half).wait_send()
    for n in range(2):
        copies = reduce_copies(n)
        copies[1].wait_send()
        copies[2].wait_send()
    for ch in range(NCH):
        settle(ch)


def widen_kernel(
    dn_h,
    up_h,
    qkv_h,
    out_h,
    small,
    mixed_in,
    tgrad_in,
    dn_o,
    up_o,
    qkv_o,
    out_o,
    mixed_o,
    tgrad_o,
    gain_o,
    shift_o,
    upb_o,
    downb_o,
    dn_b,
    up_b,
    qkv_b,
    out_b,
    dn_f,
    up_f,
    qkv_f,
    out_f,
    isem,
    osem,
):
    f = lax.axis_index("fsdp")
    sources = (up_h, dn_h, qkv_h, out_h)
    brief = (up_b, dn_b, qkv_b, out_b)
    wide = (up_f, dn_f, qkv_f, out_f)
    results = (up_o, dn_o, qkv_o, out_o)
    heights = (128, 256, 128, 128)

    def fetch(n, i):
        if n == 1:
            src = dn_h.at[pl.ds(2 * i, 2)]
        else:
            src = sources[n].at[i]
        return pltpu.make_async_copy(src, brief[n].at[i], isem.at[n, i])

    def put(n, i):
        if n == 3:
            return pltpu.make_async_copy(out_f, out_o, osem.at[3, 0])
        rows = pl.ds(i * heights[n], heights[n])
        return pltpu.make_async_copy(wide[n].at[rows], results[n].at[rows], osem.at[n, i])

    for n in range(4):
        for i in range(8):
            fetch(n, i).start()
    half = D // FSDP
    low_half = f == 0
    pick = jnp.where(low_half, small[:, :half], small[:, half:])
    gain_o[...] = pick[3]
    shift_o[...] = pick[4]
    downb_o[...] = pick[2]
    upb_o[:1024] = small[0]
    upb_o[1024:] = small[1]
    mixed_o[...] = mixed_in[...]
    tgrad_o[...] = tgrad_in[...]
    for n in range(4):
        for i in range(8):
            fetch(n, i).wait()
            values = brief[n][i].astype(F32)
            if n == 3:
                out_f[:, i * 128 : i * 128 + 128] = values.T
            else:
                wide[n][i * heights[n] : (i + 1) * heights[n], :] = values.reshape(
                    heights[n], -1
                )
                put(n, i).start()
    put(3, 0).start()
    for n in range(3):
        for i in range(8):
            put(n, i).wait()
    put(3, 0).wait()


def widen(dn, up, qkv, out_t, small, mixed, tokens_grad):
    vm = pl.BlockSpec(memory_space=pltpu.VMEM)
    hbm = pl.BlockSpec(memory_space=pl.ANY)
    half = D // FSDP
    feeds = FF // FSDP
    heads = 3 * D // FSDP
    return pl.pallas_call(
        widen_kernel,
        out_shape=(
            jax.ShapeDtypeStruct((feeds, D), F32),
            jax.ShapeDtypeStruct((D, feeds), F32),
            jax.ShapeDtypeStruct((D, heads), F32),
            jax.ShapeDtypeStruct((half, D), F32),
            jax.ShapeDtypeStruct((ROWS, D), BF16),
            jax.ShapeDtypeStruct((ROWS, D), BF16),
            jax.ShapeDtypeStruct((half,), F32),
            jax.ShapeDtypeStruct((half,), F32),
            jax.ShapeDtypeStruct((feeds,), F32),
            jax.ShapeDtypeStruct((half,), F32),
        ),
        in_specs=[hbm] * 4 + [vm] * 3,
        out_specs=(hbm,) * 4 + (vm,) * 6,
        scratch_shapes=[
            pltpu.VMEM((8, 2, 128, D), BF16),
            pltpu.VMEM((8, 128, feeds), BF16),
            pltpu.VMEM((8, 128, heads), BF16),
            pltpu.VMEM((8, 128, half), BF16),
            pltpu.VMEM((feeds, D), F32),
            pltpu.VMEM((D, feeds), F32),
            pltpu.VMEM((D, heads), F32),
            pltpu.VMEM((half, D), F32),
            pltpu.SemaphoreType.DMA((4, 8)),
            pltpu.SemaphoreType.DMA((4, 8)),
        ],
        compiler_params=pltpu.CompilerParams(vmem_limit_bytes=56 * 2**20),
    )(
        dn.reshape(16, 128, D),
        up.reshape(8, 128, feeds),
        qkv.reshape(8, 128, heads),
        out_t.reshape(8, 128, half),
        small,
        mixed,
        tokens_grad,
    )


def turn_table():
    lane = np.arange(HEAD_DIM)
    speeds = (10000.0 ** (-(lane // 2 * 2) / ROT_DIM)).astype(np.float32)
    phase = np.arange(LENGTH, dtype=np.float32)[:, None] * speeds[None, :]
    turning = (lane < ROT_DIM)[None, :]
    sign = np.where(lane % 2 == 0, -1.0, 1.0)[None, :]
    cosine = np.where(turning, np.cos(phase), 1.0)
    sine = np.where(turning, np.sin(phase) * sign, 0.0)
    table = np.concatenate((cosine, sine), axis=1).astype(np.float32)
    return table.reshape(4 * CHIPS, HALF, 2 * HEAD_DIM)


def fused_device(
    tokens,
    block_pairs,
    norm_gain,
    norm_bias,
    qkv_weight,
    out_weight,
    up_weight,
    up_bias,
    down_weight,
    down_bias,
    cotangent,
):
    vm = pl.BlockSpec(memory_space=pltpu.VMEM)
    sme = pl.BlockSpec(memory_space=pltpu.SMEM)
    hbm = pl.BlockSpec(memory_space=pl.ANY)
    dma = pltpu.SemaphoreType.DMA
    scratch = [
        pltpu.SMEM((96,), jnp.int32),
        pltpu.VMEM((4 * CHIPS, HALF, 128), F32),
        pltpu.VMEM((2, 8, 512), F32),
        pltpu.VMEM((ROWS, D), BF16),
        pltpu.VMEM((ALL, D), BF16),
        pltpu.VMEM((ALL, D), BF16),
        pltpu.VMEM((3, D, 256), BF16),
        pltpu.VMEM((256, D), BF16),
        pltpu.VMEM((D, 1024), BF16),
        pltpu.VMEM((1024, D), BF16),
        pltpu.VMEM((ALL, 1024), BF16),
        pltpu.VMEM((ALL, 1024), BF16),
        pltpu.VMEM((CHIPS, 2, 2, 4, HALF, 128), BF16),
        pltpu.VMEM((2 * CHIPS, 2, 4, HALF, 128), BF16),
        pltpu.VMEM((LENGTH, HEAD_DIM), BF16),
        pltpu.VMEM((LENGTH, HEAD_DIM), BF16),
        pltpu.VMEM((LENGTH, HEAD_DIM), BF16),
        pltpu.VMEM((LENGTH, HEAD_DIM), BF16),
        pltpu.VMEM((HEAD_DIM, LENGTH), BF16),
        pltpu.VMEM((HEAD_DIM, LENGTH), BF16),
        pltpu.VMEM((HEAD_DIM, LENGTH), BF16),
        pltpu.VMEM((LENGTH, QB), F32),
        pltpu.VMEM((LENGTH, HEAD_DIM), F32),
        pltpu.VMEM((LENGTH, HEAD_DIM), F32),
        pltpu.VMEM((2, 4 * CHIPS, HALF, 128), BF16),
        pltpu.VMEM((CHIPS, SEQS, 2, 4, HALF, 128), BF16),
        pltpu.VMEM((ALL, 256), BF16),
        pltpu.VMEM((3, ALL, 256), BF16),
        pltpu.VMEM((NCH, 2, 2, 2, 128, 256), BF16),
        pltpu.VMEM((NCH, 2, 2, 128, 256), BF16),
        pltpu.VMEM((NCH, 2, 128, 256), BF16),
        pltpu.VMEM((NCH, 128, 256), BF16),
        pltpu.VMEM((128, 256), BF16),
        pltpu.VMEM((2, ROWS, D), F32),
        pltpu.VMEM((2, 2, ROWS, D), BF16),
        pltpu.VMEM((2, ROWS, D), BF16),
        pltpu.VMEM((2, 2, ROWS, D), BF16),
        pltpu.VMEM((2, ROWS, D), BF16),
        pltpu.VMEM((8, D), F32),
        pltpu.VMEM((4, 8, D), F32),
        pltpu.VMEM((CHIPS, 8, D), F32),
        dma((6,)),
        dma((9,)),
        dma((9,)),
        dma((CHIPS, 2, 2)),
        dma((CHIPS, 2, 2)),
        dma((CHIPS, SEQS, 2)),
        dma((CHIPS, SEQS, 2)),
        dma((NCH, 3)),
        dma((NCH, 3)),
        dma((NCH, 3)),
        dma((NCH, 3)),
        dma((NCH,)),
        dma((NCH,)),
        dma((NCH,)),
        dma((2, 3)),
        dma((2, 3)),
        dma((10,)),
        dma((11,)),
    ]
    mixed, tokens_grad, small, dn, up, qkv, out_t = pl.pallas_call(
        fused_kernel,
        out_shape=(
            jax.ShapeDtypeStruct((ROWS, D), BF16),
            jax.ShapeDtypeStruct((ROWS, D), BF16),
            jax.ShapeDtypeStruct((8, D), F32),
            jax.ShapeDtypeStruct((2, 2, 2, 2, 128, D), BF16),
            jax.ShapeDtypeStruct((2, 2, 2, 128, FF // FSDP), BF16),
            jax.ShapeDtypeStruct((2, 2, 2, 128, 3 * D // FSDP), BF16),
            jax.ShapeDtypeStruct((2, 2, 2, 128, D // FSDP), BF16),
        ),
        in_specs=[sme] + [vm] * 4 + [hbm, vm, vm] + [hbm] * 4,
        out_specs=(vm, vm, vm, hbm, hbm, hbm, hbm),
        scratch_shapes=scratch,
        compiler_params=pltpu.CompilerParams(
            collective_id=0, has_side_effects=True, vmem_limit_bytes=63 * 2**20
        ),
    )(
        block_pairs,
        norm_gain,
        norm_bias,
        down_bias,
        up_bias,
        jnp.asarray(turn_table()),
        tokens,
        cotangent,
        qkv_weight,
        out_weight,
        up_weight,
        down_weight,
    )
    dn, up, qkv, out, mixed, tokens_grad, gain, shift, upb, downb = widen(
        dn, up, qkv, out_t, small, mixed, tokens_grad
    )
    return mixed, tokens_grad, gain, shift, qkv, out, up, upb, dn, downb


def solution(mesh):
    in_specs = (
        P(("fsdp", "ctx"), None),
        P(),
        P("fsdp"),
        P("fsdp"),
        P(None, "fsdp"),
        P("fsdp", None),
        P(None, "fsdp"),
        P("fsdp"),
        P("fsdp", None),
        P("fsdp"),
        P(("fsdp", "ctx"), None),
    )
    out_specs = (
        P(("fsdp", "ctx"), None),
        P(("fsdp", "ctx"), None),
        P("fsdp"),
        P("fsdp"),
        P(None, "fsdp"),
        P("fsdp", None),
        P(None, "fsdp"),
        P("fsdp"),
        P("fsdp", None),
        P("fsdp"),
    )
    plan = fused_device if fits(mesh) else per_device
    return jax.shard_map(
        plan, mesh=mesh, in_specs=in_specs, out_specs=out_specs, check_vma=False
    )
```

```python
import functools
import math

import jax
import jax.numpy as jnp
import numpy as np
from jax import lax
from jax.experimental import pallas as pl
from jax.experimental.pallas import tpu as pltpu
from jax.sharding import PartitionSpec as P

D = 1024
HEAD_DIM = 64
ROT_DIM = 32
HEADS = 16
SEQ_DEV_TOK = 128
SEQS = 2


EPS = 1e-05
HIGHEST = lax.Precision.HIGHEST
masked_score = -1e30


def layer_norm(values, gain_values, shift_values):
    center = values - jnp.mean(values, axis=-1, keepdims=True)
    spread = jnp.mean(center * center, axis=-1, keepdims=True)
    return center * lax.rsqrt(spread + EPS) * gain_values + shift_values


def rotary_tables(places, window):
    lanes = jnp.arange(window, dtype=jnp.int32)
    within_head = lanes % HEAD_DIM
    turning = within_head < ROT_DIM
    steps_up = (within_head // 2 * 2).astype(jnp.float32)
    speeds = 10000.0 ** (-steps_up / ROT_DIM)
    phase = places.astype(jnp.float32)[:, None] * speeds[None, :]
    cos_full = jnp.where(turning[None, :], jnp.cos(phase), 1.0)
    sin_full = jnp.where(turning[None, :], jnp.sin(phase), 0.0)
    row_lane = lanes[:, None]
    col_lane = lanes[None, :]
    same_head = row_lane // HEAD_DIM == col_lane // HEAD_DIM
    col_within = col_lane % HEAD_DIM
    col_turns = same_head & (col_within < ROT_DIM)
    even_col = col_within % 2 == 0
    minus_part = jnp.where(col_turns & even_col & (row_lane == col_lane + 1), -1.0, 0.0)
    plus_part = jnp.where(
        col_turns & jnp.logical_not(even_col) & (row_lane == col_lane - 1), 1.0, 0.0
    )
    swap_table = (minus_part + plus_part).astype(jnp.float32)
    return (cos_full, sin_full, swap_table)


def smooth_gate(values):
    return jax.nn.gelu(values, approximate=True)


def positions(first_row, row_count, pair_table, devices, seq_rows):
    indices = first_row + jnp.arange(row_count, dtype=jnp.int32)
    owners = indices // seq_rows
    within = indices % seq_rows
    half_rows = seq_rows // 2
    matches = owners[:, None] == jnp.arange(devices, dtype=jnp.int32)[None, :]
    chosen = jnp.sum(jnp.where(matches, pair_table[None, :], 0), axis=1)
    block_index = jnp.where(within < half_rows, chosen, 2 * devices - 1 - chosen)
    return block_index * half_rows + within % half_rows


def in_groups(row_count, seq_rows):
    group_rows = math.gcd(row_count // seq_rows, 8) * seq_rows
    return (group_rows, row_count // group_rows)


def split_groups(array, group_rows, turns):
    return array.reshape((turns, group_rows) + array.shape[1:])


def grad_scores(
    query_rows,
    out_grads,
    log_sums,
    row_dots,
    query_places,
    key_rows,
    value_rows,
    key_places,
    factor,
):
    scores = (
        jnp.einsum("qshe,kshe->shqk", query_rows, key_rows, preferred_element_type=jnp.float32)
        * factor
    )
    allowed = key_places[None, :] <= query_places[:, None]
    chances = jnp.exp(jnp.where(allowed, scores - log_sums[..., None], masked_score))
    prob_grads = jnp.einsum(
        "qshe,kshe->shqk", out_grads, value_rows, preferred_element_type=jnp.float32
    )
    return (chances, (chances * (prob_grads - row_dots[..., None])).astype(jnp.bfloat16))


def per_device(
    tokens,
    block_pairs,
    norm_gain,
    norm_bias,
    qkv_weight,
    out_weight,
    up_weight,
    up_bias,
    down_weight,
    down_bias,
    cotangent,
):
    devices = lax.axis_size("ctx")
    own_index = lax.axis_index("ctx")
    seq_rows = SEQ_DEV_TOK
    seq_count = SEQS
    heads = HEADS
    head_size = HEAD_DIM
    width = D
    factor = HEAD_DIM ** (-0.5)
    all_rows = seq_rows * seq_count
    window = math.gcd(width, 128)
    gathered = (
        lax.all_gather(norm_gain, "fsdp", axis=0, tiled=True),
        lax.all_gather(norm_bias, "fsdp", axis=0, tiled=True),
        lax.all_gather(qkv_weight, "fsdp", axis=1, tiled=True),
        lax.all_gather(out_weight, "fsdp", axis=0, tiled=True),
        lax.all_gather(up_weight, "fsdp", axis=1, tiled=True),
        lax.all_gather(up_bias, "fsdp", axis=0, tiled=True),
        lax.all_gather(down_weight, "fsdp", axis=0, tiled=True),
        lax.all_gather(down_bias, "fsdp", axis=0, tiled=True),
    )
    gain_low, shift_low, w_qkv, w_out, w_up, b_up, w_down, b_down = gathered
    inputs = tokens.astype(jnp.float32)
    gain_values = gain_low.astype(jnp.float32)
    shift_values = shift_low.astype(jnp.float32)
    normed_low = layer_norm(inputs, gain_values, shift_values).astype(jnp.bfloat16)
    mixed_qkv = jnp.dot(normed_low, w_qkv, preferred_element_type=jnp.float32).reshape(
        seq_rows, seq_count, 3 * width
    )
    own_places = positions(own_index * seq_rows, seq_rows, block_pairs, devices, seq_rows)
    cos_full, sin_full, swap_table = rotary_tables(own_places, window)

    def turn_both(values):
        shaped = values.reshape(seq_rows, seq_count, 2 * width // window, window)
        swapped = jnp.einsum("rsgw,wv->rsgv", shaped, swap_table, precision=HIGHEST)
        turned_rows = shaped * cos_full[:, None, None, :] + swapped * sin_full[:, None, None, :]
        return turned_rows.reshape(seq_rows, seq_count, 2 * width)

    query_key = mixed_qkv[:, :, : 2 * width]
    turned = turn_both(query_key)
    queries = (
        turned[:, :, :width].astype(jnp.bfloat16).reshape(seq_rows, seq_count, heads, head_size)
    )
    key_rows = (
        turned[:, :, width:].astype(jnp.bfloat16).reshape(seq_rows, seq_count, heads, head_size)
    )
    value_rows = (
        mixed_qkv[:, :, 2 * width :]
        .astype(jnp.bfloat16)
        .reshape(seq_rows, seq_count, heads, head_size)
    )
    start_state = (
        jnp.full((seq_count, heads, seq_rows), masked_score, jnp.float32),
        jnp.zeros((seq_count, heads, seq_rows), jnp.float32),
        jnp.zeros((seq_count, heads, seq_rows, head_size), jnp.float32),
    )
    piece_keys = lax.all_gather(key_rows, "ctx", axis=0, tiled=True)
    piece_values = lax.all_gather(value_rows, "ctx", axis=0, tiled=True)
    group_rows, turns = in_groups(piece_keys.shape[0], seq_rows)

    def attend_step(inner, item):
        block_keys, block_values, turn = item
        key_places = positions(turn * group_rows, group_rows, block_pairs, devices, seq_rows)
        scores = (
            jnp.einsum("qshe,kshe->shqk", queries, block_keys, preferred_element_type=jnp.float32)
            * factor
        )
        allowed = key_places[None, :] <= own_places[:, None]
        running, totals, accum = inner
        fresh = jnp.maximum(running, jnp.max(jnp.where(allowed, scores, masked_score), axis=-1))
        weights = jnp.exp(jnp.where(allowed, scores - fresh[..., None], masked_score))
        fading = jnp.exp(running - fresh)
        totals = totals * fading + jnp.sum(weights, axis=-1)
        accum = accum * fading[..., None] + jnp.einsum(
            "shqk,kshe->shqe",
            weights.astype(jnp.bfloat16),
            block_values,
            preferred_element_type=jnp.float32,
        )
        return ((fresh, totals, accum), None)

    inner, _ = lax.scan(
        attend_step,
        start_state,
        (
            split_groups(piece_keys, group_rows, turns),
            split_groups(piece_values, group_rows, turns),
            jnp.arange(turns, dtype=jnp.int32),
        ),
    )
    running, totals, accum = inner
    log_sums = running + jnp.log(totals)
    attended = jnp.transpose(accum / totals[..., None], (2, 0, 1, 3))
    attn_low = attended.reshape(all_rows, width).astype(jnp.bfloat16)
    attention = jnp.dot(attn_low, w_out, preferred_element_type=jnp.float32)
    up_pre = jnp.dot(normed_low, w_up, preferred_element_type=jnp.float32) + b_up.astype(
        jnp.float32
    )
    hidden_low = smooth_gate(up_pre).astype(jnp.bfloat16)
    result = (
        inputs
        + attention
        + jnp.dot(hidden_low, w_down, preferred_element_type=jnp.float32)
        + b_down.astype(jnp.float32)
    )
    mixed = result.astype(jnp.bfloat16)
    again = (
        lax.all_gather(norm_gain, "fsdp", axis=0, tiled=True),
        lax.all_gather(norm_bias, "fsdp", axis=0, tiled=True),
        lax.all_gather(qkv_weight, "fsdp", axis=1, tiled=True),
        lax.all_gather(out_weight, "fsdp", axis=0, tiled=True),
        lax.all_gather(up_weight, "fsdp", axis=1, tiled=True),
        lax.all_gather(up_bias, "fsdp", axis=0, tiled=True),
        lax.all_gather(down_weight, "fsdp", axis=0, tiled=True),
        lax.all_gather(down_bias, "fsdp", axis=0, tiled=True),
    )
    gain_low, shift_low, w_qkv, w_out, w_up, b_up, w_down, b_down = again
    out_grad = cotangent.astype(jnp.float32)
    attn_grads = (
        jnp.einsum("td,ed->te", cotangent, w_out, preferred_element_type=jnp.float32)
        .astype(jnp.bfloat16)
        .reshape(seq_rows, seq_count, heads, head_size)
    )
    dots_rows = jnp.sum(attn_grads.astype(jnp.float32) * attended, axis=-1)
    row_dots = jnp.transpose(dots_rows, (1, 2, 0))
    empty_rows = jnp.zeros((seq_rows, seq_count, heads, head_size), jnp.float32)
    whole_keys, whole_values = (
        lax.all_gather(key_rows, "ctx", axis=0, tiled=True),
        lax.all_gather(value_rows, "ctx", axis=0, tiled=True),
    )
    piece_keys = whole_keys
    piece_values = whole_values
    query_group_rows, turns = in_groups(piece_keys.shape[0], seq_rows)

    def query_step(inner, item):
        block_keys, block_values, turn = item
        key_places = positions(
            0 + turn * query_group_rows, query_group_rows, block_pairs, devices, seq_rows
        )
        chances, score_grads = grad_scores(
            queries,
            attn_grads,
            log_sums,
            row_dots,
            own_places,
            block_keys,
            block_values,
            key_places,
            factor,
        )
        return (
            inner
            + jnp.einsum(
                "shqk,kshe->qshe", score_grads, block_keys, preferred_element_type=jnp.float32
            )
            * factor,
            None,
        )

    inner, _ = lax.scan(
        query_step,
        empty_rows,
        (
            split_groups(piece_keys, query_group_rows, turns),
            split_groups(piece_values, query_group_rows, turns),
            jnp.arange(turns, dtype=jnp.int32),
        ),
    )
    query_grad = inner
    piece_keys = whole_keys
    piece_values = whole_values
    key_group_rows, turns = in_groups(seq_rows * lax.axis_size("ctx"), seq_rows)

    def key_step(inner, item):
        block_keys, block_values, turn = item
        key_places = positions(
            turn * key_group_rows, key_group_rows, block_pairs, devices, seq_rows
        )
        chances, score_grads = grad_scores(
            queries,
            attn_grads,
            log_sums,
            row_dots,
            own_places,
            block_keys,
            block_values,
            key_places,
            factor,
        )
        key_part = (
            jnp.einsum("shqk,qshe->kshe", score_grads, queries, preferred_element_type=jnp.float32)
            * factor
        )
        value_part = jnp.einsum(
            "shqk,qshe->kshe",
            chances.astype(jnp.bfloat16),
            attn_grads,
            preferred_element_type=jnp.float32,
        )
        stacked = jnp.stack(
            (
                key_part.reshape(key_group_rows, seq_count, width),
                value_part.reshape(key_group_rows, seq_count, width),
            ),
            axis=2,
        )
        return (inner, stacked)

    _, blocks_out = lax.scan(
        key_step,
        jnp.zeros((), jnp.float32),
        (
            split_groups(piece_keys, key_group_rows, turns),
            split_groups(piece_values, key_group_rows, turns),
            jnp.arange(turns, dtype=jnp.int32),
        ),
    )
    summed_terms = lax.psum_scatter(
        blocks_out.reshape(seq_rows * lax.axis_size("ctx"), seq_count, 2, width),
        "ctx",
        scatter_dimension=0,
        tiled=True,
    )
    key_grad = summed_terms[:, :, 0].reshape(seq_rows, seq_count, heads, head_size)
    value_grad = summed_terms[:, :, 1].reshape(seq_rows, seq_count, heads, head_size)
    _, turn_back = jax.vjp(turn_both, query_key)
    both_grads = jnp.concatenate(
        (
            query_grad.reshape(seq_rows, seq_count, width),
            key_grad.reshape(seq_rows, seq_count, width),
        ),
        axis=2,
    )
    (pre_grads,) = turn_back(both_grads)
    qkv_grad = (
        jnp.concatenate((pre_grads, value_grad.reshape(seq_rows, seq_count, width)), axis=2)
        .reshape(all_rows, 3 * width)
        .astype(jnp.bfloat16)
    )
    hidden_grad = jnp.einsum("td,fd->tf", cotangent, w_down, preferred_element_type=jnp.float32)
    _, gate_back = jax.vjp(smooth_gate, up_pre)
    (up_grad,) = gate_back(hidden_grad)
    up_low = up_grad.astype(jnp.bfloat16)
    normed_grad = jnp.einsum(
        "tc,dc->td", qkv_grad, w_qkv, preferred_element_type=jnp.float32
    ) + jnp.einsum("tf,df->td", up_low, w_up, preferred_element_type=jnp.float32)
    _, norm_back = jax.vjp(
        layer_norm, inputs, gain_low.astype(jnp.float32), shift_low.astype(jnp.float32)
    )
    input_part, gain_grad, shift_grad = norm_back(normed_grad)
    tokens_grad = (out_grad + input_part).astype(jnp.bfloat16)
    qkv_wgrad = jnp.einsum("td,tc->dc", normed_low, qkv_grad, preferred_element_type=jnp.float32)
    out_wgrad = jnp.einsum("td,te->de", attn_low, cotangent, preferred_element_type=jnp.float32)
    up_wgrad = jnp.einsum("td,tf->df", normed_low, up_low, preferred_element_type=jnp.float32)
    up_bgrad = jnp.sum(up_low.astype(jnp.float32), axis=0)
    down_wgrad = jnp.einsum("tf,td->fd", hidden_low, cotangent, preferred_element_type=jnp.float32)
    down_bgrad = jnp.sum(out_grad, axis=0)
    shares = (
        lax.psum_scatter(
            gain_grad.astype(jnp.bfloat16), "fsdp", scatter_dimension=0, tiled=True
        ).astype(jnp.float32),
        lax.psum_scatter(
            shift_grad.astype(jnp.bfloat16), "fsdp", scatter_dimension=0, tiled=True
        ).astype(jnp.float32),
        lax.psum_scatter(
            qkv_wgrad.astype(jnp.bfloat16), "fsdp", scatter_dimension=1, tiled=True
        ).astype(jnp.float32),
        lax.psum_scatter(
            out_wgrad.astype(jnp.bfloat16), "fsdp", scatter_dimension=0, tiled=True
        ).astype(jnp.float32),
        lax.psum_scatter(
            up_wgrad.astype(jnp.bfloat16), "fsdp", scatter_dimension=1, tiled=True
        ).astype(jnp.float32),
        lax.psum_scatter(
            up_bgrad.astype(jnp.bfloat16), "fsdp", scatter_dimension=0, tiled=True
        ).astype(jnp.float32),
        lax.psum_scatter(
            down_wgrad.astype(jnp.bfloat16), "fsdp", scatter_dimension=0, tiled=True
        ).astype(jnp.float32),
        lax.psum_scatter(
            down_bgrad.astype(jnp.bfloat16), "fsdp", scatter_dimension=0, tiled=True
        ).astype(jnp.float32),
    )
    share_gain, share_shift, share_qkv, share_out, share_up, share_upb, share_down, share_downb = (
        shares
    )
    totals_out = lax.psum(
        (
            share_gain,
            share_shift,
            share_qkv,
            share_out,
            share_up,
            share_upb,
            share_down,
            share_downb,
        ),
        "ctx",
    )
    sum_gain, sum_shift, sum_qkv, sum_out, sum_up, sum_upb, sum_down, sum_downb = totals_out
    return (
        mixed,
        tokens_grad,
        sum_gain,
        sum_shift,
        sum_qkv,
        sum_out,
        sum_up,
        sum_upb,
        sum_down,
        sum_downb,
    )


F32 = jnp.float32
BF16 = jnp.bfloat16
FF = 4096
FSDP = 2
CHIPS = 8
ROWS = SEQ_DEV_TOK * SEQS
ALL = 4 * ROWS
LENGTH = CHIPS * 2 * SEQ_DEV_TOK
HALF = SEQ_DEV_TOK // 2
QB = 512
NCH = 12
MASKS = (1, 2, 4)
SCATTER = {2: (1, 0, 2), 5: (1, 0, 2), 6: (2, 0, 1)}
GATHER = {0: (2, 0, 1), 5: (2, 0, 1), 8: (1, 2, 0), 9: (2, 0, 1)}
MIDDLE = {3: (2, 1, 0), 7: (2, 1, 0), 10: (2, 1, 0), 11: (2, 1, 0)}
SCALE = HEAD_DIM**-0.5


def fits(mesh):
    return mesh.shape["fsdp"] == FSDP and mesh.shape["ctx"] == 2 * CHIPS


def dot(left, right):
    return lax.dot_general(left, right, (((1,), (0,)), ((), ())), preferred_element_type=F32)


def dot_nt(left, right):
    return lax.dot_general(left, right, (((1,), (1,)), ((), ())), preferred_element_type=F32)


def dot_tn(left, right):
    return lax.dot_general(left, right, (((0,), (0,)), ((), ())), preferred_element_type=F32)


def turn(values, cosine, sine):
    lane = lax.broadcasted_iota(jnp.int32, values.shape, 1)
    width = values.shape[1]
    other = jnp.where(
        lane % 2 == 0, pltpu.roll(values, width - 1, 1), pltpu.roll(values, 1, 1)
    )
    return values * cosine + other * sine


def gate(values):
    inner = 0.7978845608028654 * (values + 0.044715 * values * values * values)
    th = jnp.tanh(inner)
    half = 0.5 * (1.0 + th)
    slope = half + (0.5 * values) * (1.0 - th * th) * (
        0.7978845608028654 * (1.0 + 3 * 0.044715 * values * values)
    )
    return values * half, slope


def fused_kernel(
    pairs_ref,
    gain_ref,
    shift_ref,
    downb_ref,
    upb_ref,
    turns_h,
    tok_ref,
    cot_ref,
    wqkv_h,
    wout_h,
    wup_h,
    wdn_h,
    mixed_ref,
    tgrad_ref,
    small_ref,
    odn,
    oup,
    oqkv,
    oout,
    spots_ref,
    turns,
    vall,
    xs,
    nrm,
    gal,
    wq,
    wout,
    wup,
    wdn,
    hid,
    upg,
    sbuf,
    rbuf,
    aq,
    ag,
    ak,
    av,
    akt,
    avt,
    agt,
    sco,
    dka,
    dva,
    osrt,
    rb2,
    aall,
    dqkv,
    mats,
    rs0,
    rs1,
    rs2,
    xsw,
    rsm,
    own_acc,
    red_s,
    red_x,
    red_r,
    red_xr,
    sm,
    smg,
    sma,
    lsem,
    gsend,
    grecv,
    asend,
    arecv,
    osend,
    orecv,
    rssend,
    rsrecv,
    agsend,
    agrecv,
    clocal,
    csend,
    crecv,
    dsend,
    drecv,
    smsend,
    smrecv,
):
    f = lax.axis_index("fsdp")
    c = lax.axis_index("ctx")
    k = c % 2
    p = c // 2
    zz = p // 2
    yy = p % 2
    xpart = (1 - f, c)
    sibling = (f, 2 * p + 1 - k)
    diagonal = (1 - f, 2 * p + 1 - k)
    own = 2 * f + k
    sibb = 2 * f + 1 - k
    xb = 2 * (1 - f) + k
    dg = 2 * (1 - f) + 1 - k
    MESH = pl.DeviceIdType.MESH

    def member(q):
        return (f, 2 * q + k)

    def remote(src, dst, ssem, rsem, device):
        return pltpu.make_async_remote_copy(
            src_ref=src,
            dst_ref=dst,
            send_sem=ssem,
            recv_sem=rsem,
            device_id=device,
            device_id_type=MESH,
        )

    def rows(b):
        return pl.ds(pl.multiple_of(b * ROWS, ROWS), ROWS)

    def lanes(i, n):
        return pl.ds(pl.multiple_of(i * n, n), n)

    loads = [
        pltpu.make_async_copy(wqkv_h.at[:, lanes(k, 256)], wq.at[f], lsem.at[0]),
        pltpu.make_async_copy(
            wqkv_h.at[:, pl.ds(pl.multiple_of(1024 + 256 * k, 256), 256)], wq.at[1 + f], lsem.at[1]
        ),
        pltpu.make_async_copy(wup_h.at[:, lanes(k, 1024)], wup, lsem.at[2]),
        pltpu.make_async_copy(wdn_h.at[lanes(k, 1024), :], wdn, lsem.at[3]),
        pltpu.make_async_copy(wout_h.at[lanes(k, 256), :], wout, lsem.at[4]),
        pltpu.make_async_copy(turns_h, turns, lsem.at[5]),
    ]
    for load in loads:
        load.start()
    barrier = pltpu.get_barrier_semaphore()
    for device in [xpart, sibling, diagonal] + [member(p ^ i) for i in range(1, CHIPS)]:
        pl.semaphore_signal(barrier, inc=1, device_id=device, device_id_type=MESH)
    pl.semaphore_wait(barrier, 3 + CHIPS - 1)

    def row_of(ref, at):
        return ref[pl.ds(at, 512)].astype(F32).reshape(1, 512)

    vall[f] = jnp.concatenate(
        [row_of(gain_ref, 0), row_of(shift_ref, 0), row_of(downb_ref, 0)]
        + [row_of(upb_ref, 512 * i) for i in range(4)]
        + [jnp.zeros((1, 512), F32)],
        axis=0,
    )
    vec_copy = remote(vall.at[f], vall.at[f], gsend.at[0], grecv.at[0], xpart)
    vec_copy.start()
    swap_copy = remote(
        wqkv_h.at[:, pl.ds(pl.multiple_of(512 + 256 * k, 256), 256)],
        wq.at[2 * f],
        gsend.at[1],
        grecv.at[1],
        xpart,
    )
    swap_copy.start()

    def table_row(b, carry):
        holder = jnp.int32(0)
        half = jnp.int32(0)
        for i in range(2 * CHIPS):
            first = (pairs_ref[i] == b).astype(jnp.int32)
            last = (4 * CHIPS - 1 - pairs_ref[i] == b).astype(jnp.int32)
            holder = holder + i * (first + last)
            half = half + last
        spots_ref[b] = jnp.minimum(holder, 2 * CHIPS - 1)
        spots_ref[4 * CHIPS + b] = jnp.minimum(half, 1)
        return carry

    lax.fori_loop(0, 4 * CHIPS, table_row, 0)

    def table_pair(i, carry):
        spots_ref[64 + 2 * i] = pairs_ref[i]
        spots_ref[64 + 2 * i + 1] = 4 * CHIPS - 1 - pairs_ref[i]
        return carry

    lax.fori_loop(0, 2 * CHIPS, table_pair, 0)
    vec_copy.wait()
    gain = jnp.concatenate([vall[0, 0:1, :], vall[1, 0:1, :]], axis=1).astype(F32)
    shift = jnp.concatenate([vall[0, 1:2, :], vall[1, 1:2, :]], axis=1).astype(F32)
    down_b = jnp.concatenate([vall[0, 2:3, :], vall[1, 2:3, :]], axis=1).astype(F32)

    step = 64

    def norm_rows(i, carry):
        here = pl.ds(pl.multiple_of(i * step, step), step)
        there = pl.ds(pl.multiple_of(own * ROWS + i * step, step), step)
        row = lax.broadcasted_iota(jnp.int32, (step, ROWS), 0) + i * step
        col = lax.broadcasted_iota(jnp.int32, (step, ROWS), 1)
        pick = (col == 2 * (row % SEQ_DEV_TOK) + row // SEQ_DEV_TOK).astype(F32).astype(BF16)
        values = dot(pick, tok_ref[...])
        gal[there, :] = dot(pick, cot_ref[...]).astype(BF16)
        xs[here, :] = values.astype(BF16)
        center = values - jnp.mean(values, axis=1, keepdims=True)
        spread = jnp.mean(center * center, axis=1, keepdims=True)
        nrm[there, :] = (center * lax.rsqrt(spread + EPS) * gain + shift).astype(BF16)
        return carry

    lax.fori_loop(0, ROWS // step, norm_rows, 0)

    def spread_copy(buf, b, n, device):
        return remote(buf.at[rows(b)], buf.at[rows(b)], gsend.at[n], grecv.at[n], device)

    n_sib = spread_copy(nrm, own, 2, sibling)
    n_x = spread_copy(nrm, own, 3, xpart)
    g_sib = spread_copy(gal, own, 4, sibling)
    g_x = spread_copy(gal, own, 5, xpart)
    n_dg = spread_copy(nrm, xb, 6, sibling)
    g_dg = spread_copy(gal, xb, 7, sibling)

    def up_part_of(b, i):
        at = k * 1024 + i * 256
        bias = vall[f, pl.ds(3 + at // 512, 1), pl.ds(pl.multiple_of(at % 512, 256), 256)]
        return gate(dot(nrm[rows(b), :], wup[:, lanes(i, 256)]) + bias)

    def feed_block(b):
        def part(i, carry):
            cols = lanes(i, 256)
            value, slope = up_part_of(b, i)
            hid[rows(b), cols] = value.astype(BF16)
            back = dot_nt(gal[rows(b), :], wdn[cols, :])
            upg[rows(b), cols] = (back * slope).astype(BF16)
            return carry

        lax.fori_loop(0, 4, part, 0)

    def feed_up(b, n):
        def part(i, carry):
            cols = lanes(i, 256)
            value, slope = up_part_of(b, i)
            hid[rows(b), cols] = value.astype(BF16)
            own_acc[n, :, cols] = slope
            return carry

        lax.fori_loop(0, 4, part, 0)

    def feed_back(b, n):
        def part(i, carry):
            cols = lanes(i, 256)
            back = dot_nt(gal[rows(b), :], wdn[cols, :])
            upg[rows(b), cols] = (back * own_acc[n, :, cols]).astype(BF16)
            return carry

        lax.fori_loop(0, 4, part, 0)

    def put_heads(first, second, fq, kq, t):
        for h in range(4):
            sbuf[2 * h + fq, t, kq] = jnp.concatenate(
                [first[:, 64 * h : 64 * h + 64], second[:, 64 * h : 64 * h + 64]], axis=1
            ).reshape(4, HALF, 128)

    def turned(values, kq):
        table = jnp.concatenate(
            [turns[spots_ref[64 + 2 * (2 * p + kq) + half]] for half in range(2)], axis=0
        )
        cosine = jnp.concatenate([table[:, :64], table[:, :64]], axis=1)
        sine = jnp.concatenate([table[:, 64:], table[:, 64:]], axis=1)
        parts = []
        for s in range(SEQS):
            line = []
            for half in range(2):
                piece = values[128 * s : 128 * s + 128, 128 * half : 128 * half + 128]
                line.append(turn(piece, cosine, sine))
            parts.append(jnp.concatenate(line, axis=1))
        return jnp.concatenate(parts, axis=0).astype(BF16)

    def kg_block(b, fq, kq):
        key = dot(nrm[rows(b), :], wq[1])
        grads = dot_nt(gal[rows(b), :], wout[...]).astype(BF16)
        put_heads(turned(key, kq), grads, fq, kq, 0)

    def qv_block(b, fq, kq):
        query = dot(nrm[rows(b), :], wq[0])
        value = dot(nrm[rows(b), :], wq[2]).astype(BF16)
        put_heads(turned(query, kq) * BF16(SCALE), value, fq, kq, 1)

    def in_copy(q, t, kq):
        return remote(
            sbuf.at[q, t, kq],
            rbuf.at[2 * p + kq, t],
            asend.at[q, t, kq],
            arecv.at[p, t, kq],
            member(q),
        )

    def send_block(fq, kq, t):
        for i in range(4):
            q = 2 * (zz ^ i) + fq
            if i == 0:

                @pl.when(fq == yy)
                def _():
                    pltpu.make_async_copy(
                        sbuf.at[q, t, kq], rbuf.at[2 * p + kq, t], arecv.at[p, t, kq]
                    ).start()

                @pl.when(fq != yy)
                def _():
                    in_copy(q, t, kq).start()
            else:
                in_copy(q, t, kq).start()

    def sent_block(fq, kq, t):
        for i in range(4):
            q = 2 * (zz ^ i) + fq
            if i == 0:

                @pl.when(fq != yy)
                def _():
                    in_copy(q, t, kq).wait_send()
            else:
                in_copy(q, t, kq).wait_send()

    def store_rows(ch, i, values):
        mats[ch, i // 2, i % 2] = values.reshape(2, 128, 256)

    def down_part(i, carry):
        full = dot_tn(hid[:, lanes(i, 256)], gal[...]).astype(BF16)
        for cc in range(4):
            store_rows(cc, i, full[:, 256 * cc : 256 * cc + 256])
        return carry

    def up_part(i, carry):
        full = dot_tn(nrm[:, lanes(i, 256)], upg[...]).astype(BF16)
        for cc in range(4):
            store_rows(4 + cc, i, full[:, 256 * cc : 256 * cc + 256])
        return carry

    bits = [(p // mask) % 2 for mask in MASKS]
    every = slice(None)

    def block_index(free, other=None):
        return tuple(
            every if dim in free else (1 - bits[dim] if dim == other else bits[dim])
            for dim in range(3)
        )

    def scatter_order(ch):
        return SCATTER.get(ch, (0, 1, 2))

    def gather_order(ch):
        return GATHER.get(ch, (2, 1, 0))

    rsb = (rs0, rs1, rs2)

    middle = jnp.logical_or(zz == 1, zz == 2)
    outer = jnp.logical_not(middle)
    half_z = zz // 2
    inner_chip = 2 * (1 + half_z) + yy
    other_chip = 2 * (3 - zz) + yy
    outer_chip = 6 * half_z + yy

    def middle_in(ch, ph):
        if ph == 0:
            src, dst, q = mats.at[ch, 1 - yy], rs0.at[ch], p ^ 1
        elif ph == 1:
            src, dst, q = mats.at[ch, yy], rsm.at[sorted(MIDDLE).index(ch)], inner_chip
        else:
            src, dst, q = mats.at[ch, yy, :, 1 - half_z], rs1.at[ch], other_chip
        return remote(src, dst, rssend.at[ch, ph], rsrecv.at[ch, ph], member(q))

    def middle_out(ch, step):
        order = MIDDLE[ch]
        kind = order[step]
        done = order[:step]
        index = (every if 0 in done else yy, every, every if 2 in done else half_z)
        there = out_slice(ch, k, index)
        src = middle_shard(ch) if step == 0 else there
        q = (p ^ 1, outer_chip, other_chip)[kind]
        return remote(src, there, agsend.at[ch, step], agrecv.at[ch, step], member(q))

    def middle_shard(ch):
        return xsw if ch == 10 else mats.at[ch, yy, :, half_z]

    def middle_swap():
        return remote(mats.at[10, yy, :, half_z], xsw, gsend.at[8], grecv.at[8], xpart)

    def middle_local(ch):
        there = out_slice(ch, k, (yy, every, half_z))
        return pltpu.make_async_copy(middle_shard(ch), there, clocal.at[ch])

    def sends_out(ch, step):
        order = MIDDLE[ch]
        return order[step] == 0 and 1 in order[:step]

    def wait_out(ch, step):
        if sends_out(ch, step):
            middle_out(ch, step).wait_recv()
        else:

            @pl.when(outer if MIDDLE[ch][step] == 1 else middle)
            def _():
                middle_out(ch, step).wait_recv()

    def start_out(ch, step):
        if sends_out(ch, step):
            middle_out(ch, step).start()
        else:

            @pl.when(middle)
            def _():
                middle_out(ch, step).start()

    def add_blocks(ch, pairs):
        for here, there in pairs:
            mats[(ch,) + here] = (mats[(ch,) + here].astype(F32) + there.astype(F32)).astype(BF16)

    def advance_middle(ch, stage):
        if stage == 0:
            middle_in(ch, 0).start()
        elif stage == 1:
            middle_in(ch, 0).wait_recv()
            add_blocks(ch, [((yy, i, j), rs0[ch, i, j]) for i in range(2) for j in range(2)])

            @pl.when(outer)
            def _():
                middle_in(ch, 1).start()
        elif stage == 2:

            @pl.when(middle)
            def _():
                middle_in(ch, 1).wait_recv()
                n = sorted(MIDDLE).index(ch)
                add_blocks(ch, [((yy, i, j), rsm[n, i, j]) for i in range(2) for j in range(2)])
                middle_in(ch, 2).start()
        elif stage == 3:

            @pl.when(middle)
            def _():
                middle_in(ch, 2).wait_recv()
                add_blocks(ch, [((yy, i, half_z), rs1[ch, i]) for i in range(2)])
                if ch == 10:
                    middle_swap().start()
                    middle_swap().wait_recv()
                middle_local(ch).start()
                middle_out(ch, 0).start()
        elif stage == 4:
            wait_out(ch, 0)

            @pl.when(middle)
            def _():
                middle_local(ch).wait()

            start_out(ch, 1)
        elif stage == 5:
            wait_out(ch, 1)
            start_out(ch, 2)
        elif stage == 6:
            wait_out(ch, 2)
            core_copy(ch).start()
        elif stage == 7:
            core_copy(ch).wait_recv()

    def settle_middle(ch):
        middle_in(ch, 0).wait_send()

        @pl.when(outer)
        def _():
            middle_in(ch, 1).wait_send()

        @pl.when(middle)
        def _():
            middle_in(ch, 2).wait_send()
            if ch == 10:
                middle_swap().wait_send()

        for step in range(3):
            if sends_out(ch, step):
                middle_out(ch, step).wait_send()
            else:

                @pl.when(middle)
                def _():
                    middle_out(ch, step).wait_send()

        core_copy(ch).wait_send()

    def rs_copy(ch, ph):
        order = scatter_order(ch)
        return remote(
            mats.at[(ch,) + block_index(order[ph + 1 :], order[ph])],
            rsb[ph].at[ch],
            rssend.at[ch, ph],
            rsrecv.at[ch, ph],
            member(p ^ MASKS[order[ph]]),
        )

    def rs_add(ch, ph):
        free = sorted(scatter_order(ch)[ph + 1 :])
        rs_copy(ch, ph).wait_recv()
        for n in range(2 ** len(free)):
            spot = {dim: (n >> i) % 2 for i, dim in enumerate(free)}
            here = (ch,) + tuple(spot.get(dim, bits[dim]) for dim in range(3))
            there = (ch,) + tuple(spot[dim] for dim in free)
            mats[here] = (mats[here].astype(F32) + rsb[ph][there].astype(F32)).astype(BF16)

    def out_slice(ch, kk, index):
        if ch < 4:
            return odn.at[(kk,) + index + (every, slice(256 * ch, 256 * ch + 256))]
        if ch < 8:
            start, out = kk * 1024 + (ch - 4) * 256, oup
        elif ch < 11:
            start, out = (0, 1024, 512)[ch - 8] + kk * 256, oqkv
        else:
            start, out = kk * 256, oout
        return out.at[index + (every, pl.ds(pl.multiple_of(start, 256), 256))]

    def shard(ch):
        if ch == 10:
            return xsw.at[0]
        return mats.at[(ch,) + block_index(())]

    def swap_shard():
        return remote(
            mats.at[(10,) + block_index(())], xsw.at[0], gsend.at[8], grecv.at[8], xpart
        )

    def local_copy(ch):
        return pltpu.make_async_copy(
            shard(ch), out_slice(ch, k, block_index(())), clocal.at[ch]
        )

    def ag_copy(ch, step):
        order = gather_order(ch)
        there = out_slice(ch, k, block_index(order[:step]))
        return remote(
            shard(ch) if step == 0 else there,
            there,
            agsend.at[ch, step],
            agrecv.at[ch, step],
            member(p ^ MASKS[order[step]]),
        )

    def core_copy(ch):
        return remote(
            out_slice(ch, k, (every,) * 3),
            out_slice(ch, k, (every,) * 3),
            csend.at[ch],
            crecv.at[ch],
            sibling,
        )

    def advance(ch, stage):
        if ch in MIDDLE:
            advance_middle(ch, stage)
        elif stage == 0:
            rs_copy(ch, 0).start()
        elif stage <= 2:
            rs_add(ch, stage - 1)
            rs_copy(ch, stage).start()
        elif stage == 3:
            rs_add(ch, 2)
            if ch == 10:
                swap_shard().start()
                swap_shard().wait_recv()
            local_copy(ch).start()
            ag_copy(ch, 0).start()
        elif stage == 4:
            ag_copy(ch, 0).wait_recv()
            local_copy(ch).wait()
            ag_copy(ch, 1).start()
        elif stage == 5:
            ag_copy(ch, 1).wait_recv()
            ag_copy(ch, 2).start()
        elif stage == 6:
            ag_copy(ch, 2).wait_recv()
            core_copy(ch).start()
        elif stage == 7:
            core_copy(ch).wait_recv()

    def settle(ch):
        if ch in MIDDLE:
            settle_middle(ch)
            return
        for ph in range(3):
            rs_copy(ch, ph).wait_send()
            ag_copy(ch, ph).wait_send()
        core_copy(ch).wait_send()
        if ch == 10:
            swap_shard().wait_send()

    def load_half(place, t, u):
        return rbuf[spots_ref[place], t, 2 * u + spots_ref[32 + place]]

    def sort_unit(u):
        def sort_rows(i, carry):
            here = pl.ds(pl.multiple_of(i * 128, 128), 128)
            kg = jnp.concatenate([load_half(2 * i, 0, u), load_half(2 * i + 1, 0, u)], axis=0)
            qv = jnp.concatenate([load_half(2 * i, 1, u), load_half(2 * i + 1, 1, u)], axis=0)
            ak[here, :] = kg[:, :64]
            ag[here, :] = kg[:, 64:]
            aq[here, :] = qv[:, :64]
            av[here, :] = qv[:, 64:]
            kgt = kg.T
            akt[:, here] = kgt[:64, :]
            agt[:, here] = kgt[64:, :]
            avt[:, here] = qv.T[64:, :]
            return carry

        lax.fori_loop(0, LENGTH // 128, sort_rows, 0)

    def fold(values):
        return values.reshape(values.shape[0] // 8, 8, values.shape[1])

    def query_block(qb):
        mine = slice(qb * QB, qb * QB + QB)
        tiles = [slice(i * QB, i * QB + QB) for i in range(qb + 1)]
        query = aq[mine, :]
        grads = ag[mine, :]
        top = jnp.full((8, QB), masked_score, F32)
        for i, tile in enumerate(tiles):
            score = dot_nt(ak[tile, :], query)
            if i == qb:
                row = lax.broadcasted_iota(jnp.int32, (QB, QB), 0)
                col = lax.broadcasted_iota(jnp.int32, (QB, QB), 1)
                score = jnp.where(row <= col, score, masked_score)
            sco[tile, :] = score
            top = jnp.maximum(top, jnp.max(fold(score), axis=0))
        top = jnp.max(top, axis=0, keepdims=True)
        total = jnp.zeros((8, QB), F32)
        mix = jnp.zeros((HEAD_DIM, QB), F32)
        for tile in tiles:
            weights = jnp.exp(sco[tile, :] - top)
            sco[tile, :] = weights
            total = total + jnp.sum(fold(weights), axis=0)
            mix = mix + dot(avt[:, tile], weights.astype(BF16))
        inverse = 1.0 / jnp.sum(total, axis=0, keepdims=True)
        mix = mix * inverse
        dots = jnp.sum(agt[:, mine].astype(F32) * mix, axis=0, keepdims=True)
        back = jnp.zeros((HEAD_DIM, QB), F32)
        for i, tile in enumerate(tiles):
            chances = sco[tile, :] * inverse
            slopes = dot_nt(av[tile, :], grads)
            score_grads = (chances * (slopes - dots)).astype(BF16)
            value_part = dot(chances.astype(BF16), grads)
            key_part = dot(score_grads, query)
            if qb == LENGTH // QB - 1:
                dva[tile, :] = value_part
                dka[tile, :] = key_part
            else:
                dva[tile, :] += value_part
                dka[tile, :] += key_part
            back = back + dot(akt[:, tile], score_grads)
        place(0, qb, jnp.concatenate([mix, back * SCALE], axis=0).T)

    def place(t, qb, both):
        n = QB // HALF
        table = turns[qb * n : qb * n + n].reshape(QB, 128)
        cosine = jnp.concatenate([jnp.ones((QB, 64), F32), table[:, :64]], axis=1)
        sine = jnp.concatenate([jnp.zeros((QB, 64), F32), -table[:, 64:]], axis=1)
        osrt[t, qb * n : qb * n + n] = turn(both, cosine, sine).astype(BF16).reshape(n, HALF, 128)

    def finish_half(u, half):
        for qb in (2 * half, 2 * half + 1):
            mine = slice(qb * QB, qb * QB + QB)
            place(1, qb, jnp.concatenate([dva[mine, :], dka[mine, :]], axis=1))

        def unsort(i, carry):
            for t in range(2):
                sbuf[i // 2, u, t, 2 * half + i % 2] = osrt[t, spots_ref[64 + 2 * i + half]]
            return carry

        lax.fori_loop(0, 2 * CHIPS, unsort, 0)

    def send_half(u, half):
        pltpu.make_async_copy(
            out_part(sbuf, p, u, half), out_part(rb2, p, u, half), orecv.at[p, u, half]
        ).start()
        for i in (4, 6, 2, 5, 7, 3, 1):
            out_copy(p ^ i, u, half).start()

    def out_part(buf, q, u, half):
        return buf.at[q, u, :, pl.ds(2 * half, 2)]

    def out_copy(q, u, half):
        return remote(
            out_part(sbuf, q, u, half),
            out_part(rb2, p, u, half),
            osend.at[q, u, half],
            orecv.at[p, u, half],
            member(q),
        )

    def run(*steps):
        for ch, stage in steps:
            advance(ch, stage)

    def out_rows(q, u, t, kq):
        return jnp.concatenate([rb2[q, u, t, kq], rb2[q, u, t, 2 + kq]], axis=0)

    def att_part(i, carry):
        here = lanes(i, 256)
        left = nrm[:, here]
        for slot in range(3):
            at = 8 + (slot - f + 3) % 3
            store_rows(at, i, dot_tn(left, dqkv[slot]).astype(BF16))
        store_rows(11, i, dot_tn(gal[:, here], aall[...]).astype(BF16))
        return carry

    def normed_part(b, cols):
        here = rows(b)
        total = dot_nt(upg[here, :], wup[cols, :])
        for slot in range(3):
            total = total + dot_nt(dqkv[slot, here, :], wq[slot, cols, :])
        return total

    def mixed_part(b, cols):
        here = rows(b)
        return dot(hid[here, :], wdn[:, cols]) + dot(aall[here, :], wout[:, cols])

    def reduce_copies(n):
        return (
            remote(red_s.at[n, 0], red_r.at[n, 0], dsend.at[n, 0], drecv.at[n, 0], sibling),
            remote(red_s.at[n, 1], red_r.at[n, 1], dsend.at[n, 1], drecv.at[n, 1], sibling),
            remote(red_x.at[n], red_xr.at[n], dsend.at[n, 2], drecv.at[n, 2], xpart),
        )

    parts = (normed_part, mixed_part)

    def reduce_first(n):
        copies = reduce_copies(n)
        for slot, b in ((1, dg), (0, sibb)):

            def fill(i, carry):
                red_s[n, slot, :, lanes(i, 256)] = parts[n](b, lanes(i, 256)).astype(BF16)
                return carry

            lax.fori_loop(0, 4, fill, 0)
            copies[slot].start()

    def reduce_second(n):
        copies = reduce_copies(n)
        copies[1].wait_recv()

        def fill(i, carry):
            cols = lanes(i, 256)
            red_x[n, :, cols] = (
                parts[n](xb, cols) + red_r[n, 1, :, cols].astype(F32)
            ).astype(BF16)
            return carry

        lax.fori_loop(0, 4, fill, 0)
        copies[2].start()

    def reduce_third(n):
        copies = reduce_copies(n)

        def fill(i, carry):
            cols = lanes(i, 256)
            own_acc[n, :, cols] = parts[n](own, cols)
            return carry

        lax.fori_loop(0, 4, fill, 0)
        copies[0].wait_recv()
        copies[2].wait_recv()

        def finish(i, carry):
            cols = lanes(i, 256)
            own_acc[n, :, cols] = (
                own_acc[n, :, cols]
                + red_r[n, 0, :, cols].astype(F32)
                + red_xr[n, :, cols].astype(F32)
            )
            return carry

        lax.fori_loop(0, 4, finish, 0)

    def out_pick():
        row = lax.broadcasted_iota(jnp.int32, (ROWS, ROWS), 0)
        col = lax.broadcasted_iota(jnp.int32, (ROWS, ROWS), 1)
        return (row == 2 * (col % SEQ_DEV_TOK) + col // SEQ_DEV_TOK).astype(F32).astype(BF16)

    def back_rows(i, carry):
        dgain, dshift = carry
        here = pl.ds(pl.multiple_of(i * step, step), step)
        there = pl.ds(pl.multiple_of(own * ROWS + i * step, step), step)
        values = xs[here, :].astype(F32)
        center = values - jnp.mean(values, axis=1, keepdims=True)
        spread = lax.rsqrt(jnp.mean(center * center, axis=1, keepdims=True) + EPS)
        hat = center * spread
        grads = own_acc[0, here, :]
        dgain = dgain + jnp.sum(grads * hat, axis=0, keepdims=True)
        dshift = dshift + jnp.sum(grads, axis=0, keepdims=True)
        inner = grads * gain
        inner = spread * (
            inner
            - jnp.mean(inner, axis=1, keepdims=True)
            - hat * jnp.mean(inner * hat, axis=1, keepdims=True)
        )
        xs2 = gal[there, :].astype(F32) + inner
        red_s[0, 0, here, :] = xs2.astype(BF16)
        return dgain, dshift

    def mixed_rows(i, carry):
        here = pl.ds(pl.multiple_of(i * step, step), step)
        red_s[1, 0, here, :] = (xs[here, :].astype(F32) + own_acc[1, here, :] + down_b).astype(
            BF16
        )
        return carry

    for copy in (n_sib, n_x):
        copy.start()
    for copy in (g_sib, g_x):
        copy.start()
    for load in loads:
        load.wait()
    kg_block(own, f, k)
    send_block(f, k, 0)
    n_sib.wait_recv()
    g_sib.wait_recv()
    kg_block(sibb, f, 1 - k)
    send_block(f, 1 - k, 0)
    swap_copy.wait_recv()
    qv_block(sibb, f, 1 - k)
    send_block(f, 1 - k, 1)
    feed_block(sibb)
    qv_block(own, f, k)
    send_block(f, k, 1)
    n_x.wait_recv()
    n_dg.start()
    qv_block(xb, 1 - f, k)
    send_block(1 - f, k, 1)
    n_dg.wait_recv()
    qv_block(dg, 1 - f, 1 - k)
    send_block(1 - f, 1 - k, 1)
    feed_up(xb, 0)
    feed_block(own)
    feed_up(dg, 1)
    g_x.wait_recv()
    g_dg.start()
    kg_block(xb, 1 - f, k)
    send_block(1 - f, k, 0)
    g_dg.wait_recv()
    feed_back(dg, 1)
    kg_block(dg, 1 - f, 1 - k)
    send_block(1 - f, 1 - k, 0)
    lax.fori_loop(0, 4, down_part, 0)
    run((2, 0))
    feed_back(xb, 0)
    lax.fori_loop(0, 4, up_part, 0)
    sm[...] = jnp.zeros_like(sm)
    sm[0:1, :] = jnp.sum(upg[...].astype(F32), axis=0, keepdims=True)
    sm[2:3, :] = jnp.sum(gal[...].astype(F32), axis=0, keepdims=True)
    run((6, 0), (5, 0), (2, 1), (7, 0))
    for fq, kq in ((f, k), (f, 1 - k), (1 - f, k), (1 - f, 1 - k)):
        for t in range(2):
            sent_block(fq, kq, t)
    for q in range(CHIPS):
        for t in range(2):
            for kq in range(2):
                pltpu.make_async_copy(
                    rbuf.at[2 * q + kq, t], rbuf.at[2 * q + kq, t], arecv.at[q, t, kq]
                ).wait()

    sort_unit(0)
    run((1, 0))
    query_block(3)
    query_block(2)
    finish_half(0, 1)
    send_half(0, 1)
    run((6, 1))
    query_block(1)
    query_block(0)
    finish_half(0, 0)
    send_half(0, 0)
    run((3, 0))
    sort_unit(1)
    query_block(3)
    query_block(2)
    finish_half(1, 1)
    run((7, 1), (6, 2), (0, 0))
    query_block(1)
    query_block(0)
    finish_half(1, 0)
    send_half(1, 1)
    send_half(1, 0)
    run((4, 0), (3, 1), (6, 3))
    run((1, 1), (0, 1))
    run((5, 1), (2, 2), (7, 2))
    for q in range(CHIPS):
        for u in range(SEQS):
            for half in range(2):
                arrived = out_part(rb2, q, u, half)
                pltpu.make_async_copy(arrived, arrived, orecv.at[q, u, half]).wait()

    for fq in range(2):
        for kq in range(2):
            for u in range(SEQS):
                at = (2 * fq + kq) * ROWS + u * 128
                here = slice(at, at + 128)
                for pair in range(2):
                    cols = slice(128 * pair, 128 * pair + 128)
                    x0 = out_rows(4 * pair + fq, u, 0, kq)
                    x1 = out_rows(4 * pair + 2 + fq, u, 0, kq)
                    y0 = out_rows(4 * pair + fq, u, 1, kq)
                    y1 = out_rows(4 * pair + 2 + fq, u, 1, kq)
                    aall[here, cols] = jnp.concatenate([x0[:, :64], x1[:, :64]], axis=1)
                    dqkv[0, here, cols] = jnp.concatenate([x0[:, 64:], x1[:, 64:]], axis=1)
                    dqkv[2, here, cols] = jnp.concatenate([y0[:, :64], y1[:, :64]], axis=1)
                    dqkv[1, here, cols] = jnp.concatenate([y0[:, 64:], y1[:, 64:]], axis=1)

    lax.fori_loop(0, 4, att_part, 0)
    run((9, 0), (11, 0), (4, 1), (7, 3), (10, 0), (6, 4), (5, 2), (3, 2))
    run((7, 4), (2, 3), (1, 2), (3, 3), (9, 1), (7, 5))
    reduce_first(0)
    run((2, 4), (8, 0), (5, 3), (4, 2), (3, 4), (10, 1), (1, 3))
    reduce_second(0)
    run((7, 6), (9, 2), (2, 5), (6, 5), (4, 3), (8, 1))
    run((0, 2), (5, 4), (1, 4), (10, 2), (8, 2), (9, 3), (4, 4), (3, 5))
    run((11, 1), (10, 3), (8, 3), (0, 3), (9, 4), (5, 5), (4, 5))
    reduce_first(1)
    run((3, 6), (11, 2), (10, 4), (8, 4), (1, 5), (2, 6))
    reduce_second(1)
    run((9, 5))
    reduce_third(0)
    reduce_copies(0)[0].wait_send()
    dgain, dshift = lax.fori_loop(
        0, ROWS // step, back_rows, (jnp.zeros((1, D), F32), jnp.zeros((1, D), F32))
    )
    tgrad_ref[...] = dot(out_pick(), red_s[0, 0]).astype(BF16)
    sm[3:4, :] = dgain
    sm[4:5, :] = dshift

    small_copies = [
        remote(sm, smg.at[own], smsend.at[0], smrecv.at[own], sibling),
        remote(sm, smg.at[own], smsend.at[1], smrecv.at[own], xpart),
        remote(sm, smg.at[own], smsend.at[2], smrecv.at[own], diagonal),
    ]
    for copy in small_copies:
        copy.start()

    run((0, 4), (10, 5), (11, 3), (11, 4), (4, 6), (8, 5))
    run((0, 5), (6, 6), (3, 7), (6, 7), (4, 7))
    reduce_third(1)
    reduce_copies(1)[0].wait_send()
    lax.fori_loop(0, ROWS // step, mixed_rows, 0)
    mixed_ref[...] = dot(out_pick(), red_s[1, 0]).astype(BF16)

    run((10, 6), (9, 6), (11, 5), (8, 6), (7, 7))
    run((5, 6), (1, 6), (9, 7), (10, 7), (2, 7))
    smg[own] = sm[...]
    for b in (sibb, xb, dg):
        remote(sm, smg.at[b], smsend.at[0], smrecv.at[b], sibling).wait_recv()
    for copy in small_copies:
        copy.wait_send()
    first_b = 2 * f
    sma[p, 0:1, :] = smg[first_b, 0:1, :]
    sma[p, 1:2, :] = smg[first_b + 1, 0:1, :]
    sma[p, 2:3, :] = sm[2:3, :]
    sma[p, 3:8, :] = smg[0, 3:8, :] + smg[1, 3:8, :] + smg[2, 3:8, :] + smg[3, 3:8, :]
    sm_copies = [
        remote(sma.at[p], sma.at[p], smsend.at[2 + i], smrecv.at[3 + i], member(p ^ i))
        for i in range(1, CHIPS)
    ]
    for copy in sm_copies:
        copy.start()

    run((0, 6), (1, 7), (11, 6), (8, 7), (5, 7), (0, 7), (11, 7))
    total = jnp.zeros((8, D), F32)
    for copy in sm_copies:
        copy.wait()
    for q in range(CHIPS):
        total = total + sma[q]
    small_ref[...] = total

    for copy in (vec_copy,):
        pass
    swap_copy.wait_send()
    for copy in (n_sib, n_x, g_sib, g_x, n_dg, g_dg):
        copy.wait_send()
    for u in range(SEQS):
        for i in range(1, CHIPS):
            for half in range(2):
                out_copy(p ^ i, u, half).wait_send()
    for n in range(2):
        copies = reduce_copies(n)
        copies[1].wait_send()
        copies[2].wait_send()
    for ch in range(NCH):
        settle(ch)


def widen_kernel(
    dn_h,
    up_h,
    qkv_h,
    out_h,
    small,
    mixed_in,
    tgrad_in,
    dn_o,
    up_o,
    qkv_o,
    out_o,
    mixed_o,
    tgrad_o,
    gain_o,
    shift_o,
    upb_o,
    downb_o,
    dn_b,
    up_b,
    qkv_b,
    out_b,
    dn_f,
    up_f,
    qkv_f,
    out_f,
    isem,
    osem,
):
    f = lax.axis_index("fsdp")
    sources = (up_h, dn_h, qkv_h, out_h)
    brief = (up_b, dn_b, qkv_b, out_b)
    wide = (up_f, dn_f, qkv_f, out_f)
    results = (up_o, dn_o, qkv_o, out_o)
    heights = (128, 256, 128, 128)

    def fetch(n, i):
        if n == 1:
            src = dn_h.at[pl.ds(2 * i, 2)]
        else:
            src = sources[n].at[i]
        return pltpu.make_async_copy(src, brief[n].at[i], isem.at[n, i])

    def put(n, i):
        if n == 3:
            return pltpu.make_async_copy(out_f, out_o, osem.at[3, 0])
        rows = pl.ds(i * heights[n], heights[n])
        return pltpu.make_async_copy(wide[n].at[rows], results[n].at[rows], osem.at[n, i])

    for n in range(4):
        for i in range(8):
            fetch(n, i).start()
    half = D // FSDP
    low_half = f == 0
    pick = jnp.where(low_half, small[:, :half], small[:, half:])
    gain_o[...] = pick[3]
    shift_o[...] = pick[4]
    downb_o[...] = pick[2]
    upb_o[:1024] = small[0]
    upb_o[1024:] = small[1]
    mixed_o[...] = mixed_in[...]
    tgrad_o[...] = tgrad_in[...]
    for n in range(4):
        for i in range(8):
            fetch(n, i).wait()
            values = brief[n][i].astype(F32)
            if n == 3:
                out_f[:, i * 128 : i * 128 + 128] = values.T
            else:
                wide[n][i * heights[n] : (i + 1) * heights[n], :] = values.reshape(
                    heights[n], -1
                )
                put(n, i).start()
    put(3, 0).start()
    for n in range(3):
        for i in range(8):
            put(n, i).wait()
    put(3, 0).wait()


def widen(dn, up, qkv, out_t, small, mixed, tokens_grad):
    vm = pl.BlockSpec(memory_space=pltpu.VMEM)
    hbm = pl.BlockSpec(memory_space=pl.ANY)
    half = D // FSDP
    feeds = FF // FSDP
    heads = 3 * D // FSDP
    return pl.pallas_call(
        widen_kernel,
        out_shape=(
            jax.ShapeDtypeStruct((feeds, D), F32),
            jax.ShapeDtypeStruct((D, feeds), F32),
            jax.ShapeDtypeStruct((D, heads), F32),
            jax.ShapeDtypeStruct((half, D), F32),
            jax.ShapeDtypeStruct((ROWS, D), BF16),
            jax.ShapeDtypeStruct((ROWS, D), BF16),
            jax.ShapeDtypeStruct((half,), F32),
            jax.ShapeDtypeStruct((half,), F32),
            jax.ShapeDtypeStruct((feeds,), F32),
            jax.ShapeDtypeStruct((half,), F32),
        ),
        in_specs=[hbm] * 4 + [vm] * 3,
        out_specs=(hbm,) * 4 + (vm,) * 6,
        scratch_shapes=[
            pltpu.VMEM((8, 2, 128, D), BF16),
            pltpu.VMEM((8, 128, feeds), BF16),
            pltpu.VMEM((8, 128, heads), BF16),
            pltpu.VMEM((8, 128, half), BF16),
            pltpu.VMEM((feeds, D), F32),
            pltpu.VMEM((D, feeds), F32),
            pltpu.VMEM((D, heads), F32),
            pltpu.VMEM((half, D), F32),
            pltpu.SemaphoreType.DMA((4, 8)),
            pltpu.SemaphoreType.DMA((4, 8)),
        ],
        compiler_params=pltpu.CompilerParams(vmem_limit_bytes=56 * 2**20),
    )(
        dn.reshape(16, 128, D),
        up.reshape(8, 128, feeds),
        qkv.reshape(8, 128, heads),
        out_t.reshape(8, 128, half),
        small,
        mixed,
        tokens_grad,
    )


def turn_table():
    lane = np.arange(HEAD_DIM)
    speeds = (10000.0 ** (-(lane // 2 * 2) / ROT_DIM)).astype(np.float32)
    phase = np.arange(LENGTH, dtype=np.float32)[:, None] * speeds[None, :]
    turning = (lane < ROT_DIM)[None, :]
    sign = np.where(lane % 2 == 0, -1.0, 1.0)[None, :]
    cosine = np.where(turning, np.cos(phase), 1.0)
    sine = np.where(turning, np.sin(phase) * sign, 0.0)
    table = np.concatenate((cosine, sine), axis=1).astype(np.float32)
    return table.reshape(4 * CHIPS, HALF, 2 * HEAD_DIM)


def fused_device(
    tokens,
    block_pairs,
    norm_gain,
    norm_bias,
    qkv_weight,
    out_weight,
    up_weight,
    up_bias,
    down_weight,
    down_bias,
    cotangent,
):
    vm = pl.BlockSpec(memory_space=pltpu.VMEM)
    sme = pl.BlockSpec(memory_space=pltpu.SMEM)
    hbm = pl.BlockSpec(memory_space=pl.ANY)
    dma = pltpu.SemaphoreType.DMA
    scratch = [
        pltpu.SMEM((96,), jnp.int32),
        pltpu.VMEM((4 * CHIPS, HALF, 128), F32),
        pltpu.VMEM((2, 8, 512), F32),
        pltpu.VMEM((ROWS, D), BF16),
        pltpu.VMEM((ALL, D), BF16),
        pltpu.VMEM((ALL, D), BF16),
        pltpu.VMEM((3, D, 256), BF16),
        pltpu.VMEM((256, D), BF16),
        pltpu.VMEM((D, 1024), BF16),
        pltpu.VMEM((1024, D), BF16),
        pltpu.VMEM((ALL, 1024), BF16),
        pltpu.VMEM((ALL, 1024), BF16),
        pltpu.VMEM((CHIPS, 2, 2, 4, HALF, 128), BF16),
        pltpu.VMEM((2 * CHIPS, 2, 4, HALF, 128), BF16),
        pltpu.VMEM((LENGTH, HEAD_DIM), BF16),
        pltpu.VMEM((LENGTH, HEAD_DIM), BF16),
        pltpu.VMEM((LENGTH, HEAD_DIM), BF16),
        pltpu.VMEM((LENGTH, HEAD_DIM), BF16),
        pltpu.VMEM((HEAD_DIM, LENGTH), BF16),
        pltpu.VMEM((HEAD_DIM, LENGTH), BF16),
        pltpu.VMEM((HEAD_DIM, LENGTH), BF16),
        pltpu.VMEM((LENGTH, QB), F32),
        pltpu.VMEM((LENGTH, HEAD_DIM), F32),
        pltpu.VMEM((LENGTH, HEAD_DIM), F32),
        pltpu.VMEM((2, 4 * CHIPS, HALF, 128), BF16),
        pltpu.VMEM((CHIPS, SEQS, 2, 4, HALF, 128), BF16),
        pltpu.VMEM((ALL, 256), BF16),
        pltpu.VMEM((3, ALL, 256), BF16),
        pltpu.VMEM((NCH, 2, 2, 2, 128, 256), BF16),
        pltpu.VMEM((NCH, 2, 2, 128, 256), BF16),
        pltpu.VMEM((NCH, 2, 128, 256), BF16),
        pltpu.VMEM((NCH, 128, 256), BF16),
        pltpu.VMEM((2, 128, 256), BF16),
        pltpu.VMEM((max(len(MIDDLE), 1), 2, 2, 128, 256), BF16),
        pltpu.VMEM((2, ROWS, D), F32),
        pltpu.VMEM((2, 2, ROWS, D), BF16),
        pltpu.VMEM((2, ROWS, D), BF16),
        pltpu.VMEM((2, 2, ROWS, D), BF16),
        pltpu.VMEM((2, ROWS, D), BF16),
        pltpu.VMEM((8, D), F32),
        pltpu.VMEM((4, 8, D), F32),
        pltpu.VMEM((CHIPS, 8, D), F32),
        dma((6,)),
        dma((9,)),
        dma((9,)),
        dma((CHIPS, 2, 2)),
        dma((CHIPS, 2, 2)),
        dma((CHIPS, SEQS, 2)),
        dma((CHIPS, SEQS, 2)),
        dma((NCH, 3)),
        dma((NCH, 3)),
        dma((NCH, 3)),
        dma((NCH, 3)),
        dma((NCH,)),
        dma((NCH,)),
        dma((NCH,)),
        dma((2, 3)),
        dma((2, 3)),
        dma((10,)),
        dma((11,)),
    ]
    mixed, tokens_grad, small, dn, up, qkv, out_t = pl.pallas_call(
        fused_kernel,
        out_shape=(
            jax.ShapeDtypeStruct((ROWS, D), BF16),
            jax.ShapeDtypeStruct((ROWS, D), BF16),
            jax.ShapeDtypeStruct((8, D), F32),
            jax.ShapeDtypeStruct((2, 2, 2, 2, 128, D), BF16),
            jax.ShapeDtypeStruct((2, 2, 2, 128, FF // FSDP), BF16),
            jax.ShapeDtypeStruct((2, 2, 2, 128, 3 * D // FSDP), BF16),
            jax.ShapeDtypeStruct((2, 2, 2, 128, D // FSDP), BF16),
        ),
        in_specs=[sme] + [vm] * 4 + [hbm, vm, vm] + [hbm] * 4,
        out_specs=(vm, vm, vm, hbm, hbm, hbm, hbm),
        scratch_shapes=scratch,
        compiler_params=pltpu.CompilerParams(
            collective_id=0, has_side_effects=True, vmem_limit_bytes=63 * 2**20
        ),
    )(
        block_pairs,
        norm_gain,
        norm_bias,
        down_bias,
        up_bias,
        jnp.asarray(turn_table()),
        tokens,
        cotangent,
        qkv_weight,
        out_weight,
        up_weight,
        down_weight,
    )
    dn, up, qkv, out, mixed, tokens_grad, gain, shift, upb, downb = widen(
        dn, up, qkv, out_t, small, mixed, tokens_grad
    )
    return mixed, tokens_grad, gain, shift, qkv, out, up, upb, dn, downb


def solution(mesh):
    in_specs = (
        P(("fsdp", "ctx"), None),
        P(),
        P("fsdp"),
        P("fsdp"),
        P(None, "fsdp"),
        P("fsdp", None),
        P(None, "fsdp"),
        P("fsdp"),
        P("fsdp", None),
        P("fsdp"),
        P(("fsdp", "ctx"), None),
    )
    out_specs = (
        P(("fsdp", "ctx"), None),
        P(("fsdp", "ctx"), None),
        P("fsdp"),
        P("fsdp"),
        P(None, "fsdp"),
        P("fsdp", None),
        P(None, "fsdp"),
        P("fsdp"),
        P("fsdp", None),
        P("fsdp"),
    )
    plan = fused_device if fits(mesh) else per_device
    return jax.shard_map(
        plan, mesh=mesh, in_specs=in_specs, out_specs=out_specs, check_vma=False
    )
```

```python
import functools
import math

import jax
import jax.numpy as jnp
import numpy as np
from jax import lax
from jax.experimental import pallas as pl
from jax.experimental.pallas import tpu as pltpu
from jax.sharding import PartitionSpec as P

D = 1024
HEAD_DIM = 64
ROT_DIM = 32
HEADS = 16
SEQ_DEV_TOK = 128
SEQS = 2


EPS = 1e-05
HIGHEST = lax.Precision.HIGHEST
masked_score = -1e30


def layer_norm(values, gain_values, shift_values):
    center = values - jnp.mean(values, axis=-1, keepdims=True)
    spread = jnp.mean(center * center, axis=-1, keepdims=True)
    return center * lax.rsqrt(spread + EPS) * gain_values + shift_values


def rotary_tables(places, window):
    lanes = jnp.arange(window, dtype=jnp.int32)
    within_head = lanes % HEAD_DIM
    turning = within_head < ROT_DIM
    steps_up = (within_head // 2 * 2).astype(jnp.float32)
    speeds = 10000.0 ** (-steps_up / ROT_DIM)
    phase = places.astype(jnp.float32)[:, None] * speeds[None, :]
    cos_full = jnp.where(turning[None, :], jnp.cos(phase), 1.0)
    sin_full = jnp.where(turning[None, :], jnp.sin(phase), 0.0)
    row_lane = lanes[:, None]
    col_lane = lanes[None, :]
    same_head = row_lane // HEAD_DIM == col_lane // HEAD_DIM
    col_within = col_lane % HEAD_DIM
    col_turns = same_head & (col_within < ROT_DIM)
    even_col = col_within % 2 == 0
    minus_part = jnp.where(col_turns & even_col & (row_lane == col_lane + 1), -1.0, 0.0)
    plus_part = jnp.where(
        col_turns & jnp.logical_not(even_col) & (row_lane == col_lane - 1), 1.0, 0.0
    )
    swap_table = (minus_part + plus_part).astype(jnp.float32)
    return (cos_full, sin_full, swap_table)


def smooth_gate(values):
    return jax.nn.gelu(values, approximate=True)


def positions(first_row, row_count, pair_table, devices, seq_rows):
    indices = first_row + jnp.arange(row_count, dtype=jnp.int32)
    owners = indices // seq_rows
    within = indices % seq_rows
    half_rows = seq_rows // 2
    matches = owners[:, None] == jnp.arange(devices, dtype=jnp.int32)[None, :]
    chosen = jnp.sum(jnp.where(matches, pair_table[None, :], 0), axis=1)
    block_index = jnp.where(within < half_rows, chosen, 2 * devices - 1 - chosen)
    return block_index * half_rows + within % half_rows


def in_groups(row_count, seq_rows):
    group_rows = math.gcd(row_count // seq_rows, 8) * seq_rows
    return (group_rows, row_count // group_rows)


def split_groups(array, group_rows, turns):
    return array.reshape((turns, group_rows) + array.shape[1:])


def grad_scores(
    query_rows,
    out_grads,
    log_sums,
    row_dots,
    query_places,
    key_rows,
    value_rows,
    key_places,
    factor,
):
    scores = (
        jnp.einsum("qshe,kshe->shqk", query_rows, key_rows, preferred_element_type=jnp.float32)
        * factor
    )
    allowed = key_places[None, :] <= query_places[:, None]
    chances = jnp.exp(jnp.where(allowed, scores - log_sums[..., None], masked_score))
    prob_grads = jnp.einsum(
        "qshe,kshe->shqk", out_grads, value_rows, preferred_element_type=jnp.float32
    )
    return (chances, (chances * (prob_grads - row_dots[..., None])).astype(jnp.bfloat16))


def per_device(
    tokens,
    block_pairs,
    norm_gain,
    norm_bias,
    qkv_weight,
    out_weight,
    up_weight,
    up_bias,
    down_weight,
    down_bias,
    cotangent,
):
    devices = lax.axis_size("ctx")
    own_index = lax.axis_index("ctx")
    seq_rows = SEQ_DEV_TOK
    seq_count = SEQS
    heads = HEADS
    head_size = HEAD_DIM
    width = D
    factor = HEAD_DIM ** (-0.5)
    all_rows = seq_rows * seq_count
    window = math.gcd(width, 128)
    gathered = (
        lax.all_gather(norm_gain, "fsdp", axis=0, tiled=True),
        lax.all_gather(norm_bias, "fsdp", axis=0, tiled=True),
        lax.all_gather(qkv_weight, "fsdp", axis=1, tiled=True),
        lax.all_gather(out_weight, "fsdp", axis=0, tiled=True),
        lax.all_gather(up_weight, "fsdp", axis=1, tiled=True),
        lax.all_gather(up_bias, "fsdp", axis=0, tiled=True),
        lax.all_gather(down_weight, "fsdp", axis=0, tiled=True),
        lax.all_gather(down_bias, "fsdp", axis=0, tiled=True),
    )
    gain_low, shift_low, w_qkv, w_out, w_up, b_up, w_down, b_down = gathered
    inputs = tokens.astype(jnp.float32)
    gain_values = gain_low.astype(jnp.float32)
    shift_values = shift_low.astype(jnp.float32)
    normed_low = layer_norm(inputs, gain_values, shift_values).astype(jnp.bfloat16)
    mixed_qkv = jnp.dot(normed_low, w_qkv, preferred_element_type=jnp.float32).reshape(
        seq_rows, seq_count, 3 * width
    )
    own_places = positions(own_index * seq_rows, seq_rows, block_pairs, devices, seq_rows)
    cos_full, sin_full, swap_table = rotary_tables(own_places, window)

    def turn_both(values):
        shaped = values.reshape(seq_rows, seq_count, 2 * width // window, window)
        swapped = jnp.einsum("rsgw,wv->rsgv", shaped, swap_table, precision=HIGHEST)
        turned_rows = shaped * cos_full[:, None, None, :] + swapped * sin_full[:, None, None, :]
        return turned_rows.reshape(seq_rows, seq_count, 2 * width)

    query_key = mixed_qkv[:, :, : 2 * width]
    turned = turn_both(query_key)
    queries = (
        turned[:, :, :width].astype(jnp.bfloat16).reshape(seq_rows, seq_count, heads, head_size)
    )
    key_rows = (
        turned[:, :, width:].astype(jnp.bfloat16).reshape(seq_rows, seq_count, heads, head_size)
    )
    value_rows = (
        mixed_qkv[:, :, 2 * width :]
        .astype(jnp.bfloat16)
        .reshape(seq_rows, seq_count, heads, head_size)
    )
    start_state = (
        jnp.full((seq_count, heads, seq_rows), masked_score, jnp.float32),
        jnp.zeros((seq_count, heads, seq_rows), jnp.float32),
        jnp.zeros((seq_count, heads, seq_rows, head_size), jnp.float32),
    )
    piece_keys = lax.all_gather(key_rows, "ctx", axis=0, tiled=True)
    piece_values = lax.all_gather(value_rows, "ctx", axis=0, tiled=True)
    group_rows, turns = in_groups(piece_keys.shape[0], seq_rows)

    def attend_step(inner, item):
        block_keys, block_values, turn = item
        key_places = positions(turn * group_rows, group_rows, block_pairs, devices, seq_rows)
        scores = (
            jnp.einsum("qshe,kshe->shqk", queries, block_keys, preferred_element_type=jnp.float32)
            * factor
        )
        allowed = key_places[None, :] <= own_places[:, None]
        running, totals, accum = inner
        fresh = jnp.maximum(running, jnp.max(jnp.where(allowed, scores, masked_score), axis=-1))
        weights = jnp.exp(jnp.where(allowed, scores - fresh[..., None], masked_score))
        fading = jnp.exp(running - fresh)
        totals = totals * fading + jnp.sum(weights, axis=-1)
        accum = accum * fading[..., None] + jnp.einsum(
            "shqk,kshe->shqe",
            weights.astype(jnp.bfloat16),
            block_values,
            preferred_element_type=jnp.float32,
        )
        return ((fresh, totals, accum), None)

    inner, _ = lax.scan(
        attend_step,
        start_state,
        (
            split_groups(piece_keys, group_rows, turns),
            split_groups(piece_values, group_rows, turns),
            jnp.arange(turns, dtype=jnp.int32),
        ),
    )
    running, totals, accum = inner
    log_sums = running + jnp.log(totals)
    attended = jnp.transpose(accum / totals[..., None], (2, 0, 1, 3))
    attn_low = attended.reshape(all_rows, width).astype(jnp.bfloat16)
    attention = jnp.dot(attn_low, w_out, preferred_element_type=jnp.float32)
    up_pre = jnp.dot(normed_low, w_up, preferred_element_type=jnp.float32) + b_up.astype(
        jnp.float32
    )
    hidden_low = smooth_gate(up_pre).astype(jnp.bfloat16)
    result = (
        inputs
        + attention
        + jnp.dot(hidden_low, w_down, preferred_element_type=jnp.float32)
        + b_down.astype(jnp.float32)
    )
    mixed = result.astype(jnp.bfloat16)
    again = (
        lax.all_gather(norm_gain, "fsdp", axis=0, tiled=True),
        lax.all_gather(norm_bias, "fsdp", axis=0, tiled=True),
        lax.all_gather(qkv_weight, "fsdp", axis=1, tiled=True),
        lax.all_gather(out_weight, "fsdp", axis=0, tiled=True),
        lax.all_gather(up_weight, "fsdp", axis=1, tiled=True),
        lax.all_gather(up_bias, "fsdp", axis=0, tiled=True),
        lax.all_gather(down_weight, "fsdp", axis=0, tiled=True),
        lax.all_gather(down_bias, "fsdp", axis=0, tiled=True),
    )
    gain_low, shift_low, w_qkv, w_out, w_up, b_up, w_down, b_down = again
    out_grad = cotangent.astype(jnp.float32)
    attn_grads = (
        jnp.einsum("td,ed->te", cotangent, w_out, preferred_element_type=jnp.float32)
        .astype(jnp.bfloat16)
        .reshape(seq_rows, seq_count, heads, head_size)
    )
    dots_rows = jnp.sum(attn_grads.astype(jnp.float32) * attended, axis=-1)
    row_dots = jnp.transpose(dots_rows, (1, 2, 0))
    empty_rows = jnp.zeros((seq_rows, seq_count, heads, head_size), jnp.float32)
    whole_keys, whole_values = (
        lax.all_gather(key_rows, "ctx", axis=0, tiled=True),
        lax.all_gather(value_rows, "ctx", axis=0, tiled=True),
    )
    piece_keys = whole_keys
    piece_values = whole_values
    query_group_rows, turns = in_groups(piece_keys.shape[0], seq_rows)

    def query_step(inner, item):
        block_keys, block_values, turn = item
        key_places = positions(
            0 + turn * query_group_rows, query_group_rows, block_pairs, devices, seq_rows
        )
        chances, score_grads = grad_scores(
            queries,
            attn_grads,
            log_sums,
            row_dots,
            own_places,
            block_keys,
            block_values,
            key_places,
            factor,
        )
        return (
            inner
            + jnp.einsum(
                "shqk,kshe->qshe", score_grads, block_keys, preferred_element_type=jnp.float32
            )
            * factor,
            None,
        )

    inner, _ = lax.scan(
        query_step,
        empty_rows,
        (
            split_groups(piece_keys, query_group_rows, turns),
            split_groups(piece_values, query_group_rows, turns),
            jnp.arange(turns, dtype=jnp.int32),
        ),
    )
    query_grad = inner
    piece_keys = whole_keys
    piece_values = whole_values
    key_group_rows, turns = in_groups(seq_rows * lax.axis_size("ctx"), seq_rows)

    def key_step(inner, item):
        block_keys, block_values, turn = item
        key_places = positions(
            turn * key_group_rows, key_group_rows, block_pairs, devices, seq_rows
        )
        chances, score_grads = grad_scores(
            queries,
            attn_grads,
            log_sums,
            row_dots,
            own_places,
            block_keys,
            block_values,
            key_places,
            factor,
        )
        key_part = (
            jnp.einsum("shqk,qshe->kshe", score_grads, queries, preferred_element_type=jnp.float32)
            * factor
        )
        value_part = jnp.einsum(
            "shqk,qshe->kshe",
            chances.astype(jnp.bfloat16),
            attn_grads,
            preferred_element_type=jnp.float32,
        )
        stacked = jnp.stack(
            (
                key_part.reshape(key_group_rows, seq_count, width),
                value_part.reshape(key_group_rows, seq_count, width),
            ),
            axis=2,
        )
        return (inner, stacked)

    _, blocks_out = lax.scan(
        key_step,
        jnp.zeros((), jnp.float32),
        (
            split_groups(piece_keys, key_group_rows, turns),
            split_groups(piece_values, key_group_rows, turns),
            jnp.arange(turns, dtype=jnp.int32),
        ),
    )
    summed_terms = lax.psum_scatter(
        blocks_out.reshape(seq_rows * lax.axis_size("ctx"), seq_count, 2, width),
        "ctx",
        scatter_dimension=0,
        tiled=True,
    )
    key_grad = summed_terms[:, :, 0].reshape(seq_rows, seq_count, heads, head_size)
    value_grad = summed_terms[:, :, 1].reshape(seq_rows, seq_count, heads, head_size)
    _, turn_back = jax.vjp(turn_both, query_key)
    both_grads = jnp.concatenate(
        (
            query_grad.reshape(seq_rows, seq_count, width),
            key_grad.reshape(seq_rows, seq_count, width),
        ),
        axis=2,
    )
    (pre_grads,) = turn_back(both_grads)
    qkv_grad = (
        jnp.concatenate((pre_grads, value_grad.reshape(seq_rows, seq_count, width)), axis=2)
        .reshape(all_rows, 3 * width)
        .astype(jnp.bfloat16)
    )
    hidden_grad = jnp.einsum("td,fd->tf", cotangent, w_down, preferred_element_type=jnp.float32)
    _, gate_back = jax.vjp(smooth_gate, up_pre)
    (up_grad,) = gate_back(hidden_grad)
    up_low = up_grad.astype(jnp.bfloat16)
    normed_grad = jnp.einsum(
        "tc,dc->td", qkv_grad, w_qkv, preferred_element_type=jnp.float32
    ) + jnp.einsum("tf,df->td", up_low, w_up, preferred_element_type=jnp.float32)
    _, norm_back = jax.vjp(
        layer_norm, inputs, gain_low.astype(jnp.float32), shift_low.astype(jnp.float32)
    )
    input_part, gain_grad, shift_grad = norm_back(normed_grad)
    tokens_grad = (out_grad + input_part).astype(jnp.bfloat16)
    qkv_wgrad = jnp.einsum("td,tc->dc", normed_low, qkv_grad, preferred_element_type=jnp.float32)
    out_wgrad = jnp.einsum("td,te->de", attn_low, cotangent, preferred_element_type=jnp.float32)
    up_wgrad = jnp.einsum("td,tf->df", normed_low, up_low, preferred_element_type=jnp.float32)
    up_bgrad = jnp.sum(up_low.astype(jnp.float32), axis=0)
    down_wgrad = jnp.einsum("tf,td->fd", hidden_low, cotangent, preferred_element_type=jnp.float32)
    down_bgrad = jnp.sum(out_grad, axis=0)
    shares = (
        lax.psum_scatter(
            gain_grad.astype(jnp.bfloat16), "fsdp", scatter_dimension=0, tiled=True
        ).astype(jnp.float32),
        lax.psum_scatter(
            shift_grad.astype(jnp.bfloat16), "fsdp", scatter_dimension=0, tiled=True
        ).astype(jnp.float32),
        lax.psum_scatter(
            qkv_wgrad.astype(jnp.bfloat16), "fsdp", scatter_dimension=1, tiled=True
        ).astype(jnp.float32),
        lax.psum_scatter(
            out_wgrad.astype(jnp.bfloat16), "fsdp", scatter_dimension=0, tiled=True
        ).astype(jnp.float32),
        lax.psum_scatter(
            up_wgrad.astype(jnp.bfloat16), "fsdp", scatter_dimension=1, tiled=True
        ).astype(jnp.float32),
        lax.psum_scatter(
            up_bgrad.astype(jnp.bfloat16), "fsdp", scatter_dimension=0, tiled=True
        ).astype(jnp.float32),
        lax.psum_scatter(
            down_wgrad.astype(jnp.bfloat16), "fsdp", scatter_dimension=0, tiled=True
        ).astype(jnp.float32),
        lax.psum_scatter(
            down_bgrad.astype(jnp.bfloat16), "fsdp", scatter_dimension=0, tiled=True
        ).astype(jnp.float32),
    )
    share_gain, share_shift, share_qkv, share_out, share_up, share_upb, share_down, share_downb = (
        shares
    )
    totals_out = lax.psum(
        (
            share_gain,
            share_shift,
            share_qkv,
            share_out,
            share_up,
            share_upb,
            share_down,
            share_downb,
        ),
        "ctx",
    )
    sum_gain, sum_shift, sum_qkv, sum_out, sum_up, sum_upb, sum_down, sum_downb = totals_out
    return (
        mixed,
        tokens_grad,
        sum_gain,
        sum_shift,
        sum_qkv,
        sum_out,
        sum_up,
        sum_upb,
        sum_down,
        sum_downb,
    )


F32 = jnp.float32
BF16 = jnp.bfloat16
FF = 4096
FSDP = 2
CHIPS = 8
ROWS = SEQ_DEV_TOK * SEQS
ALL = 4 * ROWS
LENGTH = CHIPS * 2 * SEQ_DEV_TOK
HALF = SEQ_DEV_TOK // 2
QB = 512
NCH = 12
MASKS = (1, 2, 4)
SCATTER = {4: (1, 0, 2), 5: (2, 0, 1), 7: (1, 0, 2)}
GATHER = {2: (2, 0, 1), 3: (2, 0, 1), 4: (2, 0, 1), 8: (2, 0, 1)}
MIDDLE = {0: (2, 1, 0), 6: (2, 1, 0), 9: (2, 1, 0), 10: (2, 1, 0), 11: (2, 1, 0)}
SCALE = HEAD_DIM**-0.5


def fits(mesh):
    return mesh.shape["fsdp"] == FSDP and mesh.shape["ctx"] == 2 * CHIPS


def dot(left, right):
    return lax.dot_general(left, right, (((1,), (0,)), ((), ())), preferred_element_type=F32)


def dot_nt(left, right):
    return lax.dot_general(left, right, (((1,), (1,)), ((), ())), preferred_element_type=F32)


def dot_tn(left, right):
    return lax.dot_general(left, right, (((0,), (0,)), ((), ())), preferred_element_type=F32)


def turn(values, cosine, sine):
    lane = lax.broadcasted_iota(jnp.int32, values.shape, 1)
    width = values.shape[1]
    other = jnp.where(
        lane % 2 == 0, pltpu.roll(values, width - 1, 1), pltpu.roll(values, 1, 1)
    )
    return values * cosine + other * sine


def gate(values):
    inner = 0.7978845608028654 * (values + 0.044715 * values * values * values)
    th = jnp.tanh(inner)
    half = 0.5 * (1.0 + th)
    slope = half + (0.5 * values) * (1.0 - th * th) * (
        0.7978845608028654 * (1.0 + 3 * 0.044715 * values * values)
    )
    return values * half, slope


def fused_kernel(
    pairs_ref,
    gain_ref,
    shift_ref,
    downb_ref,
    upb_ref,
    turns_h,
    tok_ref,
    cot_ref,
    wqkv_h,
    wout_h,
    wup_h,
    wdn_h,
    mixed_ref,
    tgrad_ref,
    small_ref,
    odn,
    oup,
    oqkv,
    oout,
    spots_ref,
    turns,
    vall,
    xs,
    nrm,
    gal,
    wq,
    wout,
    wup,
    wdn,
    hid,
    upg,
    sbuf,
    rbuf,
    aq,
    ag,
    ak,
    av,
    akt,
    avt,
    agt,
    sco,
    dka,
    dva,
    osrt,
    rb2,
    aall,
    dqkv,
    mats,
    rs0,
    rs1,
    rs2,
    xsw,
    rsm,
    own_acc,
    red_s,
    red_x,
    red_r,
    red_xr,
    sm,
    smg,
    sma,
    lsem,
    gsend,
    grecv,
    asend,
    arecv,
    osend,
    orecv,
    rssend,
    rsrecv,
    agsend,
    agrecv,
    clocal,
    csend,
    crecv,
    dsend,
    drecv,
    smsend,
    smrecv,
):
    f = lax.axis_index("fsdp")
    c = lax.axis_index("ctx")
    k = c % 2
    p = c // 2
    zz = p // 2
    yy = p % 2
    xpart = (1 - f, c)
    sibling = (f, 2 * p + 1 - k)
    diagonal = (1 - f, 2 * p + 1 - k)
    own = 2 * f + k
    sibb = 2 * f + 1 - k
    xb = 2 * (1 - f) + k
    dg = 2 * (1 - f) + 1 - k
    MESH = pl.DeviceIdType.MESH

    def member(q):
        return (f, 2 * q + k)

    def remote(src, dst, ssem, rsem, device):
        return pltpu.make_async_remote_copy(
            src_ref=src,
            dst_ref=dst,
            send_sem=ssem,
            recv_sem=rsem,
            device_id=device,
            device_id_type=MESH,
        )

    def rows(b):
        return pl.ds(pl.multiple_of(b * ROWS, ROWS), ROWS)

    def lanes(i, n):
        return pl.ds(pl.multiple_of(i * n, n), n)

    loads = [
        pltpu.make_async_copy(wqkv_h.at[:, lanes(k, 256)], wq.at[f], lsem.at[0]),
        pltpu.make_async_copy(
            wqkv_h.at[:, pl.ds(pl.multiple_of(1024 + 256 * k, 256), 256)], wq.at[1 + f], lsem.at[1]
        ),
        pltpu.make_async_copy(wup_h.at[:, lanes(k, 1024)], wup, lsem.at[2]),
        pltpu.make_async_copy(wdn_h.at[lanes(k, 1024), :], wdn, lsem.at[3]),
        pltpu.make_async_copy(wout_h.at[lanes(k, 256), :], wout, lsem.at[4]),
        pltpu.make_async_copy(turns_h, turns, lsem.at[5]),
    ]
    for load in loads:
        load.start()
    barrier = pltpu.get_barrier_semaphore()
    for device in [xpart, sibling, diagonal] + [member(p ^ i) for i in range(1, CHIPS)]:
        pl.semaphore_signal(barrier, inc=1, device_id=device, device_id_type=MESH)
    pl.semaphore_wait(barrier, 3 + CHIPS - 1)

    def row_of(ref, at):
        return ref[pl.ds(at, 512)].astype(F32).reshape(1, 512)

    vall[f] = jnp.concatenate(
        [row_of(gain_ref, 0), row_of(shift_ref, 0), row_of(downb_ref, 0)]
        + [row_of(upb_ref, 512 * i) for i in range(4)]
        + [jnp.zeros((1, 512), F32)],
        axis=0,
    )
    vec_copy = remote(vall.at[f], vall.at[f], gsend.at[0], grecv.at[0], xpart)
    vec_copy.start()
    swap_copy = remote(
        wqkv_h.at[:, pl.ds(pl.multiple_of(512 + 256 * k, 256), 256)],
        wq.at[2 * f],
        gsend.at[1],
        grecv.at[1],
        xpart,
    )
    swap_copy.start()

    def table_pair(i, carry):
        spots_ref[64 + 2 * i] = pairs_ref[i]
        spots_ref[64 + 2 * i + 1] = 4 * CHIPS - 1 - pairs_ref[i]
        return carry

    lax.fori_loop(0, 2 * CHIPS, table_pair, 0)
    step = 64

    def norm_rows(i, carry):
        here = pl.ds(pl.multiple_of(i * step, step), step)
        there = pl.ds(pl.multiple_of(own * ROWS + i * step, step), step)
        row = lax.broadcasted_iota(jnp.int32, (step, ROWS), 0) + i * step
        col = lax.broadcasted_iota(jnp.int32, (step, ROWS), 1)
        pick = (col == 2 * (row % SEQ_DEV_TOK) + row // SEQ_DEV_TOK).astype(F32).astype(BF16)
        values = dot(pick, tok_ref[...])
        gal[there, :] = dot(pick, cot_ref[...]).astype(BF16)
        xs[here, :] = values.astype(BF16)
        center = values - jnp.mean(values, axis=1, keepdims=True)
        spread = jnp.mean(center * center, axis=1, keepdims=True)
        own_acc[0, here, :] = center * lax.rsqrt(spread + EPS)
        return carry

    lax.fori_loop(0, ROWS // step, norm_rows, 0)
    vec_copy.wait()
    gain = jnp.concatenate([vall[0, 0:1, :], vall[1, 0:1, :]], axis=1).astype(F32)
    shift = jnp.concatenate([vall[0, 1:2, :], vall[1, 1:2, :]], axis=1).astype(F32)
    down_b = jnp.concatenate([vall[0, 2:3, :], vall[1, 2:3, :]], axis=1).astype(F32)


    def scale_rows(i, carry):
        here = pl.ds(pl.multiple_of(i * step, step), step)
        there = pl.ds(pl.multiple_of(own * ROWS + i * step, step), step)
        nrm[there, :] = (own_acc[0, here, :] * gain + shift).astype(BF16)
        return carry

    lax.fori_loop(0, ROWS // step, scale_rows, 0)

    def spread_copy(buf, b, n, device):
        return remote(buf.at[rows(b)], buf.at[rows(b)], gsend.at[n], grecv.at[n], device)

    n_sib = spread_copy(nrm, own, 2, sibling)
    n_x = spread_copy(nrm, own, 3, xpart)
    g_sib = spread_copy(gal, own, 4, sibling)
    g_x = spread_copy(gal, own, 5, xpart)
    n_dg = spread_copy(nrm, xb, 6, sibling)
    g_dg = spread_copy(gal, xb, 7, sibling)

    def up_part_of(b, i):
        at = k * 1024 + i * 256
        bias = vall[f, pl.ds(3 + at // 512, 1), pl.ds(pl.multiple_of(at % 512, 256), 256)]
        return gate(dot(nrm[rows(b), :], wup[:, lanes(i, 256)]) + bias)

    def feed_block(b):
        def part(i, carry):
            cols = lanes(i, 256)
            value, slope = up_part_of(b, i)
            hid[rows(b), cols] = value.astype(BF16)
            back = dot_nt(gal[rows(b), :], wdn[cols, :])
            upg[rows(b), cols] = (back * slope).astype(BF16)
            return carry

        lax.fori_loop(0, 4, part, 0)

    def feed_up(b, n):
        def part(i, carry):
            cols = lanes(i, 256)
            value, slope = up_part_of(b, i)
            hid[rows(b), cols] = value.astype(BF16)
            own_acc[n, :, cols] = slope
            return carry

        lax.fori_loop(0, 4, part, 0)

    def feed_back(b, n):
        def part(i, carry):
            cols = lanes(i, 256)
            back = dot_nt(gal[rows(b), :], wdn[cols, :])
            upg[rows(b), cols] = (back * own_acc[n, :, cols]).astype(BF16)
            return carry

        lax.fori_loop(0, 4, part, 0)

    def put_heads(first, second, fq, kq, t):
        for h in range(4):
            sbuf[2 * h + fq, t, kq] = jnp.concatenate(
                [first[:, 64 * h : 64 * h + 64], second[:, 64 * h : 64 * h + 64]], axis=1
            ).reshape(4, HALF, 128)

    def turned(values, kq):
        table = jnp.concatenate(
            [turns[spots_ref[64 + 2 * (2 * p + kq) + half]] for half in range(2)], axis=0
        )
        cosine = jnp.concatenate([table[:, :64], table[:, :64]], axis=1)
        sine = jnp.concatenate([table[:, 64:], table[:, 64:]], axis=1)
        parts = []
        for s in range(SEQS):
            line = []
            for half in range(2):
                piece = values[128 * s : 128 * s + 128, 128 * half : 128 * half + 128]
                line.append(turn(piece, cosine, sine))
            parts.append(jnp.concatenate(line, axis=1))
        return jnp.concatenate(parts, axis=0).astype(BF16)

    def kg_block(b, fq, kq):
        key = dot(nrm[rows(b), :], wq[1])
        grads = dot_nt(gal[rows(b), :], wout[...]).astype(BF16)
        put_heads(turned(key, kq), grads, fq, kq, 0)

    def qv_block(b, fq, kq):
        query = dot(nrm[rows(b), :], wq[0])
        value = dot(nrm[rows(b), :], wq[2]).astype(BF16)
        put_heads(turned(query, kq) * BF16(SCALE), value, fq, kq, 1)

    def in_copy(q, t, kq):
        return remote(
            sbuf.at[q, t, kq],
            rbuf.at[2 * p + kq, t],
            asend.at[q, t, kq],
            arecv.at[p, t, kq],
            member(q),
        )

    def send_block(fq, kq, t):
        for i in range(4):
            q = 2 * (zz ^ i) + fq
            if i == 0:

                @pl.when(fq == yy)
                def _():
                    pltpu.make_async_copy(
                        sbuf.at[q, t, kq], rbuf.at[2 * p + kq, t], arecv.at[p, t, kq]
                    ).start()

                @pl.when(fq != yy)
                def _():
                    in_copy(q, t, kq).start()
            else:
                in_copy(q, t, kq).start()

    def sent_block(fq, kq, t):
        for i in range(4):
            q = 2 * (zz ^ i) + fq
            if i == 0:

                @pl.when(fq != yy)
                def _():
                    in_copy(q, t, kq).wait_send()
            else:
                in_copy(q, t, kq).wait_send()

    def store_rows(ch, i, values):
        mats[ch, i // 2, i % 2] = values.reshape(2, 128, 256)

    def down_part(i, carry):
        full = dot_tn(hid[:, lanes(i, 256)], gal[...]).astype(BF16)
        for cc in range(4):
            store_rows(cc, i, full[:, 256 * cc : 256 * cc + 256])
        return carry

    def up_part(i, carry):
        full = dot_tn(nrm[:, lanes(i, 256)], upg[...]).astype(BF16)
        for cc in range(4):
            store_rows(4 + cc, i, full[:, 256 * cc : 256 * cc + 256])
        return carry

    bits = [(p // mask) % 2 for mask in MASKS]
    every = slice(None)

    def block_index(free, other=None):
        return tuple(
            every if dim in free else (1 - bits[dim] if dim == other else bits[dim])
            for dim in range(3)
        )

    def scatter_order(ch):
        return SCATTER.get(ch, (0, 1, 2))

    def gather_order(ch):
        return GATHER.get(ch, (2, 1, 0))

    rsb = (rs0, rs1, rs2)

    middle = jnp.logical_or(zz == 1, zz == 2)
    outer = jnp.logical_not(middle)
    half_z = zz // 2
    inner_chip = 2 * (1 + half_z) + yy
    other_chip = 2 * (3 - zz) + yy
    outer_chip = 6 * half_z + yy

    def middle_in(ch, ph):
        if ph == 0:
            src, dst, q = mats.at[ch, 1 - yy], rs0.at[ch], p ^ 1
        elif ph == 1:
            src, dst, q = mats.at[ch, yy], rsm.at[sorted(MIDDLE).index(ch)], inner_chip
        else:
            src, dst, q = mats.at[ch, yy, :, 1 - half_z], rs1.at[ch], other_chip
        return remote(src, dst, rssend.at[ch, ph], rsrecv.at[ch, ph], member(q))

    def middle_out(ch, step):
        order = MIDDLE[ch]
        kind = order[step]
        done = order[:step]
        index = (every if 0 in done else yy, every, every if 2 in done else half_z)
        there = out_slice(ch, k, index)
        src = middle_shard(ch) if step == 0 else there
        q = (p ^ 1, outer_chip, other_chip)[kind]
        return remote(src, there, agsend.at[ch, step], agrecv.at[ch, step], member(q))

    def middle_shard(ch):
        return xsw if ch == 10 else mats.at[ch, yy, :, half_z]

    def middle_swap():
        return remote(mats.at[10, yy, :, half_z], xsw, gsend.at[8], grecv.at[8], xpart)

    def middle_local(ch):
        there = out_slice(ch, k, (yy, every, half_z))
        return pltpu.make_async_copy(middle_shard(ch), there, clocal.at[ch])

    def sends_out(ch, step):
        order = MIDDLE[ch]
        return order[step] == 0 and 1 in order[:step]

    def wait_out(ch, step):
        if sends_out(ch, step):
            middle_out(ch, step).wait_recv()
        else:

            @pl.when(outer if MIDDLE[ch][step] == 1 else middle)
            def _():
                middle_out(ch, step).wait_recv()

    def start_out(ch, step):
        if sends_out(ch, step):
            middle_out(ch, step).start()
        else:

            @pl.when(middle)
            def _():
                middle_out(ch, step).start()

    def add_blocks(ch, pairs):
        for here, there in pairs:
            mats[(ch,) + here] = (mats[(ch,) + here].astype(F32) + there.astype(F32)).astype(BF16)

    def advance_middle(ch, stage):
        if stage == 0:
            middle_in(ch, 0).start()
        elif stage == 1:
            middle_in(ch, 0).wait_recv()
            add_blocks(ch, [((yy, i, j), rs0[ch, i, j]) for i in range(2) for j in range(2)])

            @pl.when(outer)
            def _():
                middle_in(ch, 1).start()
        elif stage == 2:

            @pl.when(middle)
            def _():
                middle_in(ch, 1).wait_recv()
                n = sorted(MIDDLE).index(ch)
                add_blocks(ch, [((yy, i, j), rsm[n, i, j]) for i in range(2) for j in range(2)])
                middle_in(ch, 2).start()
        elif stage == 3:

            @pl.when(middle)
            def _():
                middle_in(ch, 2).wait_recv()
                add_blocks(ch, [((yy, i, half_z), rs1[ch, i]) for i in range(2)])
                if ch == 10:
                    middle_swap().start()
                    middle_swap().wait_recv()
                middle_local(ch).start()
                middle_out(ch, 0).start()
        elif stage == 4:
            wait_out(ch, 0)

            @pl.when(middle)
            def _():
                middle_local(ch).wait()

            start_out(ch, 1)
        elif stage == 5:
            wait_out(ch, 1)
            start_out(ch, 2)
        elif stage == 6:
            wait_out(ch, 2)
            core_copy(ch).start()
        elif stage == 7:
            core_copy(ch).wait_recv()

    def settle_middle(ch):
        middle_in(ch, 0).wait_send()

        @pl.when(outer)
        def _():
            middle_in(ch, 1).wait_send()

        @pl.when(middle)
        def _():
            middle_in(ch, 2).wait_send()
            if ch == 10:
                middle_swap().wait_send()

        for step in range(3):
            if sends_out(ch, step):
                middle_out(ch, step).wait_send()
            else:

                @pl.when(middle)
                def _():
                    middle_out(ch, step).wait_send()

        core_copy(ch).wait_send()

    def rs_copy(ch, ph):
        order = scatter_order(ch)
        return remote(
            mats.at[(ch,) + block_index(order[ph + 1 :], order[ph])],
            rsb[ph].at[ch],
            rssend.at[ch, ph],
            rsrecv.at[ch, ph],
            member(p ^ MASKS[order[ph]]),
        )

    def rs_add(ch, ph):
        free = sorted(scatter_order(ch)[ph + 1 :])
        rs_copy(ch, ph).wait_recv()
        for n in range(2 ** len(free)):
            spot = {dim: (n >> i) % 2 for i, dim in enumerate(free)}
            here = (ch,) + tuple(spot.get(dim, bits[dim]) for dim in range(3))
            there = (ch,) + tuple(spot[dim] for dim in free)
            mats[here] = (mats[here].astype(F32) + rsb[ph][there].astype(F32)).astype(BF16)

    def out_slice(ch, kk, index):
        if ch < 4:
            return odn.at[(kk,) + index + (every, slice(256 * ch, 256 * ch + 256))]
        if ch < 8:
            start, out = kk * 1024 + (ch - 4) * 256, oup
        elif ch < 11:
            start, out = (0, 1024, 512)[ch - 8] + kk * 256, oqkv
        else:
            start, out = kk * 256, oout
        return out.at[index + (every, pl.ds(pl.multiple_of(start, 256), 256))]

    def shard(ch):
        if ch == 10:
            return xsw.at[0]
        return mats.at[(ch,) + block_index(())]

    def swap_shard():
        return remote(
            mats.at[(10,) + block_index(())], xsw.at[0], gsend.at[8], grecv.at[8], xpart
        )

    def local_copy(ch):
        return pltpu.make_async_copy(
            shard(ch), out_slice(ch, k, block_index(())), clocal.at[ch]
        )

    def ag_copy(ch, step):
        order = gather_order(ch)
        there = out_slice(ch, k, block_index(order[:step]))
        return remote(
            shard(ch) if step == 0 else there,
            there,
            agsend.at[ch, step],
            agrecv.at[ch, step],
            member(p ^ MASKS[order[step]]),
        )

    def core_copy(ch):
        return remote(
            out_slice(ch, k, (every,) * 3),
            out_slice(ch, k, (every,) * 3),
            csend.at[ch],
            crecv.at[ch],
            sibling,
        )

    def advance(ch, stage):
        if ch in MIDDLE:
            advance_middle(ch, stage)
        elif stage == 0:
            rs_copy(ch, 0).start()
        elif stage <= 2:
            rs_add(ch, stage - 1)
            rs_copy(ch, stage).start()
        elif stage == 3:
            rs_add(ch, 2)
            if ch == 10:
                swap_shard().start()
                swap_shard().wait_recv()
            local_copy(ch).start()
            ag_copy(ch, 0).start()
        elif stage == 4:
            ag_copy(ch, 0).wait_recv()
            local_copy(ch).wait()
            ag_copy(ch, 1).start()
        elif stage == 5:
            ag_copy(ch, 1).wait_recv()
            ag_copy(ch, 2).start()
        elif stage == 6:
            ag_copy(ch, 2).wait_recv()
            core_copy(ch).start()
        elif stage == 7:
            core_copy(ch).wait_recv()

    def settle(ch):
        if ch in MIDDLE:
            settle_middle(ch)
            return
        for ph in range(3):
            rs_copy(ch, ph).wait_send()
            ag_copy(ch, ph).wait_send()
        core_copy(ch).wait_send()
        if ch == 10:
            swap_shard().wait_send()

    def load_half(place, t, u):
        return rbuf[spots_ref[place], t, 2 * u + spots_ref[32 + place]]

    def sort_unit(u):
        def sort_rows(i, carry):
            here = pl.ds(pl.multiple_of(i * 128, 128), 128)
            kg = jnp.concatenate([load_half(2 * i, 0, u), load_half(2 * i + 1, 0, u)], axis=0)
            qv = jnp.concatenate([load_half(2 * i, 1, u), load_half(2 * i + 1, 1, u)], axis=0)
            ak[here, :] = kg[:, :64]
            ag[here, :] = kg[:, 64:]
            aq[here, :] = qv[:, :64]
            av[here, :] = qv[:, 64:]
            kgt = kg.T
            akt[:, here] = kgt[:64, :]
            agt[:, here] = kgt[64:, :]
            avt[:, here] = qv.T[64:, :]
            return carry

        lax.fori_loop(0, LENGTH // 128, sort_rows, 0)

    def fold(values):
        return values.reshape(values.shape[0] // 8, 8, values.shape[1])

    def query_block(qb):
        mine = slice(qb * QB, qb * QB + QB)
        tiles = [slice(i * QB, i * QB + QB) for i in range(qb + 1)]
        query = aq[mine, :]
        grads = ag[mine, :]
        top = jnp.full((8, QB), masked_score, F32)
        for i, tile in enumerate(tiles):
            score = dot_nt(ak[tile, :], query)
            if i == qb:
                row = lax.broadcasted_iota(jnp.int32, (QB, QB), 0)
                col = lax.broadcasted_iota(jnp.int32, (QB, QB), 1)
                score = jnp.where(row <= col, score, masked_score)
            sco[tile, :] = score
            top = jnp.maximum(top, jnp.max(fold(score), axis=0))
        top = jnp.max(top, axis=0, keepdims=True)
        total = jnp.zeros((8, QB), F32)
        mix = jnp.zeros((HEAD_DIM, QB), F32)
        for tile in tiles:
            weights = jnp.exp(sco[tile, :] - top)
            sco[tile, :] = weights
            total = total + jnp.sum(fold(weights), axis=0)
            mix = mix + dot(avt[:, tile], weights.astype(BF16))
        inverse = 1.0 / jnp.sum(total, axis=0, keepdims=True)
        mix = mix * inverse
        dots = jnp.sum(agt[:, mine].astype(F32) * mix, axis=0, keepdims=True)
        back = jnp.zeros((HEAD_DIM, QB), F32)
        for i, tile in enumerate(tiles):
            chances = sco[tile, :] * inverse
            slopes = dot_nt(av[tile, :], grads)
            score_grads = (chances * (slopes - dots)).astype(BF16)
            value_part = dot(chances.astype(BF16), grads)
            key_part = dot(score_grads, query)
            if qb == LENGTH // QB - 1:
                dva[tile, :] = value_part
                dka[tile, :] = key_part
            else:
                dva[tile, :] += value_part
                dka[tile, :] += key_part
            back = back + dot(akt[:, tile], score_grads)
        place(0, qb, jnp.concatenate([mix, back * SCALE], axis=0).T)

    def place(t, qb, both):
        n = QB // HALF
        table = turns[qb * n : qb * n + n].reshape(QB, 128)
        cosine = jnp.concatenate([jnp.ones((QB, 64), F32), table[:, :64]], axis=1)
        sine = jnp.concatenate([jnp.zeros((QB, 64), F32), -table[:, 64:]], axis=1)
        osrt[t, qb * n : qb * n + n] = turn(both, cosine, sine).astype(BF16).reshape(n, HALF, 128)

    def finish_half(u, half):
        for qb in (2 * half, 2 * half + 1):
            mine = slice(qb * QB, qb * QB + QB)
            place(1, qb, jnp.concatenate([dva[mine, :], dka[mine, :]], axis=1))

        def unsort(i, carry):
            for t in range(2):
                sbuf[i // 2, u, t, 2 * half + i % 2] = osrt[t, spots_ref[64 + 2 * i + half]]
            return carry

        lax.fori_loop(0, 2 * CHIPS, unsort, 0)

    def send_half(u, half):
        pltpu.make_async_copy(
            out_part(sbuf, p, u, half), out_part(rb2, p, u, half), orecv.at[p, u, half]
        ).start()
        for i in (4, 6, 2, 5, 7, 3, 1):
            out_copy(p ^ i, u, half).start()

    def out_part(buf, q, u, half):
        return buf.at[q, u, :, pl.ds(2 * half, 2)]

    def out_copy(q, u, half):
        return remote(
            out_part(sbuf, q, u, half),
            out_part(rb2, p, u, half),
            osend.at[q, u, half],
            orecv.at[p, u, half],
            member(q),
        )

    def run(*steps):
        for ch, stage in steps:
            advance(ch, stage)

    def out_rows(q, u, t, kq):
        return jnp.concatenate([rb2[q, u, t, kq], rb2[q, u, t, 2 + kq]], axis=0)

    def att_part(i, carry):
        here = lanes(i, 256)
        left = nrm[:, here]
        for slot in range(3):
            at = 8 + (slot - f + 3) % 3
            store_rows(at, i, dot_tn(left, dqkv[slot]).astype(BF16))
        store_rows(11, i, dot_tn(gal[:, here], aall[...]).astype(BF16))
        return carry

    def normed_part(b, cols):
        here = rows(b)
        total = dot_nt(upg[here, :], wup[cols, :])
        for slot in range(3):
            total = total + dot_nt(dqkv[slot, here, :], wq[slot, cols, :])
        return total

    def mixed_part(b, cols):
        here = rows(b)
        return dot(hid[here, :], wdn[:, cols]) + dot(aall[here, :], wout[:, cols])

    def reduce_copies(n):
        return (
            remote(red_s.at[n, 0], red_r.at[n, 0], dsend.at[n, 0], drecv.at[n, 0], sibling),
            remote(red_s.at[n, 1], red_r.at[n, 1], dsend.at[n, 1], drecv.at[n, 1], sibling),
            remote(red_x.at[n], red_xr.at[n], dsend.at[n, 2], drecv.at[n, 2], xpart),
        )

    parts = (normed_part, mixed_part)

    def reduce_first(n):
        copies = reduce_copies(n)
        for slot, b in ((1, dg), (0, sibb)):

            def fill(i, carry):
                red_s[n, slot, :, lanes(i, 256)] = parts[n](b, lanes(i, 256)).astype(BF16)
                return carry

            lax.fori_loop(0, 4, fill, 0)
            copies[slot].start()

    def reduce_second(n):
        copies = reduce_copies(n)
        copies[1].wait_recv()

        def fill(i, carry):
            cols = lanes(i, 256)
            red_x[n, :, cols] = (
                parts[n](xb, cols) + red_r[n, 1, :, cols].astype(F32)
            ).astype(BF16)
            return carry

        lax.fori_loop(0, 4, fill, 0)
        copies[2].start()

    def reduce_third(n):
        copies = reduce_copies(n)

        def fill(i, carry):
            cols = lanes(i, 256)
            own_acc[n, :, cols] = parts[n](own, cols)
            return carry

        lax.fori_loop(0, 4, fill, 0)
        copies[0].wait_recv()
        copies[2].wait_recv()

        def finish(i, carry):
            cols = lanes(i, 256)
            own_acc[n, :, cols] = (
                own_acc[n, :, cols]
                + red_r[n, 0, :, cols].astype(F32)
                + red_xr[n, :, cols].astype(F32)
            )
            return carry

        lax.fori_loop(0, 4, finish, 0)

    def out_pick():
        row = lax.broadcasted_iota(jnp.int32, (ROWS, ROWS), 0)
        col = lax.broadcasted_iota(jnp.int32, (ROWS, ROWS), 1)
        return (row == 2 * (col % SEQ_DEV_TOK) + col // SEQ_DEV_TOK).astype(F32).astype(BF16)

    def back_rows(i, carry):
        dgain, dshift = carry
        here = pl.ds(pl.multiple_of(i * step, step), step)
        there = pl.ds(pl.multiple_of(own * ROWS + i * step, step), step)
        values = xs[here, :].astype(F32)
        center = values - jnp.mean(values, axis=1, keepdims=True)
        spread = lax.rsqrt(jnp.mean(center * center, axis=1, keepdims=True) + EPS)
        hat = center * spread
        grads = own_acc[0, here, :]
        dgain = dgain + jnp.sum(grads * hat, axis=0, keepdims=True)
        dshift = dshift + jnp.sum(grads, axis=0, keepdims=True)
        inner = grads * gain
        inner = spread * (
            inner
            - jnp.mean(inner, axis=1, keepdims=True)
            - hat * jnp.mean(inner * hat, axis=1, keepdims=True)
        )
        xs2 = gal[there, :].astype(F32) + inner
        red_s[0, 0, here, :] = xs2.astype(BF16)
        return dgain, dshift

    def mixed_rows(i, carry):
        here = pl.ds(pl.multiple_of(i * step, step), step)
        red_s[1, 0, here, :] = (xs[here, :].astype(F32) + own_acc[1, here, :] + down_b).astype(
            BF16
        )
        return carry

    for copy in (n_sib, n_x):
        copy.start()
    for load in loads:
        load.wait()
    kg_block(own, f, k)
    send_block(f, k, 0)
    for copy in (g_sib, g_x):
        copy.start()
    n_sib.wait_recv()
    g_sib.wait_recv()
    kg_block(sibb, f, 1 - k)
    send_block(f, 1 - k, 0)
    swap_copy.wait_recv()
    qv_block(sibb, f, 1 - k)
    send_block(f, 1 - k, 1)
    qv_block(own, f, k)
    send_block(f, k, 1)
    feed_block(own)
    def table_row(b, carry):
        holder = jnp.int32(0)
        half = jnp.int32(0)
        for i in range(2 * CHIPS):
            first = (pairs_ref[i] == b).astype(jnp.int32)
            last = (4 * CHIPS - 1 - pairs_ref[i] == b).astype(jnp.int32)
            holder = holder + i * (first + last)
            half = half + last
        spots_ref[b] = jnp.minimum(holder, 2 * CHIPS - 1)
        spots_ref[4 * CHIPS + b] = jnp.minimum(half, 1)
        return carry

    lax.fori_loop(0, 4 * CHIPS, table_row, 0)

    n_x.wait_recv()
    n_dg.start()
    qv_block(xb, 1 - f, k)
    send_block(1 - f, k, 1)
    n_dg.wait_recv()
    qv_block(dg, 1 - f, 1 - k)
    send_block(1 - f, 1 - k, 1)
    feed_up(dg, 1)
    feed_up(xb, 0)
    g_x.wait_recv()
    g_dg.start()
    kg_block(xb, 1 - f, k)
    send_block(1 - f, k, 0)
    feed_block(sibb)
    feed_back(xb, 0)
    g_dg.wait_recv()
    kg_block(dg, 1 - f, 1 - k)
    send_block(1 - f, 1 - k, 0)
    feed_back(dg, 1)
    lax.fori_loop(0, 4, up_part, 0)
    sm[...] = jnp.zeros_like(sm)
    sm[0:1, :] = jnp.sum(upg[...].astype(F32), axis=0, keepdims=True)
    sm[2:3, :] = jnp.sum(gal[...].astype(F32), axis=0, keepdims=True)
    run((4, 0))
    lax.fori_loop(0, 4, down_part, 0)
    run((5, 0), (7, 0))
    for fq, kq in ((f, k), (f, 1 - k), (1 - f, k), (1 - f, 1 - k)):
        for t in range(2):
            sent_block(fq, kq, t)
    for q in range(CHIPS):
        for t in range(2):
            for kq in range(2):
                pltpu.make_async_copy(
                    rbuf.at[2 * q + kq, t], rbuf.at[2 * q + kq, t], arecv.at[q, t, kq]
                ).wait()

    sort_unit(0)
    run((0, 0), (3, 0))
    query_block(3)
    query_block(2)
    finish_half(0, 1)
    send_half(0, 1)
    query_block(1)
    query_block(0)
    finish_half(0, 0)
    send_half(0, 0)
    run((5, 1))
    sort_unit(1)
    run((6, 0))
    query_block(3)
    query_block(2)
    finish_half(1, 1)
    run((4, 1))
    query_block(1)
    query_block(0)
    finish_half(1, 0)
    run((0, 1), (5, 2))
    send_half(1, 0)
    run((1, 0))
    send_half(1, 1)
    run((4, 2), (5, 3))
    run((2, 0), (0, 2), (1, 1), (6, 1), (3, 1))
    for q in range(CHIPS):
        for u in range(SEQS):
            for half in range(2):
                arrived = out_part(rb2, q, u, half)
                pltpu.make_async_copy(arrived, arrived, orecv.at[q, u, half]).wait()

    for fq in range(2):
        for kq in range(2):
            for u in range(SEQS):
                at = (2 * fq + kq) * ROWS + u * 128
                here = slice(at, at + 128)
                for pair in range(2):
                    cols = slice(128 * pair, 128 * pair + 128)
                    x0 = out_rows(4 * pair + fq, u, 0, kq)
                    x1 = out_rows(4 * pair + 2 + fq, u, 0, kq)
                    y0 = out_rows(4 * pair + fq, u, 1, kq)
                    y1 = out_rows(4 * pair + 2 + fq, u, 1, kq)
                    aall[here, cols] = jnp.concatenate([x0[:, :64], x1[:, :64]], axis=1)
                    dqkv[0, here, cols] = jnp.concatenate([x0[:, 64:], x1[:, 64:]], axis=1)
                    dqkv[2, here, cols] = jnp.concatenate([y0[:, :64], y1[:, :64]], axis=1)
                    dqkv[1, here, cols] = jnp.concatenate([y0[:, 64:], y1[:, 64:]], axis=1)

    run((7, 1))
    lax.fori_loop(0, 4, att_part, 0)
    run((9, 0), (4, 3), (2, 1), (1, 2), (8, 0), (5, 4))
    run((0, 3))
    reduce_first(0)
    run((6, 2), (10, 0), (9, 1), (0, 4), (2, 2), (4, 4), (6, 3), (8, 1))
    run((1, 3), (3, 2), (6, 4), (10, 1), (11, 0), (9, 2), (2, 3), (0, 5))
    reduce_second(0)
    run((9, 3), (5, 5), (4, 5), (8, 2), (9, 4), (10, 2), (3, 3), (7, 2))
    run((11, 1), (0, 6), (2, 4), (6, 5), (10, 3), (1, 4), (9, 5), (5, 6))
    run((8, 3), (2, 5), (10, 4))
    run((0, 7), (11, 2), (3, 4), (1, 5), (11, 3), (6, 6), (4, 6), (7, 3))
    run((11, 4), (8, 4))
    reduce_first(1)
    run((10, 5), (2, 6), (4, 7))
    reduce_second(1)
    run((7, 4), (3, 5), (1, 6), (8, 5))
    reduce_third(0)
    reduce_copies(0)[0].wait_send()
    dgain, dshift = lax.fori_loop(
        0, ROWS // step, back_rows, (jnp.zeros((1, D), F32), jnp.zeros((1, D), F32))
    )
    tgrad_ref[...] = dot(out_pick(), red_s[0, 0]).astype(BF16)
    sm[3:4, :] = dgain
    sm[4:5, :] = dshift

    small_copies = [
        remote(sm, smg.at[own], smsend.at[0], smrecv.at[own], sibling),
        remote(sm, smg.at[own], smsend.at[1], smrecv.at[own], xpart),
        remote(sm, smg.at[own], smsend.at[2], smrecv.at[own], diagonal),
    ]
    for copy in small_copies:
        copy.start()

    run((11, 5), (7, 5), (10, 6), (9, 6))
    reduce_third(1)
    reduce_copies(1)[0].wait_send()
    lax.fori_loop(0, ROWS // step, mixed_rows, 0)
    mixed_ref[...] = dot(out_pick(), red_s[1, 0]).astype(BF16)

    run((5, 7), (3, 6), (2, 7))
    smg[own] = sm[...]
    for b in (sibb, xb, dg):
        remote(sm, smg.at[b], smsend.at[0], smrecv.at[b], sibling).wait_recv()
    for copy in small_copies:
        copy.wait_send()
    first_b = 2 * f
    sma[p, 0:1, :] = smg[first_b, 0:1, :]
    sma[p, 1:2, :] = smg[first_b + 1, 0:1, :]
    sma[p, 2:3, :] = sm[2:3, :]
    sma[p, 3:8, :] = smg[0, 3:8, :] + smg[1, 3:8, :] + smg[2, 3:8, :] + smg[3, 3:8, :]
    sm_copies = [
        remote(sma.at[p], sma.at[p], smsend.at[2 + i], smrecv.at[3 + i], member(p ^ i))
        for i in range(1, CHIPS)
    ]
    for copy in sm_copies:
        copy.start()

    run((11, 6), (9, 7), (1, 7), (7, 6), (8, 6), (11, 7), (8, 7), (7, 7))
    run((10, 7), (3, 7), (6, 7))
    total = jnp.zeros((8, D), F32)
    for copy in sm_copies:
        copy.wait()
    for q in range(CHIPS):
        total = total + sma[q]
    small_ref[...] = total

    for copy in (vec_copy,):
        pass
    swap_copy.wait_send()
    for copy in (n_sib, n_x, g_sib, g_x, n_dg, g_dg):
        copy.wait_send()
    for u in range(SEQS):
        for i in range(1, CHIPS):
            for half in range(2):
                out_copy(p ^ i, u, half).wait_send()
    for n in range(2):
        copies = reduce_copies(n)
        copies[1].wait_send()
        copies[2].wait_send()
    for ch in range(NCH):
        settle(ch)


def widen_kernel(
    dn_h,
    up_h,
    qkv_h,
    out_h,
    small,
    mixed_in,
    tgrad_in,
    dn_o,
    up_o,
    qkv_o,
    out_o,
    mixed_o,
    tgrad_o,
    gain_o,
    shift_o,
    upb_o,
    downb_o,
    dn_b,
    up_b,
    qkv_b,
    out_b,
    dn_f,
    up_f,
    qkv_f,
    out_f,
    isem,
    osem,
):
    f = lax.axis_index("fsdp")
    sources = (up_h, dn_h, qkv_h, out_h)
    brief = (up_b, dn_b, qkv_b, out_b)
    wide = (up_f, dn_f, qkv_f, out_f)
    results = (up_o, dn_o, qkv_o, out_o)
    heights = (128, 256, 128, 128)

    def fetch(n, i):
        if n == 1:
            src = dn_h.at[pl.ds(2 * i, 2)]
        else:
            src = sources[n].at[i]
        return pltpu.make_async_copy(src, brief[n].at[i], isem.at[n, i])

    def put(n, i):
        if n == 3:
            return pltpu.make_async_copy(out_f, out_o, osem.at[3, 0])
        rows = pl.ds(i * heights[n], heights[n])
        return pltpu.make_async_copy(wide[n].at[rows], results[n].at[rows], osem.at[n, i])

    for n in range(4):
        for i in range(8):
            fetch(n, i).start()
    half = D // FSDP
    low_half = f == 0
    pick = jnp.where(low_half, small[:, :half], small[:, half:])
    gain_o[...] = pick[3]
    shift_o[...] = pick[4]
    downb_o[...] = pick[2]
    upb_o[:1024] = small[0]
    upb_o[1024:] = small[1]
    mixed_o[...] = mixed_in[...]
    tgrad_o[...] = tgrad_in[...]
    for n in range(4):
        for i in range(8):
            fetch(n, i).wait()
            values = brief[n][i].astype(F32)
            if n == 3:
                out_f[:, i * 128 : i * 128 + 128] = values.T
            else:
                wide[n][i * heights[n] : (i + 1) * heights[n], :] = values.reshape(
                    heights[n], -1
                )
                put(n, i).start()
    put(3, 0).start()
    for n in range(3):
        for i in range(8):
            put(n, i).wait()
    put(3, 0).wait()


def widen(dn, up, qkv, out_t, small, mixed, tokens_grad):
    vm = pl.BlockSpec(memory_space=pltpu.VMEM)
    hbm = pl.BlockSpec(memory_space=pl.ANY)
    half = D // FSDP
    feeds = FF // FSDP
    heads = 3 * D // FSDP
    return pl.pallas_call(
        widen_kernel,
        out_shape=(
            jax.ShapeDtypeStruct((feeds, D), F32),
            jax.ShapeDtypeStruct((D, feeds), F32),
            jax.ShapeDtypeStruct((D, heads), F32),
            jax.ShapeDtypeStruct((half, D), F32),
            jax.ShapeDtypeStruct((ROWS, D), BF16),
            jax.ShapeDtypeStruct((ROWS, D), BF16),
            jax.ShapeDtypeStruct((half,), F32),
            jax.ShapeDtypeStruct((half,), F32),
            jax.ShapeDtypeStruct((feeds,), F32),
            jax.ShapeDtypeStruct((half,), F32),
        ),
        in_specs=[hbm] * 4 + [vm] * 3,
        out_specs=(hbm,) * 4 + (vm,) * 6,
        scratch_shapes=[
            pltpu.VMEM((8, 2, 128, D), BF16),
            pltpu.VMEM((8, 128, feeds), BF16),
            pltpu.VMEM((8, 128, heads), BF16),
            pltpu.VMEM((8, 128, half), BF16),
            pltpu.VMEM((feeds, D), F32),
            pltpu.VMEM((D, feeds), F32),
            pltpu.VMEM((D, heads), F32),
            pltpu.VMEM((half, D), F32),
            pltpu.SemaphoreType.DMA((4, 8)),
            pltpu.SemaphoreType.DMA((4, 8)),
        ],
        compiler_params=pltpu.CompilerParams(vmem_limit_bytes=56 * 2**20),
    )(
        dn.reshape(16, 128, D),
        up.reshape(8, 128, feeds),
        qkv.reshape(8, 128, heads),
        out_t.reshape(8, 128, half),
        small,
        mixed,
        tokens_grad,
    )


def turn_table():
    lane = np.arange(HEAD_DIM)
    speeds = (10000.0 ** (-(lane // 2 * 2) / ROT_DIM)).astype(np.float32)
    phase = np.arange(LENGTH, dtype=np.float32)[:, None] * speeds[None, :]
    turning = (lane < ROT_DIM)[None, :]
    sign = np.where(lane % 2 == 0, -1.0, 1.0)[None, :]
    cosine = np.where(turning, np.cos(phase), 1.0)
    sine = np.where(turning, np.sin(phase) * sign, 0.0)
    table = np.concatenate((cosine, sine), axis=1).astype(np.float32)
    return table.reshape(4 * CHIPS, HALF, 2 * HEAD_DIM)


def fused_device(
    tokens,
    block_pairs,
    norm_gain,
    norm_bias,
    qkv_weight,
    out_weight,
    up_weight,
    up_bias,
    down_weight,
    down_bias,
    cotangent,
):
    vm = pl.BlockSpec(memory_space=pltpu.VMEM)
    sme = pl.BlockSpec(memory_space=pltpu.SMEM)
    hbm = pl.BlockSpec(memory_space=pl.ANY)
    dma = pltpu.SemaphoreType.DMA
    scratch = [
        pltpu.SMEM((96,), jnp.int32),
        pltpu.VMEM((4 * CHIPS, HALF, 128), F32),
        pltpu.VMEM((2, 8, 512), F32),
        pltpu.VMEM((ROWS, D), BF16),
        pltpu.VMEM((ALL, D), BF16),
        pltpu.VMEM((ALL, D), BF16),
        pltpu.VMEM((3, D, 256), BF16),
        pltpu.VMEM((256, D), BF16),
        pltpu.VMEM((D, 1024), BF16),
        pltpu.VMEM((1024, D), BF16),
        pltpu.VMEM((ALL, 1024), BF16),
        pltpu.VMEM((ALL, 1024), BF16),
        pltpu.VMEM((CHIPS, 2, 2, 4, HALF, 128), BF16),
        pltpu.VMEM((2 * CHIPS, 2, 4, HALF, 128), BF16),
        pltpu.VMEM((LENGTH, HEAD_DIM), BF16),
        pltpu.VMEM((LENGTH, HEAD_DIM), BF16),
        pltpu.VMEM((LENGTH, HEAD_DIM), BF16),
        pltpu.VMEM((LENGTH, HEAD_DIM), BF16),
        pltpu.VMEM((HEAD_DIM, LENGTH), BF16),
        pltpu.VMEM((HEAD_DIM, LENGTH), BF16),
        pltpu.VMEM((HEAD_DIM, LENGTH), BF16),
        pltpu.VMEM((LENGTH, QB), F32),
        pltpu.VMEM((LENGTH, HEAD_DIM), F32),
        pltpu.VMEM((LENGTH, HEAD_DIM), F32),
        pltpu.VMEM((2, 4 * CHIPS, HALF, 128), BF16),
        pltpu.VMEM((CHIPS, SEQS, 2, 4, HALF, 128), BF16),
        pltpu.VMEM((ALL, 256), BF16),
        pltpu.VMEM((3, ALL, 256), BF16),
        pltpu.VMEM((NCH, 2, 2, 2, 128, 256), BF16),
        pltpu.VMEM((NCH, 2, 2, 128, 256), BF16),
        pltpu.VMEM((NCH, 2, 128, 256), BF16),
        pltpu.VMEM((NCH, 128, 256), BF16),
        pltpu.VMEM((2, 128, 256), BF16),
        pltpu.VMEM((max(len(MIDDLE), 1), 2, 2, 128, 256), BF16),
        pltpu.VMEM((2, ROWS, D), F32),
        pltpu.VMEM((2, 2, ROWS, D), BF16),
        pltpu.VMEM((2, ROWS, D), BF16),
        pltpu.VMEM((2, 2, ROWS, D), BF16),
        pltpu.VMEM((2, ROWS, D), BF16),
        pltpu.VMEM((8, D), F32),
        pltpu.VMEM((4, 8, D), F32),
        pltpu.VMEM((CHIPS, 8, D), F32),
        dma((6,)),
        dma((9,)),
        dma((9,)),
        dma((CHIPS, 2, 2)),
        dma((CHIPS, 2, 2)),
        dma((CHIPS, SEQS, 2)),
        dma((CHIPS, SEQS, 2)),
        dma((NCH, 3)),
        dma((NCH, 3)),
        dma((NCH, 3)),
        dma((NCH, 3)),
        dma((NCH,)),
        dma((NCH,)),
        dma((NCH,)),
        dma((2, 3)),
        dma((2, 3)),
        dma((10,)),
        dma((11,)),
    ]
    mixed, tokens_grad, small, dn, up, qkv, out_t = pl.pallas_call(
        fused_kernel,
        out_shape=(
            jax.ShapeDtypeStruct((ROWS, D), BF16),
            jax.ShapeDtypeStruct((ROWS, D), BF16),
            jax.ShapeDtypeStruct((8, D), F32),
            jax.ShapeDtypeStruct((2, 2, 2, 2, 128, D), BF16),
            jax.ShapeDtypeStruct((2, 2, 2, 128, FF // FSDP), BF16),
            jax.ShapeDtypeStruct((2, 2, 2, 128, 3 * D // FSDP), BF16),
            jax.ShapeDtypeStruct((2, 2, 2, 128, D // FSDP), BF16),
        ),
        in_specs=[sme] + [vm] * 4 + [hbm, vm, vm] + [hbm] * 4,
        out_specs=(vm, vm, vm, hbm, hbm, hbm, hbm),
        scratch_shapes=scratch,
        compiler_params=pltpu.CompilerParams(
            collective_id=0, has_side_effects=True, vmem_limit_bytes=63 * 2**20
        ),
    )(
        block_pairs,
        norm_gain,
        norm_bias,
        down_bias,
        up_bias,
        jnp.asarray(turn_table()),
        tokens,
        cotangent,
        qkv_weight,
        out_weight,
        up_weight,
        down_weight,
    )
    dn, up, qkv, out, mixed, tokens_grad, gain, shift, upb, downb = widen(
        dn, up, qkv, out_t, small, mixed, tokens_grad
    )
    return mixed, tokens_grad, gain, shift, qkv, out, up, upb, dn, downb


def solution(mesh):
    in_specs = (
        P(("fsdp", "ctx"), None),
        P(),
        P("fsdp"),
        P("fsdp"),
        P(None, "fsdp"),
        P("fsdp", None),
        P(None, "fsdp"),
        P("fsdp"),
        P("fsdp", None),
        P("fsdp"),
        P(("fsdp", "ctx"), None),
    )
    out_specs = (
        P(("fsdp", "ctx"), None),
        P(("fsdp", "ctx"), None),
        P("fsdp"),
        P("fsdp"),
        P(None, "fsdp"),
        P("fsdp", None),
        P(None, "fsdp"),
        P("fsdp"),
        P("fsdp", None),
        P("fsdp"),
    )
    plan = fused_device if fits(mesh) else per_device
    return jax.shard_map(
        plan, mesh=mesh, in_specs=in_specs, out_specs=out_specs, check_vma=False
    )
```

```python
import functools
import math

import jax
import jax.numpy as jnp
import numpy as np
from jax import lax
from jax.experimental import pallas as pl
from jax.experimental.pallas import tpu as pltpu
from jax.sharding import PartitionSpec as P

D = 1024
HEAD_DIM = 64
ROT_DIM = 32
HEADS = 16
SEQ_DEV_TOK = 128
SEQS = 2


EPS = 1e-05
HIGHEST = lax.Precision.HIGHEST
masked_score = -1e30


def layer_norm(values, gain_values, shift_values):
    center = values - jnp.mean(values, axis=-1, keepdims=True)
    spread = jnp.mean(center * center, axis=-1, keepdims=True)
    return center * lax.rsqrt(spread + EPS) * gain_values + shift_values


def rotary_tables(places, window):
    lanes = jnp.arange(window, dtype=jnp.int32)
    within_head = lanes % HEAD_DIM
    turning = within_head < ROT_DIM
    steps_up = (within_head // 2 * 2).astype(jnp.float32)
    speeds = 10000.0 ** (-steps_up / ROT_DIM)
    phase = places.astype(jnp.float32)[:, None] * speeds[None, :]
    cos_full = jnp.where(turning[None, :], jnp.cos(phase), 1.0)
    sin_full = jnp.where(turning[None, :], jnp.sin(phase), 0.0)
    row_lane = lanes[:, None]
    col_lane = lanes[None, :]
    same_head = row_lane // HEAD_DIM == col_lane // HEAD_DIM
    col_within = col_lane % HEAD_DIM
    col_turns = same_head & (col_within < ROT_DIM)
    even_col = col_within % 2 == 0
    minus_part = jnp.where(col_turns & even_col & (row_lane == col_lane + 1), -1.0, 0.0)
    plus_part = jnp.where(
        col_turns & jnp.logical_not(even_col) & (row_lane == col_lane - 1), 1.0, 0.0
    )
    swap_table = (minus_part + plus_part).astype(jnp.float32)
    return (cos_full, sin_full, swap_table)


def smooth_gate(values):
    return jax.nn.gelu(values, approximate=True)


def positions(first_row, row_count, pair_table, devices, seq_rows):
    indices = first_row + jnp.arange(row_count, dtype=jnp.int32)
    owners = indices // seq_rows
    within = indices % seq_rows
    half_rows = seq_rows // 2
    matches = owners[:, None] == jnp.arange(devices, dtype=jnp.int32)[None, :]
    chosen = jnp.sum(jnp.where(matches, pair_table[None, :], 0), axis=1)
    block_index = jnp.where(within < half_rows, chosen, 2 * devices - 1 - chosen)
    return block_index * half_rows + within % half_rows


def in_groups(row_count, seq_rows):
    group_rows = math.gcd(row_count // seq_rows, 8) * seq_rows
    return (group_rows, row_count // group_rows)


def split_groups(array, group_rows, turns):
    return array.reshape((turns, group_rows) + array.shape[1:])


def grad_scores(
    query_rows,
    out_grads,
    log_sums,
    row_dots,
    query_places,
    key_rows,
    value_rows,
    key_places,
    factor,
):
    scores = (
        jnp.einsum("qshe,kshe->shqk", query_rows, key_rows, preferred_element_type=jnp.float32)
        * factor
    )
    allowed = key_places[None, :] <= query_places[:, None]
    chances = jnp.exp(jnp.where(allowed, scores - log_sums[..., None], masked_score))
    prob_grads = jnp.einsum(
        "qshe,kshe->shqk", out_grads, value_rows, preferred_element_type=jnp.float32
    )
    return (chances, (chances * (prob_grads - row_dots[..., None])).astype(jnp.bfloat16))


def per_device(
    tokens,
    block_pairs,
    norm_gain,
    norm_bias,
    qkv_weight,
    out_weight,
    up_weight,
    up_bias,
    down_weight,
    down_bias,
    cotangent,
):
    devices = lax.axis_size("ctx")
    own_index = lax.axis_index("ctx")
    seq_rows = SEQ_DEV_TOK
    seq_count = SEQS
    heads = HEADS
    head_size = HEAD_DIM
    width = D
    factor = HEAD_DIM ** (-0.5)
    all_rows = seq_rows * seq_count
    window = math.gcd(width, 128)
    gathered = (
        lax.all_gather(norm_gain, "fsdp", axis=0, tiled=True),
        lax.all_gather(norm_bias, "fsdp", axis=0, tiled=True),
        lax.all_gather(qkv_weight, "fsdp", axis=1, tiled=True),
        lax.all_gather(out_weight, "fsdp", axis=0, tiled=True),
        lax.all_gather(up_weight, "fsdp", axis=1, tiled=True),
        lax.all_gather(up_bias, "fsdp", axis=0, tiled=True),
        lax.all_gather(down_weight, "fsdp", axis=0, tiled=True),
        lax.all_gather(down_bias, "fsdp", axis=0, tiled=True),
    )
    gain_low, shift_low, w_qkv, w_out, w_up, b_up, w_down, b_down = gathered
    inputs = tokens.astype(jnp.float32)
    gain_values = gain_low.astype(jnp.float32)
    shift_values = shift_low.astype(jnp.float32)
    normed_low = layer_norm(inputs, gain_values, shift_values).astype(jnp.bfloat16)
    mixed_qkv = jnp.dot(normed_low, w_qkv, preferred_element_type=jnp.float32).reshape(
        seq_rows, seq_count, 3 * width
    )
    own_places = positions(own_index * seq_rows, seq_rows, block_pairs, devices, seq_rows)
    cos_full, sin_full, swap_table = rotary_tables(own_places, window)

    def turn_both(values):
        shaped = values.reshape(seq_rows, seq_count, 2 * width // window, window)
        swapped = jnp.einsum("rsgw,wv->rsgv", shaped, swap_table, precision=HIGHEST)
        turned_rows = shaped * cos_full[:, None, None, :] + swapped * sin_full[:, None, None, :]
        return turned_rows.reshape(seq_rows, seq_count, 2 * width)

    query_key = mixed_qkv[:, :, : 2 * width]
    turned = turn_both(query_key)
    queries = (
        turned[:, :, :width].astype(jnp.bfloat16).reshape(seq_rows, seq_count, heads, head_size)
    )
    key_rows = (
        turned[:, :, width:].astype(jnp.bfloat16).reshape(seq_rows, seq_count, heads, head_size)
    )
    value_rows = (
        mixed_qkv[:, :, 2 * width :]
        .astype(jnp.bfloat16)
        .reshape(seq_rows, seq_count, heads, head_size)
    )
    start_state = (
        jnp.full((seq_count, heads, seq_rows), masked_score, jnp.float32),
        jnp.zeros((seq_count, heads, seq_rows), jnp.float32),
        jnp.zeros((seq_count, heads, seq_rows, head_size), jnp.float32),
    )
    piece_keys = lax.all_gather(key_rows, "ctx", axis=0, tiled=True)
    piece_values = lax.all_gather(value_rows, "ctx", axis=0, tiled=True)
    group_rows, turns = in_groups(piece_keys.shape[0], seq_rows)

    def attend_step(inner, item):
        block_keys, block_values, turn = item
        key_places = positions(turn * group_rows, group_rows, block_pairs, devices, seq_rows)
        scores = (
            jnp.einsum("qshe,kshe->shqk", queries, block_keys, preferred_element_type=jnp.float32)
            * factor
        )
        allowed = key_places[None, :] <= own_places[:, None]
        running, totals, accum = inner
        fresh = jnp.maximum(running, jnp.max(jnp.where(allowed, scores, masked_score), axis=-1))
        weights = jnp.exp(jnp.where(allowed, scores - fresh[..., None], masked_score))
        fading = jnp.exp(running - fresh)
        totals = totals * fading + jnp.sum(weights, axis=-1)
        accum = accum * fading[..., None] + jnp.einsum(
            "shqk,kshe->shqe",
            weights.astype(jnp.bfloat16),
            block_values,
            preferred_element_type=jnp.float32,
        )
        return ((fresh, totals, accum), None)

    inner, _ = lax.scan(
        attend_step,
        start_state,
        (
            split_groups(piece_keys, group_rows, turns),
            split_groups(piece_values, group_rows, turns),
            jnp.arange(turns, dtype=jnp.int32),
        ),
    )
    running, totals, accum = inner
    log_sums = running + jnp.log(totals)
    attended = jnp.transpose(accum / totals[..., None], (2, 0, 1, 3))
    attn_low = attended.reshape(all_rows, width).astype(jnp.bfloat16)
    attention = jnp.dot(attn_low, w_out, preferred_element_type=jnp.float32)
    up_pre = jnp.dot(normed_low, w_up, preferred_element_type=jnp.float32) + b_up.astype(
        jnp.float32
    )
    hidden_low = smooth_gate(up_pre).astype(jnp.bfloat16)
    result = (
        inputs
        + attention
        + jnp.dot(hidden_low, w_down, preferred_element_type=jnp.float32)
        + b_down.astype(jnp.float32)
    )
    mixed = result.astype(jnp.bfloat16)
    again = (
        lax.all_gather(norm_gain, "fsdp", axis=0, tiled=True),
        lax.all_gather(norm_bias, "fsdp", axis=0, tiled=True),
        lax.all_gather(qkv_weight, "fsdp", axis=1, tiled=True),
        lax.all_gather(out_weight, "fsdp", axis=0, tiled=True),
        lax.all_gather(up_weight, "fsdp", axis=1, tiled=True),
        lax.all_gather(up_bias, "fsdp", axis=0, tiled=True),
        lax.all_gather(down_weight, "fsdp", axis=0, tiled=True),
        lax.all_gather(down_bias, "fsdp", axis=0, tiled=True),
    )
    gain_low, shift_low, w_qkv, w_out, w_up, b_up, w_down, b_down = again
    out_grad = cotangent.astype(jnp.float32)
    attn_grads = (
        jnp.einsum("td,ed->te", cotangent, w_out, preferred_element_type=jnp.float32)
        .astype(jnp.bfloat16)
        .reshape(seq_rows, seq_count, heads, head_size)
    )
    dots_rows = jnp.sum(attn_grads.astype(jnp.float32) * attended, axis=-1)
    row_dots = jnp.transpose(dots_rows, (1, 2, 0))
    empty_rows = jnp.zeros((seq_rows, seq_count, heads, head_size), jnp.float32)
    whole_keys, whole_values = (
        lax.all_gather(key_rows, "ctx", axis=0, tiled=True),
        lax.all_gather(value_rows, "ctx", axis=0, tiled=True),
    )
    piece_keys = whole_keys
    piece_values = whole_values
    query_group_rows, turns = in_groups(piece_keys.shape[0], seq_rows)

    def query_step(inner, item):
        block_keys, block_values, turn = item
        key_places = positions(
            0 + turn * query_group_rows, query_group_rows, block_pairs, devices, seq_rows
        )
        chances, score_grads = grad_scores(
            queries,
            attn_grads,
            log_sums,
            row_dots,
            own_places,
            block_keys,
            block_values,
            key_places,
            factor,
        )
        return (
            inner
            + jnp.einsum(
                "shqk,kshe->qshe", score_grads, block_keys, preferred_element_type=jnp.float32
            )
            * factor,
            None,
        )

    inner, _ = lax.scan(
        query_step,
        empty_rows,
        (
            split_groups(piece_keys, query_group_rows, turns),
            split_groups(piece_values, query_group_rows, turns),
            jnp.arange(turns, dtype=jnp.int32),
        ),
    )
    query_grad = inner
    piece_keys = whole_keys
    piece_values = whole_values
    key_group_rows, turns = in_groups(seq_rows * lax.axis_size("ctx"), seq_rows)

    def key_step(inner, item):
        block_keys, block_values, turn = item
        key_places = positions(
            turn * key_group_rows, key_group_rows, block_pairs, devices, seq_rows
        )
        chances, score_grads = grad_scores(
            queries,
            attn_grads,
            log_sums,
            row_dots,
            own_places,
            block_keys,
            block_values,
            key_places,
            factor,
        )
        key_part = (
            jnp.einsum("shqk,qshe->kshe", score_grads, queries, preferred_element_type=jnp.float32)
            * factor
        )
        value_part = jnp.einsum(
            "shqk,qshe->kshe",
            chances.astype(jnp.bfloat16),
            attn_grads,
            preferred_element_type=jnp.float32,
        )
        stacked = jnp.stack(
            (
                key_part.reshape(key_group_rows, seq_count, width),
                value_part.reshape(key_group_rows, seq_count, width),
            ),
            axis=2,
        )
        return (inner, stacked)

    _, blocks_out = lax.scan(
        key_step,
        jnp.zeros((), jnp.float32),
        (
            split_groups(piece_keys, key_group_rows, turns),
            split_groups(piece_values, key_group_rows, turns),
            jnp.arange(turns, dtype=jnp.int32),
        ),
    )
    summed_terms = lax.psum_scatter(
        blocks_out.reshape(seq_rows * lax.axis_size("ctx"), seq_count, 2, width),
        "ctx",
        scatter_dimension=0,
        tiled=True,
    )
    key_grad = summed_terms[:, :, 0].reshape(seq_rows, seq_count, heads, head_size)
    value_grad = summed_terms[:, :, 1].reshape(seq_rows, seq_count, heads, head_size)
    _, turn_back = jax.vjp(turn_both, query_key)
    both_grads = jnp.concatenate(
        (
            query_grad.reshape(seq_rows, seq_count, width),
            key_grad.reshape(seq_rows, seq_count, width),
        ),
        axis=2,
    )
    (pre_grads,) = turn_back(both_grads)
    qkv_grad = (
        jnp.concatenate((pre_grads, value_grad.reshape(seq_rows, seq_count, width)), axis=2)
        .reshape(all_rows, 3 * width)
        .astype(jnp.bfloat16)
    )
    hidden_grad = jnp.einsum("td,fd->tf", cotangent, w_down, preferred_element_type=jnp.float32)
    _, gate_back = jax.vjp(smooth_gate, up_pre)
    (up_grad,) = gate_back(hidden_grad)
    up_low = up_grad.astype(jnp.bfloat16)
    normed_grad = jnp.einsum(
        "tc,dc->td", qkv_grad, w_qkv, preferred_element_type=jnp.float32
    ) + jnp.einsum("tf,df->td", up_low, w_up, preferred_element_type=jnp.float32)
    _, norm_back = jax.vjp(
        layer_norm, inputs, gain_low.astype(jnp.float32), shift_low.astype(jnp.float32)
    )
    input_part, gain_grad, shift_grad = norm_back(normed_grad)
    tokens_grad = (out_grad + input_part).astype(jnp.bfloat16)
    qkv_wgrad = jnp.einsum("td,tc->dc", normed_low, qkv_grad, preferred_element_type=jnp.float32)
    out_wgrad = jnp.einsum("td,te->de", attn_low, cotangent, preferred_element_type=jnp.float32)
    up_wgrad = jnp.einsum("td,tf->df", normed_low, up_low, preferred_element_type=jnp.float32)
    up_bgrad = jnp.sum(up_low.astype(jnp.float32), axis=0)
    down_wgrad = jnp.einsum("tf,td->fd", hidden_low, cotangent, preferred_element_type=jnp.float32)
    down_bgrad = jnp.sum(out_grad, axis=0)
    shares = (
        lax.psum_scatter(
            gain_grad.astype(jnp.bfloat16), "fsdp", scatter_dimension=0, tiled=True
        ).astype(jnp.float32),
        lax.psum_scatter(
            shift_grad.astype(jnp.bfloat16), "fsdp", scatter_dimension=0, tiled=True
        ).astype(jnp.float32),
        lax.psum_scatter(
            qkv_wgrad.astype(jnp.bfloat16), "fsdp", scatter_dimension=1, tiled=True
        ).astype(jnp.float32),
        lax.psum_scatter(
            out_wgrad.astype(jnp.bfloat16), "fsdp", scatter_dimension=0, tiled=True
        ).astype(jnp.float32),
        lax.psum_scatter(
            up_wgrad.astype(jnp.bfloat16), "fsdp", scatter_dimension=1, tiled=True
        ).astype(jnp.float32),
        lax.psum_scatter(
            up_bgrad.astype(jnp.bfloat16), "fsdp", scatter_dimension=0, tiled=True
        ).astype(jnp.float32),
        lax.psum_scatter(
            down_wgrad.astype(jnp.bfloat16), "fsdp", scatter_dimension=0, tiled=True
        ).astype(jnp.float32),
        lax.psum_scatter(
            down_bgrad.astype(jnp.bfloat16), "fsdp", scatter_dimension=0, tiled=True
        ).astype(jnp.float32),
    )
    share_gain, share_shift, share_qkv, share_out, share_up, share_upb, share_down, share_downb = (
        shares
    )
    totals_out = lax.psum(
        (
            share_gain,
            share_shift,
            share_qkv,
            share_out,
            share_up,
            share_upb,
            share_down,
            share_downb,
        ),
        "ctx",
    )
    sum_gain, sum_shift, sum_qkv, sum_out, sum_up, sum_upb, sum_down, sum_downb = totals_out
    return (
        mixed,
        tokens_grad,
        sum_gain,
        sum_shift,
        sum_qkv,
        sum_out,
        sum_up,
        sum_upb,
        sum_down,
        sum_downb,
    )


F32 = jnp.float32
BF16 = jnp.bfloat16
FF = 4096
FSDP = 2
CHIPS = 8
ROWS = SEQ_DEV_TOK * SEQS
ALL = 4 * ROWS
LENGTH = CHIPS * 2 * SEQ_DEV_TOK
HALF = SEQ_DEV_TOK // 2
QB = 512
NCH = 12
MASKS = (1, 2, 4)
SCATTER = {4: (1, 0, 2), 5: (2, 0, 1), 7: (1, 0, 2)}
GATHER = {2: (2, 0, 1), 3: (2, 0, 1), 4: (2, 0, 1), 8: (2, 0, 1)}
MIDDLE = {0: (2, 1, 0), 6: (2, 1, 0), 9: (2, 1, 0), 10: (2, 1, 0), 11: (2, 1, 0)}
SCALE = HEAD_DIM**-0.5


def fits(mesh):
    return mesh.shape["fsdp"] == FSDP and mesh.shape["ctx"] == 2 * CHIPS


def dot(left, right):
    return lax.dot_general(left, right, (((1,), (0,)), ((), ())), preferred_element_type=F32)


def dot_nt(left, right):
    return lax.dot_general(left, right, (((1,), (1,)), ((), ())), preferred_element_type=F32)


def dot_tn(left, right):
    return lax.dot_general(left, right, (((0,), (0,)), ((), ())), preferred_element_type=F32)


def turn(values, cosine, sine):
    lane = lax.broadcasted_iota(jnp.int32, values.shape, 1)
    width = values.shape[1]
    other = jnp.where(
        lane % 2 == 0, pltpu.roll(values, width - 1, 1), pltpu.roll(values, 1, 1)
    )
    return values * cosine + other * sine


def gate(values):
    inner = 0.7978845608028654 * (values + 0.044715 * values * values * values)
    th = jnp.tanh(inner)
    half = 0.5 * (1.0 + th)
    slope = half + (0.5 * values) * (1.0 - th * th) * (
        0.7978845608028654 * (1.0 + 3 * 0.044715 * values * values)
    )
    return values * half, slope


def fused_kernel(
    pairs_ref,
    gain_ref,
    shift_ref,
    downb_ref,
    upb_ref,
    turns_h,
    tok_ref,
    cot_ref,
    wqkv_h,
    wout_h,
    wup_h,
    wdn_h,
    mixed_ref,
    tgrad_ref,
    small_ref,
    odn,
    oup,
    oqkv,
    oout,
    spots_ref,
    turns,
    vall,
    xs,
    nrm,
    gal,
    wq,
    wout,
    wup,
    wdn,
    hid,
    upg,
    sbuf,
    rbuf,
    aq,
    ag,
    ak,
    av,
    akt,
    avt,
    agt,
    sco,
    dka,
    dva,
    osrt,
    rb2,
    aall,
    dqkv,
    mats,
    rs0,
    rs1,
    rs2,
    xsw,
    rsm,
    own_acc,
    red_s,
    red_x,
    red_r,
    red_xr,
    sm,
    smg,
    sma,
    lsem,
    gsend,
    grecv,
    asend,
    arecv,
    osend,
    orecv,
    rssend,
    rsrecv,
    agsend,
    agrecv,
    clocal,
    csend,
    crecv,
    dsend,
    drecv,
    smsend,
    smrecv,
):
    f = lax.axis_index("fsdp")
    c = lax.axis_index("ctx")
    k = c % 2
    p = c // 2
    zz = p // 2
    yy = p % 2
    xpart = (1 - f, c)
    sibling = (f, 2 * p + 1 - k)
    diagonal = (1 - f, 2 * p + 1 - k)
    own = 2 * f + k
    sibb = 2 * f + 1 - k
    xb = 2 * (1 - f) + k
    dg = 2 * (1 - f) + 1 - k
    MESH = pl.DeviceIdType.MESH

    def member(q):
        return (f, 2 * q + k)

    def remote(src, dst, ssem, rsem, device):
        return pltpu.make_async_remote_copy(
            src_ref=src,
            dst_ref=dst,
            send_sem=ssem,
            recv_sem=rsem,
            device_id=device,
            device_id_type=MESH,
        )

    def rows(b):
        return pl.ds(pl.multiple_of(b * ROWS, ROWS), ROWS)

    def lanes(i, n):
        return pl.ds(pl.multiple_of(i * n, n), n)

    loads = [
        pltpu.make_async_copy(wqkv_h.at[:, lanes(k, 256)], wq.at[f], lsem.at[0]),
        pltpu.make_async_copy(
            wqkv_h.at[:, pl.ds(pl.multiple_of(1024 + 256 * k, 256), 256)], wq.at[1 + f], lsem.at[1]
        ),
        pltpu.make_async_copy(wup_h.at[:, lanes(k, 1024)], wup, lsem.at[2]),
        pltpu.make_async_copy(wdn_h.at[lanes(k, 1024), :], wdn, lsem.at[3]),
        pltpu.make_async_copy(wout_h.at[lanes(k, 256), :], wout, lsem.at[4]),
        pltpu.make_async_copy(turns_h, turns, lsem.at[5]),
    ]
    for load in loads:
        load.start()
    barrier = pltpu.get_barrier_semaphore()
    for device in [xpart, sibling, diagonal] + [member(p ^ i) for i in range(1, CHIPS)]:
        pl.semaphore_signal(barrier, inc=1, device_id=device, device_id_type=MESH)
    pl.semaphore_wait(barrier, 3 + CHIPS - 1)

    def row_of(ref, at):
        return ref[pl.ds(at, 512)].astype(F32).reshape(1, 512)

    vall[f] = jnp.concatenate(
        [row_of(gain_ref, 0), row_of(shift_ref, 0), row_of(downb_ref, 0)]
        + [row_of(upb_ref, 512 * i) for i in range(4)]
        + [jnp.zeros((1, 512), F32)],
        axis=0,
    )
    vec_copy = remote(vall.at[f], vall.at[f], gsend.at[0], grecv.at[0], xpart)
    vec_copy.start()
    swap_copy = remote(
        wqkv_h.at[:, pl.ds(pl.multiple_of(512 + 256 * k, 256), 256)],
        wq.at[2 * f],
        gsend.at[1],
        grecv.at[1],
        xpart,
    )
    swap_copy.start()

    def table_pair(i, carry):
        spots_ref[64 + 2 * i] = pairs_ref[i]
        spots_ref[64 + 2 * i + 1] = 4 * CHIPS - 1 - pairs_ref[i]
        return carry

    lax.fori_loop(0, 2 * CHIPS, table_pair, 0)
    step = 64

    def norm_rows(i, carry):
        here = pl.ds(pl.multiple_of(i * step, step), step)
        there = pl.ds(pl.multiple_of(own * ROWS + i * step, step), step)
        row = lax.broadcasted_iota(jnp.int32, (step, ROWS), 0) + i * step
        col = lax.broadcasted_iota(jnp.int32, (step, ROWS), 1)
        pick = (col == 2 * (row % SEQ_DEV_TOK) + row // SEQ_DEV_TOK).astype(F32).astype(BF16)
        values = dot(pick, tok_ref[...])
        gal[there, :] = dot(pick, cot_ref[...]).astype(BF16)
        xs[here, :] = values.astype(BF16)
        center = values - jnp.mean(values, axis=1, keepdims=True)
        spread = jnp.mean(center * center, axis=1, keepdims=True)
        own_acc[0, here, :] = center * lax.rsqrt(spread + EPS)
        return carry

    lax.fori_loop(0, ROWS // step, norm_rows, 0)
    vec_copy.wait()
    gain = jnp.concatenate([vall[0, 0:1, :], vall[1, 0:1, :]], axis=1).astype(F32)
    shift = jnp.concatenate([vall[0, 1:2, :], vall[1, 1:2, :]], axis=1).astype(F32)
    down_b = jnp.concatenate([vall[0, 2:3, :], vall[1, 2:3, :]], axis=1).astype(F32)


    def scale_rows(i, carry):
        here = pl.ds(pl.multiple_of(i * step, step), step)
        there = pl.ds(pl.multiple_of(own * ROWS + i * step, step), step)
        nrm[there, :] = (own_acc[0, here, :] * gain + shift).astype(BF16)
        return carry

    lax.fori_loop(0, ROWS // step, scale_rows, 0)

    def spread_copy(buf, b, n, device):
        return remote(buf.at[rows(b)], buf.at[rows(b)], gsend.at[n], grecv.at[n], device)

    n_sib = spread_copy(nrm, own, 2, sibling)
    n_x = spread_copy(nrm, own, 3, xpart)
    g_sib = spread_copy(gal, own, 4, sibling)
    g_x = spread_copy(gal, own, 5, xpart)
    n_dg = spread_copy(nrm, xb, 6, sibling)
    g_dg = spread_copy(gal, xb, 7, sibling)

    def up_part_of(b, i):
        at = k * 1024 + i * 256
        bias = vall[f, pl.ds(3 + at // 512, 1), pl.ds(pl.multiple_of(at % 512, 256), 256)]
        return gate(dot(nrm[rows(b), :], wup[:, lanes(i, 256)]) + bias)

    def feed_block(b):
        def part(i, carry):
            cols = lanes(i, 256)
            value, slope = up_part_of(b, i)
            hid[rows(b), cols] = value.astype(BF16)
            back = dot_nt(gal[rows(b), :], wdn[cols, :])
            upg[rows(b), cols] = (back * slope).astype(BF16)
            return carry

        lax.fori_loop(0, 4, part, 0)

    def feed_up(b, n):
        def part(i, carry):
            cols = lanes(i, 256)
            value, slope = up_part_of(b, i)
            hid[rows(b), cols] = value.astype(BF16)
            own_acc[n, :, cols] = slope
            return carry

        lax.fori_loop(0, 4, part, 0)

    def feed_back(b, n):
        def part(i, carry):
            cols = lanes(i, 256)
            back = dot_nt(gal[rows(b), :], wdn[cols, :])
            upg[rows(b), cols] = (back * own_acc[n, :, cols]).astype(BF16)
            return carry

        lax.fori_loop(0, 4, part, 0)

    def put_heads(first, second, fq, kq, t):
        for h in range(4):
            sbuf[2 * h + fq, t, kq] = jnp.concatenate(
                [first[:, 64 * h : 64 * h + 64], second[:, 64 * h : 64 * h + 64]], axis=1
            ).reshape(4, HALF, 128)

    def turned(values, kq):
        table = jnp.concatenate(
            [turns[spots_ref[64 + 2 * (2 * p + kq) + half]] for half in range(2)], axis=0
        )
        cosine = jnp.concatenate([table[:, :64], table[:, :64]], axis=1)
        sine = jnp.concatenate([table[:, 64:], table[:, 64:]], axis=1)
        parts = []
        for s in range(SEQS):
            line = []
            for half in range(2):
                piece = values[128 * s : 128 * s + 128, 128 * half : 128 * half + 128]
                line.append(turn(piece, cosine, sine))
            parts.append(jnp.concatenate(line, axis=1))
        return jnp.concatenate(parts, axis=0).astype(BF16)

    def kg_block(b, fq, kq):
        key = dot(nrm[rows(b), :], wq[1])
        grads = dot_nt(gal[rows(b), :], wout[...]).astype(BF16)
        put_heads(turned(key, kq), grads, fq, kq, 0)

    def qv_block(b, fq, kq):
        query = dot(nrm[rows(b), :], wq[0])
        value = dot(nrm[rows(b), :], wq[2]).astype(BF16)
        put_heads(turned(query, kq) * BF16(SCALE), value, fq, kq, 1)

    def in_copy(q, t, kq):
        return remote(
            sbuf.at[q, t, kq],
            rbuf.at[2 * p + kq, t],
            asend.at[q, t, kq],
            arecv.at[p, t, kq],
            member(q),
        )

    def send_block(fq, kq, t):
        for i in range(4):
            q = 2 * (zz ^ i) + fq
            if i == 0:

                @pl.when(fq == yy)
                def _():
                    pltpu.make_async_copy(
                        sbuf.at[q, t, kq], rbuf.at[2 * p + kq, t], arecv.at[p, t, kq]
                    ).start()

                @pl.when(fq != yy)
                def _():
                    in_copy(q, t, kq).start()
            else:
                in_copy(q, t, kq).start()

    def sent_block(fq, kq, t):
        for i in range(4):
            q = 2 * (zz ^ i) + fq
            if i == 0:

                @pl.when(fq != yy)
                def _():
                    in_copy(q, t, kq).wait_send()
            else:
                in_copy(q, t, kq).wait_send()

    def store_rows(ch, i, values):
        mats[ch, i // 2, i % 2] = values.reshape(2, 128, 256)

    def down_part(i, carry):
        full = dot_tn(hid[:, lanes(i, 256)], gal[...]).astype(BF16)
        for cc in range(4):
            store_rows(cc, i, full[:, 256 * cc : 256 * cc + 256])
        return carry

    def up_part(i, carry):
        full = dot_tn(nrm[:, lanes(i, 256)], upg[...]).astype(BF16)
        for cc in range(4):
            store_rows(4 + cc, i, full[:, 256 * cc : 256 * cc + 256])
        return carry

    bits = [(p // mask) % 2 for mask in MASKS]
    every = slice(None)

    def block_index(free, other=None):
        return tuple(
            every if dim in free else (1 - bits[dim] if dim == other else bits[dim])
            for dim in range(3)
        )

    def scatter_order(ch):
        return SCATTER.get(ch, (0, 1, 2))

    def gather_order(ch):
        return GATHER.get(ch, (2, 1, 0))

    rsb = (rs0, rs1, rs2)

    middle = jnp.logical_or(zz == 1, zz == 2)
    outer = jnp.logical_not(middle)
    half_z = zz // 2
    inner_chip = 2 * (1 + half_z) + yy
    other_chip = 2 * (3 - zz) + yy
    outer_chip = 6 * half_z + yy

    def middle_in(ch, ph):
        if ph == 0:
            src, dst, q = mats.at[ch, 1 - yy], rs0.at[ch], p ^ 1
        elif ph == 1:
            src, dst, q = mats.at[ch, yy], rsm.at[sorted(MIDDLE).index(ch)], inner_chip
        else:
            src, dst, q = mats.at[ch, yy, :, 1 - half_z], rs1.at[ch], other_chip
        return remote(src, dst, rssend.at[ch, ph], rsrecv.at[ch, ph], member(q))

    def middle_out(ch, step):
        order = MIDDLE[ch]
        kind = order[step]
        done = order[:step]
        index = (every if 0 in done else yy, every, every if 2 in done else half_z)
        there = out_slice(ch, k, index)
        src = middle_shard(ch) if step == 0 else there
        q = (p ^ 1, outer_chip, other_chip)[kind]
        return remote(src, there, agsend.at[ch, step], agrecv.at[ch, step], member(q))

    def middle_shard(ch):
        return xsw if ch == 10 else mats.at[ch, yy, :, half_z]

    def middle_swap():
        return remote(mats.at[10, yy, :, half_z], xsw, gsend.at[8], grecv.at[8], xpart)

    def middle_local(ch):
        there = out_slice(ch, k, (yy, every, half_z))
        return pltpu.make_async_copy(middle_shard(ch), there, clocal.at[ch])

    def sends_out(ch, step):
        order = MIDDLE[ch]
        return order[step] == 0 and 1 in order[:step]

    def wait_out(ch, step):
        if sends_out(ch, step):
            middle_out(ch, step).wait_recv()
        else:

            @pl.when(outer if MIDDLE[ch][step] == 1 else middle)
            def _():
                middle_out(ch, step).wait_recv()

    def start_out(ch, step):
        if sends_out(ch, step):
            middle_out(ch, step).start()
        else:

            @pl.when(middle)
            def _():
                middle_out(ch, step).start()

    def add_blocks(ch, pairs):
        for here, there in pairs:
            mats[(ch,) + here] = (mats[(ch,) + here].astype(F32) + there.astype(F32)).astype(BF16)

    def advance_middle(ch, stage):
        if stage == 0:
            middle_in(ch, 0).start()
        elif stage == 1:
            middle_in(ch, 0).wait_recv()
            add_blocks(ch, [((yy, i, j), rs0[ch, i, j]) for i in range(2) for j in range(2)])

            @pl.when(outer)
            def _():
                middle_in(ch, 1).start()
        elif stage == 2:

            @pl.when(middle)
            def _():
                middle_in(ch, 1).wait_recv()
                n = sorted(MIDDLE).index(ch)
                add_blocks(ch, [((yy, i, j), rsm[n, i, j]) for i in range(2) for j in range(2)])
                middle_in(ch, 2).start()
        elif stage == 3:

            @pl.when(middle)
            def _():
                middle_in(ch, 2).wait_recv()
                add_blocks(ch, [((yy, i, half_z), rs1[ch, i]) for i in range(2)])
                if ch == 10:
                    middle_swap().start()
                    middle_swap().wait_recv()
                middle_local(ch).start()
                middle_out(ch, 0).start()
        elif stage == 4:
            wait_out(ch, 0)

            @pl.when(middle)
            def _():
                middle_local(ch).wait()

            start_out(ch, 1)
        elif stage == 5:
            wait_out(ch, 1)
            start_out(ch, 2)
        elif stage == 6:
            wait_out(ch, 2)
            core_copy(ch).start()
        elif stage == 7:
            core_copy(ch).wait_recv()

    def settle_middle(ch):
        middle_in(ch, 0).wait_send()

        @pl.when(outer)
        def _():
            middle_in(ch, 1).wait_send()

        @pl.when(middle)
        def _():
            middle_in(ch, 2).wait_send()
            if ch == 10:
                middle_swap().wait_send()

        for step in range(3):
            if sends_out(ch, step):
                middle_out(ch, step).wait_send()
            else:

                @pl.when(middle)
                def _():
                    middle_out(ch, step).wait_send()

        core_copy(ch).wait_send()

    def rs_copy(ch, ph):
        order = scatter_order(ch)
        return remote(
            mats.at[(ch,) + block_index(order[ph + 1 :], order[ph])],
            rsb[ph].at[ch],
            rssend.at[ch, ph],
            rsrecv.at[ch, ph],
            member(p ^ MASKS[order[ph]]),
        )

    def rs_add(ch, ph):
        free = sorted(scatter_order(ch)[ph + 1 :])
        rs_copy(ch, ph).wait_recv()
        for n in range(2 ** len(free)):
            spot = {dim: (n >> i) % 2 for i, dim in enumerate(free)}
            here = (ch,) + tuple(spot.get(dim, bits[dim]) for dim in range(3))
            there = (ch,) + tuple(spot[dim] for dim in free)
            mats[here] = (mats[here].astype(F32) + rsb[ph][there].astype(F32)).astype(BF16)

    def out_slice(ch, kk, index):
        if ch < 4:
            return odn.at[(kk,) + index + (every, slice(256 * ch, 256 * ch + 256))]
        if ch < 8:
            start, out = kk * 1024 + (ch - 4) * 256, oup
        elif ch < 11:
            start, out = (0, 1024, 512)[ch - 8] + kk * 256, oqkv
        else:
            start, out = kk * 256, oout
        return out.at[index + (every, pl.ds(pl.multiple_of(start, 256), 256))]

    def shard(ch):
        if ch == 10:
            return xsw.at[0]
        return mats.at[(ch,) + block_index(())]

    def swap_shard():
        return remote(
            mats.at[(10,) + block_index(())], xsw.at[0], gsend.at[8], grecv.at[8], xpart
        )

    def local_copy(ch):
        return pltpu.make_async_copy(
            shard(ch), out_slice(ch, k, block_index(())), clocal.at[ch]
        )

    def ag_copy(ch, step):
        order = gather_order(ch)
        there = out_slice(ch, k, block_index(order[:step]))
        return remote(
            shard(ch) if step == 0 else there,
            there,
            agsend.at[ch, step],
            agrecv.at[ch, step],
            member(p ^ MASKS[order[step]]),
        )

    def core_copy(ch):
        return remote(
            out_slice(ch, k, (every,) * 3),
            out_slice(ch, k, (every,) * 3),
            csend.at[ch],
            crecv.at[ch],
            sibling,
        )

    def advance(ch, stage):
        if ch in MIDDLE:
            advance_middle(ch, stage)
        elif stage == 0:
            rs_copy(ch, 0).start()
        elif stage <= 2:
            rs_add(ch, stage - 1)
            rs_copy(ch, stage).start()
        elif stage == 3:
            rs_add(ch, 2)
            if ch == 10:
                swap_shard().start()
                swap_shard().wait_recv()
            local_copy(ch).start()
            ag_copy(ch, 0).start()
        elif stage == 4:
            ag_copy(ch, 0).wait_recv()
            local_copy(ch).wait()
            ag_copy(ch, 1).start()
        elif stage == 5:
            ag_copy(ch, 1).wait_recv()
            ag_copy(ch, 2).start()
        elif stage == 6:
            ag_copy(ch, 2).wait_recv()
            core_copy(ch).start()
        elif stage == 7:
            core_copy(ch).wait_recv()

    def settle(ch):
        if ch in MIDDLE:
            settle_middle(ch)
            return
        for ph in range(3):
            rs_copy(ch, ph).wait_send()
            ag_copy(ch, ph).wait_send()
        core_copy(ch).wait_send()
        if ch == 10:
            swap_shard().wait_send()

    def load_half(place, t, u):
        return rbuf[spots_ref[place], t, 2 * u + spots_ref[32 + place]]

    def sort_unit(u):
        def sort_rows(i, carry):
            here = pl.ds(pl.multiple_of(i * 128, 128), 128)
            kg = jnp.concatenate([load_half(2 * i, 0, u), load_half(2 * i + 1, 0, u)], axis=0)
            qv = jnp.concatenate([load_half(2 * i, 1, u), load_half(2 * i + 1, 1, u)], axis=0)
            ak[here, :] = kg[:, :64]
            ag[here, :] = kg[:, 64:]
            aq[here, :] = qv[:, :64]
            av[here, :] = qv[:, 64:]
            kgt = kg.T
            akt[:, here] = kgt[:64, :]
            agt[:, here] = kgt[64:, :]
            avt[:, here] = qv.T[64:, :]
            return carry

        lax.fori_loop(0, LENGTH // 128, sort_rows, 0)

    def fold(values):
        return values.reshape(values.shape[0] // 8, 8, values.shape[1])

    def query_block(qb):
        mine = slice(qb * QB, qb * QB + QB)
        tiles = [slice(i * QB, i * QB + QB) for i in range(qb + 1)]
        query = aq[mine, :]
        grads = ag[mine, :]
        top = jnp.full((8, QB), masked_score, F32)
        for i, tile in enumerate(tiles):
            score = dot_nt(ak[tile, :], query)
            if i == qb:
                row = lax.broadcasted_iota(jnp.int32, (QB, QB), 0)
                col = lax.broadcasted_iota(jnp.int32, (QB, QB), 1)
                score = jnp.where(row <= col, score, masked_score)
            sco[tile, :] = score
            top = jnp.maximum(top, jnp.max(fold(score), axis=0))
        top = jnp.max(top, axis=0, keepdims=True)
        total = jnp.zeros((8, QB), F32)
        mix = jnp.zeros((HEAD_DIM, QB), F32)
        for tile in tiles:
            weights = jnp.exp(sco[tile, :] - top)
            sco[tile, :] = weights
            total = total + jnp.sum(fold(weights), axis=0)
            mix = mix + dot(avt[:, tile], weights.astype(BF16))
        inverse = 1.0 / jnp.sum(total, axis=0, keepdims=True)
        mix = mix * inverse
        dots = jnp.sum(agt[:, mine].astype(F32) * mix, axis=0, keepdims=True)
        back = jnp.zeros((HEAD_DIM, QB), F32)
        for i, tile in enumerate(tiles):
            chances = sco[tile, :] * inverse
            slopes = dot_nt(av[tile, :], grads)
            score_grads = (chances * (slopes - dots)).astype(BF16)
            value_part = dot(chances.astype(BF16), grads)
            key_part = dot(score_grads, query)
            if qb == LENGTH // QB - 1:
                dva[tile, :] = value_part
                dka[tile, :] = key_part
            else:
                dva[tile, :] += value_part
                dka[tile, :] += key_part
            back = back + dot(akt[:, tile], score_grads)
        place(0, qb, jnp.concatenate([mix, back * SCALE], axis=0).T)

    def place(t, qb, both):
        n = QB // HALF
        table = turns[qb * n : qb * n + n].reshape(QB, 128)
        cosine = jnp.concatenate([jnp.ones((QB, 64), F32), table[:, :64]], axis=1)
        sine = jnp.concatenate([jnp.zeros((QB, 64), F32), -table[:, 64:]], axis=1)
        osrt[t, qb * n : qb * n + n] = turn(both, cosine, sine).astype(BF16).reshape(n, HALF, 128)

    def finish_half(u, half):
        for qb in (2 * half, 2 * half + 1):
            mine = slice(qb * QB, qb * QB + QB)
            place(1, qb, jnp.concatenate([dva[mine, :], dka[mine, :]], axis=1))

        def unsort(i, carry):
            for t in range(2):
                sbuf[i // 2, u, t, 2 * half + i % 2] = osrt[t, spots_ref[64 + 2 * i + half]]
            return carry

        lax.fori_loop(0, 2 * CHIPS, unsort, 0)

    def send_half(u, half):
        pltpu.make_async_copy(
            out_part(sbuf, p, u, half), out_part(rb2, p, u, half), orecv.at[p, u, half]
        ).start()
        for i in (4, 6, 2, 5, 7, 3, 1):
            out_copy(p ^ i, u, half).start()

    def out_part(buf, q, u, half):
        return buf.at[q, u, :, pl.ds(2 * half, 2)]

    def out_copy(q, u, half):
        return remote(
            out_part(sbuf, q, u, half),
            out_part(rb2, p, u, half),
            osend.at[q, u, half],
            orecv.at[p, u, half],
            member(q),
        )

    def run(*steps):
        for ch, stage in steps:
            advance(ch, stage)

    def out_rows(q, u, t, kq):
        return jnp.concatenate([rb2[q, u, t, kq], rb2[q, u, t, 2 + kq]], axis=0)

    def att_part(i, carry):
        here = lanes(i, 256)
        left = nrm[:, here]
        for slot in range(3):
            at = 8 + (slot - f + 3) % 3
            store_rows(at, i, dot_tn(left, dqkv[slot]).astype(BF16))
        store_rows(11, i, dot_tn(gal[:, here], aall[...]).astype(BF16))
        return carry

    def normed_part(b, cols):
        here = rows(b)
        total = dot_nt(upg[here, :], wup[cols, :])
        for slot in range(3):
            total = total + dot_nt(dqkv[slot, here, :], wq[slot, cols, :])
        return total

    def mixed_part(b, cols):
        here = rows(b)
        return dot(hid[here, :], wdn[:, cols]) + dot(aall[here, :], wout[:, cols])

    def reduce_copies(n):
        return (
            remote(red_s.at[n, 0], red_r.at[n, 0], dsend.at[n, 0], drecv.at[n, 0], sibling),
            remote(red_s.at[n, 1], red_r.at[n, 1], dsend.at[n, 1], drecv.at[n, 1], sibling),
            remote(red_x.at[n], red_xr.at[n], dsend.at[n, 2], drecv.at[n, 2], xpart),
        )

    parts = (normed_part, mixed_part)

    def reduce_first(n):
        copies = reduce_copies(n)
        for slot, b in ((1, dg), (0, sibb)):

            def fill(i, carry):
                red_s[n, slot, :, lanes(i, 256)] = parts[n](b, lanes(i, 256)).astype(BF16)
                return carry

            lax.fori_loop(0, 4, fill, 0)
            copies[slot].start()

    def reduce_second(n):
        copies = reduce_copies(n)
        copies[1].wait_recv()

        def fill(i, carry):
            cols = lanes(i, 256)
            red_x[n, :, cols] = (
                parts[n](xb, cols) + red_r[n, 1, :, cols].astype(F32)
            ).astype(BF16)
            return carry

        lax.fori_loop(0, 4, fill, 0)
        copies[2].start()

    def reduce_third(n):
        copies = reduce_copies(n)

        def fill(i, carry):
            cols = lanes(i, 256)
            own_acc[n, :, cols] = parts[n](own, cols)
            return carry

        lax.fori_loop(0, 4, fill, 0)
        copies[0].wait_recv()
        copies[2].wait_recv()

        def finish(i, carry):
            cols = lanes(i, 256)
            own_acc[n, :, cols] = (
                own_acc[n, :, cols]
                + red_r[n, 0, :, cols].astype(F32)
                + red_xr[n, :, cols].astype(F32)
            )
            return carry

        lax.fori_loop(0, 4, finish, 0)

    def out_pick():
        row = lax.broadcasted_iota(jnp.int32, (ROWS, ROWS), 0)
        col = lax.broadcasted_iota(jnp.int32, (ROWS, ROWS), 1)
        return (row == 2 * (col % SEQ_DEV_TOK) + col // SEQ_DEV_TOK).astype(F32).astype(BF16)

    def back_rows(i, carry):
        dgain, dshift = carry
        here = pl.ds(pl.multiple_of(i * step, step), step)
        there = pl.ds(pl.multiple_of(own * ROWS + i * step, step), step)
        values = xs[here, :].astype(F32)
        center = values - jnp.mean(values, axis=1, keepdims=True)
        spread = lax.rsqrt(jnp.mean(center * center, axis=1, keepdims=True) + EPS)
        hat = center * spread
        grads = own_acc[0, here, :]
        dgain = dgain + jnp.sum(grads * hat, axis=0, keepdims=True)
        dshift = dshift + jnp.sum(grads, axis=0, keepdims=True)
        inner = grads * gain
        inner = spread * (
            inner
            - jnp.mean(inner, axis=1, keepdims=True)
            - hat * jnp.mean(inner * hat, axis=1, keepdims=True)
        )
        xs2 = gal[there, :].astype(F32) + inner
        red_s[0, 0, here, :] = xs2.astype(BF16)
        return dgain, dshift

    def mixed_rows(i, carry):
        here = pl.ds(pl.multiple_of(i * step, step), step)
        red_s[1, 0, here, :] = (xs[here, :].astype(F32) + own_acc[1, here, :] + down_b).astype(
            BF16
        )
        return carry

    for copy in (n_sib, n_x):
        copy.start()
    for load in loads:
        load.wait()
    kg_block(own, f, k)
    send_block(f, k, 0)
    for copy in (g_sib, g_x):
        copy.start()
    n_sib.wait_recv()
    g_sib.wait_recv()
    kg_block(sibb, f, 1 - k)
    send_block(f, 1 - k, 0)
    swap_copy.wait_recv()
    qv_block(sibb, f, 1 - k)
    send_block(f, 1 - k, 1)
    qv_block(own, f, k)
    send_block(f, k, 1)
    feed_block(own)
    def table_row(b, carry):
        holder = jnp.int32(0)
        half = jnp.int32(0)
        for i in range(2 * CHIPS):
            first = (pairs_ref[i] == b).astype(jnp.int32)
            last = (4 * CHIPS - 1 - pairs_ref[i] == b).astype(jnp.int32)
            holder = holder + i * (first + last)
            half = half + last
        spots_ref[b] = jnp.minimum(holder, 2 * CHIPS - 1)
        spots_ref[4 * CHIPS + b] = jnp.minimum(half, 1)
        return carry

    lax.fori_loop(0, 4 * CHIPS, table_row, 0)

    n_x.wait_recv()
    n_dg.start()
    qv_block(xb, 1 - f, k)
    send_block(1 - f, k, 1)
    n_dg.wait_recv()
    qv_block(dg, 1 - f, 1 - k)
    send_block(1 - f, 1 - k, 1)
    feed_up(dg, 1)
    feed_up(xb, 0)
    g_x.wait_recv()
    g_dg.start()
    kg_block(xb, 1 - f, k)
    send_block(1 - f, k, 0)
    feed_block(sibb)
    feed_back(xb, 0)
    g_dg.wait_recv()
    kg_block(dg, 1 - f, 1 - k)
    send_block(1 - f, 1 - k, 0)
    feed_back(dg, 1)
    lax.fori_loop(0, 4, up_part, 0)
    sm[...] = jnp.zeros_like(sm)
    sm[0:1, :] = jnp.sum(upg[...].astype(F32), axis=0, keepdims=True)
    sm[2:3, :] = jnp.sum(gal[...].astype(F32), axis=0, keepdims=True)
    run((4, 0))
    lax.fori_loop(0, 4, down_part, 0)
    run((5, 0), (7, 0))
    for fq, kq in ((f, k), (f, 1 - k), (1 - f, k), (1 - f, 1 - k)):
        for t in range(2):
            sent_block(fq, kq, t)
    for q in range(CHIPS):
        for t in range(2):
            for kq in range(2):
                pltpu.make_async_copy(
                    rbuf.at[2 * q + kq, t], rbuf.at[2 * q + kq, t], arecv.at[q, t, kq]
                ).wait()

    sort_unit(0)
    run((0, 0), (3, 0))
    query_block(3)
    query_block(2)
    finish_half(0, 1)
    send_half(0, 1)
    query_block(1)
    query_block(0)
    finish_half(0, 0)
    send_half(0, 0)
    run((5, 1))
    sort_unit(1)
    run((6, 0))
    query_block(3)
    query_block(2)
    finish_half(1, 1)
    run((4, 1))
    query_block(1)
    query_block(0)
    finish_half(1, 0)
    run((0, 1), (5, 2))
    send_half(1, 0)
    run((1, 0))
    send_half(1, 1)
    run((4, 2), (5, 3))
    run((2, 0), (0, 2), (1, 1), (6, 1), (3, 1))
    for q in range(CHIPS):
        for u in range(SEQS):
            for half in range(2):
                arrived = out_part(rb2, q, u, half)
                pltpu.make_async_copy(arrived, arrived, orecv.at[q, u, half]).wait()

    for fq in range(2):
        for kq in range(2):
            for u in range(SEQS):
                at = (2 * fq + kq) * ROWS + u * 128
                here = slice(at, at + 128)
                for pair in range(2):
                    cols = slice(128 * pair, 128 * pair + 128)
                    x0 = out_rows(4 * pair + fq, u, 0, kq)
                    x1 = out_rows(4 * pair + 2 + fq, u, 0, kq)
                    y0 = out_rows(4 * pair + fq, u, 1, kq)
                    y1 = out_rows(4 * pair + 2 + fq, u, 1, kq)
                    aall[here, cols] = jnp.concatenate([x0[:, :64], x1[:, :64]], axis=1)
                    dqkv[0, here, cols] = jnp.concatenate([x0[:, 64:], x1[:, 64:]], axis=1)
                    dqkv[2, here, cols] = jnp.concatenate([y0[:, :64], y1[:, :64]], axis=1)
                    dqkv[1, here, cols] = jnp.concatenate([y0[:, 64:], y1[:, 64:]], axis=1)

    run((7, 1))
    lax.fori_loop(0, 4, att_part, 0)
    run((9, 0), (4, 3), (2, 1), (1, 2), (8, 0), (5, 4))
    run((0, 3))
    reduce_first(0)
    run((6, 2), (10, 0), (9, 1), (0, 4), (2, 2), (4, 4), (6, 3), (8, 1))
    run((1, 3), (3, 2), (6, 4), (10, 1), (11, 0), (9, 2), (2, 3), (0, 5))
    reduce_second(0)
    run((9, 3), (5, 5), (4, 5), (8, 2), (9, 4), (10, 2), (3, 3), (7, 2))
    run((11, 1), (0, 6), (2, 4), (6, 5), (10, 3), (1, 4), (9, 5), (5, 6))
    run((8, 3), (2, 5), (10, 4))
    run((0, 7), (11, 2), (3, 4), (1, 5), (11, 3), (6, 6), (4, 6), (7, 3))
    run((11, 4), (8, 4))
    reduce_first(1)
    run((10, 5), (2, 6), (4, 7))
    reduce_second(1)
    run((7, 4), (3, 5), (1, 6), (8, 5))
    reduce_third(0)
    reduce_copies(0)[0].wait_send()
    dgain, dshift = lax.fori_loop(
        0, ROWS // step, back_rows, (jnp.zeros((1, D), F32), jnp.zeros((1, D), F32))
    )
    tgrad_ref[...] = dot(out_pick(), red_s[0, 0]).astype(BF16)
    sm[3:4, :] = dgain
    sm[4:5, :] = dshift

    small_copies = [
        remote(sm, smg.at[own], smsend.at[0], smrecv.at[own], sibling),
        remote(sm, smg.at[own], smsend.at[1], smrecv.at[own], xpart),
        remote(sm, smg.at[own], smsend.at[2], smrecv.at[own], diagonal),
    ]
    for copy in small_copies:
        copy.start()

    run((11, 5), (7, 5), (10, 6), (9, 6))
    reduce_third(1)
    reduce_copies(1)[0].wait_send()
    lax.fori_loop(0, ROWS // step, mixed_rows, 0)
    mixed_ref[...] = dot(out_pick(), red_s[1, 0]).astype(BF16)

    run((5, 7), (3, 6), (2, 7))
    smg[own] = sm[...]
    for b in (sibb, xb, dg):
        remote(sm, smg.at[b], smsend.at[0], smrecv.at[b], sibling).wait_recv()
    for copy in small_copies:
        copy.wait_send()
    first_b = 2 * f
    sma[p, 0:1, :] = smg[first_b, 0:1, :]
    sma[p, 1:2, :] = smg[first_b + 1, 0:1, :]
    sma[p, 2:3, :] = sm[2:3, :]
    sma[p, 3:8, :] = smg[0, 3:8, :] + smg[1, 3:8, :] + smg[2, 3:8, :] + smg[3, 3:8, :]
    sm_copies = [
        remote(sma.at[p], sma.at[p], smsend.at[2 + i], smrecv.at[3 + i], member(p ^ i))
        for i in range(1, CHIPS)
    ]
    for copy in sm_copies:
        copy.start()

    run((11, 6), (9, 7), (1, 7), (7, 6), (8, 6), (11, 7), (8, 7), (7, 7))
    run((10, 7), (3, 7), (6, 7))
    total = jnp.zeros((8, D), F32)
    for copy in sm_copies:
        copy.wait()
    for q in range(CHIPS):
        total = total + sma[q]
    small_ref[...] = total

    for copy in (vec_copy,):
        pass
    swap_copy.wait_send()
    for copy in (n_sib, n_x, g_sib, g_x, n_dg, g_dg):
        copy.wait_send()
    for u in range(SEQS):
        for i in range(1, CHIPS):
            for half in range(2):
                out_copy(p ^ i, u, half).wait_send()
    for n in range(2):
        copies = reduce_copies(n)
        copies[1].wait_send()
        copies[2].wait_send()
    for ch in range(NCH):
        settle(ch)


def widen_kernel(
    dn_h,
    up_h,
    qkv_h,
    out_h,
    small_h,
    mixed_h,
    tgrad_h,
    dn_o,
    up_o,
    qkv_o,
    out_o,
    mixed_o,
    tgrad_o,
    gain_o,
    shift_o,
    upb_o,
    downb_o,
    dn_b,
    up_b,
    qkv_b,
    out_b,
    dn_f,
    up_f,
    qkv_f,
    out_f,
    small,
    gain_f,
    shift_f,
    downb_f,
    upb_f,
    both,
    isem,
    osem,
    psem,
):
    f = lax.axis_index("fsdp")
    brief = (up_b, dn_b, qkv_b, out_b)
    wide = (up_f, dn_f, qkv_f, out_f)
    results = (up_o, dn_o, qkv_o, out_o)
    heights = (128, 256, 128, 128)
    half = D // FSDP

    def fetch(n, i):
        src = dn_h.at[pl.ds(2 * i, 2)] if n == 1 else (up_h, dn_h, qkv_h, out_h)[n].at[i]
        return pltpu.make_async_copy(src, brief[n].at[i], isem.at[n, i])

    def put(n, i):
        if n == 3:
            return pltpu.make_async_copy(out_f, out_o, osem.at[3, 0])
        rows = pl.ds(i * heights[n], heights[n])
        return pltpu.make_async_copy(wide[n].at[rows], results[n].at[rows], osem.at[n, i])

    order = [(n, i) for n in (1, 3, 0, 2) for i in range(8)]
    for n, i in order:
        fetch(n, i).start()
    get_small = pltpu.make_async_copy(small_h, small, psem.at[0])
    get_small.start()
    gets = [
        pltpu.make_async_copy(mixed_h, both.at[0], psem.at[1]),
        pltpu.make_async_copy(tgrad_h, both.at[1], psem.at[2]),
    ]
    for copy in gets:
        copy.start()
    puts = []
    for n, i in order:
        fetch(n, i).wait()
        values = brief[n][i].astype(F32)
        if n == 3:
            out_f[:, i * 128 : i * 128 + 128] = values.T
        else:
            wide[n][i * heights[n] : (i + 1) * heights[n], :] = values.reshape(heights[n], -1)
        if n < 3 or i == 7:
            puts.append(put(n, i))
            puts[-1].start()
        if (n, i) == (1, 0):
            get_small.wait()
            pick = jnp.where(f == 0, small[:, :half], small[:, half:])
            vectors = ((3, gain_f, gain_o), (4, shift_f, shift_o), (2, downb_f, downb_o))
            for row, (at, near, out) in enumerate(vectors):
                near[...] = pick[at]
                puts.append(pltpu.make_async_copy(near, out, psem.at[3 + row]))
                puts[-1].start()
            for slot, out in ((0, mixed_o), (1, tgrad_o)):
                gets[slot].wait()
                puts.append(pltpu.make_async_copy(both.at[slot], out, psem.at[1 + slot]))
                puts[-1].start()
            upb_f[:1024] = small[0]
            upb_f[1024:] = small[1]
            puts.append(pltpu.make_async_copy(upb_f, upb_o, psem.at[6]))
            puts[-1].start()
    for copy in puts:
        copy.wait()


def widen(dn, up, qkv, out_t, small, mixed, tokens_grad):
    hbm = pl.BlockSpec(memory_space=pl.ANY)
    half = D // FSDP
    feeds = FF // FSDP
    heads = 3 * D // FSDP
    return pl.pallas_call(
        widen_kernel,
        out_shape=(
            jax.ShapeDtypeStruct((feeds, D), F32),
            jax.ShapeDtypeStruct((D, feeds), F32),
            jax.ShapeDtypeStruct((D, heads), F32),
            jax.ShapeDtypeStruct((half, D), F32),
            jax.ShapeDtypeStruct((ROWS, D), BF16),
            jax.ShapeDtypeStruct((ROWS, D), BF16),
            jax.ShapeDtypeStruct((half,), F32),
            jax.ShapeDtypeStruct((half,), F32),
            jax.ShapeDtypeStruct((feeds,), F32),
            jax.ShapeDtypeStruct((half,), F32),
        ),
        in_specs=[hbm] * 7,
        out_specs=(hbm,) * 10,
        scratch_shapes=[
            pltpu.VMEM((8, 2, 128, D), BF16),
            pltpu.VMEM((8, 128, feeds), BF16),
            pltpu.VMEM((8, 128, heads), BF16),
            pltpu.VMEM((8, 128, half), BF16),
            pltpu.VMEM((feeds, D), F32),
            pltpu.VMEM((D, feeds), F32),
            pltpu.VMEM((D, heads), F32),
            pltpu.VMEM((half, D), F32),
            pltpu.VMEM((8, D), F32),
            pltpu.VMEM((half,), F32),
            pltpu.VMEM((half,), F32),
            pltpu.VMEM((half,), F32),
            pltpu.VMEM((feeds,), F32),
            pltpu.VMEM((2, ROWS, D), BF16),
            pltpu.SemaphoreType.DMA((4, 8)),
            pltpu.SemaphoreType.DMA((4, 8)),
            pltpu.SemaphoreType.DMA((7,)),
        ],
        compiler_params=pltpu.CompilerParams(vmem_limit_bytes=56 * 2**20),
    )(
        dn.reshape(16, 128, D),
        up.reshape(8, 128, feeds),
        qkv.reshape(8, 128, heads),
        out_t.reshape(8, 128, half),
        small,
        mixed,
        tokens_grad,
    )


def turn_table():
    lane = np.arange(HEAD_DIM)
    speeds = (10000.0 ** (-(lane // 2 * 2) / ROT_DIM)).astype(np.float32)
    phase = np.arange(LENGTH, dtype=np.float32)[:, None] * speeds[None, :]
    turning = (lane < ROT_DIM)[None, :]
    sign = np.where(lane % 2 == 0, -1.0, 1.0)[None, :]
    cosine = np.where(turning, np.cos(phase), 1.0)
    sine = np.where(turning, np.sin(phase) * sign, 0.0)
    table = np.concatenate((cosine, sine), axis=1).astype(np.float32)
    return table.reshape(4 * CHIPS, HALF, 2 * HEAD_DIM)


def fused_device(
    tokens,
    block_pairs,
    norm_gain,
    norm_bias,
    qkv_weight,
    out_weight,
    up_weight,
    up_bias,
    down_weight,
    down_bias,
    cotangent,
):
    vm = pl.BlockSpec(memory_space=pltpu.VMEM)
    sme = pl.BlockSpec(memory_space=pltpu.SMEM)
    hbm = pl.BlockSpec(memory_space=pl.ANY)
    dma = pltpu.SemaphoreType.DMA
    scratch = [
        pltpu.SMEM((96,), jnp.int32),
        pltpu.VMEM((4 * CHIPS, HALF, 128), F32),
        pltpu.VMEM((2, 8, 512), F32),
        pltpu.VMEM((ROWS, D), BF16),
        pltpu.VMEM((ALL, D), BF16),
        pltpu.VMEM((ALL, D), BF16),
        pltpu.VMEM((3, D, 256), BF16),
        pltpu.VMEM((256, D), BF16),
        pltpu.VMEM((D, 1024), BF16),
        pltpu.VMEM((1024, D), BF16),
        pltpu.VMEM((ALL, 1024), BF16),
        pltpu.VMEM((ALL, 1024), BF16),
        pltpu.VMEM((CHIPS, 2, 2, 4, HALF, 128), BF16),
        pltpu.VMEM((2 * CHIPS, 2, 4, HALF, 128), BF16),
        pltpu.VMEM((LENGTH, HEAD_DIM), BF16),
        pltpu.VMEM((LENGTH, HEAD_DIM), BF16),
        pltpu.VMEM((LENGTH, HEAD_DIM), BF16),
        pltpu.VMEM((LENGTH, HEAD_DIM), BF16),
        pltpu.VMEM((HEAD_DIM, LENGTH), BF16),
        pltpu.VMEM((HEAD_DIM, LENGTH), BF16),
        pltpu.VMEM((HEAD_DIM, LENGTH), BF16),
        pltpu.VMEM((LENGTH, QB), F32),
        pltpu.VMEM((LENGTH, HEAD_DIM), F32),
        pltpu.VMEM((LENGTH, HEAD_DIM), F32),
        pltpu.VMEM((2, 4 * CHIPS, HALF, 128), BF16),
        pltpu.VMEM((CHIPS, SEQS, 2, 4, HALF, 128), BF16),
        pltpu.VMEM((ALL, 256), BF16),
        pltpu.VMEM((3, ALL, 256), BF16),
        pltpu.VMEM((NCH, 2, 2, 2, 128, 256), BF16),
        pltpu.VMEM((NCH, 2, 2, 128, 256), BF16),
        pltpu.VMEM((NCH, 2, 128, 256), BF16),
        pltpu.VMEM((NCH, 128, 256), BF16),
        pltpu.VMEM((2, 128, 256), BF16),
        pltpu.VMEM((max(len(MIDDLE), 1), 2, 2, 128, 256), BF16),
        pltpu.VMEM((2, ROWS, D), F32),
        pltpu.VMEM((2, 2, ROWS, D), BF16),
        pltpu.VMEM((2, ROWS, D), BF16),
        pltpu.VMEM((2, 2, ROWS, D), BF16),
        pltpu.VMEM((2, ROWS, D), BF16),
        pltpu.VMEM((8, D), F32),
        pltpu.VMEM((4, 8, D), F32),
        pltpu.VMEM((CHIPS, 8, D), F32),
        dma((6,)),
        dma((9,)),
        dma((9,)),
        dma((CHIPS, 2, 2)),
        dma((CHIPS, 2, 2)),
        dma((CHIPS, SEQS, 2)),
        dma((CHIPS, SEQS, 2)),
        dma((NCH, 3)),
        dma((NCH, 3)),
        dma((NCH, 3)),
        dma((NCH, 3)),
        dma((NCH,)),
        dma((NCH,)),
        dma((NCH,)),
        dma((2, 3)),
        dma((2, 3)),
        dma((10,)),
        dma((11,)),
    ]
    mixed, tokens_grad, small, dn, up, qkv, out_t = pl.pallas_call(
        fused_kernel,
        out_shape=(
            jax.ShapeDtypeStruct((ROWS, D), BF16),
            jax.ShapeDtypeStruct((ROWS, D), BF16),
            jax.ShapeDtypeStruct((8, D), F32),
            jax.ShapeDtypeStruct((2, 2, 2, 2, 128, D), BF16),
            jax.ShapeDtypeStruct((2, 2, 2, 128, FF // FSDP), BF16),
            jax.ShapeDtypeStruct((2, 2, 2, 128, 3 * D // FSDP), BF16),
            jax.ShapeDtypeStruct((2, 2, 2, 128, D // FSDP), BF16),
        ),
        in_specs=[sme] + [vm] * 4 + [hbm, vm, vm] + [hbm] * 4,
        out_specs=(vm, vm, vm, hbm, hbm, hbm, hbm),
        scratch_shapes=scratch,
        compiler_params=pltpu.CompilerParams(
            collective_id=0, has_side_effects=True, vmem_limit_bytes=63 * 2**20
        ),
    )(
        block_pairs,
        norm_gain,
        norm_bias,
        down_bias,
        up_bias,
        jnp.asarray(turn_table()),
        tokens,
        cotangent,
        qkv_weight,
        out_weight,
        up_weight,
        down_weight,
    )
    dn, up, qkv, out, mixed, tokens_grad, gain, shift, upb, downb = widen(
        dn, up, qkv, out_t, small, mixed, tokens_grad
    )
    return mixed, tokens_grad, gain, shift, qkv, out, up, upb, dn, downb


def solution(mesh):
    in_specs = (
        P(("fsdp", "ctx"), None),
        P(),
        P("fsdp"),
        P("fsdp"),
        P(None, "fsdp"),
        P("fsdp", None),
        P(None, "fsdp"),
        P("fsdp"),
        P("fsdp", None),
        P("fsdp"),
        P(("fsdp", "ctx"), None),
    )
    out_specs = (
        P(("fsdp", "ctx"), None),
        P(("fsdp", "ctx"), None),
        P("fsdp"),
        P("fsdp"),
        P(None, "fsdp"),
        P("fsdp", None),
        P(None, "fsdp"),
        P("fsdp"),
        P("fsdp", None),
        P("fsdp"),
    )
    plan = fused_device if fits(mesh) else per_device
    return jax.shard_map(
        plan, mesh=mesh, in_specs=in_specs, out_specs=out_specs, check_vma=False
    )
```
